32 devices in a mesh: rep: 2 (over y), tp: 16 (over z, x, core).
Axes of the slice: x: 2, y: 2, z: 4, core: 2. Of those that a mesh axis runs over, the one named last changes fastest.
Arguments:
- hidden: bfloat16 [192, 28672], P('rep', 'tp'), parts along dimension 0, may hold values from -6 to 6
- down_matrix: bfloat16 [28672, 8192], P('tp'), may hold values from -0.046875 to 0.046875
- shrink_matrices: bfloat16 [32, 28672, 64], P(('rep', 'tp')), parts along dimension 0, may hold values from -0.03125 to 0.03125
- expand_matrices: bfloat16 [32, 8192, 64], P(('rep', 'tp')), parts along dimension 0, may hold values from -0.75 to 0.75
- adapter_of_row: int32 [192], P('rep'), parts along dimension 0, may hold values from 0 to 15, as said below
- adapter_holder_slot: int32 [32], P('rep'), parts along dimension 0, may hold values from 0 to 15, each once
Outputs:
- projected: bfloat16 [192, 8192], P('rep', 'tp'), parts along dimension 0
The draws below stay inside these ranges and needn't reach their ends.
There are 2 independent parts, one for each index of `rep`. The reference program is written for one: setup_inputs(seed, part) draws one part's arguments, and reference() takes and returns one part's arrays. A program takes and returns all parts, laid end to end along the dimension named above; an argument that names none is the same for every part. Nothing has to cross between parts.
Inputs may be any that keep to these rules, and one draw needn't show every extreme that they name: `adapter_of_row`: rows come in aligned blocks of 4 rows that share one adapter; adapter numbers never fall along the rows; every adapter has rows, no adapter has more than 20, and some adapter has exactly 20. `adapter_holder_slot`: each device of tp holds exactly one adapter.
All inputs are finite; a program needn't handle non-finite values.
Results may differ from the reference program's by a relative error of at most 0.0027.
Values may be sent and summed in bfloat16 or wider, within the bound.
No kernel may reach another device: no remote copies, remote signals or barrier semaphores. Data moves between devices by JAX's collectives and lax.ppermute only.
A program may use at most 128 MiB of HBM per device.

```python
import jax
import jax.numpy as jnp
from jax import lax

MODEL_WIDTH = 8192
HIDDEN_WIDTH = 28672
ADAPTER_RANK = 64
BLOCK = 4
ROWS = 96
REPLICA_ADAPTERS = 16
MOST = 20


def draw_adapter_of_row(key, part):
    key = jax.random.fold_in(key, 11)
    first_key, second_key = jax.random.split(key)
    block_count = ROWS // BLOCK
    most_blocks = MOST // BLOCK
    spare = most_blocks - 2
    order = jax.random.permutation(first_key, REPLICA_ADAPTERS)
    busiest = order[0]
    leftover = block_count - REPLICA_ADAPTERS - (most_blocks - 1)
    places = jax.random.permutation(second_key, (REPLICA_ADAPTERS - 1) * spare)[:leftover]
    others = order[1 + places // spare]
    every_one = jnp.arange(REPLICA_ADAPTERS, dtype=jnp.int32)
    heavy = jnp.full((most_blocks - 1,), busiest, dtype=jnp.int32)
    block_ids = jnp.sort(jnp.concatenate([every_one, heavy, others.astype(jnp.int32)]))
    return jnp.repeat(block_ids, BLOCK).astype(jnp.int32)


def raised(drawn, key, source, target, parts, factor):
    def block_of(axis_at):
        return (jnp.arange(drawn.shape[axis_at]) // (drawn.shape[axis_at] // parts)).reshape((-1,) + (1,) * (drawn.ndim - 1 - axis_at))

    first = jax.random.permutation(key, parts)[block_of(target)]
    far = (block_of(target) + parts // 2) % parts
    return jnp.where((block_of(source) == first) | (block_of(source) == far), factor * drawn, drawn)


def levels(rng, shape, shards, least, high):
    def one(dim, parts):
        heights = jax.random.uniform(jax.random.fold_in(jax.random.fold_in(rng, 6), dim), (parts,), jnp.float32, least / len(shards), high / len(shards))
        return jnp.repeat(jnp.exp(heights), shape[dim] // parts).reshape((-1,) + (1,) * (len(shape) - dim - 1))

    factor_of = one(*shards[0])
    for cut in shards[1:]:
        factor_of = factor_of * one(*cut)
    return factor_of


def normal_values(key, dims, spread, most, cuts=(), kind=jnp.bfloat16):
    gain = levels(key, dims, cuts, -0.22, 0.18) if cuts else 1.0
    values = jax.random.normal(key, dims, jnp.float32) * spread * gain
    return jnp.minimum(jnp.maximum(values, -most), most).astype(kind)


def noise_with(key, shape, spread, bound, cuts, heavy, held_as=jnp.bfloat16):
    result = spread * jax.random.normal(key, shape, jnp.float32)
    if cuts:
        result = result * levels(key, shape, cuts, -0.22, 0.18)
    return jnp.clip(raised(result, jax.random.fold_in(key, 3), *heavy), -bound, bound).astype(held_as)


def setup_inputs(seed: int = 0, part: int = 0) -> dict:
    seeds = jax.random.split(jax.random.key(seed), 7)
    part_splits = jax.random.split(jax.random.fold_in(seeds[6], part), 7)
    return {
        "hidden": normal_values(part_splits[0], (ROWS, HIDDEN_WIDTH), 1.0, 6.0, ((1, 16),)),
        "down_matrix": noise_with(seeds[1], (HIDDEN_WIDTH, MODEL_WIDTH), HIDDEN_WIDTH ** -0.5, 0.046875, ((0, 16),), (0, 1, 16, 2.0)),
        "shrink_matrices": normal_values(part_splits[2], (REPLICA_ADAPTERS, HIDDEN_WIDTH, ADAPTER_RANK), HIDDEN_WIDTH ** -0.5, 0.03125, ((0, 16),)),
        "expand_matrices": normal_values(part_splits[3], (REPLICA_ADAPTERS, MODEL_WIDTH, ADAPTER_RANK), ADAPTER_RANK ** -0.5, 0.75, ((0, 16),)),
        "adapter_of_row": draw_adapter_of_row(jax.random.fold_in(jax.random.fold_in(seeds[6], part), 71), part),
        "adapter_holder_slot": jax.random.permutation(part_splits[5], REPLICA_ADAPTERS).astype(jnp.int32),
    }


ADAPTER_SCALE = 0.5


def reference(hidden, down_matrix, shrink_matrices, expand_matrices, adapter_of_row, adapter_holder_slot):
    base_partial_sum = jnp.dot(hidden, down_matrix, preferred_element_type=jnp.float32)
    row_slot = adapter_holder_slot[adapter_of_row].astype(jnp.int32)
    blocks = hidden.shape[0] // BLOCK
    block_slot = row_slot.reshape(blocks, BLOCK)[:, 0]
    hidden_blocks = hidden.reshape(blocks, BLOCK, hidden.shape[1])

    def one_block(block_item):
        block_rows, current_slot = block_item
        shrink_result = lax.dynamic_index_in_dim(shrink_matrices, current_slot, 0, keepdims=False)
        expand_result = lax.dynamic_index_in_dim(expand_matrices, current_slot, 0, keepdims=False)
        rank_rows = jnp.dot(block_rows, shrink_result, preferred_element_type=jnp.float32).astype(jnp.bfloat16)
        return lax.dot_general(rank_rows, expand_result, (((1,), (1,)), ((), ())), preferred_element_type=jnp.float32)

    adapter_result = lax.map(one_block, (hidden_blocks, block_slot))
    reduced_output = base_partial_sum + ADAPTER_SCALE * adapter_result.reshape(base_partial_sum.shape)
    return reduced_output.astype(jnp.bfloat16)
```

```python
import functools

import jax
import jax.numpy as jnp
from jax import lax
from jax.experimental import pallas as pl
from jax.experimental.pallas import tpu as pltpu
from jax.sharding import PartitionSpec as P

ADAPTER_SCALE = 0.5
BLOCK = 4
MOST = 20
LANES = 128
F16_TOP = 14.0


def xor_permute(value, group, offset):
    return lax.ppermute(value, "tp", [(i, i ^ offset) for i in range(group)])


def column_blocks_kernel(order_ref, hidden_ref, down_ref, out_ref):
    product = jnp.dot(hidden_ref[...], down_ref[...], preferred_element_type=jnp.float32)
    for lane in range(out_ref.shape[0]):
        out_ref[lane] = product[:, lane * LANES : (lane + 1) * LANES]


def column_blocks(hidden, down_matrix, order, width):
    rows, depth = hidden.shape
    count = order.shape[0]
    parts = width // LANES
    return pl.pallas_call(
        column_blocks_kernel,
        out_shape=jax.ShapeDtypeStruct((count * parts, rows, LANES), jnp.float32),
        grid_spec=pltpu.PrefetchScalarGridSpec(
            num_scalar_prefetch=1,
            grid=(count,),
            in_specs=[
                pl.BlockSpec((rows, depth), lambda j, order_ref: (0, 0)),
                pl.BlockSpec((depth, width), lambda j, order_ref: (0, order_ref[j])),
            ],
            out_specs=pl.BlockSpec((parts, rows, LANES), lambda j, order_ref: (j, 0, 0)),
        ),
        compiler_params=pltpu.CompilerParams(vmem_limit_bytes=40 * 2**20),
        cost_estimate=pl.CostEstimate(
            flops=2 * rows * depth * width * count,
            bytes_accessed=2 * depth * width * count + 4 * rows * width * count,
            transcendentals=0,
        ),
    )(order, hidden, down_matrix)


def pack_scaled(value):
    peak = jnp.max(jnp.abs(value), axis=(0, 2), keepdims=True)
    exponent = jnp.ceil(jnp.log2(jnp.maximum(peak, 2.0**-100)))
    scaled = (value * jnp.exp2(F16_TOP - exponent)).astype(jnp.float16)
    marks = jnp.broadcast_to(exponent, (1,) + value.shape[1:]).astype(jnp.float16)
    return jnp.concatenate([scaled, marks], axis=0)


def unpack_scaled(packed):
    exponent = packed[-1:].astype(jnp.float32)
    return packed[:-1].astype(jnp.float32) * jnp.exp2(exponent - F16_TOP)


def base_blocks(hidden, down_matrix, group, me, width):
    rows = hidden.shape[0]
    parts = width // LANES
    quads = list(range(0, group, 4))
    odd_order = [q + 1 for q in quads] + [q + 3 for q in quads]
    even_order = quads + [q + 2 for q in quads]
    odd = column_blocks(hidden, down_matrix, me ^ jnp.array(odd_order, jnp.int32), width)
    odd_in = xor_permute(odd, group, 1)
    even = column_blocks(hidden, down_matrix, me ^ jnp.array(even_order, jnp.int32), width)
    chip = even + odd_in
    half = len(quads) * parts
    pair_in = xor_permute(pack_scaled(chip[half:]), group, 2)
    pair = chip[:half] + unpack_scaled(pair_in)
    total = pair[:parts]
    arrived = [
        xor_permute(pack_scaled(pair[i * parts : (i + 1) * parts]), group, quads[i])
        for i in range(1, len(quads))
    ]
    for packed in arrived:
        total = total + unpack_scaled(packed)
    return jnp.transpose(total, (1, 0, 2)).reshape(rows, width)


def shards(
    hidden, down_matrix, shrink_matrices, expand_matrices, adapter_of_row, adapter_holder_slot
):
    group = lax.axis_size("tp")
    me = lax.axis_index("tp")
    rows, depth = hidden.shape
    model_width = down_matrix.shape[1]
    width = model_width // group
    rank = shrink_matrices.shape[2]
    blocks = MOST // BLOCK
    adapter_ids = jnp.arange(group, dtype=jnp.int32)

    row_match = adapter_of_row[:, None] == adapter_ids[None, :]
    row_slot = jnp.sum(jnp.where(row_match, adapter_holder_slot[None, :], 0), axis=1)
    slot_mask = row_slot[None, :] == adapter_ids[:, None]
    before = jnp.cumsum(slot_mask.astype(jnp.int32), axis=1) - 1
    place = jnp.where(slot_mask, before, -1)
    pick = place[:, None, :] == jnp.arange(MOST, dtype=jnp.int32)[None, :, None]
    pick = pick.reshape(group * MOST, rows)
    pick16 = pick.astype(jnp.bfloat16)

    packed = jnp.dot(pick16, hidden, preferred_element_type=jnp.float32).astype(jnp.bfloat16)
    packed = packed.reshape(group * blocks, BLOCK, depth)
    gathered = lax.all_to_all(packed, "tp", split_axis=0, concat_axis=0, tiled=True)

    if width % LANES == 0 and depth % LANES == 0:
        base = base_blocks(hidden, down_matrix, group, me, width)
    else:
        partial_value = jnp.dot(hidden, down_matrix, preferred_element_type=jnp.float32)
        base = lax.psum_scatter(partial_value, "tp", scatter_dimension=1, tiled=True)

    gathered = gathered.reshape(group, MOST, depth)
    shrink_parts = shrink_matrices.reshape(group, depth, rank)
    rank_rows = lax.dot_general(
        jnp.transpose(gathered, (1, 0, 2)).reshape(MOST, group * depth),
        shrink_matrices[0],
        (((1,), (0,)), ((), ())),
        preferred_element_type=jnp.float32,
    ).astype(jnp.bfloat16)
    adapter_out = lax.dot_general(
        rank_rows, expand_matrices[0], (((1,), (1,)), ((), ())), preferred_element_type=jnp.float32
    ).astype(jnp.bfloat16)
    adapter_out = jnp.transpose(adapter_out.reshape(blocks, BLOCK, group, width), (2, 0, 1, 3))
    adapter_in = lax.all_to_all(
        adapter_out.reshape(group * blocks, BLOCK, width), "tp", split_axis=0, concat_axis=0, tiled=True
    )
    adapter_rows = lax.dot_general(
        pick16,
        adapter_in.reshape(group * MOST, width),
        (((0,), (0,)), ((), ())),
        preferred_element_type=jnp.float32,
    )
    return (base + ADAPTER_SCALE * adapter_rows).astype(jnp.bfloat16)


def solution(mesh):
    in_specs = (
        P("rep", "tp"),
        P("tp", None),
        P(("rep", "tp"), None, None),
        P(("rep", "tp"), None, None),
        P("rep"),
        P("rep"),
    )
    out_specs = P("rep", "tp")
    return jax.shard_map(shards, mesh=mesh, in_specs=in_specs, out_specs=out_specs, check_vma=False)
```

```python
import functools

import jax
import jax.numpy as jnp
from jax import lax
from jax.experimental import pallas as pl
from jax.experimental.pallas import tpu as pltpu
from jax.sharding import PartitionSpec as P

ADAPTER_SCALE = 0.5
BLOCK = 4
MOST = 20
LANES = 128
F16_TOP = 14.0


def xor_permute(value, group, offset):
    return lax.ppermute(value, "tp", [(i, i ^ offset) for i in range(group)])


def column_blocks_kernel(order_ref, hidden_ref, down_ref, out_ref):
    product = jnp.dot(hidden_ref[...], down_ref[...], preferred_element_type=jnp.float32)
    for lane in range(out_ref.shape[0]):
        out_ref[lane] = product[:, lane * LANES : (lane + 1) * LANES]


def column_blocks(hidden, down_matrix, order, width):
    rows, depth = hidden.shape
    count = order.shape[0]
    parts = width // LANES
    return pl.pallas_call(
        column_blocks_kernel,
        out_shape=jax.ShapeDtypeStruct((count * parts, rows, LANES), jnp.float32),
        grid_spec=pltpu.PrefetchScalarGridSpec(
            num_scalar_prefetch=1,
            grid=(count,),
            in_specs=[
                pl.BlockSpec((rows, depth), lambda j, order_ref: (0, 0)),
                pl.BlockSpec((depth, width), lambda j, order_ref: (0, order_ref[j])),
            ],
            out_specs=pl.BlockSpec((parts, rows, LANES), lambda j, order_ref: (j, 0, 0)),
        ),
        compiler_params=pltpu.CompilerParams(vmem_limit_bytes=40 * 2**20),
        cost_estimate=pl.CostEstimate(
            flops=2 * rows * depth * width * count,
            bytes_accessed=2 * depth * width * count + 4 * rows * width * count,
            transcendentals=0,
        ),
    )(order, hidden, down_matrix)


def pack_scaled(value):
    peak = jnp.max(jnp.abs(value), axis=(0, 2), keepdims=True)
    exponent = jnp.ceil(jnp.log2(jnp.maximum(peak, 2.0**-100)))
    scaled = (value * jnp.exp2(F16_TOP - exponent)).astype(jnp.float16)
    marks = jnp.broadcast_to(exponent, (1,) + value.shape[1:]).astype(jnp.float16)
    return jnp.concatenate([scaled, marks], axis=0)


def unpack_scaled(packed):
    exponent = packed[-1:].astype(jnp.float32)
    return packed[:-1].astype(jnp.float32) * jnp.exp2(exponent - F16_TOP)


def base_blocks(hidden, down_matrix, group, order, width):
    rows = hidden.shape[0]
    parts = width // LANES
    quads = list(range(0, group, 4))
    odd = column_blocks(hidden, down_matrix, order[: group // 2], width)
    odd_in = xor_permute(odd, group, 1)
    even = column_blocks(hidden, down_matrix, order[group // 2 :], width)
    chip = even + odd_in
    half = len(quads) * parts
    pair_in = xor_permute(pack_scaled(chip[half:]), group, 2)
    pair = chip[:half] + unpack_scaled(pair_in)
    total = pair[:parts]
    arrived = [
        xor_permute(pack_scaled(pair[i * parts : (i + 1) * parts]), group, quads[i])
        for i in range(1, len(quads))
    ]
    for packed in arrived:
        total = total + unpack_scaled(packed)
    return jnp.transpose(total, (1, 0, 2)).reshape(rows, width)


def pack_kernel(blocks, orders, me_ref, slot_ref, adapter_ref, hidden_ref, packed_ref, pick_ref, order_ref):
    rows = hidden_ref.shape[0]
    group = slot_ref.shape[0]
    for i, offset in enumerate(orders):
        order_ref[i] = me_ref[0] ^ offset
    ids = lax.broadcasted_iota(jnp.int32, (group, 1), 0)
    slots = jnp.zeros((group, 1), jnp.int32)
    for adapter in range(group):
        slots = jnp.where(ids == adapter, slot_ref[adapter], slots)
    adapter = adapter_ref[...]
    first = jnp.sum((adapter < ids).astype(jnp.int32), axis=1, keepdims=True)
    shift = jnp.where(adapter == ids, slots * (blocks * BLOCK) - first, 0)
    place = jnp.sum(shift, axis=0, keepdims=True) + lax.broadcasted_iota(jnp.int32, (1, rows), 1)
    spots = lax.broadcasted_iota(jnp.int32, (group * blocks * BLOCK, rows), 0)
    pick = jnp.where(spots == place, 1.0, 0.0).astype(jnp.bfloat16)
    pick_ref[...] = pick
    packed = jnp.dot(pick, hidden_ref[...], preferred_element_type=jnp.float32)
    packed_ref[...] = packed.astype(jnp.bfloat16).reshape(packed_ref.shape)


def pack_rows(hidden, adapter_of_row, adapter_holder_slot, me, orders):
    rows, depth = hidden.shape
    group = adapter_holder_slot.shape[0]
    blocks = MOST // BLOCK
    vmem = pl.BlockSpec(memory_space=pltpu.VMEM)
    smem = pl.BlockSpec(memory_space=pltpu.SMEM)
    return pl.pallas_call(
        functools.partial(pack_kernel, blocks, orders),
        out_shape=(
            jax.ShapeDtypeStruct((group * blocks, BLOCK, depth), jnp.bfloat16),
            jax.ShapeDtypeStruct((group * MOST, rows), jnp.bfloat16),
            jax.ShapeDtypeStruct((len(orders),), jnp.int32),
        ),
        in_specs=[smem, smem, vmem, vmem],
        out_specs=(vmem, vmem, smem),
        compiler_params=pltpu.CompilerParams(vmem_limit_bytes=24 * 2**20),
    )(me.reshape(1), adapter_holder_slot, adapter_of_row.reshape(1, rows), hidden)


def adapter_kernel(rows_ref, shrink_ref, expand_ref, out_ref, total_ref):
    step = pl.program_id(0)
    block, depth = rows_ref.shape[1:]
    blocks = MOST // BLOCK
    sources = rows_ref.shape[0] // blocks
    total = jnp.zeros(total_ref.shape, jnp.float32)
    for source in range(sources):
        own = rows_ref[source * blocks : (source + 1) * blocks].reshape(MOST, depth)
        total += lax.dot_general(
            own,
            shrink_ref[:, source * depth : (source + 1) * depth],
            (((1,), (1,)), ((), ())),
            preferred_element_type=jnp.float32,
        )

    @pl.when(step == 0)
    def _():
        total_ref[...] = total

    @pl.when(step > 0)
    def _():
        total_ref[...] += total

    @pl.when(step == pl.num_programs(0) - 1)
    def _():
        rank_rows = total_ref[...].astype(jnp.bfloat16)
        width = out_ref.shape[2]
        for target in range(out_ref.shape[0] // blocks):
            piece = jnp.dot(
                rank_rows,
                expand_ref[:, target * width : (target + 1) * width],
                preferred_element_type=jnp.float32,
            )
            out_ref[target * blocks : (target + 1) * blocks] = piece.astype(jnp.bfloat16).reshape(
                blocks, BLOCK, width
            )


def adapter_output(gathered, shrink, expand, group):
    rank, hidden_width = shrink.shape
    model_width = expand.shape[1]
    depth = gathered.shape[2]
    blocks = MOST // BLOCK
    width = model_width // group
    steps = 4
    sources = group // steps
    return pl.pallas_call(
        adapter_kernel,
        out_shape=jax.ShapeDtypeStruct((group * blocks, BLOCK, width), jnp.bfloat16),
        grid=(steps,),
        in_specs=[
            pl.BlockSpec((sources * blocks, BLOCK, depth), lambda i: (i, 0, 0)),
            pl.BlockSpec((rank, sources * depth), lambda i: (0, i)),
            pl.BlockSpec((rank, model_width), lambda i: (0, 0)),
        ],
        out_specs=pl.BlockSpec((group * blocks, BLOCK, width), lambda i: (0, 0, 0)),
        scratch_shapes=[pltpu.VMEM((MOST, rank), jnp.float32)],
        compiler_params=pltpu.CompilerParams(vmem_limit_bytes=32 * 2**20),
        cost_estimate=pl.CostEstimate(
            flops=2 * MOST * rank * (hidden_width + model_width),
            bytes_accessed=2 * rank * (hidden_width + model_width) + 2 * MOST * hidden_width,
            transcendentals=0,
        ),
    )(gathered, shrink, expand)


def shards_by_blocks(
    hidden, down_matrix, shrink_matrices, expand_matrices, adapter_of_row, adapter_holder_slot
):
    group = lax.axis_size("tp")
    me = lax.axis_index("tp")
    rows, depth = hidden.shape
    width = down_matrix.shape[1] // group
    quads = list(range(0, group, 4))
    orders = [q + k for k in (1, 3, 0, 2) for q in quads]
    packed, pick, order = pack_rows(hidden, adapter_of_row, adapter_holder_slot, me, orders)
    gathered = lax.all_to_all(packed, "tp", split_axis=0, concat_axis=0, tiled=True)
    base = base_blocks(hidden, down_matrix, group, order, width)
    shrink = jnp.swapaxes(shrink_matrices, 1, 2)[0]
    expand = jnp.swapaxes(expand_matrices, 1, 2)[0]
    adapter_out = adapter_output(gathered, shrink, expand, group)
    adapter_in = lax.all_to_all(adapter_out, "tp", split_axis=0, concat_axis=0, tiled=True)
    adapter_rows = lax.dot_general(
        pick,
        adapter_in.reshape(group * MOST, width),
        (((0,), (0,)), ((), ())),
        preferred_element_type=jnp.float32,
    )
    return (base + ADAPTER_SCALE * adapter_rows).astype(jnp.bfloat16)


def shards(
    hidden, down_matrix, shrink_matrices, expand_matrices, adapter_of_row, adapter_holder_slot
):
    group = lax.axis_size("tp")
    rows, depth = hidden.shape
    width = down_matrix.shape[1] // group
    if width % LANES == 0 and depth % LANES == 0 and group % 4 == 0:
        return shards_by_blocks(
            hidden, down_matrix, shrink_matrices, expand_matrices, adapter_of_row, adapter_holder_slot
        )
    blocks = MOST // BLOCK
    adapter_ids = jnp.arange(group, dtype=jnp.int32)
    row_match = adapter_of_row[:, None] == adapter_ids[None, :]
    row_slot = jnp.sum(jnp.where(row_match, adapter_holder_slot[None, :], 0), axis=1)
    slot_mask = row_slot[None, :] == adapter_ids[:, None]
    before = jnp.cumsum(slot_mask.astype(jnp.int32), axis=1) - 1
    place = jnp.where(slot_mask, before, -1)
    pick = place[:, None, :] == jnp.arange(MOST, dtype=jnp.int32)[None, :, None]
    pick = pick.reshape(group * MOST, rows).astype(jnp.bfloat16)
    packed = jnp.dot(pick, hidden, preferred_element_type=jnp.float32).astype(jnp.bfloat16)
    packed = packed.reshape(group * blocks, BLOCK, depth)
    gathered = lax.all_to_all(packed, "tp", split_axis=0, concat_axis=0, tiled=True)
    partial_value = jnp.dot(hidden, down_matrix, preferred_element_type=jnp.float32)
    base = lax.psum_scatter(partial_value, "tp", scatter_dimension=1, tiled=True)
    own_rows = jnp.transpose(gathered.reshape(group, MOST, depth), (1, 0, 2))
    rank_rows = jnp.dot(
        own_rows.reshape(MOST, group * depth), shrink_matrices[0], preferred_element_type=jnp.float32
    ).astype(jnp.bfloat16)
    adapter_out = lax.dot_general(
        rank_rows, expand_matrices[0], (((1,), (1,)), ((), ())), preferred_element_type=jnp.float32
    ).astype(jnp.bfloat16)
    adapter_out = jnp.transpose(adapter_out.reshape(blocks, BLOCK, group, width), (2, 0, 1, 3))
    adapter_in = lax.all_to_all(
        adapter_out.reshape(group * blocks, BLOCK, width), "tp", split_axis=0, concat_axis=0, tiled=True
    )
    adapter_rows = lax.dot_general(
        pick,
        adapter_in.reshape(group * MOST, width),
        (((0,), (0,)), ((), ())),
        preferred_element_type=jnp.float32,
    )
    return (base + ADAPTER_SCALE * adapter_rows).astype(jnp.bfloat16)


def solution(mesh):
    in_specs = (
        P("rep", "tp"),
        P("tp", None),
        P(("rep", "tp"), None, None),
        P(("rep", "tp"), None, None),
        P("rep"),
        P("rep"),
    )
    out_specs = P("rep", "tp")
    return jax.shard_map(shards, mesh=mesh, in_specs=in_specs, out_specs=out_specs, check_vma=False)
```

```python
import functools

import jax
import jax.numpy as jnp
from jax import lax
from jax.experimental import pallas as pl
from jax.experimental.pallas import tpu as pltpu
from jax.sharding import PartitionSpec as P

ADAPTER_SCALE = 0.5
BLOCK = 4
MOST = 20
LANES = 128
F16_TOP = 14.0


def xor_permute(value, group, offset):
    return lax.ppermute(value, "tp", [(i, i ^ offset) for i in range(group)])


def column_blocks_kernel(order_ref, hidden_ref, down_ref, out_ref, held_ref, sems):
    count, depth, width = held_ref.shape
    parts = width // LANES
    pieces = sems.shape[1]
    cut = depth // pieces

    def copy(block, piece):
        start = pl.multiple_of(order_ref[block] * width, LANES)
        lines = pl.ds(piece * cut, cut)
        return pltpu.make_async_copy(
            down_ref.at[lines, pl.ds(start, width)], held_ref.at[block, lines], sems.at[block, piece]
        )

    for block in range(count):
        for piece in range(pieces):
            copy(block, piece).start()
    for block in range(count):
        for piece in range(pieces):
            copy(block, piece).wait()
        product = jnp.dot(hidden_ref[...], held_ref[block], preferred_element_type=jnp.float32)
        for lane in range(parts):
            out_ref[block * parts + lane] = product[:, lane * LANES : (lane + 1) * LANES]


def column_blocks(hidden, down_matrix, order, width):
    rows, depth = hidden.shape
    count = order.shape[0]
    pieces = 2 if depth % 32 == 0 else 1
    vmem = pl.BlockSpec(memory_space=pltpu.VMEM)
    return pl.pallas_call(
        column_blocks_kernel,
        out_shape=jax.ShapeDtypeStruct((count * width // LANES, rows, LANES), jnp.float32),
        in_specs=[
            pl.BlockSpec(memory_space=pltpu.SMEM),
            vmem,
            pl.BlockSpec(memory_space=pl.ANY),
        ],
        out_specs=vmem,
        scratch_shapes=[
            pltpu.VMEM((count, depth, width), jnp.bfloat16),
            pltpu.SemaphoreType.DMA((count, pieces)),
        ],
        compiler_params=pltpu.CompilerParams(vmem_limit_bytes=40 * 2**20),
    )(order, hidden, down_matrix)


def pack_scaled(value):
    peak = jnp.max(jnp.abs(value), axis=(0, 2), keepdims=True)
    exponent = jnp.ceil(jnp.log2(jnp.maximum(peak, 2.0**-100)))
    scaled = (value * jnp.exp2(F16_TOP - exponent)).astype(jnp.float16)
    marks = jnp.broadcast_to(exponent, (1,) + value.shape[1:]).astype(jnp.float16)
    return jnp.concatenate([scaled, marks], axis=0)


def unpack_scaled(packed):
    exponent = packed[-1:].astype(jnp.float32)
    return packed[:-1].astype(jnp.float32) * jnp.exp2(exponent - F16_TOP)


def base_blocks(hidden, down_matrix, group, order, width):
    rows = hidden.shape[0]
    parts = width // LANES
    quads = list(range(0, group, 4))
    odd = column_blocks(hidden, down_matrix, order[: group // 2], width)
    odd_in = xor_permute(odd, group, 1)
    even = column_blocks(hidden, down_matrix, order[group // 2 :], width)
    chip = even + odd_in
    half = len(quads) * parts
    pair_in = xor_permute(pack_scaled(chip[half:]), group, 2)
    pair = chip[:half] + unpack_scaled(pair_in)
    total = pair[:parts]
    arrived = [
        xor_permute(pack_scaled(pair[i * parts : (i + 1) * parts]), group, quads[i])
        for i in range(1, len(quads))
    ]
    for packed in arrived:
        total = total + unpack_scaled(packed)
    return jnp.transpose(total, (1, 0, 2)).reshape(rows, width)


def pack_kernel(blocks, orders, me_ref, slot_ref, adapter_ref, hidden_ref, packed_ref, pick_ref, order_ref):
    rows = hidden_ref.shape[0]
    group = slot_ref.shape[0]
    for i, offset in enumerate(orders):
        order_ref[i] = me_ref[0] ^ offset
    ids = lax.broadcasted_iota(jnp.int32, (group, 1), 0)
    slots = jnp.zeros((group, 1), jnp.int32)
    for adapter in range(group):
        slots = jnp.where(ids == adapter, slot_ref[adapter], slots)
    adapter = adapter_ref[...]
    first = jnp.sum((adapter < ids).astype(jnp.int32), axis=1, keepdims=True)
    shift = jnp.where(adapter == ids, slots * (blocks * BLOCK) - first, 0)
    place = jnp.sum(shift, axis=0, keepdims=True) + lax.broadcasted_iota(jnp.int32, (1, rows), 1)
    spots = lax.broadcasted_iota(jnp.int32, (group * blocks * BLOCK, rows), 0)
    pick = jnp.where(spots == place, 1.0, 0.0).astype(jnp.bfloat16)
    pick_ref[...] = pick
    packed = jnp.dot(pick, hidden_ref[...], preferred_element_type=jnp.float32)
    packed_ref[...] = packed.astype(jnp.bfloat16).reshape(packed_ref.shape)


def pack_rows(hidden, adapter_of_row, adapter_holder_slot, me, orders):
    rows, depth = hidden.shape
    group = adapter_holder_slot.shape[0]
    blocks = MOST // BLOCK
    vmem = pl.BlockSpec(memory_space=pltpu.VMEM)
    smem = pl.BlockSpec(memory_space=pltpu.SMEM)
    return pl.pallas_call(
        functools.partial(pack_kernel, blocks, orders),
        out_shape=(
            jax.ShapeDtypeStruct((group * blocks, BLOCK, depth), jnp.bfloat16),
            jax.ShapeDtypeStruct((group * MOST, rows), jnp.bfloat16),
            jax.ShapeDtypeStruct((len(orders),), jnp.int32),
        ),
        in_specs=[smem, smem, vmem, vmem],
        out_specs=(vmem, vmem, smem),
        compiler_params=pltpu.CompilerParams(vmem_limit_bytes=24 * 2**20),
    )(me.reshape(1), adapter_holder_slot, adapter_of_row.reshape(1, rows), hidden)


def adapter_kernel(rows_ref, shrink_ref, expand_ref, out_ref, total_ref):
    step = pl.program_id(0)
    block, depth = rows_ref.shape[1:]
    blocks = MOST // BLOCK
    sources = rows_ref.shape[0] // blocks
    total = jnp.zeros(total_ref.shape, jnp.float32)
    for source in range(sources):
        own = rows_ref[source * blocks : (source + 1) * blocks].reshape(MOST, depth)
        total += lax.dot_general(
            own,
            shrink_ref[:, source * depth : (source + 1) * depth],
            (((1,), (1,)), ((), ())),
            preferred_element_type=jnp.float32,
        )

    @pl.when(step == 0)
    def _():
        total_ref[...] = total

    @pl.when(step > 0)
    def _():
        total_ref[...] += total

    @pl.when(step == pl.num_programs(0) - 1)
    def _():
        rank_rows = total_ref[...].astype(jnp.bfloat16)
        width = out_ref.shape[2]
        for target in range(out_ref.shape[0] // blocks):
            piece = jnp.dot(
                rank_rows,
                expand_ref[:, target * width : (target + 1) * width],
                preferred_element_type=jnp.float32,
            )
            out_ref[target * blocks : (target + 1) * blocks] = piece.astype(jnp.bfloat16).reshape(
                blocks, BLOCK, width
            )


def adapter_output(gathered, shrink, expand, group):
    rank, hidden_width = shrink.shape
    model_width = expand.shape[1]
    depth = gathered.shape[2]
    blocks = MOST // BLOCK
    width = model_width // group
    steps = 4
    sources = group // steps
    return pl.pallas_call(
        adapter_kernel,
        out_shape=jax.ShapeDtypeStruct((group * blocks, BLOCK, width), jnp.bfloat16),
        grid=(steps,),
        in_specs=[
            pl.BlockSpec((sources * blocks, BLOCK, depth), lambda i: (i, 0, 0)),
            pl.BlockSpec((rank, sources * depth), lambda i: (0, i)),
            pl.BlockSpec((rank, model_width), lambda i: (0, 0)),
        ],
        out_specs=pl.BlockSpec((group * blocks, BLOCK, width), lambda i: (0, 0, 0)),
        scratch_shapes=[pltpu.VMEM((MOST, rank), jnp.float32)],
        compiler_params=pltpu.CompilerParams(vmem_limit_bytes=32 * 2**20),
        cost_estimate=pl.CostEstimate(
            flops=2 * MOST * rank * (hidden_width + model_width),
            bytes_accessed=2 * rank * (hidden_width + model_width) + 2 * MOST * hidden_width,
            transcendentals=0,
        ),
    )(gathered, shrink, expand)


def shards_by_blocks(
    hidden, down_matrix, shrink_matrices, expand_matrices, adapter_of_row, adapter_holder_slot
):
    group = lax.axis_size("tp")
    me = lax.axis_index("tp")
    rows, depth = hidden.shape
    width = down_matrix.shape[1] // group
    quads = list(range(0, group, 4))
    orders = [q + k for k in (1, 3, 0, 2) for q in quads]
    packed, pick, order = pack_rows(hidden, adapter_of_row, adapter_holder_slot, me, orders)
    gathered = lax.all_to_all(packed, "tp", split_axis=0, concat_axis=0, tiled=True)
    base = base_blocks(hidden, down_matrix, group, order, width)
    shrink = jnp.swapaxes(shrink_matrices, 1, 2)[0]
    expand = jnp.swapaxes(expand_matrices, 1, 2)[0]
    adapter_out = adapter_output(gathered, shrink, expand, group)
    adapter_in = lax.all_to_all(adapter_out, "tp", split_axis=0, concat_axis=0, tiled=True)
    adapter_rows = lax.dot_general(
        pick,
        adapter_in.reshape(group * MOST, width),
        (((0,), (0,)), ((), ())),
        preferred_element_type=jnp.float32,
    )
    return (base + ADAPTER_SCALE * adapter_rows).astype(jnp.bfloat16)


def shards(
    hidden, down_matrix, shrink_matrices, expand_matrices, adapter_of_row, adapter_holder_slot
):
    group = lax.axis_size("tp")
    rows, depth = hidden.shape
    width = down_matrix.shape[1] // group
    if width % LANES == 0 and depth % LANES == 0 and group % 4 == 0:
        return shards_by_blocks(
            hidden, down_matrix, shrink_matrices, expand_matrices, adapter_of_row, adapter_holder_slot
        )
    blocks = MOST // BLOCK
    adapter_ids = jnp.arange(group, dtype=jnp.int32)
    row_match = adapter_of_row[:, None] == adapter_ids[None, :]
    row_slot = jnp.sum(jnp.where(row_match, adapter_holder_slot[None, :], 0), axis=1)
    slot_mask = row_slot[None, :] == adapter_ids[:, None]
    before = jnp.cumsum(slot_mask.astype(jnp.int32), axis=1) - 1
    place = jnp.where(slot_mask, before, -1)
    pick = place[:, None, :] == jnp.arange(MOST, dtype=jnp.int32)[None, :, None]
    pick = pick.reshape(group * MOST, rows).astype(jnp.bfloat16)
    packed = jnp.dot(pick, hidden, preferred_element_type=jnp.float32).astype(jnp.bfloat16)
    packed = packed.reshape(group * blocks, BLOCK, depth)
    gathered = lax.all_to_all(packed, "tp", split_axis=0, concat_axis=0, tiled=True)
    partial_value = jnp.dot(hidden, down_matrix, preferred_element_type=jnp.float32)
    base = lax.psum_scatter(partial_value, "tp", scatter_dimension=1, tiled=True)
    own_rows = jnp.transpose(gathered.reshape(group, MOST, depth), (1, 0, 2))
    rank_rows = jnp.dot(
        own_rows.reshape(MOST, group * depth), shrink_matrices[0], preferred_element_type=jnp.float32
    ).astype(jnp.bfloat16)
    adapter_out = lax.dot_general(
        rank_rows, expand_matrices[0], (((1,), (1,)), ((), ())), preferred_element_type=jnp.float32
    ).astype(jnp.bfloat16)
    adapter_out = jnp.transpose(adapter_out.reshape(blocks, BLOCK, group, width), (2, 0, 1, 3))
    adapter_in = lax.all_to_all(
        adapter_out.reshape(group * blocks, BLOCK, width), "tp", split_axis=0, concat_axis=0, tiled=True
    )
    adapter_rows = lax.dot_general(
        pick,
        adapter_in.reshape(group * MOST, width),
        (((0,), (0,)), ((), ())),
        preferred_element_type=jnp.float32,
    )
    return (base + ADAPTER_SCALE * adapter_rows).astype(jnp.bfloat16)


def solution(mesh):
    in_specs = (
        P("rep", "tp"),
        P("tp", None),
        P(("rep", "tp"), None, None),
        P(("rep", "tp"), None, None),
        P("rep"),
        P("rep"),
    )
    out_specs = P("rep", "tp")
    return jax.shard_map(shards, mesh=mesh, in_specs=in_specs, out_specs=out_specs, check_vma=False)
```

```python
import functools

import jax
import jax.numpy as jnp
from jax import lax
from jax.experimental import pallas as pl
from jax.experimental.pallas import tpu as pltpu
from jax.sharding import PartitionSpec as P

ADAPTER_SCALE = 0.5
BLOCK = 4
MOST = 20
LANES = 128
F16_TOP = 14.0


def in_hbm(value):
    return pltpu.with_memory_space_constraint(value, pltpu.HBM)


def xor_permute(value, group, offset):
    return lax.ppermute(value, "tp", [(i, i ^ offset) for i in range(group)])


def column_blocks_kernel(order_ref, hidden_hbm, down_ref, out_ref, hidden_ref, held_ref, hidden_sem, sems):
    count, depth, width = held_ref.shape
    parts = width // LANES
    pieces = sems.shape[1]
    cut = depth // pieces

    def copy(block, piece):
        start = pl.multiple_of(order_ref[block] * width, LANES)
        lines = pl.ds(piece * cut, cut)
        return pltpu.make_async_copy(
            down_ref.at[lines, pl.ds(start, width)], held_ref.at[block, lines], sems.at[block, piece]
        )

    hidden_copy = pltpu.make_async_copy(hidden_hbm, hidden_ref, hidden_sem)
    hidden_copy.start()
    for block in range(count):
        for piece in range(pieces):
            copy(block, piece).start()
    hidden_copy.wait()
    for block in range(count):
        for piece in range(pieces):
            copy(block, piece).wait()
        product = jnp.dot(hidden_ref[...], held_ref[block], preferred_element_type=jnp.float32)
        for lane in range(parts):
            out_ref[block * parts + lane] = product[:, lane * LANES : (lane + 1) * LANES]


def column_blocks(hidden, down_matrix, order, width):
    rows, depth = hidden.shape
    count = order.shape[0]
    pieces = 2 if depth % 32 == 0 else 1
    return pl.pallas_call(
        column_blocks_kernel,
        out_shape=jax.ShapeDtypeStruct((count * width // LANES, rows, LANES), jnp.float32),
        in_specs=[
            pl.BlockSpec(memory_space=pltpu.SMEM),
            pl.BlockSpec(memory_space=pltpu.HBM),
            pl.BlockSpec(memory_space=pltpu.HBM),
        ],
        out_specs=pl.BlockSpec(memory_space=pltpu.VMEM),
        scratch_shapes=[
            pltpu.VMEM((rows, depth), jnp.bfloat16),
            pltpu.VMEM((count, depth, width), jnp.bfloat16),
            pltpu.SemaphoreType.DMA,
            pltpu.SemaphoreType.DMA((count, pieces)),
        ],
        compiler_params=pltpu.CompilerParams(vmem_limit_bytes=40 * 2**20),
        cost_estimate=pl.CostEstimate(flops=1000, bytes_accessed=1000, transcendentals=0),
    )(order, in_hbm(hidden), in_hbm(down_matrix))


def pack_scaled(value):
    peak = jnp.max(jnp.abs(value), axis=(0, 2), keepdims=True)
    exponent = jnp.ceil(jnp.log2(jnp.maximum(peak, 2.0**-100)))
    scaled = (value * jnp.exp2(F16_TOP - exponent)).astype(jnp.float16)
    marks = jnp.broadcast_to(exponent, (1,) + value.shape[1:]).astype(jnp.float16)
    return jnp.concatenate([scaled, marks], axis=0)


def unpack_scaled(packed):
    exponent = packed[-1:].astype(jnp.float32)
    return packed[:-1].astype(jnp.float32) * jnp.exp2(exponent - F16_TOP)


def base_blocks(hidden, down_matrix, group, order, width):
    rows = hidden.shape[0]
    parts = width // LANES
    quads = list(range(0, group, 4))
    odd = column_blocks(hidden, down_matrix, order[: group // 2], width)
    odd_in = xor_permute(odd, group, 1)
    even = column_blocks(hidden, down_matrix, order[group // 2 :], width)
    chip = even + odd_in
    half = len(quads) * parts
    pair_in = xor_permute(pack_scaled(chip[half:]), group, 2)
    pair = chip[:half] + unpack_scaled(pair_in)
    total = pair[:parts]
    arrived = [
        xor_permute(pack_scaled(pair[i * parts : (i + 1) * parts]), group, quads[i])
        for i in range(1, len(quads))
    ]
    for packed in arrived:
        total = total + unpack_scaled(packed)
    return jnp.transpose(total, (1, 0, 2)).reshape(rows, width)


def pack_kernel(
    blocks,
    orders,
    me_ref,
    slot_hbm,
    adapter_hbm,
    hidden_hbm,
    packed_ref,
    pick_ref,
    order_ref,
    slot_ref,
    adapter_ref,
    hidden_ref,
    sems,
):
    rows = hidden_ref.shape[0]
    group = slot_ref.shape[0]
    copies = [
        pltpu.make_async_copy(slot_hbm, slot_ref, sems.at[0]),
        pltpu.make_async_copy(adapter_hbm, adapter_ref, sems.at[1]),
        pltpu.make_async_copy(hidden_hbm, hidden_ref, sems.at[2]),
    ]
    for copy in copies:
        copy.start()
    for i, offset in enumerate(orders):
        order_ref[i] = me_ref[0] ^ offset
    ids = lax.broadcasted_iota(jnp.int32, (group, 1), 0)
    slots = jnp.zeros((group, 1), jnp.int32)
    copies[0].wait()
    for adapter in range(group):
        slots = jnp.where(ids == adapter, slot_ref[adapter], slots)
    copies[1].wait()
    adapter = adapter_ref[...]
    first = jnp.sum((adapter < ids).astype(jnp.int32), axis=1, keepdims=True)
    shift = jnp.where(adapter == ids, slots * (blocks * BLOCK) - first, 0)
    place = jnp.sum(shift, axis=0, keepdims=True) + lax.broadcasted_iota(jnp.int32, (1, rows), 1)
    spots = lax.broadcasted_iota(jnp.int32, (group * blocks * BLOCK, rows), 0)
    pick = jnp.where(spots == place, 1.0, 0.0).astype(jnp.bfloat16)
    pick_ref[...] = pick
    copies[2].wait()
    packed = jnp.dot(pick, hidden_ref[...], preferred_element_type=jnp.float32)
    packed_ref[...] = packed.astype(jnp.bfloat16).reshape(packed_ref.shape)


def pack_rows(hidden, adapter_of_row, adapter_holder_slot, me, orders):
    rows, depth = hidden.shape
    group = adapter_holder_slot.shape[0]
    blocks = MOST // BLOCK
    vmem = pl.BlockSpec(memory_space=pltpu.VMEM)
    smem = pl.BlockSpec(memory_space=pltpu.SMEM)
    anywhere = pl.BlockSpec(memory_space=pltpu.HBM)
    return pl.pallas_call(
        functools.partial(pack_kernel, blocks, orders),
        out_shape=(
            jax.ShapeDtypeStruct((group * blocks, BLOCK, depth), jnp.bfloat16),
            jax.ShapeDtypeStruct((group * MOST, rows), jnp.bfloat16),
            jax.ShapeDtypeStruct((len(orders),), jnp.int32),
        ),
        in_specs=[smem, anywhere, anywhere, anywhere],
        out_specs=(vmem, vmem, smem),
        scratch_shapes=[
            pltpu.SMEM((group,), jnp.int32),
            pltpu.VMEM((1, rows), jnp.int32),
            pltpu.VMEM((rows, depth), jnp.bfloat16),
            pltpu.SemaphoreType.DMA((3,)),
        ],
        compiler_params=pltpu.CompilerParams(vmem_limit_bytes=24 * 2**20),
    )(me.reshape(1), in_hbm(adapter_holder_slot), in_hbm(adapter_of_row.reshape(1, rows)), in_hbm(hidden))


def adapter_kernel(rows_ref, shrink_ref, expand_ref, out_ref, total_ref):
    step = pl.program_id(0)
    block, depth = rows_ref.shape[1:]
    blocks = MOST // BLOCK
    sources = rows_ref.shape[0] // blocks
    total = jnp.zeros(total_ref.shape, jnp.float32)
    for source in range(sources):
        own = rows_ref[source * blocks : (source + 1) * blocks].reshape(MOST, depth)
        total += lax.dot_general(
            own,
            shrink_ref[:, source * depth : (source + 1) * depth],
            (((1,), (1,)), ((), ())),
            preferred_element_type=jnp.float32,
        )

    @pl.when(step == 0)
    def _():
        total_ref[...] = total

    @pl.when(step > 0)
    def _():
        total_ref[...] += total

    @pl.when(step == pl.num_programs(0) - 1)
    def _():
        rank_rows = total_ref[...].astype(jnp.bfloat16)
        width = out_ref.shape[2]
        for target in range(out_ref.shape[0] // blocks):
            piece = jnp.dot(
                rank_rows,
                expand_ref[:, target * width : (target + 1) * width],
                preferred_element_type=jnp.float32,
            )
            out_ref[target * blocks : (target + 1) * blocks] = piece.astype(jnp.bfloat16).reshape(
                blocks, BLOCK, width
            )


def adapter_output(gathered, shrink, expand, group):
    rank, hidden_width = shrink.shape
    model_width = expand.shape[1]
    depth = gathered.shape[2]
    blocks = MOST // BLOCK
    width = model_width // group
    steps = 4
    sources = group // steps
    return pl.pallas_call(
        adapter_kernel,
        out_shape=jax.ShapeDtypeStruct((group * blocks, BLOCK, width), jnp.bfloat16),
        grid=(steps,),
        in_specs=[
            pl.BlockSpec((sources * blocks, BLOCK, depth), lambda i: (i, 0, 0)),
            pl.BlockSpec((rank, sources * depth), lambda i: (0, i)),
            pl.BlockSpec((rank, model_width), lambda i: (0, 0)),
        ],
        out_specs=pl.BlockSpec((group * blocks, BLOCK, width), lambda i: (0, 0, 0)),
        scratch_shapes=[pltpu.VMEM((MOST, rank), jnp.float32)],
        compiler_params=pltpu.CompilerParams(vmem_limit_bytes=32 * 2**20),
        cost_estimate=pl.CostEstimate(
            flops=2 * MOST * rank * (hidden_width + model_width),
            bytes_accessed=2 * rank * (hidden_width + model_width) + 2 * MOST * hidden_width,
            transcendentals=0,
        ),
    )(gathered, in_hbm(shrink), in_hbm(expand))


def shards_by_blocks(
    hidden, down_matrix, shrink_matrices, expand_matrices, adapter_of_row, adapter_holder_slot
):
    group = lax.axis_size("tp")
    me = lax.axis_index("tp")
    rows, depth = hidden.shape
    width = down_matrix.shape[1] // group
    quads = list(range(0, group, 4))
    orders = [q + k for k in (1, 3, 0, 2) for q in quads]
    packed, pick, order = pack_rows(hidden, adapter_of_row, adapter_holder_slot, me, orders)
    gathered = lax.all_to_all(packed, "tp", split_axis=0, concat_axis=0, tiled=True)
    base = base_blocks(hidden, down_matrix, group, order, width)
    shrink = jnp.swapaxes(shrink_matrices, 1, 2)[0]
    expand = jnp.swapaxes(expand_matrices, 1, 2)[0]
    adapter_out = adapter_output(gathered, shrink, expand, group)
    adapter_in = lax.all_to_all(adapter_out, "tp", split_axis=0, concat_axis=0, tiled=True)
    adapter_rows = lax.dot_general(
        pick,
        adapter_in.reshape(group * MOST, width),
        (((0,), (0,)), ((), ())),
        preferred_element_type=jnp.float32,
    )
    return (base + ADAPTER_SCALE * adapter_rows).astype(jnp.bfloat16)


def shards(
    hidden, down_matrix, shrink_matrices, expand_matrices, adapter_of_row, adapter_holder_slot
):
    group = lax.axis_size("tp")
    rows, depth = hidden.shape
    width = down_matrix.shape[1] // group
    if width % LANES == 0 and depth % LANES == 0 and group % 4 == 0:
        return shards_by_blocks(
            hidden, down_matrix, shrink_matrices, expand_matrices, adapter_of_row, adapter_holder_slot
        )
    blocks = MOST // BLOCK
    adapter_ids = jnp.arange(group, dtype=jnp.int32)
    row_match = adapter_of_row[:, None] == adapter_ids[None, :]
    row_slot = jnp.sum(jnp.where(row_match, adapter_holder_slot[None, :], 0), axis=1)
    slot_mask = row_slot[None, :] == adapter_ids[:, None]
    before = jnp.cumsum(slot_mask.astype(jnp.int32), axis=1) - 1
    place = jnp.where(slot_mask, before, -1)
    pick = place[:, None, :] == jnp.arange(MOST, dtype=jnp.int32)[None, :, None]
    pick = pick.reshape(group * MOST, rows).astype(jnp.bfloat16)
    packed = jnp.dot(pick, hidden, preferred_element_type=jnp.float32).astype(jnp.bfloat16)
    packed = packed.reshape(group * blocks, BLOCK, depth)
    gathered = lax.all_to_all(packed, "tp", split_axis=0, concat_axis=0, tiled=True)
    partial_value = jnp.dot(hidden, down_matrix, preferred_element_type=jnp.float32)
    base = lax.psum_scatter(partial_value, "tp", scatter_dimension=1, tiled=True)
    own_rows = jnp.transpose(gathered.reshape(group, MOST, depth), (1, 0, 2))
    rank_rows = jnp.dot(
        own_rows.reshape(MOST, group * depth), shrink_matrices[0], preferred_element_type=jnp.float32
    ).astype(jnp.bfloat16)
    adapter_out = lax.dot_general(
        rank_rows, expand_matrices[0], (((1,), (1,)), ((), ())), preferred_element_type=jnp.float32
    ).astype(jnp.bfloat16)
    adapter_out = jnp.transpose(adapter_out.reshape(blocks, BLOCK, group, width), (2, 0, 1, 3))
    adapter_in = lax.all_to_all(
        adapter_out.reshape(group * blocks, BLOCK, width), "tp", split_axis=0, concat_axis=0, tiled=True
    )
    adapter_rows = lax.dot_general(
        pick,
        adapter_in.reshape(group * MOST, width),
        (((0,), (0,)), ((), ())),
        preferred_element_type=jnp.float32,
    )
    return (base + ADAPTER_SCALE * adapter_rows).astype(jnp.bfloat16)


def solution(mesh):
    in_specs = (
        P("rep", "tp"),
        P("tp", None),
        P(("rep", "tp"), None, None),
        P(("rep", "tp"), None, None),
        P("rep"),
        P("rep"),
    )
    out_specs = P("rep", "tp")
    return jax.shard_map(shards, mesh=mesh, in_specs=in_specs, out_specs=out_specs, check_vma=False)
```

```python
import functools

import jax
import jax.numpy as jnp
from jax import lax
from jax.experimental import pallas as pl
from jax.experimental.pallas import tpu as pltpu
from jax.sharding import PartitionSpec as P

ADAPTER_SCALE = 0.5
BLOCK = 4
MOST = 20
LANES = 128
F16_TOP = 14.0
IN_FLIGHT = 3


def in_hbm(value):
    return pltpu.with_memory_space_constraint(value, pltpu.HBM)


def xor_permute(value, group, offset):
    return lax.ppermute(value, "tp", [(i, i ^ offset) for i in range(group)])


def column_blocks_kernel(order_ref, hidden_hbm, down_ref, out_ref, hidden_ref, held_ref, hidden_sem, sems):
    count, depth, width = held_ref.shape
    parts = width // LANES
    pieces = sems.shape[1]
    cut = depth // pieces

    def copy(block, piece):
        start = pl.multiple_of(order_ref[block] * width, LANES)
        lines = pl.ds(piece * cut, cut)
        return pltpu.make_async_copy(
            down_ref.at[lines, pl.ds(start, width)], held_ref.at[block, lines], sems.at[block, piece]
        )

    hidden_copy = pltpu.make_async_copy(hidden_hbm, hidden_ref, hidden_sem)
    hidden_copy.start()
    for block in range(min(IN_FLIGHT, count)):
        for piece in range(pieces):
            copy(block, piece).start()
    hidden_copy.wait()
    for block in range(count):
        for piece in range(pieces):
            copy(block, piece).wait()
        if block + IN_FLIGHT < count:
            for piece in range(pieces):
                copy(block + IN_FLIGHT, piece).start()
        product = jnp.dot(hidden_ref[...], held_ref[block], preferred_element_type=jnp.float32)
        for lane in range(parts):
            out_ref[block * parts + lane] = product[:, lane * LANES : (lane + 1) * LANES]


def column_blocks(hidden, down_matrix, order, width):
    rows, depth = hidden.shape
    count = order.shape[0]
    pieces = 2 if depth % 32 == 0 else 1
    return pl.pallas_call(
        column_blocks_kernel,
        out_shape=jax.ShapeDtypeStruct((count * width // LANES, rows, LANES), jnp.float32),
        in_specs=[
            pl.BlockSpec(memory_space=pltpu.SMEM),
            pl.BlockSpec(memory_space=pltpu.HBM),
            pl.BlockSpec(memory_space=pltpu.HBM),
        ],
        out_specs=pl.BlockSpec(memory_space=pltpu.VMEM),
        scratch_shapes=[
            pltpu.VMEM((rows, depth), jnp.bfloat16),
            pltpu.VMEM((count, depth, width), jnp.bfloat16),
            pltpu.SemaphoreType.DMA,
            pltpu.SemaphoreType.DMA((count, pieces)),
        ],
        compiler_params=pltpu.CompilerParams(vmem_limit_bytes=40 * 2**20),
        cost_estimate=pl.CostEstimate(flops=1000, bytes_accessed=1000, transcendentals=0),
    )(order, in_hbm(hidden), in_hbm(down_matrix))


def pack_scaled(value):
    peak = jnp.max(jnp.abs(value), axis=(0, 2), keepdims=True)
    exponent = jnp.ceil(jnp.log2(jnp.maximum(peak, 2.0**-100)))
    scaled = (value * jnp.exp2(F16_TOP - exponent)).astype(jnp.float16)
    marks = jnp.broadcast_to(exponent, (1,) + value.shape[1:]).astype(jnp.float16)
    return jnp.concatenate([scaled, marks], axis=0)


def unpack_scaled(packed):
    exponent = packed[-1:].astype(jnp.float32)
    return packed[:-1].astype(jnp.float32) * jnp.exp2(exponent - F16_TOP)


def chip_sums(hidden, down_matrix, group, order, width):
    def work():
        odd = column_blocks(hidden, down_matrix, order[: group // 2], width)
        odd_in = xor_permute(odd, group, 1)
        even = column_blocks(hidden, down_matrix, order[group // 2 :], width)
        chip = even + odd_in
        half = chip.shape[0] // 2
        return chip[:half], pack_scaled(chip[half:])

    def idle():
        rows = hidden.shape[0]
        half = group * width // LANES // 4
        return (
            jnp.zeros((half, rows, LANES), jnp.float32),
            jnp.zeros((half + 1, rows, LANES), jnp.float16),
        )

    return lax.cond(order[0] >= 0, work, idle)


def base_blocks(hidden, down_matrix, group, order, width):
    rows = hidden.shape[0]
    parts = width // LANES
    kept, sent = chip_sums(hidden, down_matrix, group, order, width)
    pair = kept + unpack_scaled(xor_permute(sent, group, 2))
    total = pair[:parts]
    arrived = [
        xor_permute(pack_scaled(pair[i * parts : (i + 1) * parts]), group, 4 * i)
        for i in range(1, group // 4)
    ]
    for packed in arrived:
        total = total + unpack_scaled(packed)
    return jnp.transpose(total, (1, 0, 2)).reshape(rows, width)


def pack_kernel(
    blocks,
    orders,
    me_ref,
    slot_hbm,
    adapter_hbm,
    hidden_hbm,
    packed_ref,
    pick_ref,
    order_ref,
    slot_ref,
    adapter_ref,
    hidden_ref,
    sems,
):
    rows = hidden_ref.shape[0]
    group = slot_ref.shape[0]
    copies = [
        pltpu.make_async_copy(slot_hbm, slot_ref, sems.at[0]),
        pltpu.make_async_copy(adapter_hbm, adapter_ref, sems.at[1]),
        pltpu.make_async_copy(hidden_hbm, hidden_ref, sems.at[2]),
    ]
    for copy in copies:
        copy.start()
    for i, offset in enumerate(orders):
        order_ref[i] = me_ref[0] ^ offset
    ids = lax.broadcasted_iota(jnp.int32, (group, 1), 0)
    slots = jnp.zeros((group, 1), jnp.int32)
    copies[0].wait()
    for adapter in range(group):
        slots = jnp.where(ids == adapter, slot_ref[adapter], slots)
    copies[1].wait()
    adapter = adapter_ref[...]
    first = jnp.sum((adapter < ids).astype(jnp.int32), axis=1, keepdims=True)
    shift = jnp.where(adapter == ids, slots * (blocks * BLOCK) - first, 0)
    place = jnp.sum(shift, axis=0, keepdims=True) + lax.broadcasted_iota(jnp.int32, (1, rows), 1)
    spots = lax.broadcasted_iota(jnp.int32, (group * blocks * BLOCK, rows), 0)
    pick = jnp.where(spots == place, 1.0, 0.0).astype(jnp.bfloat16)
    pick_ref[...] = pick
    copies[2].wait()
    packed = jnp.dot(pick, hidden_ref[...], preferred_element_type=jnp.float32)
    packed_ref[...] = packed.astype(jnp.bfloat16).reshape(packed_ref.shape)


def pack_rows(hidden, adapter_of_row, adapter_holder_slot, me, orders):
    rows, depth = hidden.shape
    group = adapter_holder_slot.shape[0]
    blocks = MOST // BLOCK
    vmem = pl.BlockSpec(memory_space=pltpu.VMEM)
    smem = pl.BlockSpec(memory_space=pltpu.SMEM)
    anywhere = pl.BlockSpec(memory_space=pltpu.HBM)
    return pl.pallas_call(
        functools.partial(pack_kernel, blocks, orders),
        out_shape=(
            jax.ShapeDtypeStruct((group * blocks, BLOCK, depth), jnp.bfloat16),
            jax.ShapeDtypeStruct((group * MOST, rows), jnp.bfloat16),
            jax.ShapeDtypeStruct((len(orders),), jnp.int32),
        ),
        in_specs=[smem, anywhere, anywhere, anywhere],
        out_specs=(vmem, vmem, smem),
        scratch_shapes=[
            pltpu.SMEM((group,), jnp.int32),
            pltpu.VMEM((1, rows), jnp.int32),
            pltpu.VMEM((rows, depth), jnp.bfloat16),
            pltpu.SemaphoreType.DMA((3,)),
        ],
        compiler_params=pltpu.CompilerParams(vmem_limit_bytes=24 * 2**20),
    )(me.reshape(1), in_hbm(adapter_holder_slot), in_hbm(adapter_of_row.reshape(1, rows)), in_hbm(hidden))


def adapter_kernel(rows_ref, shrink_ref, expand_ref, out_ref, total_ref):
    step = pl.program_id(0)
    block, depth = rows_ref.shape[1:]
    blocks = MOST // BLOCK
    sources = rows_ref.shape[0] // blocks
    total = jnp.zeros(total_ref.shape, jnp.float32)
    for source in range(sources):
        own = rows_ref[source * blocks : (source + 1) * blocks].reshape(MOST, depth)
        total += lax.dot_general(
            own,
            shrink_ref[:, source * depth : (source + 1) * depth],
            (((1,), (1,)), ((), ())),
            preferred_element_type=jnp.float32,
        )

    @pl.when(step == 0)
    def _():
        total_ref[...] = total

    @pl.when(step > 0)
    def _():
        total_ref[...] += total

    @pl.when(step == pl.num_programs(0) - 1)
    def _():
        rank_rows = total_ref[...].astype(jnp.bfloat16)
        width = out_ref.shape[2]
        for target in range(out_ref.shape[0] // blocks):
            piece = jnp.dot(
                rank_rows,
                expand_ref[:, target * width : (target + 1) * width],
                preferred_element_type=jnp.float32,
            )
            out_ref[target * blocks : (target + 1) * blocks] = piece.astype(jnp.bfloat16).reshape(
                blocks, BLOCK, width
            )


def adapter_output(gathered, shrink, expand, group):
    rank, hidden_width = shrink.shape
    model_width = expand.shape[1]
    depth = gathered.shape[2]
    blocks = MOST // BLOCK
    width = model_width // group
    steps = 4
    sources = group // steps
    return pl.pallas_call(
        adapter_kernel,
        out_shape=jax.ShapeDtypeStruct((group * blocks, BLOCK, width), jnp.bfloat16),
        grid=(steps,),
        in_specs=[
            pl.BlockSpec((sources * blocks, BLOCK, depth), lambda i: (i, 0, 0)),
            pl.BlockSpec((rank, sources * depth), lambda i: (0, i)),
            pl.BlockSpec((rank, model_width), lambda i: (0, 0)),
        ],
        out_specs=pl.BlockSpec((group * blocks, BLOCK, width), lambda i: (0, 0, 0)),
        scratch_shapes=[pltpu.VMEM((MOST, rank), jnp.float32)],
        compiler_params=pltpu.CompilerParams(vmem_limit_bytes=32 * 2**20),
        cost_estimate=pl.CostEstimate(
            flops=2 * MOST * rank * (hidden_width + model_width),
            bytes_accessed=2 * rank * (hidden_width + model_width) + 2 * MOST * hidden_width,
            transcendentals=0,
        ),
    )(gathered, in_hbm(shrink), in_hbm(expand))


def shards_by_blocks(
    hidden, down_matrix, shrink_matrices, expand_matrices, adapter_of_row, adapter_holder_slot
):
    group = lax.axis_size("tp")
    me = lax.axis_index("tp")
    rows, depth = hidden.shape
    width = down_matrix.shape[1] // group
    quads = list(range(0, group, 4))
    orders = [q + k for k in (1, 3, 0, 2) for q in quads]
    packed, pick, order = pack_rows(hidden, adapter_of_row, adapter_holder_slot, me, orders)
    gathered = lax.all_to_all(packed, "tp", split_axis=0, concat_axis=0, tiled=True)
    base = base_blocks(hidden, down_matrix, group, order, width)
    shrink = jnp.swapaxes(shrink_matrices, 1, 2)[0]
    expand = jnp.swapaxes(expand_matrices, 1, 2)[0]
    adapter_out = adapter_output(gathered, shrink, expand, group)
    adapter_in = lax.all_to_all(adapter_out, "tp", split_axis=0, concat_axis=0, tiled=True)
    adapter_rows = lax.dot_general(
        pick,
        adapter_in.reshape(group * MOST, width),
        (((0,), (0,)), ((), ())),
        preferred_element_type=jnp.float32,
    )
    return (base + ADAPTER_SCALE * adapter_rows).astype(jnp.bfloat16)


def shards(
    hidden, down_matrix, shrink_matrices, expand_matrices, adapter_of_row, adapter_holder_slot
):
    group = lax.axis_size("tp")
    rows, depth = hidden.shape
    width = down_matrix.shape[1] // group
    if width % LANES == 0 and depth % LANES == 0 and group % 4 == 0:
        return shards_by_blocks(
            hidden, down_matrix, shrink_matrices, expand_matrices, adapter_of_row, adapter_holder_slot
        )
    blocks = MOST // BLOCK
    adapter_ids = jnp.arange(group, dtype=jnp.int32)
    row_match = adapter_of_row[:, None] == adapter_ids[None, :]
    row_slot = jnp.sum(jnp.where(row_match, adapter_holder_slot[None, :], 0), axis=1)
    slot_mask = row_slot[None, :] == adapter_ids[:, None]
    before = jnp.cumsum(slot_mask.astype(jnp.int32), axis=1) - 1
    place = jnp.where(slot_mask, before, -1)
    pick = place[:, None, :] == jnp.arange(MOST, dtype=jnp.int32)[None, :, None]
    pick = pick.reshape(group * MOST, rows).astype(jnp.bfloat16)
    packed = jnp.dot(pick, hidden, preferred_element_type=jnp.float32).astype(jnp.bfloat16)
    packed = packed.reshape(group * blocks, BLOCK, depth)
    gathered = lax.all_to_all(packed, "tp", split_axis=0, concat_axis=0, tiled=True)
    partial_value = jnp.dot(hidden, down_matrix, preferred_element_type=jnp.float32)
    base = lax.psum_scatter(partial_value, "tp", scatter_dimension=1, tiled=True)
    own_rows = jnp.transpose(gathered.reshape(group, MOST, depth), (1, 0, 2))
    rank_rows = jnp.dot(
        own_rows.reshape(MOST, group * depth), shrink_matrices[0], preferred_element_type=jnp.float32
    ).astype(jnp.bfloat16)
    adapter_out = lax.dot_general(
        rank_rows, expand_matrices[0], (((1,), (1,)), ((), ())), preferred_element_type=jnp.float32
    ).astype(jnp.bfloat16)
    adapter_out = jnp.transpose(adapter_out.reshape(blocks, BLOCK, group, width), (2, 0, 1, 3))
    adapter_in = lax.all_to_all(
        adapter_out.reshape(group * blocks, BLOCK, width), "tp", split_axis=0, concat_axis=0, tiled=True
    )
    adapter_rows = lax.dot_general(
        pick,
        adapter_in.reshape(group * MOST, width),
        (((0,), (0,)), ((), ())),
        preferred_element_type=jnp.float32,
    )
    return (base + ADAPTER_SCALE * adapter_rows).astype(jnp.bfloat16)


def solution(mesh):
    in_specs = (
        P("rep", "tp"),
        P("tp", None),
        P(("rep", "tp"), None, None),
        P(("rep", "tp"), None, None),
        P("rep"),
        P("rep"),
    )
    out_specs = P("rep", "tp")
    return jax.shard_map(shards, mesh=mesh, in_specs=in_specs, out_specs=out_specs, check_vma=False)
```

```python
import functools

import jax
import jax.numpy as jnp
from jax import lax
from jax.experimental import pallas as pl
from jax.experimental.pallas import tpu as pltpu
from jax.sharding import PartitionSpec as P

ADAPTER_SCALE = 0.5
BLOCK = 4
MOST = 20
LANES = 128
F16_TOP = 14.0


def in_hbm(value):
    return pltpu.with_memory_space_constraint(value, pltpu.HBM)


def xor_permute(value, group, offset):
    return lax.ppermute(value, "tp", [(i, i ^ offset) for i in range(group)])


def column_blocks_kernel(order_ref, hidden_ref, down_ref, out_ref, held_ref, sems):
    count, depth, width = held_ref.shape
    parts = width // LANES
    pieces = sems.shape[1]
    cut = depth // pieces

    def copy(block, piece):
        start = pl.multiple_of(order_ref[block] * width, LANES)
        lines = pl.ds(piece * cut, cut)
        return pltpu.make_async_copy(
            down_ref.at[lines, pl.ds(start, width)], held_ref.at[block, lines], sems.at[block, piece]
        )

    for block in range(count):
        for piece in range(pieces):
            copy(block, piece).start()
    for block in range(count):
        for piece in range(pieces):
            copy(block, piece).wait()
        product = jnp.dot(hidden_ref[...], held_ref[block], preferred_element_type=jnp.float32)
        for lane in range(parts):
            out_ref[block * parts + lane] = product[:, lane * LANES : (lane + 1) * LANES]


def column_blocks(hidden, down_matrix, order, width):
    rows, depth = hidden.shape
    count = order.shape[0]
    pieces = 2 if depth % 32 == 0 else 1
    vmem = pl.BlockSpec(memory_space=pltpu.VMEM)
    return pl.pallas_call(
        column_blocks_kernel,
        out_shape=jax.ShapeDtypeStruct((count * width // LANES, rows, LANES), jnp.float32),
        in_specs=[
            pl.BlockSpec(memory_space=pltpu.SMEM),
            vmem,
            pl.BlockSpec(memory_space=pl.ANY),
        ],
        out_specs=vmem,
        scratch_shapes=[
            pltpu.VMEM((count, depth, width), jnp.bfloat16),
            pltpu.SemaphoreType.DMA((count, pieces)),
        ],
        compiler_params=pltpu.CompilerParams(vmem_limit_bytes=40 * 2**20),
        cost_estimate=pl.CostEstimate(flops=1000, bytes_accessed=1000, transcendentals=0),
    )(order, hidden, in_hbm(down_matrix))


def pack_scaled(value):
    peak = jnp.max(jnp.abs(value), axis=(0, 2), keepdims=True)
    exponent = jnp.ceil(jnp.log2(jnp.maximum(peak, 2.0**-100)))
    scaled = (value * jnp.exp2(F16_TOP - exponent)).astype(jnp.float16)
    marks = jnp.broadcast_to(exponent, (1,) + value.shape[1:]).astype(jnp.float16)
    return jnp.concatenate([scaled, marks], axis=0)


def unpack_scaled(packed):
    exponent = packed[-1:].astype(jnp.float32)
    return packed[:-1].astype(jnp.float32) * jnp.exp2(exponent - F16_TOP)


def chip_sums(hidden, down_matrix, group, order, width):
    def work():
        odd = column_blocks(hidden, down_matrix, order[: group // 2], width)
        odd_in = xor_permute(odd, group, 1)
        even = column_blocks(hidden, down_matrix, order[group // 2 :], width)
        chip = even + odd_in
        half = chip.shape[0] // 2
        return chip[:half], pack_scaled(chip[half:])

    def idle():
        rows = hidden.shape[0]
        half = group * width // LANES // 4
        return (
            jnp.zeros((half, rows, LANES), jnp.float32),
            jnp.zeros((half + 1, rows, LANES), jnp.float16),
        )

    return lax.cond(order[0] >= 0, work, idle)


def line_sums(kept, pair_in, flag, group, width):
    rows = kept.shape[1]
    parts = width // LANES

    def work():
        pair = kept + unpack_scaled(pair_in)
        total = pair[:parts]
        arrived = [
            xor_permute(pack_scaled(pair[i * parts : (i + 1) * parts]), group, 4 * i)
            for i in range(1, group // 4)
        ]
        for packed in arrived:
            total = total + unpack_scaled(packed)
        return total

    def idle():
        return jnp.zeros((parts, rows, LANES), jnp.float32)

    return lax.cond(flag >= 0, work, idle)


def pack_kernel(
    blocks,
    orders,
    me_ref,
    slot_hbm,
    adapter_hbm,
    hidden_hbm,
    packed_ref,
    pick_ref,
    order_ref,
    kept_ref,
    slot_ref,
    adapter_ref,
    hidden_ref,
    sems,
):
    rows = hidden_ref.shape[0]
    group = slot_ref.shape[0]
    copies = [
        pltpu.make_async_copy(slot_hbm, slot_ref, sems.at[0]),
        pltpu.make_async_copy(adapter_hbm, adapter_ref, sems.at[1]),
        pltpu.make_async_copy(hidden_hbm, hidden_ref, sems.at[2]),
    ]
    for copy in copies:
        copy.start()
    for i, offset in enumerate(orders):
        order_ref[i] = me_ref[0] ^ offset
    ids = lax.broadcasted_iota(jnp.int32, (group, 1), 0)
    slots = jnp.zeros((group, 1), jnp.int32)
    copies[0].wait()
    for adapter in range(group):
        slots = jnp.where(ids == adapter, slot_ref[adapter], slots)
    copies[1].wait()
    adapter = adapter_ref[...]
    first = jnp.sum((adapter < ids).astype(jnp.int32), axis=1, keepdims=True)
    shift = jnp.where(adapter == ids, slots * (blocks * BLOCK) - first, 0)
    place = jnp.sum(shift, axis=0, keepdims=True) + lax.broadcasted_iota(jnp.int32, (1, rows), 1)
    spots = lax.broadcasted_iota(jnp.int32, (group * blocks * BLOCK, rows), 0)
    pick = jnp.where(spots == place, 1.0, 0.0).astype(jnp.bfloat16)
    pick_ref[...] = pick
    copies[2].wait()
    packed = jnp.dot(pick, hidden_ref[...], preferred_element_type=jnp.float32)
    packed_ref[...] = packed.astype(jnp.bfloat16).reshape(packed_ref.shape)
    kept_ref[...] = hidden_ref[...]


def pack_rows(hidden, adapter_of_row, adapter_holder_slot, me, orders):
    rows, depth = hidden.shape
    group = adapter_holder_slot.shape[0]
    blocks = MOST // BLOCK
    vmem = pl.BlockSpec(memory_space=pltpu.VMEM)
    smem = pl.BlockSpec(memory_space=pltpu.SMEM)
    anywhere = pl.BlockSpec(memory_space=pltpu.HBM)
    return pl.pallas_call(
        functools.partial(pack_kernel, blocks, orders),
        out_shape=(
            jax.ShapeDtypeStruct((group * blocks, BLOCK, depth), jnp.bfloat16),
            jax.ShapeDtypeStruct((group * MOST, rows), jnp.bfloat16),
            jax.ShapeDtypeStruct((len(orders),), jnp.int32),
            jax.ShapeDtypeStruct((rows, depth), jnp.bfloat16),
        ),
        in_specs=[smem, anywhere, anywhere, anywhere],
        out_specs=(vmem, vmem, smem, vmem),
        scratch_shapes=[
            pltpu.SMEM((group,), jnp.int32),
            pltpu.VMEM((1, rows), jnp.int32),
            pltpu.VMEM((rows, depth), jnp.bfloat16),
            pltpu.SemaphoreType.DMA((3,)),
        ],
        compiler_params=pltpu.CompilerParams(vmem_limit_bytes=24 * 2**20),
    )(me.reshape(1), in_hbm(adapter_holder_slot), in_hbm(adapter_of_row.reshape(1, rows)), in_hbm(hidden))


def adapter_kernel(rows_ref, shrink_ref, expand_ref, out_ref, flag_ref, total_ref):
    step = pl.program_id(0)
    flag_ref[0] = step
    block, depth = rows_ref.shape[1:]
    blocks = MOST // BLOCK
    sources = rows_ref.shape[0] // blocks
    total = jnp.zeros(total_ref.shape, jnp.float32)
    for source in range(sources):
        own = rows_ref[source * blocks : (source + 1) * blocks].reshape(MOST, depth)
        total += lax.dot_general(
            own,
            shrink_ref[:, source * depth : (source + 1) * depth],
            (((1,), (1,)), ((), ())),
            preferred_element_type=jnp.float32,
        )

    @pl.when(step == 0)
    def _():
        total_ref[...] = total

    @pl.when(step > 0)
    def _():
        total_ref[...] += total

    @pl.when(step == pl.num_programs(0) - 1)
    def _():
        rank_rows = total_ref[...].astype(jnp.bfloat16)
        width = out_ref.shape[2]
        for target in range(out_ref.shape[0] // blocks):
            piece = jnp.dot(
                rank_rows,
                expand_ref[:, target * width : (target + 1) * width],
                preferred_element_type=jnp.float32,
            )
            out_ref[target * blocks : (target + 1) * blocks] = piece.astype(jnp.bfloat16).reshape(
                blocks, BLOCK, width
            )


def adapter_output(gathered, shrink, expand, group):
    rank, hidden_width = shrink.shape
    model_width = expand.shape[1]
    depth = gathered.shape[2]
    blocks = MOST // BLOCK
    width = model_width // group
    steps = 4
    sources = group // steps
    return pl.pallas_call(
        adapter_kernel,
        out_shape=(
            jax.ShapeDtypeStruct((group * blocks, BLOCK, width), jnp.bfloat16),
            jax.ShapeDtypeStruct((1,), jnp.int32),
        ),
        grid=(steps,),
        in_specs=[
            pl.BlockSpec((sources * blocks, BLOCK, depth), lambda i: (i, 0, 0)),
            pl.BlockSpec((rank, sources * depth), lambda i: (0, i)),
            pl.BlockSpec((rank, model_width), lambda i: (0, 0)),
        ],
        out_specs=(
            pl.BlockSpec((group * blocks, BLOCK, width), lambda i: (0, 0, 0)),
            pl.BlockSpec(memory_space=pltpu.SMEM),
        ),
        scratch_shapes=[pltpu.VMEM((MOST, rank), jnp.float32)],
        compiler_params=pltpu.CompilerParams(vmem_limit_bytes=32 * 2**20),
        cost_estimate=pl.CostEstimate(
            flops=2 * MOST * rank * (hidden_width + model_width),
            bytes_accessed=2 * rank * (hidden_width + model_width) + 2 * MOST * hidden_width,
            transcendentals=0,
        ),
    )(gathered, shrink, expand)


def shards_by_blocks(
    hidden, down_matrix, shrink_matrices, expand_matrices, adapter_of_row, adapter_holder_slot
):
    group = lax.axis_size("tp")
    me = lax.axis_index("tp")
    rows, depth = hidden.shape
    width = down_matrix.shape[1] // group
    quads = list(range(0, group, 4))
    orders = [q + k for k in (1, 3, 0, 2) for q in quads]
    packed, pick, order, kept_hidden = pack_rows(
        hidden, adapter_of_row, adapter_holder_slot, me, orders
    )
    gathered = lax.all_to_all(packed, "tp", split_axis=0, concat_axis=0, tiled=True)
    kept, sent = chip_sums(kept_hidden, down_matrix, group, order, width)
    pair_in = xor_permute(sent, group, 2)
    shrink = jnp.swapaxes(shrink_matrices, 1, 2)[0]
    expand = jnp.swapaxes(expand_matrices, 1, 2)[0]
    adapter_out, flag = adapter_output(gathered, shrink, expand, group)
    adapter_in = lax.all_to_all(adapter_out, "tp", split_axis=0, concat_axis=0, tiled=True)
    total = line_sums(kept, pair_in, flag[0], group, width)
    base = jnp.transpose(total, (1, 0, 2)).reshape(rows, width)
    adapter_rows = lax.dot_general(
        pick,
        adapter_in.reshape(group * MOST, width),
        (((0,), (0,)), ((), ())),
        preferred_element_type=jnp.float32,
    )
    return (base + ADAPTER_SCALE * adapter_rows).astype(jnp.bfloat16)


def shards(
    hidden, down_matrix, shrink_matrices, expand_matrices, adapter_of_row, adapter_holder_slot
):
    group = lax.axis_size("tp")
    rows, depth = hidden.shape
    width = down_matrix.shape[1] // group
    if width % LANES == 0 and depth % LANES == 0 and group % 4 == 0:
        return shards_by_blocks(
            hidden, down_matrix, shrink_matrices, expand_matrices, adapter_of_row, adapter_holder_slot
        )
    blocks = MOST // BLOCK
    adapter_ids = jnp.arange(group, dtype=jnp.int32)
    row_match = adapter_of_row[:, None] == adapter_ids[None, :]
    row_slot = jnp.sum(jnp.where(row_match, adapter_holder_slot[None, :], 0), axis=1)
    slot_mask = row_slot[None, :] == adapter_ids[:, None]
    before = jnp.cumsum(slot_mask.astype(jnp.int32), axis=1) - 1
    place = jnp.where(slot_mask, before, -1)
    pick = place[:, None, :] == jnp.arange(MOST, dtype=jnp.int32)[None, :, None]
    pick = pick.reshape(group * MOST, rows).astype(jnp.bfloat16)
    packed = jnp.dot(pick, hidden, preferred_element_type=jnp.float32).astype(jnp.bfloat16)
    packed = packed.reshape(group * blocks, BLOCK, depth)
    gathered = lax.all_to_all(packed, "tp", split_axis=0, concat_axis=0, tiled=True)
    partial_value = jnp.dot(hidden, down_matrix, preferred_element_type=jnp.float32)
    base = lax.psum_scatter(partial_value, "tp", scatter_dimension=1, tiled=True)
    own_rows = jnp.transpose(gathered.reshape(group, MOST, depth), (1, 0, 2))
    rank_rows = jnp.dot(
        own_rows.reshape(MOST, group * depth), shrink_matrices[0], preferred_element_type=jnp.float32
    ).astype(jnp.bfloat16)
    adapter_out = lax.dot_general(
        rank_rows, expand_matrices[0], (((1,), (1,)), ((), ())), preferred_element_type=jnp.float32
    ).astype(jnp.bfloat16)
    adapter_out = jnp.transpose(adapter_out.reshape(blocks, BLOCK, group, width), (2, 0, 1, 3))
    adapter_in = lax.all_to_all(
        adapter_out.reshape(group * blocks, BLOCK, width), "tp", split_axis=0, concat_axis=0, tiled=True
    )
    adapter_rows = lax.dot_general(
        pick,
        adapter_in.reshape(group * MOST, width),
        (((0,), (0,)), ((), ())),
        preferred_element_type=jnp.float32,
    )
    return (base + ADAPTER_SCALE * adapter_rows).astype(jnp.bfloat16)


def solution(mesh):
    in_specs = (
        P("rep", "tp"),
        P("tp", None),
        P(("rep", "tp"), None, None),
        P(("rep", "tp"), None, None),
        P("rep"),
        P("rep"),
    )
    out_specs = P("rep", "tp")
    return jax.shard_map(shards, mesh=mesh, in_specs=in_specs, out_specs=out_specs, check_vma=False)
```

```python
import functools

import jax
import jax.numpy as jnp
from jax import lax
from jax.experimental import pallas as pl
from jax.experimental.pallas import tpu as pltpu
from jax.sharding import PartitionSpec as P

ADAPTER_SCALE = 0.5
BLOCK = 4
MOST = 20
LANES = 128
F16_TOP = 14.0


def in_hbm(value):
    return pltpu.with_memory_space_constraint(value, pltpu.HBM)


def xor_permute(value, group, offset):
    return lax.ppermute(value, "tp", [(i, i ^ offset) for i in range(group)])


def column_blocks_kernel(order_ref, hidden_ref, down_ref, out_ref, held_ref, sems):
    count, depth, width = held_ref.shape
    parts = width // LANES
    pieces = sems.shape[1]
    cut = depth // pieces

    def copy(block, piece):
        start = pl.multiple_of(order_ref[block] * width, LANES)
        lines = pl.ds(piece * cut, cut)
        return pltpu.make_async_copy(
            down_ref.at[lines, pl.ds(start, width)], held_ref.at[block, lines], sems.at[block, piece]
        )

    for block in range(count):
        for piece in range(pieces):
            copy(block, piece).start()
    for block in range(count):
        for piece in range(pieces):
            copy(block, piece).wait()
        product = jnp.dot(hidden_ref[...], held_ref[block], preferred_element_type=jnp.float32)
        for lane in range(parts):
            out_ref[block * parts + lane] = product[:, lane * LANES : (lane + 1) * LANES]


def column_blocks(hidden, down_matrix, order, width):
    rows, depth = hidden.shape
    count = order.shape[0]
    pieces = 2 if depth % 32 == 0 else 1
    vmem = pl.BlockSpec(memory_space=pltpu.VMEM)
    return pl.pallas_call(
        column_blocks_kernel,
        out_shape=jax.ShapeDtypeStruct((count * width // LANES, rows, LANES), jnp.float32),
        in_specs=[
            pl.BlockSpec(memory_space=pltpu.SMEM),
            vmem,
            pl.BlockSpec(memory_space=pl.ANY),
        ],
        out_specs=vmem,
        scratch_shapes=[
            pltpu.VMEM((count, depth, width), jnp.bfloat16),
            pltpu.SemaphoreType.DMA((count, pieces)),
        ],
        compiler_params=pltpu.CompilerParams(vmem_limit_bytes=40 * 2**20),
        cost_estimate=pl.CostEstimate(flops=1000, bytes_accessed=1000, transcendentals=0),
    )(order, hidden, in_hbm(down_matrix))


def pack_scaled(value):
    peak = jnp.max(jnp.abs(value), axis=(0, 2), keepdims=True)
    exponent = jnp.ceil(jnp.log2(jnp.maximum(peak, 2.0**-100)))
    scaled = (value * jnp.exp2(F16_TOP - exponent)).astype(jnp.float16)
    marks = jnp.broadcast_to(exponent, (1,) + value.shape[1:]).astype(jnp.float16)
    return jnp.concatenate([scaled, marks], axis=0)


def unpack_scaled(packed):
    exponent = packed[-1:].astype(jnp.float32)
    return packed[:-1].astype(jnp.float32) * jnp.exp2(exponent - F16_TOP)


def chip_sums(hidden, down_matrix, group, order, width):
    def work():
        odd = column_blocks(hidden, down_matrix, order[: group // 2], width)
        odd_in = xor_permute(odd, group, 1)
        even = column_blocks(hidden, down_matrix, order[group // 2 :], width)
        chip = even + odd_in
        half = chip.shape[0] // 2
        return chip[:half], pack_scaled(chip[half:])

    def idle():
        rows = hidden.shape[0]
        half = group * width // LANES // 4
        return (
            jnp.zeros((half, rows, LANES), jnp.float32),
            jnp.zeros((half + 1, rows, LANES), jnp.float16),
        )

    return lax.cond(order[0] >= 0, work, idle)


def line_sums(kept, pair_in, flag, group, width):
    rows = kept.shape[1]
    parts = width // LANES

    def work():
        pair = kept + unpack_scaled(pair_in)
        total = pair[:parts]
        arrived = [
            xor_permute(pack_scaled(pair[i * parts : (i + 1) * parts]), group, 4 * i)
            for i in range(1, group // 4)
        ]
        for packed in arrived:
            total = total + unpack_scaled(packed)
        return total

    def idle():
        return jnp.zeros((parts, rows, LANES), jnp.float32)

    return lax.cond(flag >= 0, work, idle)


def pack_kernel(
    blocks,
    orders,
    me_ref,
    slot_hbm,
    adapter_hbm,
    hidden_hbm,
    packed_ref,
    pick_ref,
    order_ref,
    kept_ref,
    slot_ref,
    adapter_ref,
    hidden_ref,
    sems,
):
    rows = hidden_ref.shape[0]
    group = slot_ref.shape[0]
    copies = [
        pltpu.make_async_copy(slot_hbm, slot_ref, sems.at[0]),
        pltpu.make_async_copy(adapter_hbm, adapter_ref, sems.at[1]),
        pltpu.make_async_copy(hidden_hbm, hidden_ref, sems.at[2]),
    ]
    for copy in copies:
        copy.start()
    for i, offset in enumerate(orders):
        order_ref[i] = me_ref[0] ^ offset
    ids = lax.broadcasted_iota(jnp.int32, (group, 1), 0)
    slots = jnp.zeros((group, 1), jnp.int32)
    copies[0].wait()
    for adapter in range(group):
        slots = jnp.where(ids == adapter, slot_ref[adapter], slots)
    copies[1].wait()
    adapter = adapter_ref[...]
    first = jnp.sum((adapter < ids).astype(jnp.int32), axis=1, keepdims=True)
    shift = jnp.where(adapter == ids, slots * (blocks * BLOCK) - first, 0)
    place = jnp.sum(shift, axis=0, keepdims=True) + lax.broadcasted_iota(jnp.int32, (1, rows), 1)
    spots = lax.broadcasted_iota(jnp.int32, (group * blocks * BLOCK, rows), 0)
    pick = jnp.where(spots == place, 1.0, 0.0).astype(jnp.bfloat16)
    pick_ref[...] = pick
    copies[2].wait()
    packed = jnp.dot(pick, hidden_ref[...], preferred_element_type=jnp.float32)
    packed_ref[...] = packed.astype(jnp.bfloat16).reshape(packed_ref.shape)
    kept_ref[...] = hidden_ref[...]


def pack_rows(hidden, adapter_of_row, adapter_holder_slot, me, orders):
    rows, depth = hidden.shape
    group = adapter_holder_slot.shape[0]
    blocks = MOST // BLOCK
    vmem = pl.BlockSpec(memory_space=pltpu.VMEM)
    smem = pl.BlockSpec(memory_space=pltpu.SMEM)
    anywhere = pl.BlockSpec(memory_space=pltpu.HBM)
    return pl.pallas_call(
        functools.partial(pack_kernel, blocks, orders),
        out_shape=(
            jax.ShapeDtypeStruct((group * blocks, BLOCK, depth), jnp.bfloat16),
            jax.ShapeDtypeStruct((group * MOST, rows), jnp.bfloat16),
            jax.ShapeDtypeStruct((len(orders),), jnp.int32),
            jax.ShapeDtypeStruct((rows, depth), jnp.bfloat16),
        ),
        in_specs=[smem, anywhere, anywhere, anywhere],
        out_specs=(vmem, vmem, smem, vmem),
        scratch_shapes=[
            pltpu.SMEM((group,), jnp.int32),
            pltpu.VMEM((1, rows), jnp.int32),
            pltpu.VMEM((rows, depth), jnp.bfloat16),
            pltpu.SemaphoreType.DMA((3,)),
        ],
        compiler_params=pltpu.CompilerParams(vmem_limit_bytes=24 * 2**20),
    )(me.reshape(1), in_hbm(adapter_holder_slot), in_hbm(adapter_of_row.reshape(1, rows)), in_hbm(hidden))


def adapter_kernel(rows_ref, shrink_ref, expand_ref, out_ref, flag_ref, total_ref):
    step = pl.program_id(0)
    flag_ref[0] = step
    block, depth = rows_ref.shape[1:]
    blocks = MOST // BLOCK
    sources = rows_ref.shape[0] // blocks
    total = jnp.zeros(total_ref.shape, jnp.float32)
    for source in range(sources):
        own = rows_ref[source * blocks : (source + 1) * blocks].reshape(MOST, depth)
        total += lax.dot_general(
            own,
            shrink_ref[:, source * depth : (source + 1) * depth],
            (((1,), (1,)), ((), ())),
            preferred_element_type=jnp.float32,
        )

    @pl.when(step == 0)
    def _():
        total_ref[...] = total

    @pl.when(step > 0)
    def _():
        total_ref[...] += total

    @pl.when(step == pl.num_programs(0) - 1)
    def _():
        rank_rows = total_ref[...].astype(jnp.bfloat16)
        width = out_ref.shape[2]
        for target in range(out_ref.shape[0] // blocks):
            piece = jnp.dot(
                rank_rows,
                expand_ref[:, target * width : (target + 1) * width],
                preferred_element_type=jnp.float32,
            )
            out_ref[target * blocks : (target + 1) * blocks] = piece.astype(jnp.bfloat16).reshape(
                blocks, BLOCK, width
            )


def adapter_output(gathered, shrink, expand, group):
    rank, hidden_width = shrink.shape
    model_width = expand.shape[1]
    depth = gathered.shape[2]
    blocks = MOST // BLOCK
    width = model_width // group
    steps = 4
    sources = group // steps
    return pl.pallas_call(
        adapter_kernel,
        out_shape=(
            jax.ShapeDtypeStruct((group * blocks, BLOCK, width), jnp.bfloat16),
            jax.ShapeDtypeStruct((1,), jnp.int32),
        ),
        grid=(steps,),
        in_specs=[
            pl.BlockSpec((sources * blocks, BLOCK, depth), lambda i: (i, 0, 0)),
            pl.BlockSpec((rank, sources * depth), lambda i: (0, i)),
            pl.BlockSpec((rank, model_width), lambda i: (0, 0)),
        ],
        out_specs=(
            pl.BlockSpec((group * blocks, BLOCK, width), lambda i: (0, 0, 0)),
            pl.BlockSpec(memory_space=pltpu.SMEM),
        ),
        scratch_shapes=[pltpu.VMEM((MOST, rank), jnp.float32)],
        compiler_params=pltpu.CompilerParams(vmem_limit_bytes=32 * 2**20),
        cost_estimate=pl.CostEstimate(
            flops=2 * MOST * rank * (hidden_width + model_width),
            bytes_accessed=2 * rank * (hidden_width + model_width) + 2 * MOST * hidden_width,
            transcendentals=0,
        ),
    )(gathered, shrink, expand)


def shards_by_blocks(
    hidden, down_matrix, shrink_matrices, expand_matrices, adapter_of_row, adapter_holder_slot
):
    group = lax.axis_size("tp")
    me = lax.axis_index("tp")
    rows, depth = hidden.shape
    width = down_matrix.shape[1] // group
    quads = list(range(0, group, 4))
    orders = [q + k for k in (1, 3, 0, 2) for q in quads]
    packed, pick, order, kept_hidden = pack_rows(
        hidden, adapter_of_row, adapter_holder_slot, me, orders
    )
    gathered = lax.all_to_all(packed, "tp", split_axis=0, concat_axis=0, tiled=True)
    kept, sent = chip_sums(kept_hidden, down_matrix, group, order, width)
    gathered, _ = lax.optimization_barrier((gathered, sent))
    pair_in = xor_permute(sent, group, 2)
    shrink = jnp.swapaxes(shrink_matrices, 1, 2)[0]
    expand = jnp.swapaxes(expand_matrices, 1, 2)[0]
    adapter_out, flag = adapter_output(gathered, shrink, expand, group)
    adapter_in = lax.all_to_all(adapter_out, "tp", split_axis=0, concat_axis=0, tiled=True)
    total = line_sums(kept, pair_in, flag[0], group, width)
    base = jnp.transpose(total, (1, 0, 2)).reshape(rows, width)
    adapter_rows = lax.dot_general(
        pick,
        adapter_in.reshape(group * MOST, width),
        (((0,), (0,)), ((), ())),
        preferred_element_type=jnp.float32,
    )
    return (base + ADAPTER_SCALE * adapter_rows).astype(jnp.bfloat16)


def shards(
    hidden, down_matrix, shrink_matrices, expand_matrices, adapter_of_row, adapter_holder_slot
):
    group = lax.axis_size("tp")
    rows, depth = hidden.shape
    width = down_matrix.shape[1] // group
    if width % LANES == 0 and depth % LANES == 0 and group % 4 == 0:
        return shards_by_blocks(
            hidden, down_matrix, shrink_matrices, expand_matrices, adapter_of_row, adapter_holder_slot
        )
    blocks = MOST // BLOCK
    adapter_ids = jnp.arange(group, dtype=jnp.int32)
    row_match = adapter_of_row[:, None] == adapter_ids[None, :]
    row_slot = jnp.sum(jnp.where(row_match, adapter_holder_slot[None, :], 0), axis=1)
    slot_mask = row_slot[None, :] == adapter_ids[:, None]
    before = jnp.cumsum(slot_mask.astype(jnp.int32), axis=1) - 1
    place = jnp.where(slot_mask, before, -1)
    pick = place[:, None, :] == jnp.arange(MOST, dtype=jnp.int32)[None, :, None]
    pick = pick.reshape(group * MOST, rows).astype(jnp.bfloat16)
    packed = jnp.dot(pick, hidden, preferred_element_type=jnp.float32).astype(jnp.bfloat16)
    packed = packed.reshape(group * blocks, BLOCK, depth)
    gathered = lax.all_to_all(packed, "tp", split_axis=0, concat_axis=0, tiled=True)
    partial_value = jnp.dot(hidden, down_matrix, preferred_element_type=jnp.float32)
    base = lax.psum_scatter(partial_value, "tp", scatter_dimension=1, tiled=True)
    own_rows = jnp.transpose(gathered.reshape(group, MOST, depth), (1, 0, 2))
    rank_rows = jnp.dot(
        own_rows.reshape(MOST, group * depth), shrink_matrices[0], preferred_element_type=jnp.float32
    ).astype(jnp.bfloat16)
    adapter_out = lax.dot_general(
        rank_rows, expand_matrices[0], (((1,), (1,)), ((), ())), preferred_element_type=jnp.float32
    ).astype(jnp.bfloat16)
    adapter_out = jnp.transpose(adapter_out.reshape(blocks, BLOCK, group, width), (2, 0, 1, 3))
    adapter_in = lax.all_to_all(
        adapter_out.reshape(group * blocks, BLOCK, width), "tp", split_axis=0, concat_axis=0, tiled=True
    )
    adapter_rows = lax.dot_general(
        pick,
        adapter_in.reshape(group * MOST, width),
        (((0,), (0,)), ((), ())),
        preferred_element_type=jnp.float32,
    )
    return (base + ADAPTER_SCALE * adapter_rows).astype(jnp.bfloat16)


def solution(mesh):
    in_specs = (
        P("rep", "tp"),
        P("tp", None),
        P(("rep", "tp"), None, None),
        P(("rep", "tp"), None, None),
        P("rep"),
        P("rep"),
    )
    out_specs = P("rep", "tp")
    return jax.shard_map(shards, mesh=mesh, in_specs=in_specs, out_specs=out_specs, check_vma=False)
```

```python
import functools

import jax
import jax.numpy as jnp
from jax import lax
from jax.experimental import pallas as pl
from jax.experimental.pallas import tpu as pltpu
from jax.sharding import PartitionSpec as P

ADAPTER_SCALE = 0.5
BLOCK = 4
MOST = 20
LANES = 128
F16_TOP = 14.0
PLANE = 4
HELD = 24


def in_hbm(value):
    return pltpu.with_memory_space_constraint(value, pltpu.HBM)


def xor_permute(value, group, offset):
    return lax.ppermute(value, "tp", [(i, i ^ offset) for i in range(group)])


def column_blocks_kernel(order_ref, hidden_ref, down_ref, out_ref, held_ref, sems):
    count, depth, width = held_ref.shape
    parts = width // LANES
    pieces = sems.shape[1]
    cut = depth // pieces

    def copy(block, piece):
        start = pl.multiple_of(order_ref[block] * width, LANES)
        lines = pl.ds(piece * cut, cut)
        return pltpu.make_async_copy(
            down_ref.at[lines, pl.ds(start, width)], held_ref.at[block, lines], sems.at[block, piece]
        )

    for block in range(count):
        for piece in range(pieces):
            copy(block, piece).start()
    for block in range(count):
        for piece in range(pieces):
            copy(block, piece).wait()
        product = jnp.dot(hidden_ref[...], held_ref[block], preferred_element_type=jnp.float32)
        for lane in range(parts):
            out_ref[block * parts + lane] = product[:, lane * LANES : (lane + 1) * LANES]


def column_blocks(hidden, down_matrix, order, width):
    rows, depth = hidden.shape
    count = order.shape[0]
    pieces = 2 if depth % 32 == 0 else 1
    vmem = pl.BlockSpec(memory_space=pltpu.VMEM)
    return pl.pallas_call(
        column_blocks_kernel,
        out_shape=jax.ShapeDtypeStruct((count * width // LANES, rows, LANES), jnp.float32),
        in_specs=[
            pl.BlockSpec(memory_space=pltpu.SMEM),
            vmem,
            pl.BlockSpec(memory_space=pl.ANY),
        ],
        out_specs=vmem,
        scratch_shapes=[
            pltpu.VMEM((count, depth, width), jnp.bfloat16),
            pltpu.SemaphoreType.DMA((count, pieces)),
        ],
        compiler_params=pltpu.CompilerParams(vmem_limit_bytes=20 * 2**20),
        cost_estimate=pl.CostEstimate(flops=1000, bytes_accessed=1000, transcendentals=0),
    )(order, hidden, in_hbm(down_matrix))


def pack_scaled(value):
    peak = jnp.max(jnp.abs(value), axis=(0, 2), keepdims=True)
    exponent = jnp.ceil(jnp.log2(jnp.maximum(peak, 2.0**-100)))
    scaled = (value * jnp.exp2(F16_TOP - exponent)).astype(jnp.float16)
    marks = jnp.broadcast_to(exponent, (1,) + value.shape[1:]).astype(jnp.float16)
    return jnp.concatenate([scaled, marks], axis=0)


def unpack_scaled(packed):
    exponent = packed[-1:].astype(jnp.float32)
    return packed[:-1].astype(jnp.float32) * jnp.exp2(exponent - F16_TOP)


def pair_sums(hidden, down_matrix, group, order, width):
    half = group * width // LANES // 4
    rows = hidden.shape[0]

    def work():
        odd = column_blocks(hidden, down_matrix, order[: group // 2], width)
        odd_in = xor_permute(odd, group, 1)
        even = column_blocks(hidden, down_matrix, order[group // 2 :], width)
        chip = even + odd_in
        pair_in = xor_permute(pack_scaled(chip[half:]), group, 2)
        return chip[:half] + unpack_scaled(pair_in)

    def idle():
        return jnp.zeros((half, rows, LANES), jnp.float32)

    return lax.cond(order[0] >= 0, work, idle)


def line_sums(pair, group, width):
    rows = pair.shape[1]
    parts = width // LANES
    arrived = [
        xor_permute(pack_scaled(pair[i * parts : (i + 1) * parts]), group, 4 * i)
        for i in range(1, group // 4)
    ]
    total = pair[:parts]
    for packed in arrived:
        total = total + unpack_scaled(packed)
    return jnp.transpose(total, (1, 0, 2)).reshape(rows, width)


def pack_kernel(
    blocks,
    orders,
    me_ref,
    slot_hbm,
    adapter_hbm,
    hidden_hbm,
    packed_ref,
    pick_ref,
    order_ref,
    kept_ref,
    slot_ref,
    adapter_ref,
    hidden_ref,
    sems,
):
    rows = hidden_ref.shape[0]
    group = slot_ref.shape[0]
    copies = [
        pltpu.make_async_copy(slot_hbm, slot_ref, sems.at[0]),
        pltpu.make_async_copy(adapter_hbm, adapter_ref, sems.at[1]),
        pltpu.make_async_copy(hidden_hbm, hidden_ref, sems.at[2]),
    ]
    for copy in copies:
        copy.start()
    for i, offset in enumerate(orders):
        order_ref[i] = me_ref[0] ^ offset
    ids = lax.broadcasted_iota(jnp.int32, (group, 1), 0)
    slots = jnp.zeros((group, 1), jnp.int32)
    copies[0].wait()
    for adapter in range(group):
        slots = jnp.where(ids == adapter, slot_ref[adapter], slots)
    copies[1].wait()
    adapter = adapter_ref[...]
    first = jnp.sum((adapter < ids).astype(jnp.int32), axis=1, keepdims=True)
    shift = jnp.where(adapter == ids, slots * (blocks * BLOCK) - first, 0)
    place = jnp.sum(shift, axis=0, keepdims=True) + lax.broadcasted_iota(jnp.int32, (1, rows), 1)
    spots = lax.broadcasted_iota(jnp.int32, (group * blocks * BLOCK, rows), 0)
    pick = jnp.where(spots == place, 1.0, 0.0).astype(jnp.bfloat16)
    for k in range(PLANE):
        line = lax.broadcasted_iota(jnp.int32, (HELD, rows), 0)
        mine = (line + (me_ref[0] ^ k) * (blocks * BLOCK) == place) & (line < blocks * BLOCK)
        pick_ref[k * HELD : (k + 1) * HELD] = jnp.where(mine, 1.0, 0.0).astype(jnp.bfloat16)
    copies[2].wait()
    packed = jnp.dot(pick, hidden_ref[...], preferred_element_type=jnp.float32)
    packed_ref[...] = packed.astype(jnp.bfloat16).reshape(packed_ref.shape)
    kept_ref[...] = hidden_ref[...]


def pack_rows(hidden, adapter_of_row, adapter_holder_slot, me, orders):
    rows, depth = hidden.shape
    group = adapter_holder_slot.shape[0]
    blocks = MOST // BLOCK
    vmem = pl.BlockSpec(memory_space=pltpu.VMEM)
    smem = pl.BlockSpec(memory_space=pltpu.SMEM)
    anywhere = pl.BlockSpec(memory_space=pltpu.HBM)
    return pl.pallas_call(
        functools.partial(pack_kernel, blocks, orders),
        out_shape=(
            jax.ShapeDtypeStruct((group * blocks, BLOCK, depth), jnp.bfloat16),
            jax.ShapeDtypeStruct((PLANE * HELD, rows), jnp.bfloat16),
            jax.ShapeDtypeStruct((len(orders),), jnp.int32),
            jax.ShapeDtypeStruct((rows, depth), jnp.bfloat16),
        ),
        in_specs=[smem, anywhere, anywhere, anywhere],
        out_specs=(vmem, vmem, smem, vmem),
        scratch_shapes=[
            pltpu.SMEM((group,), jnp.int32),
            pltpu.VMEM((1, rows), jnp.int32),
            pltpu.VMEM((rows, depth), jnp.bfloat16),
            pltpu.SemaphoreType.DMA((3,)),
        ],
        compiler_params=pltpu.CompilerParams(vmem_limit_bytes=24 * 2**20),
    )(me.reshape(1), in_hbm(adapter_holder_slot), in_hbm(adapter_of_row.reshape(1, rows)), in_hbm(hidden))


def adapter_kernel(parts, me_ref, rows_ref, shrink_ref, expand_ref, *refs):
    out_refs, total_ref = refs[:PLANE], refs[PLANE]
    step = pl.program_id(0)
    block, depth = rows_ref.shape[1:]
    blocks = MOST // BLOCK
    sources = rows_ref.shape[0] // blocks
    total = jnp.zeros((MOST, total_ref.shape[1]), jnp.float32)
    for source in range(sources):
        own = rows_ref[source * blocks : (source + 1) * blocks].reshape(MOST, depth)
        total += lax.dot_general(
            own,
            shrink_ref[:, source * depth : (source + 1) * depth],
            (((1,), (1,)), ((), ())),
            preferred_element_type=jnp.float32,
        )

    @pl.when(step == 0)
    def _():
        total_ref[...] = jnp.zeros_like(total_ref)

    total_ref[:MOST] += total

    @pl.when(step == pl.num_programs(0) - 1)
    def _():
        rank_rows = total_ref[...].astype(jnp.bfloat16)
        width = parts * LANES
        for k in range(PLANE):
            for line in range(out_refs[k].shape[0] // parts):
                target = me_ref[0] ^ (PLANE * line + k)
                columns = pl.ds(pl.multiple_of(target * width, LANES), width)
                piece = jnp.dot(rank_rows, expand_ref[:, columns], preferred_element_type=jnp.float32)
                piece = piece.astype(jnp.bfloat16)
                for part in range(parts):
                    out_refs[k][line * parts + part] = piece[:, part * LANES : (part + 1) * LANES]


def adapter_output(gathered, shrink, expand, group, me):
    rank, hidden_width = shrink.shape
    model_width = expand.shape[1]
    depth = gathered.shape[2]
    blocks = MOST // BLOCK
    parts = model_width // group // LANES
    held = (model_width // PLANE // LANES, HELD, LANES)
    steps = 4
    sources = group // steps
    return pl.pallas_call(
        functools.partial(adapter_kernel, parts),
        out_shape=[jax.ShapeDtypeStruct(held, jnp.bfloat16)] * PLANE,
        grid=(steps,),
        in_specs=[
            pl.BlockSpec(memory_space=pltpu.SMEM),
            pl.BlockSpec((sources * blocks, BLOCK, depth), lambda i: (i, 0, 0)),
            pl.BlockSpec((rank, sources * depth), lambda i: (0, i)),
            pl.BlockSpec((rank, model_width), lambda i: (0, 0)),
        ],
        out_specs=[pl.BlockSpec(held, lambda i: (0, 0, 0))] * PLANE,
        scratch_shapes=[pltpu.VMEM((HELD, rank), jnp.float32)],
        compiler_params=pltpu.CompilerParams(vmem_limit_bytes=24 * 2**20),
    )(me.reshape(1), gathered, shrink, expand)


def merge_kernel(pair_ref, pick_ref, *refs):
    in_refs, out_ref, held_ref = refs[:PLANE], refs[PLANE], refs[PLANE + 1]
    for k in range(PLANE):
        held_ref[:, k * HELD : (k + 1) * HELD] = in_refs[k][...]
    pick = pick_ref[...]
    for part in range(pair_ref.shape[0]):
        adapter_rows = lax.dot_general(
            pick, held_ref[part], (((0,), (0,)), ((), ())), preferred_element_type=jnp.float32
        )
        out_ref[part] = pair_ref[part] + ADAPTER_SCALE * adapter_rows


def merge_adapters(pair, pick, arrived):
    vmem = pl.BlockSpec(memory_space=pltpu.VMEM)
    return pl.pallas_call(
        merge_kernel,
        out_shape=jax.ShapeDtypeStruct(pair.shape, jnp.float32),
        in_specs=[vmem] * (2 + PLANE),
        out_specs=vmem,
        scratch_shapes=[pltpu.VMEM((pair.shape[0], PLANE * HELD, LANES), jnp.bfloat16)],
        compiler_params=pltpu.CompilerParams(vmem_limit_bytes=24 * 2**20),
    )(pair, pick, *arrived)


def shards_by_blocks(
    hidden, down_matrix, shrink_matrices, expand_matrices, adapter_of_row, adapter_holder_slot
):
    group = lax.axis_size("tp")
    me = lax.axis_index("tp")
    rows, depth = hidden.shape
    width = down_matrix.shape[1] // group
    quads = list(range(0, group, 4))
    orders = [q + k for k in (1, 3, 0, 2) for q in quads]
    packed, pick, order, kept_hidden = pack_rows(
        hidden, adapter_of_row, adapter_holder_slot, me, orders
    )
    gathered = lax.all_to_all(packed, "tp", split_axis=0, concat_axis=0, tiled=True)
    pair = pair_sums(kept_hidden, down_matrix, group, order, width)
    gathered, _ = lax.optimization_barrier((gathered, pair))
    shrink = jnp.swapaxes(shrink_matrices, 1, 2)[0]
    expand = jnp.swapaxes(expand_matrices, 1, 2)[0]
    outs = adapter_output(gathered, shrink, expand, group, me)
    arrived = [outs[0]] + [xor_permute(outs[k], group, k) for k in range(1, PLANE)]
    merged = merge_adapters(pair, pick, arrived)
    return line_sums(merged, group, width).astype(jnp.bfloat16)


def shards(
    hidden, down_matrix, shrink_matrices, expand_matrices, adapter_of_row, adapter_holder_slot
):
    group = lax.axis_size("tp")
    rows, depth = hidden.shape
    width = down_matrix.shape[1] // group
    if width % LANES == 0 and depth % LANES == 0 and group >= PLANE and group & (group - 1) == 0:
        return shards_by_blocks(
            hidden, down_matrix, shrink_matrices, expand_matrices, adapter_of_row, adapter_holder_slot
        )
    blocks = MOST // BLOCK
    adapter_ids = jnp.arange(group, dtype=jnp.int32)
    row_match = adapter_of_row[:, None] == adapter_ids[None, :]
    row_slot = jnp.sum(jnp.where(row_match, adapter_holder_slot[None, :], 0), axis=1)
    slot_mask = row_slot[None, :] == adapter_ids[:, None]
    before = jnp.cumsum(slot_mask.astype(jnp.int32), axis=1) - 1
    place = jnp.where(slot_mask, before, -1)
    pick = place[:, None, :] == jnp.arange(MOST, dtype=jnp.int32)[None, :, None]
    pick = pick.reshape(group * MOST, rows).astype(jnp.bfloat16)
    packed = jnp.dot(pick, hidden, preferred_element_type=jnp.float32).astype(jnp.bfloat16)
    packed = packed.reshape(group * blocks, BLOCK, depth)
    gathered = lax.all_to_all(packed, "tp", split_axis=0, concat_axis=0, tiled=True)
    partial_value = jnp.dot(hidden, down_matrix, preferred_element_type=jnp.float32)
    base = lax.psum_scatter(partial_value, "tp", scatter_dimension=1, tiled=True)
    own_rows = jnp.transpose(gathered.reshape(group, MOST, depth), (1, 0, 2))
    rank_rows = jnp.dot(
        own_rows.reshape(MOST, group * depth), shrink_matrices[0], preferred_element_type=jnp.float32
    ).astype(jnp.bfloat16)
    adapter_out = lax.dot_general(
        rank_rows, expand_matrices[0], (((1,), (1,)), ((), ())), preferred_element_type=jnp.float32
    ).astype(jnp.bfloat16)
    adapter_out = jnp.transpose(adapter_out.reshape(blocks, BLOCK, group, width), (2, 0, 1, 3))
    adapter_in = lax.all_to_all(
        adapter_out.reshape(group * blocks, BLOCK, width), "tp", split_axis=0, concat_axis=0, tiled=True
    )
    adapter_rows = lax.dot_general(
        pick,
        adapter_in.reshape(group * MOST, width),
        (((0,), (0,)), ((), ())),
        preferred_element_type=jnp.float32,
    )
    return (base + ADAPTER_SCALE * adapter_rows).astype(jnp.bfloat16)


def solution(mesh):
    in_specs = (
        P("rep", "tp"),
        P("tp", None),
        P(("rep", "tp"), None, None),
        P(("rep", "tp"), None, None),
        P("rep"),
        P("rep"),
    )
    out_specs = P("rep", "tp")
    return jax.shard_map(shards, mesh=mesh, in_specs=in_specs, out_specs=out_specs, check_vma=False)
```

```python
import functools

import jax
import jax.numpy as jnp
from jax import lax
from jax.experimental import pallas as pl
from jax.experimental.pallas import tpu as pltpu
from jax.sharding import PartitionSpec as P

ADAPTER_SCALE = 0.5
BLOCK = 4
MOST = 20
LANES = 128
F16_TOP = 14.0
PLANE = 4
HELD = 24


def in_hbm(value):
    return pltpu.with_memory_space_constraint(value, pltpu.HBM)


def xor_permute(value, group, offset):
    return lax.ppermute(value, "tp", [(i, i ^ offset) for i in range(group)])


def column_blocks_kernel(groups, order_ref, hidden_ref, down_ref, *refs):
    carried = len(refs) > groups + 2
    if carried:
        carry_in, refs = refs[0], refs[1:]
        carry = pltpu.make_async_copy(carry_in, refs[groups], refs[-1])
        refs = refs[:groups] + refs[groups + 1 : -1]
    out_refs, held_ref, sems = refs[:groups], refs[groups], refs[groups + 1]
    count, depth, width = held_ref.shape
    parts = width // LANES
    pieces = sems.shape[1]
    cut = depth // pieces

    def copy(block, piece):
        start = pl.multiple_of(order_ref[block] * width, LANES)
        lines = pl.ds(piece * cut, cut)
        return pltpu.make_async_copy(
            down_ref.at[lines, pl.ds(start, width)], held_ref.at[block, lines], sems.at[block, piece]
        )

    for block in range(count):
        for piece in range(pieces):
            copy(block, piece).start()
    if carried:
        carry.start()
    share = count // groups
    for block in range(count):
        for piece in range(pieces):
            copy(block, piece).wait()
        product = jnp.dot(hidden_ref[...], held_ref[block], preferred_element_type=jnp.float32)
        for lane in range(parts):
            out_refs[block // share][block % share * parts + lane] = product[
                :, lane * LANES : (lane + 1) * LANES
            ]
    if carried:
        carry.wait()


def column_blocks(hidden, down_matrix, order, width, groups=1, carry=None):
    rows, depth = hidden.shape
    count = order.shape[0]
    pieces = 2 if depth % 32 == 0 else 1
    vmem = pl.BlockSpec(memory_space=pltpu.VMEM)
    hbm = pl.BlockSpec(memory_space=pl.ANY)
    out_shape = [
        jax.ShapeDtypeStruct((count // groups * width // LANES, rows, LANES), jnp.float32)
    ] * groups
    operands = [order, hidden, in_hbm(down_matrix)]
    in_specs = [pl.BlockSpec(memory_space=pltpu.SMEM), vmem, hbm]
    scratch = [
        pltpu.VMEM((count, depth, width), jnp.bfloat16),
        pltpu.SemaphoreType.DMA((count, pieces)),
    ]
    if carry is not None:
        out_shape.append(jax.ShapeDtypeStruct(carry.shape, carry.dtype))
        operands.append(in_hbm(carry))
        in_specs.append(hbm)
        scratch.append(pltpu.SemaphoreType.DMA)
    return pl.pallas_call(
        functools.partial(column_blocks_kernel, groups),
        out_shape=out_shape,
        in_specs=in_specs,
        out_specs=[vmem] * len(out_shape),
        scratch_shapes=scratch,
        compiler_params=pltpu.CompilerParams(vmem_limit_bytes=(12 + 12 * groups) * 2**20),
        cost_estimate=pl.CostEstimate(flops=1000, bytes_accessed=1000, transcendentals=0),
    )(*operands)


def pack_scaled(value):
    peak = jnp.max(jnp.abs(value), axis=(0, 2), keepdims=True)
    exponent = jnp.ceil(jnp.log2(jnp.maximum(peak, 2.0**-100)))
    scaled = (value * jnp.exp2(F16_TOP - exponent)).astype(jnp.float16)
    marks = jnp.broadcast_to(exponent, (1,) + value.shape[1:]).astype(jnp.float16)
    return jnp.concatenate([scaled, marks], axis=0)


def unpack_scaled(packed):
    exponent = packed[-1:].astype(jnp.float32)
    return packed[:-1].astype(jnp.float32) * jnp.exp2(exponent - F16_TOP)


def pair_sums(hidden, down_matrix, shrink, group, order, width):
    half = group * width // LANES // 4
    rows = hidden.shape[0]
    share = group // 4

    def first():
        (far,) = column_blocks(hidden, down_matrix, order[:share], width)
        far_in = xor_permute(far, group, 1)
        (near,) = column_blocks(hidden, down_matrix, order[share : 2 * share], width)
        return pack_scaled(near + far_in)

    def first_idle():
        return jnp.zeros((half + 1, rows, LANES), jnp.float16)

    sent = lax.cond(order[0] >= 0, first, first_idle)
    pair_in = xor_permute(sent, group, 2)
    order, _ = lax.optimization_barrier((order, sent))

    def second():
        far, near, held = column_blocks(
            hidden, down_matrix, order[2 * share :], width, groups=2, carry=shrink
        )
        return near + xor_permute(far, group, 1), held

    def second_idle():
        return jnp.zeros((half, rows, LANES), jnp.float32), jnp.zeros(shrink.shape, shrink.dtype)

    kept, held = lax.cond(order[1] >= 0, second, second_idle)
    return kept + unpack_scaled(pair_in), held


def line_sums(pair, group, width):
    rows = pair.shape[1]
    parts = width // LANES
    arrived = [
        xor_permute(pack_scaled(pair[i * parts : (i + 1) * parts]), group, 4 * i)
        for i in range(1, group // 4)
    ]
    total = pair[:parts]
    for packed in arrived:
        total = total + unpack_scaled(packed)
    return jnp.transpose(total, (1, 0, 2)).reshape(rows, width)


def pack_kernel(
    blocks,
    orders,
    me_ref,
    slot_hbm,
    adapter_hbm,
    hidden_hbm,
    packed_ref,
    pick_ref,
    order_ref,
    kept_ref,
    slot_ref,
    adapter_ref,
    hidden_ref,
    sems,
):
    rows = hidden_ref.shape[0]
    group = slot_ref.shape[0]
    copies = [
        pltpu.make_async_copy(slot_hbm, slot_ref, sems.at[0]),
        pltpu.make_async_copy(adapter_hbm, adapter_ref, sems.at[1]),
        pltpu.make_async_copy(hidden_hbm, hidden_ref, sems.at[2]),
    ]
    for copy in copies:
        copy.start()
    for i, offset in enumerate(orders):
        order_ref[i] = me_ref[0] ^ offset
    ids = lax.broadcasted_iota(jnp.int32, (group, 1), 0)
    slots = jnp.zeros((group, 1), jnp.int32)
    copies[0].wait()
    for adapter in range(group):
        slots = jnp.where(ids == adapter, slot_ref[adapter], slots)
    copies[1].wait()
    adapter = adapter_ref[...]
    first = jnp.sum((adapter < ids).astype(jnp.int32), axis=1, keepdims=True)
    shift = jnp.where(adapter == ids, slots * (blocks * BLOCK) - first, 0)
    place = jnp.sum(shift, axis=0, keepdims=True) + lax.broadcasted_iota(jnp.int32, (1, rows), 1)
    spots = lax.broadcasted_iota(jnp.int32, (group * blocks * BLOCK, rows), 0)
    pick = jnp.where(spots == place, 1.0, 0.0).astype(jnp.bfloat16)
    for k in range(PLANE):
        line = lax.broadcasted_iota(jnp.int32, (HELD, rows), 0)
        mine = (line + (me_ref[0] ^ k) * (blocks * BLOCK) == place) & (line < blocks * BLOCK)
        pick_ref[k * HELD : (k + 1) * HELD] = jnp.where(mine, 1.0, 0.0).astype(jnp.bfloat16)
    copies[2].wait()
    packed = jnp.dot(pick, hidden_ref[...], preferred_element_type=jnp.float32)
    packed_ref[...] = packed.astype(jnp.bfloat16).reshape(packed_ref.shape)
    kept_ref[...] = hidden_ref[...]


def pack_rows(hidden, adapter_of_row, adapter_holder_slot, me, orders):
    rows, depth = hidden.shape
    group = adapter_holder_slot.shape[0]
    blocks = MOST // BLOCK
    vmem = pl.BlockSpec(memory_space=pltpu.VMEM)
    smem = pl.BlockSpec(memory_space=pltpu.SMEM)
    anywhere = pl.BlockSpec(memory_space=pltpu.HBM)
    return pl.pallas_call(
        functools.partial(pack_kernel, blocks, orders),
        out_shape=(
            jax.ShapeDtypeStruct((group * blocks, BLOCK, depth), jnp.bfloat16),
            jax.ShapeDtypeStruct((PLANE * HELD, rows), jnp.bfloat16),
            jax.ShapeDtypeStruct((len(orders),), jnp.int32),
            jax.ShapeDtypeStruct((rows, depth), jnp.bfloat16),
        ),
        in_specs=[smem, anywhere, anywhere, anywhere],
        out_specs=(vmem, vmem, smem, vmem),
        scratch_shapes=[
            pltpu.SMEM((group,), jnp.int32),
            pltpu.VMEM((1, rows), jnp.int32),
            pltpu.VMEM((rows, depth), jnp.bfloat16),
            pltpu.SemaphoreType.DMA((3,)),
        ],
        compiler_params=pltpu.CompilerParams(vmem_limit_bytes=24 * 2**20),
    )(me.reshape(1), in_hbm(adapter_holder_slot), in_hbm(adapter_of_row.reshape(1, rows)), in_hbm(hidden))


def adapter_kernel(parts, me_ref, rows_ref, shrink_ref, expand_ref, *refs):
    out_refs, total_ref = refs[:PLANE], refs[PLANE]
    step = pl.program_id(0)
    block, depth = rows_ref.shape[1:]
    blocks = MOST // BLOCK
    sources = rows_ref.shape[0] // blocks
    total = jnp.zeros((MOST, total_ref.shape[1]), jnp.float32)
    for source in range(sources):
        own = rows_ref[source * blocks : (source + 1) * blocks].reshape(MOST, depth)
        total += lax.dot_general(
            own,
            shrink_ref[:, source * depth : (source + 1) * depth],
            (((1,), (1,)), ((), ())),
            preferred_element_type=jnp.float32,
        )

    @pl.when(step == 0)
    def _():
        total_ref[...] = jnp.zeros_like(total_ref)

    total_ref[:MOST] += total

    @pl.when(step == pl.num_programs(0) - 1)
    def _():
        rank_rows = total_ref[...].astype(jnp.bfloat16)
        width = parts * LANES
        for k in range(PLANE):
            for line in range(out_refs[k].shape[0] // parts):
                target = me_ref[0] ^ (PLANE * line + k)
                columns = pl.ds(pl.multiple_of(target * width, LANES), width)
                piece = jnp.dot(rank_rows, expand_ref[:, columns], preferred_element_type=jnp.float32)
                piece = piece.astype(jnp.bfloat16)
                for part in range(parts):
                    out_refs[k][line * parts + part] = piece[:, part * LANES : (part + 1) * LANES]


def adapter_output(gathered, shrink, expand, group, me):
    rank, hidden_width = shrink.shape
    model_width = expand.shape[1]
    depth = gathered.shape[2]
    blocks = MOST // BLOCK
    parts = model_width // group // LANES
    held = (model_width // PLANE // LANES, HELD, LANES)
    steps = 4
    sources = group // steps
    return pl.pallas_call(
        functools.partial(adapter_kernel, parts),
        out_shape=[jax.ShapeDtypeStruct(held, jnp.bfloat16)] * PLANE,
        grid=(steps,),
        in_specs=[
            pl.BlockSpec(memory_space=pltpu.SMEM),
            pl.BlockSpec((sources * blocks, BLOCK, depth), lambda i: (i, 0, 0)),
            pl.BlockSpec((rank, sources * depth), lambda i: (0, i)),
            pl.BlockSpec((rank, model_width), lambda i: (0, 0)),
        ],
        out_specs=[pl.BlockSpec(held, lambda i: (0, 0, 0))] * PLANE,
        scratch_shapes=[pltpu.VMEM((HELD, rank), jnp.float32)],
        compiler_params=pltpu.CompilerParams(vmem_limit_bytes=24 * 2**20),
    )(me.reshape(1), gathered, shrink, expand)


def merge_kernel(pair_ref, pick_ref, *refs):
    in_refs, out_ref, held_ref = refs[:PLANE], refs[PLANE], refs[PLANE + 1]
    for k in range(PLANE):
        held_ref[:, k * HELD : (k + 1) * HELD] = in_refs[k][...]
    pick = pick_ref[...]
    for part in range(pair_ref.shape[0]):
        adapter_rows = lax.dot_general(
            pick, held_ref[part], (((0,), (0,)), ((), ())), preferred_element_type=jnp.float32
        )
        out_ref[part] = pair_ref[part] + ADAPTER_SCALE * adapter_rows


def merge_adapters(pair, pick, arrived):
    vmem = pl.BlockSpec(memory_space=pltpu.VMEM)
    return pl.pallas_call(
        merge_kernel,
        out_shape=jax.ShapeDtypeStruct(pair.shape, jnp.float32),
        in_specs=[vmem] * (2 + PLANE),
        out_specs=vmem,
        scratch_shapes=[pltpu.VMEM((pair.shape[0], PLANE * HELD, LANES), jnp.bfloat16)],
        compiler_params=pltpu.CompilerParams(vmem_limit_bytes=24 * 2**20),
    )(pair, pick, *arrived)


def shards_by_blocks(
    hidden, down_matrix, shrink_matrices, expand_matrices, adapter_of_row, adapter_holder_slot
):
    group = lax.axis_size("tp")
    me = lax.axis_index("tp")
    rows, depth = hidden.shape
    width = down_matrix.shape[1] // group
    quads = list(range(0, group, 4))
    orders = [q + k for k in (3, 2, 1, 0) for q in quads]
    packed, pick, order, kept_hidden = pack_rows(
        hidden, adapter_of_row, adapter_holder_slot, me, orders
    )
    gathered = lax.all_to_all(packed, "tp", split_axis=0, concat_axis=0, tiled=True)
    shrink = jnp.swapaxes(shrink_matrices, 1, 2)[0]
    pair, shrink = pair_sums(kept_hidden, down_matrix, shrink, group, order, width)
    gathered, _ = lax.optimization_barrier((gathered, pair))
    expand = jnp.swapaxes(expand_matrices, 1, 2)[0]
    outs = adapter_output(gathered, shrink, expand, group, me)
    arrived = [outs[0]] + [xor_permute(outs[k], group, k) for k in range(1, PLANE)]
    merged = merge_adapters(pair, pick, arrived)
    return line_sums(merged, group, width).astype(jnp.bfloat16)


def shards(
    hidden, down_matrix, shrink_matrices, expand_matrices, adapter_of_row, adapter_holder_slot
):
    group = lax.axis_size("tp")
    rows, depth = hidden.shape
    width = down_matrix.shape[1] // group
    if width % LANES == 0 and depth % LANES == 0 and group >= PLANE and group & (group - 1) == 0:
        return shards_by_blocks(
            hidden, down_matrix, shrink_matrices, expand_matrices, adapter_of_row, adapter_holder_slot
        )
    blocks = MOST // BLOCK
    adapter_ids = jnp.arange(group, dtype=jnp.int32)
    row_match = adapter_of_row[:, None] == adapter_ids[None, :]
    row_slot = jnp.sum(jnp.where(row_match, adapter_holder_slot[None, :], 0), axis=1)
    slot_mask = row_slot[None, :] == adapter_ids[:, None]
    before = jnp.cumsum(slot_mask.astype(jnp.int32), axis=1) - 1
    place = jnp.where(slot_mask, before, -1)
    pick = place[:, None, :] == jnp.arange(MOST, dtype=jnp.int32)[None, :, None]
    pick = pick.reshape(group * MOST, rows).astype(jnp.bfloat16)
    packed = jnp.dot(pick, hidden, preferred_element_type=jnp.float32).astype(jnp.bfloat16)
    packed = packed.reshape(group * blocks, BLOCK, depth)
    gathered = lax.all_to_all(packed, "tp", split_axis=0, concat_axis=0, tiled=True)
    partial_value = jnp.dot(hidden, down_matrix, preferred_element_type=jnp.float32)
    base = lax.psum_scatter(partial_value, "tp", scatter_dimension=1, tiled=True)
    own_rows = jnp.transpose(gathered.reshape(group, MOST, depth), (1, 0, 2))
    rank_rows = jnp.dot(
        own_rows.reshape(MOST, group * depth), shrink_matrices[0], preferred_element_type=jnp.float32
    ).astype(jnp.bfloat16)
    adapter_out = lax.dot_general(
        rank_rows, expand_matrices[0], (((1,), (1,)), ((), ())), preferred_element_type=jnp.float32
    ).astype(jnp.bfloat16)
    adapter_out = jnp.transpose(adapter_out.reshape(blocks, BLOCK, group, width), (2, 0, 1, 3))
    adapter_in = lax.all_to_all(
        adapter_out.reshape(group * blocks, BLOCK, width), "tp", split_axis=0, concat_axis=0, tiled=True
    )
    adapter_rows = lax.dot_general(
        pick,
        adapter_in.reshape(group * MOST, width),
        (((0,), (0,)), ((), ())),
        preferred_element_type=jnp.float32,
    )
    return (base + ADAPTER_SCALE * adapter_rows).astype(jnp.bfloat16)


def solution(mesh):
    in_specs = (
        P("rep", "tp"),
        P("tp", None),
        P(("rep", "tp"), None, None),
        P(("rep", "tp"), None, None),
        P("rep"),
        P("rep"),
    )
    out_specs = P("rep", "tp")
    return jax.shard_map(shards, mesh=mesh, in_specs=in_specs, out_specs=out_specs, check_vma=False)
```

```python
import functools

import jax
import jax.numpy as jnp
from jax import lax
from jax.experimental import pallas as pl
from jax.experimental.pallas import tpu as pltpu
from jax.sharding import PartitionSpec as P

ADAPTER_SCALE = 0.5
BLOCK = 4
MOST = 20
LANES = 128
F16_TOP = 14.0
PLANE = 4
HELD = 24


def in_hbm(value):
    return pltpu.with_memory_space_constraint(value, pltpu.HBM)


def xor_permute(value, group, offset):
    return lax.ppermute(value, "tp", [(i, i ^ offset) for i in range(group)])


def column_blocks_kernel(groups, order_ref, hidden_ref, down_ref, *refs):
    out_refs, held_ref, sems = refs[:groups], refs[groups], refs[groups + 1]
    count, depth, width = held_ref.shape
    parts = width // LANES
    pieces = sems.shape[1]
    cut = depth // pieces

    def copy(block, piece):
        start = pl.multiple_of(order_ref[block] * width, LANES)
        lines = pl.ds(piece * cut, cut)
        return pltpu.make_async_copy(
            down_ref.at[lines, pl.ds(start, width)], held_ref.at[block, lines], sems.at[block, piece]
        )

    for block in range(count):
        for piece in range(pieces):
            copy(block, piece).start()
    share = count // groups
    for block in range(count):
        for piece in range(pieces):
            copy(block, piece).wait()
        product = jnp.dot(hidden_ref[...], held_ref[block], preferred_element_type=jnp.float32)
        for lane in range(parts):
            out_refs[block // share][block % share * parts + lane] = product[
                :, lane * LANES : (lane + 1) * LANES
            ]


def column_blocks(hidden, down_matrix, order, width, groups=1):
    rows, depth = hidden.shape
    count = order.shape[0]
    pieces = 2 if depth % 32 == 0 else 1
    vmem = pl.BlockSpec(memory_space=pltpu.VMEM)
    out = jax.ShapeDtypeStruct((count // groups * width // LANES, rows, LANES), jnp.float32)
    return pl.pallas_call(
        functools.partial(column_blocks_kernel, groups),
        out_shape=[out] * groups,
        in_specs=[
            pl.BlockSpec(memory_space=pltpu.SMEM),
            vmem,
            pl.BlockSpec(memory_space=pl.ANY),
        ],
        out_specs=[vmem] * groups,
        scratch_shapes=[
            pltpu.VMEM((count, depth, width), jnp.bfloat16),
            pltpu.SemaphoreType.DMA((count, pieces)),
        ],
        compiler_params=pltpu.CompilerParams(vmem_limit_bytes=(12 + 12 * groups) * 2**20),
        cost_estimate=pl.CostEstimate(flops=1000, bytes_accessed=1000, transcendentals=0),
    )(order, hidden, in_hbm(down_matrix))


def pack_scaled(value):
    peak = jnp.max(jnp.abs(value), axis=(0, 2), keepdims=True)
    exponent = jnp.ceil(jnp.log2(jnp.maximum(peak, 2.0**-100)))
    scaled = (value * jnp.exp2(F16_TOP - exponent)).astype(jnp.float16)
    marks = jnp.broadcast_to(exponent, (1,) + value.shape[1:]).astype(jnp.float16)
    return jnp.concatenate([scaled, marks], axis=0)


def unpack_scaled(packed):
    exponent = packed[-1:].astype(jnp.float32)
    return packed[:-1].astype(jnp.float32) * jnp.exp2(exponent - F16_TOP)


def pair_sums(hidden, down_matrix, group, order, width):
    half = group * width // LANES // 4
    rows = hidden.shape[0]
    share = group // 4

    def first():
        (far,) = column_blocks(hidden, down_matrix, order[:share], width)
        far_in = xor_permute(far, group, 1)
        (near,) = column_blocks(hidden, down_matrix, order[share : 2 * share], width)
        return pack_scaled(near + far_in)

    def first_idle():
        return jnp.zeros((half + 1, rows, LANES), jnp.float16)

    def whole():
        sent = lax.cond(order[1] >= 0, first, first_idle)
        pair_in = xor_permute(sent, group, 2)
        later, _ = lax.optimization_barrier((order, sent))

        def second():
            far, near = column_blocks(hidden, down_matrix, later[2 * share :], width, groups=2)
            return near + xor_permute(far, group, 1)

        kept = lax.cond(later[2] >= 0, second, idle)
        return kept + unpack_scaled(pair_in)

    def idle():
        return jnp.zeros((half, rows, LANES), jnp.float32)

    return lax.cond(order[0] >= 0, whole, idle)


def line_sums(pair, group, width):
    rows = pair.shape[1]
    parts = width // LANES
    arrived = [
        xor_permute(pack_scaled(pair[i * parts : (i + 1) * parts]), group, 4 * i)
        for i in range(1, group // 4)
    ]
    total = pair[:parts]
    for packed in arrived:
        total = total + unpack_scaled(packed)
    return jnp.transpose(total, (1, 0, 2)).reshape(rows, width)


def pack_kernel(
    blocks, orders, me_ref, slot_hbm, adapter_hbm, hidden_hbm, other_hbm, *refs
):
    chips = len(refs) - 8
    packed_refs = refs[:chips]
    pick_ref, order_ref, kept_ref, slot_ref, adapter_ref, hidden_ref, other_ref, sems = refs[chips:]
    rows = hidden_ref.shape[0]
    group = slot_ref.shape[0]
    me = me_ref[0]
    copies = [
        pltpu.make_async_copy(slot_hbm, slot_ref, sems.at[0]),
        pltpu.make_async_copy(adapter_hbm, adapter_ref, sems.at[1]),
        pltpu.make_async_copy(hidden_hbm, hidden_ref, sems.at[2]),
        pltpu.make_async_copy(other_hbm, other_ref, sems.at[3]),
    ]
    for copy in copies:
        copy.start()
    for i, offset in enumerate(orders):
        order_ref[i] = me ^ offset
    ids = lax.broadcasted_iota(jnp.int32, (group, 1), 0)
    slots = jnp.zeros((group, 1), jnp.int32)
    copies[0].wait()
    for adapter in range(group):
        slots = jnp.where(ids == adapter, slot_ref[adapter], slots)
    copies[1].wait()
    adapter = adapter_ref[...]
    first = jnp.sum((adapter < ids).astype(jnp.int32), axis=1, keepdims=True)
    offset = jnp.sum(jnp.where(adapter == ids, slots ^ me, 0), axis=0, keepdims=True)
    first = jnp.sum(jnp.where(adapter == ids, first, 0), axis=0, keepdims=True)
    index = lax.broadcasted_iota(jnp.int32, (1, rows), 1) - first
    for k in range(PLANE):
        line = lax.broadcasted_iota(jnp.int32, (HELD, rows), 0)
        mine = (offset == k) & (index == line)
        pick_ref[k * HELD : (k + 1) * HELD] = jnp.where(mine, 1.0, 0.0).astype(jnp.bfloat16)
    held = blocks * BLOCK
    place = jnp.where((offset & 1) == 0, (offset >> 1) * held + index, -1)
    spots = lax.broadcasted_iota(jnp.int32, (chips * held, rows), 0)
    pick = jnp.where(spots == place, 1.0, 0.0).astype(jnp.bfloat16)
    for source, source_ref in enumerate((hidden_ref, other_ref)):
        copies[2 + source].wait()
        packed = jnp.dot(pick, source_ref[...], preferred_element_type=jnp.float32)
        packed = packed.astype(jnp.bfloat16).reshape(chips * blocks, BLOCK, packed.shape[1])
        for chip in range(chips):
            packed_refs[chip][source * blocks : (source + 1) * blocks] = packed[
                chip * blocks : (chip + 1) * blocks
            ]
    kept_ref[...] = hidden_ref[...]


def pack_rows(hidden, other, adapter_of_row, adapter_holder_slot, me, orders):
    rows, depth = hidden.shape
    group = adapter_holder_slot.shape[0]
    blocks = MOST // BLOCK
    chips = group // 2
    vmem = pl.BlockSpec(memory_space=pltpu.VMEM)
    smem = pl.BlockSpec(memory_space=pltpu.SMEM)
    anywhere = pl.BlockSpec(memory_space=pl.ANY)
    return pl.pallas_call(
        functools.partial(pack_kernel, blocks, orders),
        out_shape=[jax.ShapeDtypeStruct((2 * blocks, BLOCK, depth), jnp.bfloat16)] * chips
        + [
            jax.ShapeDtypeStruct((PLANE * HELD, rows), jnp.bfloat16),
            jax.ShapeDtypeStruct((len(orders),), jnp.int32),
            jax.ShapeDtypeStruct((rows, depth), jnp.bfloat16),
        ],
        in_specs=[smem] + [anywhere] * 4,
        out_specs=[vmem] * (chips + 1) + [smem, vmem],
        scratch_shapes=[
            pltpu.SMEM((group,), jnp.int32),
            pltpu.VMEM((1, rows), jnp.int32),
            pltpu.VMEM((rows, depth), jnp.bfloat16),
            pltpu.VMEM((rows, depth), jnp.bfloat16),
            pltpu.SemaphoreType.DMA((4,)),
        ],
        compiler_params=pltpu.CompilerParams(vmem_limit_bytes=24 * 2**20),
    )(
        me.reshape(1),
        in_hbm(adapter_holder_slot),
        in_hbm(adapter_of_row.reshape(1, rows)),
        in_hbm(hidden),
        other,
    )


def adapter_kernel(parts, chips, me_ref, *refs):
    row_refs, (shrink_hbm, expand_hbm) = refs[:chips], refs[chips : chips + 2]
    out_refs = refs[chips + 2 : chips + 2 + PLANE]
    shrink_ref, expand_ref, total_ref, sems, expand_sem = refs[chips + 2 + PLANE :]
    me = me_ref[0]
    block, depth = row_refs[0].shape[1:]
    blocks = MOST // BLOCK

    def copy(source):
        start = pl.multiple_of((me ^ source) * depth, LANES)
        return pltpu.make_async_copy(
            shrink_hbm.at[:, pl.ds(start, depth)], shrink_ref.at[source], sems.at[source]
        )

    for source in range(2 * chips):
        copy(source).start()
    expand_copy = pltpu.make_async_copy(expand_hbm, expand_ref, expand_sem)
    expand_copy.start()
    total = jnp.zeros((MOST, total_ref.shape[1]), jnp.float32)
    for source in range(2 * chips):
        copy(source).wait()
        part = source % 2
        own = row_refs[source // 2][part * blocks : (part + 1) * blocks].reshape(MOST, depth)
        total += lax.dot_general(
            own, shrink_ref[source], (((1,), (1,)), ((), ())), preferred_element_type=jnp.float32
        )
    total_ref[...] = jnp.zeros_like(total_ref)
    total_ref[:MOST] = total
    rank_rows = total_ref[...].astype(jnp.bfloat16)
    expand_copy.wait()
    width = parts * LANES
    for k in range(PLANE):
        for line in range(out_refs[k].shape[0] // parts):
            target = me ^ (PLANE * line + k)
            columns = pl.ds(pl.multiple_of(target * width, LANES), width)
            piece = jnp.dot(rank_rows, expand_ref[:, columns], preferred_element_type=jnp.float32)
            piece = piece.astype(jnp.bfloat16)
            for part in range(parts):
                out_refs[k][line * parts + part] = piece[:, part * LANES : (part + 1) * LANES]


def adapter_output(gathered, shrink, expand, group, me):
    rank = shrink.shape[0]
    model_width = expand.shape[1]
    depth = gathered[0].shape[2]
    parts = model_width // group // LANES
    held = (model_width // PLANE // LANES, HELD, LANES)
    vmem = pl.BlockSpec(memory_space=pltpu.VMEM)
    anywhere = pl.BlockSpec(memory_space=pl.ANY)
    return pl.pallas_call(
        functools.partial(adapter_kernel, parts, group // 2),
        out_shape=[jax.ShapeDtypeStruct(held, jnp.bfloat16)] * PLANE,
        in_specs=[pl.BlockSpec(memory_space=pltpu.SMEM)]
        + [vmem] * len(gathered)
        + [anywhere] * 2,
        out_specs=[vmem] * PLANE,
        scratch_shapes=[
            pltpu.VMEM((group, rank, depth), jnp.bfloat16),
            pltpu.VMEM((rank, model_width), jnp.bfloat16),
            pltpu.VMEM((HELD, rank), jnp.float32),
            pltpu.SemaphoreType.DMA((group,)),
            pltpu.SemaphoreType.DMA,
        ],
        compiler_params=pltpu.CompilerParams(vmem_limit_bytes=24 * 2**20),
    )(me.reshape(1), *gathered, in_hbm(shrink), in_hbm(expand))


def merge_kernel(pair_ref, pick_ref, *refs):
    in_refs, out_ref, held_ref = refs[:PLANE], refs[PLANE], refs[PLANE + 1]
    for k in range(PLANE):
        held_ref[:, k * HELD : (k + 1) * HELD] = in_refs[k][...]
    pick = pick_ref[...]
    for part in range(pair_ref.shape[0]):
        adapter_rows = lax.dot_general(
            pick, held_ref[part], (((0,), (0,)), ((), ())), preferred_element_type=jnp.float32
        )
        out_ref[part] = pair_ref[part] + ADAPTER_SCALE * adapter_rows


def merge_adapters(pair, pick, arrived):
    vmem = pl.BlockSpec(memory_space=pltpu.VMEM)
    return pl.pallas_call(
        merge_kernel,
        out_shape=jax.ShapeDtypeStruct(pair.shape, jnp.float32),
        in_specs=[vmem] * (2 + PLANE),
        out_specs=vmem,
        scratch_shapes=[pltpu.VMEM((pair.shape[0], PLANE * HELD, LANES), jnp.bfloat16)],
        compiler_params=pltpu.CompilerParams(vmem_limit_bytes=24 * 2**20),
    )(pair, pick, *arrived)


def shards_by_blocks(
    hidden, down_matrix, shrink_matrices, expand_matrices, adapter_of_row, adapter_holder_slot
):
    group = lax.axis_size("tp")
    me = lax.axis_index("tp")
    rows, depth = hidden.shape
    width = down_matrix.shape[1] // group
    quads = list(range(0, group, 4))
    orders = [q + k for k in (3, 2, 1, 0) for q in quads]
    chips = group // 2
    other = xor_permute(hidden, group, 1)
    *packed, pick, order, kept_hidden = pack_rows(
        hidden, other, adapter_of_row, adapter_holder_slot, me, orders
    )
    gathered = [packed[0]] + [xor_permute(packed[q], group, 2 * q) for q in range(1, chips)]
    pair = pair_sums(kept_hidden, down_matrix, group, order, width)
    gathered, _ = lax.optimization_barrier((gathered, pair))
    shrink = jnp.swapaxes(shrink_matrices, 1, 2)[0]
    expand = jnp.swapaxes(expand_matrices, 1, 2)[0]
    outs = adapter_output(gathered, shrink, expand, group, me)
    arrived = [outs[0]] + [xor_permute(outs[k], group, k) for k in range(1, PLANE)]
    merged = merge_adapters(pair, pick, arrived)
    return line_sums(merged, group, width).astype(jnp.bfloat16)


def shards(
    hidden, down_matrix, shrink_matrices, expand_matrices, adapter_of_row, adapter_holder_slot
):
    group = lax.axis_size("tp")
    rows, depth = hidden.shape
    width = down_matrix.shape[1] // group
    if width % LANES == 0 and depth % LANES == 0 and group >= PLANE and group & (group - 1) == 0:
        return shards_by_blocks(
            hidden, down_matrix, shrink_matrices, expand_matrices, adapter_of_row, adapter_holder_slot
        )
    blocks = MOST // BLOCK
    adapter_ids = jnp.arange(group, dtype=jnp.int32)
    row_match = adapter_of_row[:, None] == adapter_ids[None, :]
    row_slot = jnp.sum(jnp.where(row_match, adapter_holder_slot[None, :], 0), axis=1)
    slot_mask = row_slot[None, :] == adapter_ids[:, None]
    before = jnp.cumsum(slot_mask.astype(jnp.int32), axis=1) - 1
    place = jnp.where(slot_mask, before, -1)
    pick = place[:, None, :] == jnp.arange(MOST, dtype=jnp.int32)[None, :, None]
    pick = pick.reshape(group * MOST, rows).astype(jnp.bfloat16)
    packed = jnp.dot(pick, hidden, preferred_element_type=jnp.float32).astype(jnp.bfloat16)
    packed = packed.reshape(group * blocks, BLOCK, depth)
    gathered = lax.all_to_all(packed, "tp", split_axis=0, concat_axis=0, tiled=True)
    partial_value = jnp.dot(hidden, down_matrix, preferred_element_type=jnp.float32)
    base = lax.psum_scatter(partial_value, "tp", scatter_dimension=1, tiled=True)
    own_rows = jnp.transpose(gathered.reshape(group, MOST, depth), (1, 0, 2))
    rank_rows = jnp.dot(
        own_rows.reshape(MOST, group * depth), shrink_matrices[0], preferred_element_type=jnp.float32
    ).astype(jnp.bfloat16)
    adapter_out = lax.dot_general(
        rank_rows, expand_matrices[0], (((1,), (1,)), ((), ())), preferred_element_type=jnp.float32
    ).astype(jnp.bfloat16)
    adapter_out = jnp.transpose(adapter_out.reshape(blocks, BLOCK, group, width), (2, 0, 1, 3))
    adapter_in = lax.all_to_all(
        adapter_out.reshape(group * blocks, BLOCK, width), "tp", split_axis=0, concat_axis=0, tiled=True
    )
    adapter_rows = lax.dot_general(
        pick,
        adapter_in.reshape(group * MOST, width),
        (((0,), (0,)), ((), ())),
        preferred_element_type=jnp.float32,
    )
    return (base + ADAPTER_SCALE * adapter_rows).astype(jnp.bfloat16)


def solution(mesh):
    in_specs = (
        P("rep", "tp"),
        P("tp", None),
        P(("rep", "tp"), None, None),
        P(("rep", "tp"), None, None),
        P("rep"),
        P("rep"),
    )
    out_specs = P("rep", "tp")
    return jax.shard_map(shards, mesh=mesh, in_specs=in_specs, out_specs=out_specs, check_vma=False)
```

```python
import functools

import jax
import jax.numpy as jnp
from jax import lax
from jax.experimental import pallas as pl
from jax.experimental.pallas import tpu as pltpu
from jax.sharding import PartitionSpec as P

ADAPTER_SCALE = 0.5
BLOCK = 4
MOST = 20
LANES = 128
F16_TOP = 14.0
PLANE = 4
HELD = 24
IN_FLIGHT = 4


def in_hbm(value):
    return pltpu.with_memory_space_constraint(value, pltpu.HBM)


def xor_permute(value, group, offset):
    return lax.ppermute(value, "tp", [(i, i ^ offset) for i in range(group)])


def column_blocks_kernel(groups, order_ref, hidden_ref, down_ref, *refs):
    out_refs, held_ref, sems = refs[:groups], refs[groups], refs[groups + 1]
    count, depth, width = held_ref.shape
    parts = width // LANES
    pieces = sems.shape[1]
    cut = depth // pieces

    def copy(block, piece):
        start = pl.multiple_of(order_ref[block] * width, LANES)
        lines = pl.ds(piece * cut, cut)
        return pltpu.make_async_copy(
            down_ref.at[lines, pl.ds(start, width)], held_ref.at[block, lines], sems.at[block, piece]
        )

    for block in range(count):
        for piece in range(pieces):
            copy(block, piece).start()
    share = count // groups
    for block in range(count):
        for piece in range(pieces):
            copy(block, piece).wait()
        product = jnp.dot(hidden_ref[...], held_ref[block], preferred_element_type=jnp.float32)
        for lane in range(parts):
            out_refs[block // share][block % share * parts + lane] = product[
                :, lane * LANES : (lane + 1) * LANES
            ]


def column_blocks(hidden, down_matrix, order, width, groups=1):
    rows, depth = hidden.shape
    count = order.shape[0]
    pieces = 2 if depth % 32 == 0 else 1
    vmem = pl.BlockSpec(memory_space=pltpu.VMEM)
    out = jax.ShapeDtypeStruct((count // groups * width // LANES, rows, LANES), jnp.float32)
    return pl.pallas_call(
        functools.partial(column_blocks_kernel, groups),
        out_shape=[out] * groups,
        in_specs=[
            pl.BlockSpec(memory_space=pltpu.SMEM),
            vmem,
            pl.BlockSpec(memory_space=pl.ANY),
        ],
        out_specs=[vmem] * groups,
        scratch_shapes=[
            pltpu.VMEM((count, depth, width), jnp.bfloat16),
            pltpu.SemaphoreType.DMA((count, pieces)),
        ],
        compiler_params=pltpu.CompilerParams(vmem_limit_bytes=(12 + 12 * groups) * 2**20),
        cost_estimate=pl.CostEstimate(flops=1000, bytes_accessed=1000, transcendentals=0),
    )(order, hidden, in_hbm(down_matrix))


def pack_scaled(value):
    peak = jnp.max(jnp.abs(value), axis=(0, 2), keepdims=True)
    exponent = jnp.ceil(jnp.log2(jnp.maximum(peak, 2.0**-100)))
    scaled = (value * jnp.exp2(F16_TOP - exponent)).astype(jnp.float16)
    marks = jnp.broadcast_to(exponent, (1,) + value.shape[1:]).astype(jnp.float16)
    return jnp.concatenate([scaled, marks], axis=0)


def unpack_scaled(packed):
    exponent = packed[-1:].astype(jnp.float32)
    return packed[:-1].astype(jnp.float32) * jnp.exp2(exponent - F16_TOP)


def pair_sums(hidden, down_matrix, group, order, width):
    half = group * width // LANES // 4
    rows = hidden.shape[0]
    share = group // 4

    def first():
        (far,) = column_blocks(hidden, down_matrix, order[:share], width)
        far_in = xor_permute(far, group, 1)
        (near,) = column_blocks(hidden, down_matrix, order[share : 2 * share], width)
        return pack_scaled(near + far_in)

    def first_idle():
        return jnp.zeros((half + 1, rows, LANES), jnp.float16)

    def whole():
        sent = lax.cond(order[1] >= 0, first, first_idle)
        pair_in = xor_permute(sent, group, 2)
        later, _ = lax.optimization_barrier((order, sent))

        def second():
            far, near = column_blocks(hidden, down_matrix, later[2 * share :], width, groups=2)
            return near + xor_permute(far, group, 1)

        kept = lax.cond(later[2] >= 0, second, idle)
        return kept + unpack_scaled(pair_in)

    def idle():
        return jnp.zeros((half, rows, LANES), jnp.float32)

    return lax.cond(order[0] >= 0, whole, idle)


def line_sums(pair, group, width):
    rows = pair.shape[1]
    parts = width // LANES
    arrived = [
        xor_permute(pack_scaled(pair[i * parts : (i + 1) * parts]), group, 4 * i)
        for i in range(1, group // 4)
    ]
    total = pair[:parts]
    for packed in arrived:
        total = total + unpack_scaled(packed)
    return jnp.transpose(total, (1, 0, 2)).reshape(rows, width)


def pack_kernel(
    blocks,
    orders,
    me_ref,
    slot_hbm,
    adapter_hbm,
    hidden_hbm,
    other_hbm,
    packed_ref,
    pick_ref,
    order_ref,
    kept_ref,
    slot_ref,
    adapter_ref,
    hidden_ref,
    other_ref,
    sems,
):
    rows = hidden_ref.shape[0]
    group = slot_ref.shape[0]
    chips = group // 2
    me = me_ref[0]
    copies = [
        pltpu.make_async_copy(slot_hbm, slot_ref, sems.at[0]),
        pltpu.make_async_copy(adapter_hbm, adapter_ref, sems.at[1]),
        pltpu.make_async_copy(hidden_hbm, hidden_ref, sems.at[2]),
        pltpu.make_async_copy(other_hbm, other_ref, sems.at[3]),
    ]
    for copy in copies:
        copy.start()
    for i, offset in enumerate(orders):
        order_ref[i] = me ^ offset
    ids = lax.broadcasted_iota(jnp.int32, (group, 1), 0)
    slots = jnp.zeros((group, 1), jnp.int32)
    copies[0].wait()
    for adapter in range(group):
        slots = jnp.where(ids == adapter, slot_ref[adapter], slots)
    copies[1].wait()
    adapter = adapter_ref[...]
    first = jnp.sum((adapter < ids).astype(jnp.int32), axis=1, keepdims=True)
    slot = jnp.sum(jnp.where(adapter == ids, slots, 0), axis=0, keepdims=True)
    offset = slot ^ me
    first = jnp.sum(jnp.where(adapter == ids, first, 0), axis=0, keepdims=True)
    index = lax.broadcasted_iota(jnp.int32, (1, rows), 1) - first
    for k in range(PLANE):
        line = lax.broadcasted_iota(jnp.int32, (HELD, rows), 0)
        mine = (offset == k) & (index == line)
        pick_ref[k * HELD : (k + 1) * HELD] = jnp.where(mine, 1.0, 0.0).astype(jnp.bfloat16)
    held = blocks * BLOCK
    place = jnp.where((offset & 1) == 0, (slot >> 1) * held + index, -1)
    spots = lax.broadcasted_iota(jnp.int32, (chips * held, rows), 0)
    pick = jnp.where(spots == place, 1.0, 0.0).astype(jnp.bfloat16)
    for source, source_ref in enumerate((hidden_ref, other_ref)):
        copies[2 + source].wait()
        packed = jnp.dot(pick, source_ref[...], preferred_element_type=jnp.float32)
        packed = packed.astype(jnp.bfloat16).reshape(chips * blocks, BLOCK, packed.shape[1])
        for chip in range(chips):
            start = (2 * chip + source) * blocks
            packed_ref[start : start + blocks] = packed[chip * blocks : (chip + 1) * blocks]
    kept_ref[...] = hidden_ref[...]


def pack_rows(hidden, other, adapter_of_row, adapter_holder_slot, me, orders):
    rows, depth = hidden.shape
    group = adapter_holder_slot.shape[0]
    blocks = MOST // BLOCK
    vmem = pl.BlockSpec(memory_space=pltpu.VMEM)
    smem = pl.BlockSpec(memory_space=pltpu.SMEM)
    anywhere = pl.BlockSpec(memory_space=pl.ANY)
    return pl.pallas_call(
        functools.partial(pack_kernel, blocks, orders),
        out_shape=[
            jax.ShapeDtypeStruct((group * blocks, BLOCK, depth), jnp.bfloat16),
            jax.ShapeDtypeStruct((PLANE * HELD, rows), jnp.bfloat16),
            jax.ShapeDtypeStruct((len(orders),), jnp.int32),
            jax.ShapeDtypeStruct((rows, depth), jnp.bfloat16),
        ],
        in_specs=[smem] + [anywhere] * 4,
        out_specs=[vmem, vmem, smem, vmem],
        scratch_shapes=[
            pltpu.SMEM((group,), jnp.int32),
            pltpu.VMEM((1, rows), jnp.int32),
            pltpu.VMEM((rows, depth), jnp.bfloat16),
            pltpu.VMEM((rows, depth), jnp.bfloat16),
            pltpu.SemaphoreType.DMA((4,)),
        ],
        compiler_params=pltpu.CompilerParams(vmem_limit_bytes=24 * 2**20),
    )(
        me.reshape(1),
        in_hbm(adapter_holder_slot),
        in_hbm(adapter_of_row.reshape(1, rows)),
        in_hbm(hidden),
        other,
    )


def adapter_kernel(parts, me_ref, rows_ref, shrink_hbm, expand_hbm, *refs):
    out_refs = refs[:PLANE]
    shrink_ref, expand_ref, total_ref, sems, expand_sem = refs[PLANE:]
    me = me_ref[0]
    group, _, depth = shrink_ref.shape
    blocks = MOST // BLOCK

    def copy(source):
        device = source // 2 * 2 + ((me & 1) ^ (source % 2))
        start = pl.multiple_of(device * depth, LANES)
        return pltpu.make_async_copy(
            shrink_hbm.at[:, pl.ds(start, depth)], shrink_ref.at[source], sems.at[source]
        )

    for source in range(IN_FLIGHT):
        copy(source).start()
    expand_copy = pltpu.make_async_copy(expand_hbm, expand_ref, expand_sem)
    total = jnp.zeros((MOST, total_ref.shape[1]), jnp.float32)
    for source in range(group):
        copy(source).wait()
        if source + IN_FLIGHT < group:
            copy(source + IN_FLIGHT).start()
        elif source + IN_FLIGHT == group:
            expand_copy.start()
        own = rows_ref[source * blocks : (source + 1) * blocks].reshape(MOST, depth)
        total += lax.dot_general(
            own, shrink_ref[source], (((1,), (1,)), ((), ())), preferred_element_type=jnp.float32
        )
    total_ref[...] = jnp.zeros_like(total_ref)
    total_ref[:MOST] = total
    rank_rows = total_ref[...].astype(jnp.bfloat16)
    expand_copy.wait()
    width = parts * LANES
    for k in range(PLANE):
        for line in range(out_refs[k].shape[0] // parts):
            target = me ^ (PLANE * line + k)
            columns = pl.ds(pl.multiple_of(target * width, LANES), width)
            piece = jnp.dot(rank_rows, expand_ref[:, columns], preferred_element_type=jnp.float32)
            piece = piece.astype(jnp.bfloat16)
            for part in range(parts):
                out_refs[k][line * parts + part] = piece[:, part * LANES : (part + 1) * LANES]


def adapter_output(gathered, shrink, expand, group, me):
    rank = shrink.shape[0]
    model_width = expand.shape[1]
    depth = gathered.shape[2]
    parts = model_width // group // LANES
    held = (model_width // PLANE // LANES, HELD, LANES)
    vmem = pl.BlockSpec(memory_space=pltpu.VMEM)
    anywhere = pl.BlockSpec(memory_space=pl.ANY)
    return pl.pallas_call(
        functools.partial(adapter_kernel, parts),
        out_shape=[jax.ShapeDtypeStruct(held, jnp.bfloat16)] * PLANE,
        in_specs=[pl.BlockSpec(memory_space=pltpu.SMEM), vmem, anywhere, anywhere],
        out_specs=[vmem] * PLANE,
        scratch_shapes=[
            pltpu.VMEM((group, rank, depth), jnp.bfloat16),
            pltpu.VMEM((rank, model_width), jnp.bfloat16),
            pltpu.VMEM((HELD, rank), jnp.float32),
            pltpu.SemaphoreType.DMA((group,)),
            pltpu.SemaphoreType.DMA,
        ],
        compiler_params=pltpu.CompilerParams(vmem_limit_bytes=24 * 2**20),
    )(me.reshape(1), gathered, in_hbm(shrink), in_hbm(expand))


def merge_kernel(pair_ref, pick_ref, *refs):
    in_refs, out_ref, held_ref = refs[:PLANE], refs[PLANE], refs[PLANE + 1]
    for k in range(PLANE):
        held_ref[:, k * HELD : (k + 1) * HELD] = in_refs[k][...]
    pick = pick_ref[...]
    for part in range(pair_ref.shape[0]):
        adapter_rows = lax.dot_general(
            pick, held_ref[part], (((0,), (0,)), ((), ())), preferred_element_type=jnp.float32
        )
        out_ref[part] = pair_ref[part] + ADAPTER_SCALE * adapter_rows


def merge_adapters(pair, pick, arrived):
    vmem = pl.BlockSpec(memory_space=pltpu.VMEM)
    return pl.pallas_call(
        merge_kernel,
        out_shape=jax.ShapeDtypeStruct(pair.shape, jnp.float32),
        in_specs=[vmem] * (2 + PLANE),
        out_specs=vmem,
        scratch_shapes=[pltpu.VMEM((pair.shape[0], PLANE * HELD, LANES), jnp.bfloat16)],
        compiler_params=pltpu.CompilerParams(vmem_limit_bytes=24 * 2**20),
    )(pair, pick, *arrived)


def shards_by_blocks(
    hidden, down_matrix, shrink_matrices, expand_matrices, adapter_of_row, adapter_holder_slot
):
    group = lax.axis_size("tp")
    me = lax.axis_index("tp")
    rows, depth = hidden.shape
    width = down_matrix.shape[1] // group
    quads = list(range(0, group, 4))
    orders = [q + k for k in (3, 2, 1, 0) for q in quads]
    other = xor_permute(hidden, group, 1)
    packed, pick, order, kept_hidden = pack_rows(
        hidden, other, adapter_of_row, adapter_holder_slot, me, orders
    )
    same_core = [list(range(core, group, 2)) for core in range(2)]
    gathered = lax.all_to_all(
        packed, "tp", split_axis=0, concat_axis=0, axis_index_groups=same_core, tiled=True
    )
    pair = pair_sums(kept_hidden, down_matrix, group, order, width)
    gathered, _ = lax.optimization_barrier((gathered, pair))
    shrink = jnp.swapaxes(shrink_matrices, 1, 2)[0]
    expand = jnp.swapaxes(expand_matrices, 1, 2)[0]
    outs = adapter_output(gathered, shrink, expand, group, me)
    arrived = [outs[0]] + [xor_permute(outs[k], group, k) for k in range(1, PLANE)]
    merged = merge_adapters(pair, pick, arrived)
    return line_sums(merged, group, width).astype(jnp.bfloat16)


def shards(
    hidden, down_matrix, shrink_matrices, expand_matrices, adapter_of_row, adapter_holder_slot
):
    group = lax.axis_size("tp")
    rows, depth = hidden.shape
    width = down_matrix.shape[1] // group
    if width % LANES == 0 and depth % LANES == 0 and group >= PLANE and group & (group - 1) == 0:
        return shards_by_blocks(
            hidden, down_matrix, shrink_matrices, expand_matrices, adapter_of_row, adapter_holder_slot
        )
    blocks = MOST // BLOCK
    adapter_ids = jnp.arange(group, dtype=jnp.int32)
    row_match = adapter_of_row[:, None] == adapter_ids[None, :]
    row_slot = jnp.sum(jnp.where(row_match, adapter_holder_slot[None, :], 0), axis=1)
    slot_mask = row_slot[None, :] == adapter_ids[:, None]
    before = jnp.cumsum(slot_mask.astype(jnp.int32), axis=1) - 1
    place = jnp.where(slot_mask, before, -1)
    pick = place[:, None, :] == jnp.arange(MOST, dtype=jnp.int32)[None, :, None]
    pick = pick.reshape(group * MOST, rows).astype(jnp.bfloat16)
    packed = jnp.dot(pick, hidden, preferred_element_type=jnp.float32).astype(jnp.bfloat16)
    packed = packed.reshape(group * blocks, BLOCK, depth)
    gathered = lax.all_to_all(packed, "tp", split_axis=0, concat_axis=0, tiled=True)
    partial_value = jnp.dot(hidden, down_matrix, preferred_element_type=jnp.float32)
    base = lax.psum_scatter(partial_value, "tp", scatter_dimension=1, tiled=True)
    own_rows = jnp.transpose(gathered.reshape(group, MOST, depth), (1, 0, 2))
    rank_rows = jnp.dot(
        own_rows.reshape(MOST, group * depth), shrink_matrices[0], preferred_element_type=jnp.float32
    ).astype(jnp.bfloat16)
    adapter_out = lax.dot_general(
        rank_rows, expand_matrices[0], (((1,), (1,)), ((), ())), preferred_element_type=jnp.float32
    ).astype(jnp.bfloat16)
    adapter_out = jnp.transpose(adapter_out.reshape(blocks, BLOCK, group, width), (2, 0, 1, 3))
    adapter_in = lax.all_to_all(
        adapter_out.reshape(group * blocks, BLOCK, width), "tp", split_axis=0, concat_axis=0, tiled=True
    )
    adapter_rows = lax.dot_general(
        pick,
        adapter_in.reshape(group * MOST, width),
        (((0,), (0,)), ((), ())),
        preferred_element_type=jnp.float32,
    )
    return (base + ADAPTER_SCALE * adapter_rows).astype(jnp.bfloat16)


def solution(mesh):
    in_specs = (
        P("rep", "tp"),
        P("tp", None),
        P(("rep", "tp"), None, None),
        P(("rep", "tp"), None, None),
        P("rep"),
        P("rep"),
    )
    out_specs = P("rep", "tp")
    return jax.shard_map(shards, mesh=mesh, in_specs=in_specs, out_specs=out_specs, check_vma=False)
```

```python
import functools

import jax
import jax.numpy as jnp
from jax import lax
from jax.experimental import pallas as pl
from jax.experimental.pallas import tpu as pltpu
from jax.sharding import PartitionSpec as P

ADAPTER_SCALE = 0.5
BLOCK = 4
MOST = 20
LANES = 128
F16_TOP = 14.0
PLANE = 4
HELD = 24


def in_hbm(value):
    return pltpu.with_memory_space_constraint(value, pltpu.HBM)


def xor_permute(value, group, offset):
    return lax.ppermute(value, "tp", [(i, i ^ offset) for i in range(group)])


def column_blocks_kernel(groups, order_ref, hidden_ref, down_ref, *refs):
    out_refs, held_ref, sems = refs[:groups], refs[groups], refs[groups + 1]
    count, depth, width = held_ref.shape
    parts = width // LANES
    pieces = sems.shape[1]
    cut = depth // pieces

    def copy(block, piece):
        start = pl.multiple_of(order_ref[block] * width, LANES)
        lines = pl.ds(piece * cut, cut)
        return pltpu.make_async_copy(
            down_ref.at[lines, pl.ds(start, width)], held_ref.at[block, lines], sems.at[block, piece]
        )

    for block in range(count):
        for piece in range(pieces):
            copy(block, piece).start()
    share = count // groups
    for block in range(count):
        for piece in range(pieces):
            copy(block, piece).wait()
        product = jnp.dot(hidden_ref[...], held_ref[block], preferred_element_type=jnp.float32)
        for lane in range(parts):
            out_refs[block // share][block % share * parts + lane] = product[
                :, lane * LANES : (lane + 1) * LANES
            ]


def column_blocks(hidden, down_matrix, order, width, groups=1):
    rows, depth = hidden.shape
    count = order.shape[0]
    pieces = 2 if depth % 32 == 0 else 1
    vmem = pl.BlockSpec(memory_space=pltpu.VMEM)
    out = jax.ShapeDtypeStruct((count // groups * width // LANES, rows, LANES), jnp.float32)
    return pl.pallas_call(
        functools.partial(column_blocks_kernel, groups),
        out_shape=[out] * groups,
        in_specs=[
            pl.BlockSpec(memory_space=pltpu.SMEM),
            vmem,
            pl.BlockSpec(memory_space=pl.ANY),
        ],
        out_specs=[vmem] * groups,
        scratch_shapes=[
            pltpu.VMEM((count, depth, width), jnp.bfloat16),
            pltpu.SemaphoreType.DMA((count, pieces)),
        ],
        compiler_params=pltpu.CompilerParams(vmem_limit_bytes=(12 + 12 * groups) * 2**20),
        cost_estimate=pl.CostEstimate(flops=1000, bytes_accessed=1000, transcendentals=0),
    )(order, hidden, in_hbm(down_matrix))


def pack_scaled(value):
    peak = jnp.max(jnp.abs(value), axis=(0, 2), keepdims=True)
    exponent = jnp.ceil(jnp.log2(jnp.maximum(peak, 2.0**-100)))
    scaled = (value * jnp.exp2(F16_TOP - exponent)).astype(jnp.float16)
    marks = jnp.broadcast_to(exponent, (1,) + value.shape[1:]).astype(jnp.float16)
    return jnp.concatenate([scaled, marks], axis=0)


def unpack_scaled(packed):
    exponent = packed[-1:].astype(jnp.float32)
    return packed[:-1].astype(jnp.float32) * jnp.exp2(exponent - F16_TOP)


def pair_sums(hidden, down_matrix, group, order, width):
    half = group * width // LANES // PLANE
    rows = hidden.shape[0]
    share = group // PLANE

    def first():
        (far,) = column_blocks(hidden, down_matrix, order[:share], width)
        far_in = xor_permute(far, group, 1)
        (near,) = column_blocks(hidden, down_matrix, order[share : 2 * share], width)
        return pack_scaled(near + far_in)

    def first_idle():
        return jnp.zeros((half + 1, rows, LANES), jnp.float16)

    sent = lax.cond(order[0] >= 0, first, first_idle)
    pair_in = xor_permute(sent, group, 2)
    order, _ = lax.optimization_barrier((order, sent))

    def second():
        far, near = column_blocks(hidden, down_matrix, order[2 * share :], width, groups=2)
        return near + xor_permute(far, group, 1)

    def second_idle():
        return jnp.zeros((half, rows, LANES), jnp.float32)

    kept = lax.cond(order[1] >= 0, second, second_idle)
    return kept + unpack_scaled(pair_in)


def line_sums(pair, group, width):
    parts = width // LANES
    lines = group // PLANE
    sent = [pack_scaled(pair[i * parts : (i + 1) * parts]) for i in range(lines)]
    along = [list(range(first, group, PLANE)) for first in range(PLANE)]
    arrived = lax.all_to_all(
        jnp.concatenate(sent, axis=0),
        "tp",
        split_axis=0,
        concat_axis=0,
        axis_index_groups=along,
        tiled=True,
    )
    size = parts + 1
    return sum(unpack_scaled(arrived[i * size : (i + 1) * size]) for i in range(lines))


def pack_kernel(
    blocks,
    orders,
    me_ref,
    slot_hbm,
    adapter_hbm,
    hidden_hbm,
    packed_ref,
    pick_ref,
    spread_ref,
    order_ref,
    kept_ref,
    slot_ref,
    adapter_ref,
    hidden_ref,
    sems,
):
    rows = hidden_ref.shape[0]
    group = slot_ref.shape[0]
    copies = [
        pltpu.make_async_copy(slot_hbm, slot_ref, sems.at[0]),
        pltpu.make_async_copy(adapter_hbm, adapter_ref, sems.at[1]),
        pltpu.make_async_copy(hidden_hbm, hidden_ref, sems.at[2]),
    ]
    for copy in copies:
        copy.start()
    me = me_ref[0]
    for i, (line, k) in enumerate(orders):
        order_ref[i] = PLANE * line + (me % PLANE ^ k)
    ids = lax.broadcasted_iota(jnp.int32, (group, 1), 0)
    slots = jnp.zeros((group, 1), jnp.int32)
    copies[0].wait()
    for adapter in range(group):
        slots = jnp.where(ids == adapter, slot_ref[adapter], slots)
    copies[1].wait()
    adapter = adapter_ref[...]
    first = jnp.sum((adapter < ids).astype(jnp.int32), axis=1, keepdims=True)
    slot = jnp.sum(jnp.where(adapter == ids, slots, 0), axis=0, keepdims=True)
    first = jnp.sum(jnp.where(adapter == ids, first, 0), axis=0, keepdims=True)
    index = lax.broadcasted_iota(jnp.int32, (1, rows), 1) - first
    held = blocks * BLOCK
    spots = lax.broadcasted_iota(jnp.int32, (group * held, rows), 0)
    pick = jnp.where(spots == slot * held + index, 1.0, 0.0).astype(jnp.bfloat16)
    for k in range(PLANE):
        spots = lax.broadcasted_iota(jnp.int32, (HELD, rows), 0)
        mine = (slot == me ^ k) & (index == spots)
        pick_ref[k * HELD : (k + 1) * HELD] = jnp.where(mine, 1.0, 0.0).astype(jnp.bfloat16)
    lines = group // PLANE
    line = slot // PLANE
    member = (line == lax.broadcasted_iota(jnp.int32, (lines, rows), 0)).astype(jnp.float32)
    earlier = lax.broadcasted_iota(jnp.int32, (rows, rows), 0) < lax.broadcasted_iota(
        jnp.int32, (rows, rows), 1
    )
    ahead = jnp.dot(
        member.astype(jnp.bfloat16),
        jnp.where(earlier, 1.0, 0.0).astype(jnp.bfloat16),
        preferred_element_type=jnp.float32,
    )
    place = jnp.sum(member * ahead, axis=0, keepdims=True).astype(jnp.int32)
    most = spread_ref.shape[0] // lines
    spots = lax.broadcasted_iota(jnp.int32, (most, rows), 0)
    for i in range(lines):
        mine = (line == (me // PLANE) ^ i) & (place == spots)
        spread_ref[i * most : (i + 1) * most] = jnp.where(mine, 1.0, 0.0).astype(jnp.bfloat16)
    copies[2].wait()
    packed = jnp.dot(pick, hidden_ref[...], preferred_element_type=jnp.float32)
    packed_ref[...] = packed.astype(jnp.bfloat16).reshape(packed_ref.shape)
    kept_ref[...] = hidden_ref[...]


def plane_rows(rows, group):
    return min(PLANE * MOST, rows - (group - PLANE) * BLOCK)


def pack_rows(hidden, adapter_of_row, adapter_holder_slot, me, orders):
    rows, depth = hidden.shape
    group = adapter_holder_slot.shape[0]
    blocks = MOST // BLOCK
    vmem = pl.BlockSpec(memory_space=pltpu.VMEM)
    smem = pl.BlockSpec(memory_space=pltpu.SMEM)
    anywhere = pl.BlockSpec(memory_space=pltpu.HBM)
    return pl.pallas_call(
        functools.partial(pack_kernel, blocks, orders),
        out_shape=(
            jax.ShapeDtypeStruct((group * blocks, BLOCK, depth), jnp.bfloat16),
            jax.ShapeDtypeStruct((PLANE * HELD, rows), jnp.bfloat16),
            jax.ShapeDtypeStruct((group // PLANE * plane_rows(rows, group), rows), jnp.bfloat16),
            jax.ShapeDtypeStruct((len(orders),), jnp.int32),
            jax.ShapeDtypeStruct((rows, depth), jnp.bfloat16),
        ),
        in_specs=[smem, anywhere, anywhere, anywhere],
        out_specs=(vmem, vmem, vmem, smem, vmem),
        scratch_shapes=[
            pltpu.SMEM((group,), jnp.int32),
            pltpu.VMEM((1, rows), jnp.int32),
            pltpu.VMEM((rows, depth), jnp.bfloat16),
            pltpu.SemaphoreType.DMA((3,)),
        ],
        compiler_params=pltpu.CompilerParams(vmem_limit_bytes=24 * 2**20),
    )(me.reshape(1), in_hbm(adapter_holder_slot), in_hbm(adapter_of_row.reshape(1, rows)), in_hbm(hidden))


def adapter_kernel(parts, me_ref, rows_ref, expand_ref, shrink_hbm, *refs):
    out_refs = refs[:PLANE]
    shrink_ref, total_ref, sems = refs[PLANE:]
    me = me_ref[0]
    group, _, depth = shrink_ref.shape
    blocks = MOST // BLOCK

    def copy(source):
        return pltpu.make_async_copy(
            shrink_hbm.at[:, pl.ds(source * depth, depth)], shrink_ref.at[source], sems.at[source]
        )

    for source in range(group):
        copy(source).start()
    total = jnp.zeros((MOST, total_ref.shape[1]), jnp.float32)
    for source in range(group):
        copy(source).wait()
        own = rows_ref[source * blocks : (source + 1) * blocks].reshape(MOST, depth)
        total += lax.dot_general(
            own, shrink_ref[source], (((1,), (1,)), ((), ())), preferred_element_type=jnp.float32
        )
    total_ref[...] = jnp.zeros_like(total_ref)
    total_ref[:MOST] = total
    rank_rows = total_ref[...].astype(jnp.bfloat16)
    width = parts * LANES
    for k in range(PLANE):
        for line in range(group // PLANE):
            target = PLANE * line + (me % PLANE ^ k)
            columns = pl.ds(pl.multiple_of(target * width, LANES), width)
            piece = jnp.dot(rank_rows, expand_ref[:, columns], preferred_element_type=jnp.float32)
            piece = piece.astype(jnp.bfloat16)
            for part in range(parts):
                out_refs[k][line * parts + part] = piece[:, part * LANES : (part + 1) * LANES]


def adapter_output(gathered, shrink, expand, group, me):
    rank = shrink.shape[0]
    model_width = expand.shape[1]
    depth = gathered.shape[2]
    parts = model_width // group // LANES
    held = (model_width // PLANE // LANES, HELD, LANES)
    vmem = pl.BlockSpec(memory_space=pltpu.VMEM)
    return pl.pallas_call(
        functools.partial(adapter_kernel, parts),
        out_shape=[jax.ShapeDtypeStruct(held, jnp.bfloat16)] * PLANE,
        in_specs=[
            pl.BlockSpec(memory_space=pltpu.SMEM),
            vmem,
            vmem,
            pl.BlockSpec(memory_space=pl.ANY),
        ],
        out_specs=[vmem] * PLANE,
        scratch_shapes=[
            pltpu.VMEM((group, rank, depth), jnp.bfloat16),
            pltpu.VMEM((HELD, rank), jnp.float32),
            pltpu.SemaphoreType.DMA((group,)),
        ],
        compiler_params=pltpu.CompilerParams(vmem_limit_bytes=24 * 2**20),
    )(me.reshape(1), gathered, expand, in_hbm(shrink))


def line_kernel(me_ref, pick_ref, spread_ref, *refs):
    in_refs, out_refs, held_ref = refs[:PLANE], refs[PLANE:-1], refs[-1]
    lines = len(out_refs)
    parts, most = out_refs[0].shape[:2]
    for k in range(PLANE):
        held_ref[:, k * HELD : (k + 1) * HELD] = in_refs[k][...]
    pick = lax.dot_general(
        spread_ref[:most], pick_ref[...], (((1,), (1,)), ((), ())), preferred_element_type=jnp.float32
    ).astype(jnp.bfloat16)
    for i in range(lines):
        line = (me_ref[0] // PLANE) ^ i
        for part in range(parts):
            piece = jnp.dot(pick, held_ref[line * parts + part], preferred_element_type=jnp.float32)
            out_refs[i][part] = piece.astype(jnp.bfloat16)


def line_rows(pick, spread, arrived, group, me):
    lines = group // PLANE
    blocks = arrived[0].shape[0]
    most = spread.shape[0] // lines
    vmem = pl.BlockSpec(memory_space=pltpu.VMEM)
    return pl.pallas_call(
        line_kernel,
        out_shape=[jax.ShapeDtypeStruct((blocks // lines, most, LANES), jnp.bfloat16)] * lines,
        in_specs=[pl.BlockSpec(memory_space=pltpu.SMEM)] + [vmem] * (2 + PLANE),
        out_specs=[vmem] * lines,
        scratch_shapes=[pltpu.VMEM((blocks, PLANE * HELD, LANES), jnp.bfloat16)],
        compiler_params=pltpu.CompilerParams(vmem_limit_bytes=24 * 2**20),
    )(me.reshape(1), pick, spread, *arrived)


def final_kernel(base_ref, spread_ref, *refs):
    in_refs, out_ref = refs[:-1], refs[-1]
    parts, most = in_refs[0].shape[:2]
    for part in range(parts):
        total = base_ref[part]
        for i, in_ref in enumerate(in_refs):
            total += ADAPTER_SCALE * lax.dot_general(
                spread_ref[i * most : (i + 1) * most],
                in_ref[part],
                (((0,), (0,)), ((), ())),
                preferred_element_type=jnp.float32,
            )
        out_ref[:, part * LANES : (part + 1) * LANES] = total.astype(out_ref.dtype)


def add_adapters(base, spread, arrived):
    parts, rows, _ = base.shape
    vmem = pl.BlockSpec(memory_space=pltpu.VMEM)
    return pl.pallas_call(
        final_kernel,
        out_shape=jax.ShapeDtypeStruct((rows, parts * LANES), jnp.bfloat16),
        in_specs=[vmem] * (2 + len(arrived)),
        out_specs=vmem,
        compiler_params=pltpu.CompilerParams(vmem_limit_bytes=24 * 2**20),
    )(base, spread, *arrived)


def shards_by_blocks(
    hidden, down_matrix, shrink_matrices, expand_matrices, adapter_of_row, adapter_holder_slot
):
    group = lax.axis_size("tp")
    me = lax.axis_index("tp")
    rows, depth = hidden.shape
    width = down_matrix.shape[1] // group
    lines = group // PLANE
    orders = [(line, k) for k in (3, 2, 1, 0) for line in range(lines)]
    packed, pick, spread, order, kept_hidden = pack_rows(
        hidden, adapter_of_row, adapter_holder_slot, me, orders
    )
    gathered = lax.all_to_all(packed, "tp", split_axis=0, concat_axis=0, tiled=True)
    pair = pair_sums(kept_hidden, down_matrix, group, order, width)
    gathered, _ = lax.optimization_barrier((gathered, pair))
    shrink = jnp.swapaxes(shrink_matrices, 1, 2)[0]
    expand = jnp.swapaxes(expand_matrices, 1, 2)[0]
    outs = adapter_output(gathered, shrink, expand, group, me)
    pair, _ = lax.optimization_barrier((pair, outs[0]))
    base = line_sums(pair, group, width)
    arrived = [outs[0]] + [xor_permute(outs[k], group, k) for k in range(1, PLANE)]
    sent = line_rows(pick, spread, arrived, group, me)
    arrived = [sent[0]] + [xor_permute(sent[i], group, PLANE * i) for i in range(1, lines)]
    return add_adapters(base, spread, arrived)


def shards(
    hidden, down_matrix, shrink_matrices, expand_matrices, adapter_of_row, adapter_holder_slot
):
    group = lax.axis_size("tp")
    rows, depth = hidden.shape
    width = down_matrix.shape[1] // group
    if width % LANES == 0 and depth % LANES == 0 and group >= PLANE and group & (group - 1) == 0:
        return shards_by_blocks(
            hidden, down_matrix, shrink_matrices, expand_matrices, adapter_of_row, adapter_holder_slot
        )
    blocks = MOST // BLOCK
    adapter_ids = jnp.arange(group, dtype=jnp.int32)
    row_match = adapter_of_row[:, None] == adapter_ids[None, :]
    row_slot = jnp.sum(jnp.where(row_match, adapter_holder_slot[None, :], 0), axis=1)
    slot_mask = row_slot[None, :] == adapter_ids[:, None]
    before = jnp.cumsum(slot_mask.astype(jnp.int32), axis=1) - 1
    place = jnp.where(slot_mask, before, -1)
    pick = place[:, None, :] == jnp.arange(MOST, dtype=jnp.int32)[None, :, None]
    pick = pick.reshape(group * MOST, rows).astype(jnp.bfloat16)
    packed = jnp.dot(pick, hidden, preferred_element_type=jnp.float32).astype(jnp.bfloat16)
    packed = packed.reshape(group * blocks, BLOCK, depth)
    gathered = lax.all_to_all(packed, "tp", split_axis=0, concat_axis=0, tiled=True)
    partial_value = jnp.dot(hidden, down_matrix, preferred_element_type=jnp.float32)
    base = lax.psum_scatter(partial_value, "tp", scatter_dimension=1, tiled=True)
    own_rows = jnp.transpose(gathered.reshape(group, MOST, depth), (1, 0, 2))
    rank_rows = jnp.dot(
        own_rows.reshape(MOST, group * depth), shrink_matrices[0], preferred_element_type=jnp.float32
    ).astype(jnp.bfloat16)
    adapter_out = lax.dot_general(
        rank_rows, expand_matrices[0], (((1,), (1,)), ((), ())), preferred_element_type=jnp.float32
    ).astype(jnp.bfloat16)
    adapter_out = jnp.transpose(adapter_out.reshape(blocks, BLOCK, group, width), (2, 0, 1, 3))
    adapter_in = lax.all_to_all(
        adapter_out.reshape(group * blocks, BLOCK, width), "tp", split_axis=0, concat_axis=0, tiled=True
    )
    adapter_rows = lax.dot_general(
        pick,
        adapter_in.reshape(group * MOST, width),
        (((0,), (0,)), ((), ())),
        preferred_element_type=jnp.float32,
    )
    return (base + ADAPTER_SCALE * adapter_rows).astype(jnp.bfloat16)


def solution(mesh):
    in_specs = (
        P("rep", "tp"),
        P("tp", None),
        P(("rep", "tp"), None, None),
        P(("rep", "tp"), None, None),
        P("rep"),
        P("rep"),
    )
    out_specs = P("rep", "tp")
    return jax.shard_map(shards, mesh=mesh, in_specs=in_specs, out_specs=out_specs, check_vma=False)
```

```python
import functools

import jax
import jax.numpy as jnp
from jax import lax
from jax.experimental import pallas as pl
from jax.experimental.pallas import tpu as pltpu
from jax.sharding import PartitionSpec as P

ADAPTER_SCALE = 0.5
BLOCK = 4
MOST = 20
LANES = 128
F16_TOP = 14.0
PLANE = 4
HELD = 24


def in_hbm(value):
    return pltpu.with_memory_space_constraint(value, pltpu.HBM)


def xor_permute(value, group, offset):
    return lax.ppermute(value, "tp", [(i, i ^ offset) for i in range(group)])


def column_blocks_kernel(groups, order_ref, hidden_ref, down_ref, *refs):
    out_refs, held_ref, sems = refs[:groups], refs[groups], refs[groups + 1]
    count, depth, width = held_ref.shape
    parts = width // LANES
    pieces = sems.shape[1]
    cut = depth // pieces

    def copy(block, piece):
        start = pl.multiple_of(order_ref[block] * width, LANES)
        lines = pl.ds(piece * cut, cut)
        return pltpu.make_async_copy(
            down_ref.at[lines, pl.ds(start, width)], held_ref.at[block, lines], sems.at[block, piece]
        )

    for block in range(count):
        for piece in range(pieces):
            copy(block, piece).start()
    share = count // groups
    for block in range(count):
        for piece in range(pieces):
            copy(block, piece).wait()
        product = jnp.dot(hidden_ref[...], held_ref[block], preferred_element_type=jnp.float32)
        for lane in range(parts):
            out_refs[block // share][block % share * parts + lane] = product[
                :, lane * LANES : (lane + 1) * LANES
            ]


def column_blocks(hidden, down_matrix, order, width, groups=1):
    rows, depth = hidden.shape
    count = order.shape[0]
    pieces = 2 if depth % 32 == 0 else 1
    vmem = pl.BlockSpec(memory_space=pltpu.VMEM)
    out = jax.ShapeDtypeStruct((count // groups * width // LANES, rows, LANES), jnp.float32)
    return pl.pallas_call(
        functools.partial(column_blocks_kernel, groups),
        out_shape=[out] * groups,
        in_specs=[
            pl.BlockSpec(memory_space=pltpu.SMEM),
            vmem,
            pl.BlockSpec(memory_space=pl.ANY),
        ],
        out_specs=[vmem] * groups,
        scratch_shapes=[
            pltpu.VMEM((count, depth, width), jnp.bfloat16),
            pltpu.SemaphoreType.DMA((count, pieces)),
        ],
        compiler_params=pltpu.CompilerParams(vmem_limit_bytes=(12 + 12 * groups) * 2**20),
        cost_estimate=pl.CostEstimate(flops=1000, bytes_accessed=1000, transcendentals=0),
    )(order, hidden, in_hbm(down_matrix))


def pack_scaled(value):
    peak = jnp.max(jnp.abs(value), axis=(0, 2), keepdims=True)
    exponent = jnp.ceil(jnp.log2(jnp.maximum(peak, 2.0**-100)))
    scaled = (value * jnp.exp2(F16_TOP - exponent)).astype(jnp.float16)
    marks = jnp.broadcast_to(exponent, (1,) + value.shape[1:]).astype(jnp.float16)
    return jnp.concatenate([scaled, marks], axis=0)


def unpack_scaled(packed):
    exponent = packed[-1:].astype(jnp.float32)
    return packed[:-1].astype(jnp.float32) * jnp.exp2(exponent - F16_TOP)


def pair_sums(hidden, down_matrix, group, order, width):
    half = group * width // LANES // PLANE
    rows = hidden.shape[0]
    share = group // PLANE

    def first():
        (far,) = column_blocks(hidden, down_matrix, order[:share], width)
        far_in = xor_permute(far, group, 1)
        (near,) = column_blocks(hidden, down_matrix, order[share : 2 * share], width)
        return pack_scaled(near + far_in)

    def first_idle():
        return jnp.zeros((half + 1, rows, LANES), jnp.float16)

    sent = lax.cond(order[0] >= 0, first, first_idle)
    pair_in = xor_permute(sent, group, 2)
    order, _ = lax.optimization_barrier((order, sent))

    def second():
        far, near = column_blocks(hidden, down_matrix, order[2 * share :], width, groups=2)
        return near + xor_permute(far, group, 1)

    def second_idle():
        return jnp.zeros((half, rows, LANES), jnp.float32)

    kept = lax.cond(order[1] >= 0, second, second_idle)
    return kept + unpack_scaled(pair_in)


def line_sums(pair, group, width):
    parts = width // LANES
    arrived = [
        xor_permute(pack_scaled(pair[i * parts : (i + 1) * parts]), group, PLANE * i)
        for i in range(1, group // PLANE)
    ]
    total = pair[:parts]
    for packed in arrived:
        total = total + unpack_scaled(packed)
    return total


def pack_kernel(
    blocks,
    orders,
    me_ref,
    slot_hbm,
    adapter_hbm,
    hidden_hbm,
    packed_ref,
    pick_ref,
    spread_ref,
    order_ref,
    kept_ref,
    slot_ref,
    adapter_ref,
    hidden_ref,
    sems,
):
    rows = hidden_ref.shape[0]
    group = slot_ref.shape[0]
    copies = [
        pltpu.make_async_copy(slot_hbm, slot_ref, sems.at[0]),
        pltpu.make_async_copy(adapter_hbm, adapter_ref, sems.at[1]),
        pltpu.make_async_copy(hidden_hbm, hidden_ref, sems.at[2]),
    ]
    for copy in copies:
        copy.start()
    me = me_ref[0]
    for i, (line, k) in enumerate(orders):
        order_ref[i] = me ^ (PLANE * line + k)
    ids = lax.broadcasted_iota(jnp.int32, (group, 1), 0)
    slots = jnp.zeros((group, 1), jnp.int32)
    copies[0].wait()
    for adapter in range(group):
        slots = jnp.where(ids == adapter, slot_ref[adapter], slots)
    copies[1].wait()
    adapter = adapter_ref[...]
    first = jnp.sum((adapter < ids).astype(jnp.int32), axis=1, keepdims=True)
    slot = jnp.sum(jnp.where(adapter == ids, slots, 0), axis=0, keepdims=True)
    first = jnp.sum(jnp.where(adapter == ids, first, 0), axis=0, keepdims=True)
    index = lax.broadcasted_iota(jnp.int32, (1, rows), 1) - first
    held = blocks * BLOCK
    spots = lax.broadcasted_iota(jnp.int32, (group * held, rows), 0)
    pick = jnp.where(spots == slot * held + index, 1.0, 0.0).astype(jnp.bfloat16)
    for k in range(PLANE):
        spots = lax.broadcasted_iota(jnp.int32, (HELD, rows), 0)
        mine = (slot == me ^ k) & (index == spots)
        pick_ref[k * HELD : (k + 1) * HELD] = jnp.where(mine, 1.0, 0.0).astype(jnp.bfloat16)
    lines = group // PLANE
    line = slot // PLANE
    member = (line == lax.broadcasted_iota(jnp.int32, (lines, rows), 0)).astype(jnp.float32)
    earlier = lax.broadcasted_iota(jnp.int32, (rows, rows), 0) < lax.broadcasted_iota(
        jnp.int32, (rows, rows), 1
    )
    ahead = jnp.dot(
        member.astype(jnp.bfloat16),
        jnp.where(earlier, 1.0, 0.0).astype(jnp.bfloat16),
        preferred_element_type=jnp.float32,
    )
    place = jnp.sum(member * ahead, axis=0, keepdims=True).astype(jnp.int32)
    most = spread_ref.shape[0] // lines
    spots = lax.broadcasted_iota(jnp.int32, (most, rows), 0)
    for i in range(lines):
        mine = (line == (me // PLANE) ^ i) & (place == spots)
        spread_ref[i * most : (i + 1) * most] = jnp.where(mine, 1.0, 0.0).astype(jnp.bfloat16)
    copies[2].wait()
    packed = jnp.dot(pick, hidden_ref[...], preferred_element_type=jnp.float32)
    packed_ref[...] = packed.astype(jnp.bfloat16).reshape(packed_ref.shape)
    kept_ref[...] = hidden_ref[...]


def plane_rows(rows, group):
    return min(PLANE * MOST, rows - (group - PLANE) * BLOCK)


def pack_rows(hidden, adapter_of_row, adapter_holder_slot, me, orders):
    rows, depth = hidden.shape
    group = adapter_holder_slot.shape[0]
    blocks = MOST // BLOCK
    vmem = pl.BlockSpec(memory_space=pltpu.VMEM)
    smem = pl.BlockSpec(memory_space=pltpu.SMEM)
    anywhere = pl.BlockSpec(memory_space=pltpu.HBM)
    return pl.pallas_call(
        functools.partial(pack_kernel, blocks, orders),
        out_shape=(
            jax.ShapeDtypeStruct((group * blocks, BLOCK, depth), jnp.bfloat16),
            jax.ShapeDtypeStruct((PLANE * HELD, rows), jnp.bfloat16),
            jax.ShapeDtypeStruct((group // PLANE * plane_rows(rows, group), rows), jnp.bfloat16),
            jax.ShapeDtypeStruct((len(orders),), jnp.int32),
            jax.ShapeDtypeStruct((rows, depth), jnp.bfloat16),
        ),
        in_specs=[smem, anywhere, anywhere, anywhere],
        out_specs=(vmem, vmem, vmem, smem, vmem),
        scratch_shapes=[
            pltpu.SMEM((group,), jnp.int32),
            pltpu.VMEM((1, rows), jnp.int32),
            pltpu.VMEM((rows, depth), jnp.bfloat16),
            pltpu.SemaphoreType.DMA((3,)),
        ],
        compiler_params=pltpu.CompilerParams(vmem_limit_bytes=24 * 2**20),
    )(me.reshape(1), in_hbm(adapter_holder_slot), in_hbm(adapter_of_row.reshape(1, rows)), in_hbm(hidden))


def adapter_kernel(parts, me_ref, rows_ref, expand_ref, shrink_hbm, *refs):
    out_refs = refs[:PLANE]
    shrink_ref, total_ref, sems = refs[PLANE:]
    me = me_ref[0]
    group, _, depth = shrink_ref.shape
    blocks = MOST // BLOCK

    def copy(source):
        return pltpu.make_async_copy(
            shrink_hbm.at[:, pl.ds(source * depth, depth)], shrink_ref.at[source], sems.at[source]
        )

    for source in range(group):
        copy(source).start()
    total = jnp.zeros((MOST, total_ref.shape[1]), jnp.float32)
    for source in range(group):
        copy(source).wait()
        own = rows_ref[source * blocks : (source + 1) * blocks].reshape(MOST, depth)
        total += lax.dot_general(
            own, shrink_ref[source], (((1,), (1,)), ((), ())), preferred_element_type=jnp.float32
        )
    total_ref[...] = jnp.zeros_like(total_ref)
    total_ref[:MOST] = total
    rank_rows = total_ref[...].astype(jnp.bfloat16)
    width = parts * LANES
    for k in range(PLANE):
        for line in range(group // PLANE):
            target = me ^ (PLANE * line + k)
            columns = pl.ds(pl.multiple_of(target * width, LANES), width)
            piece = jnp.dot(rank_rows, expand_ref[:, columns], preferred_element_type=jnp.float32)
            piece = piece.astype(jnp.bfloat16)
            for part in range(parts):
                out_refs[k][line * parts + part] = piece[:, part * LANES : (part + 1) * LANES]


def adapter_output(gathered, shrink, expand, group, me):
    rank = shrink.shape[0]
    model_width = expand.shape[1]
    depth = gathered.shape[2]
    parts = model_width // group // LANES
    held = (model_width // PLANE // LANES, HELD, LANES)
    vmem = pl.BlockSpec(memory_space=pltpu.VMEM)
    return pl.pallas_call(
        functools.partial(adapter_kernel, parts),
        out_shape=[jax.ShapeDtypeStruct(held, jnp.bfloat16)] * PLANE,
        in_specs=[
            pl.BlockSpec(memory_space=pltpu.SMEM),
            vmem,
            vmem,
            pl.BlockSpec(memory_space=pl.ANY),
        ],
        out_specs=[vmem] * PLANE,
        scratch_shapes=[
            pltpu.VMEM((group, rank, depth), jnp.bfloat16),
            pltpu.VMEM((HELD, rank), jnp.float32),
            pltpu.SemaphoreType.DMA((group,)),
        ],
        compiler_params=pltpu.CompilerParams(vmem_limit_bytes=24 * 2**20),
    )(me.reshape(1), gathered, expand, in_hbm(shrink))


def line_kernel(pick_ref, spread_ref, *refs):
    in_refs, out_refs, held_ref = refs[:PLANE], refs[PLANE:-1], refs[-1]
    lines = len(out_refs)
    parts, most = out_refs[0].shape[:2]
    for k in range(PLANE):
        held_ref[:, k * HELD : (k + 1) * HELD] = in_refs[k][...]
    pick = lax.dot_general(
        spread_ref[:most], pick_ref[...], (((1,), (1,)), ((), ())), preferred_element_type=jnp.float32
    ).astype(jnp.bfloat16)
    for i in range(lines):
        for part in range(parts):
            piece = jnp.dot(pick, held_ref[i * parts + part], preferred_element_type=jnp.float32)
            out_refs[i][part] = piece.astype(jnp.bfloat16)


def line_rows(pick, spread, arrived, group):
    lines = group // PLANE
    blocks = arrived[0].shape[0]
    most = spread.shape[0] // lines
    vmem = pl.BlockSpec(memory_space=pltpu.VMEM)
    return pl.pallas_call(
        line_kernel,
        out_shape=[jax.ShapeDtypeStruct((blocks // lines, most, LANES), jnp.bfloat16)] * lines,
        in_specs=[vmem] * (2 + PLANE),
        out_specs=[vmem] * lines,
        scratch_shapes=[pltpu.VMEM((blocks, PLANE * HELD, LANES), jnp.bfloat16)],
        compiler_params=pltpu.CompilerParams(vmem_limit_bytes=24 * 2**20),
    )(pick, spread, *arrived)


def final_kernel(base_ref, spread_ref, *refs):
    in_refs, out_ref = refs[:-1], refs[-1]
    parts, most = in_refs[0].shape[:2]
    for part in range(parts):
        total = base_ref[part]
        for i, in_ref in enumerate(in_refs):
            total += ADAPTER_SCALE * lax.dot_general(
                spread_ref[i * most : (i + 1) * most],
                in_ref[part],
                (((0,), (0,)), ((), ())),
                preferred_element_type=jnp.float32,
            )
        out_ref[:, part * LANES : (part + 1) * LANES] = total.astype(out_ref.dtype)


def add_adapters(base, spread, arrived):
    parts, rows, _ = base.shape
    vmem = pl.BlockSpec(memory_space=pltpu.VMEM)
    return pl.pallas_call(
        final_kernel,
        out_shape=jax.ShapeDtypeStruct((rows, parts * LANES), jnp.bfloat16),
        in_specs=[vmem] * (2 + len(arrived)),
        out_specs=vmem,
        compiler_params=pltpu.CompilerParams(vmem_limit_bytes=24 * 2**20),
    )(base, spread, *arrived)


def shards_by_blocks(
    hidden, down_matrix, shrink_matrices, expand_matrices, adapter_of_row, adapter_holder_slot
):
    group = lax.axis_size("tp")
    me = lax.axis_index("tp")
    rows, depth = hidden.shape
    width = down_matrix.shape[1] // group
    lines = group // PLANE
    orders = [(line, k) for k in (3, 2, 1, 0) for line in range(lines)]
    packed, pick, spread, order, kept_hidden = pack_rows(
        hidden, adapter_of_row, adapter_holder_slot, me, orders
    )
    gathered = lax.all_to_all(packed, "tp", split_axis=0, concat_axis=0, tiled=True)
    pair = pair_sums(kept_hidden, down_matrix, group, order, width)
    gathered, _ = lax.optimization_barrier((gathered, pair))
    shrink = jnp.swapaxes(shrink_matrices, 1, 2)[0]
    expand = jnp.swapaxes(expand_matrices, 1, 2)[0]
    outs = adapter_output(gathered, shrink, expand, group, me)
    pair, _ = lax.optimization_barrier((pair, outs[0]))
    base = line_sums(pair, group, width)
    arrived = [outs[0]] + [xor_permute(outs[k], group, k) for k in range(1, PLANE)]
    sent = line_rows(pick, spread, arrived, group)
    arrived = [sent[0]] + [xor_permute(sent[i], group, PLANE * i) for i in range(1, lines)]
    return add_adapters(base, spread, arrived)


def shards(
    hidden, down_matrix, shrink_matrices, expand_matrices, adapter_of_row, adapter_holder_slot
):
    group = lax.axis_size("tp")
    rows, depth = hidden.shape
    width = down_matrix.shape[1] // group
    if width % LANES == 0 and depth % LANES == 0 and group >= PLANE and group & (group - 1) == 0:
        return shards_by_blocks(
            hidden, down_matrix, shrink_matrices, expand_matrices, adapter_of_row, adapter_holder_slot
        )
    blocks = MOST // BLOCK
    adapter_ids = jnp.arange(group, dtype=jnp.int32)
    row_match = adapter_of_row[:, None] == adapter_ids[None, :]
    row_slot = jnp.sum(jnp.where(row_match, adapter_holder_slot[None, :], 0), axis=1)
    slot_mask = row_slot[None, :] == adapter_ids[:, None]
    before = jnp.cumsum(slot_mask.astype(jnp.int32), axis=1) - 1
    place = jnp.where(slot_mask, before, -1)
    pick = place[:, None, :] == jnp.arange(MOST, dtype=jnp.int32)[None, :, None]
    pick = pick.reshape(group * MOST, rows).astype(jnp.bfloat16)
    packed = jnp.dot(pick, hidden, preferred_element_type=jnp.float32).astype(jnp.bfloat16)
    packed = packed.reshape(group * blocks, BLOCK, depth)
    gathered = lax.all_to_all(packed, "tp", split_axis=0, concat_axis=0, tiled=True)
    partial_value = jnp.dot(hidden, down_matrix, preferred_element_type=jnp.float32)
    base = lax.psum_scatter(partial_value, "tp", scatter_dimension=1, tiled=True)
    own_rows = jnp.transpose(gathered.reshape(group, MOST, depth), (1, 0, 2))
    rank_rows = jnp.dot(
        own_rows.reshape(MOST, group * depth), shrink_matrices[0], preferred_element_type=jnp.float32
    ).astype(jnp.bfloat16)
    adapter_out = lax.dot_general(
        rank_rows, expand_matrices[0], (((1,), (1,)), ((), ())), preferred_element_type=jnp.float32
    ).astype(jnp.bfloat16)
    adapter_out = jnp.transpose(adapter_out.reshape(blocks, BLOCK, group, width), (2, 0, 1, 3))
    adapter_in = lax.all_to_all(
        adapter_out.reshape(group * blocks, BLOCK, width), "tp", split_axis=0, concat_axis=0, tiled=True
    )
    adapter_rows = lax.dot_general(
        pick,
        adapter_in.reshape(group * MOST, width),
        (((0,), (0,)), ((), ())),
        preferred_element_type=jnp.float32,
    )
    return (base + ADAPTER_SCALE * adapter_rows).astype(jnp.bfloat16)


def solution(mesh):
    in_specs = (
        P("rep", "tp"),
        P("tp", None),
        P(("rep", "tp"), None, None),
        P(("rep", "tp"), None, None),
        P("rep"),
        P("rep"),
    )
    out_specs = P("rep", "tp")
    return jax.shard_map(shards, mesh=mesh, in_specs=in_specs, out_specs=out_specs, check_vma=False)
```

```python
import functools

import jax
import jax.numpy as jnp
from jax import lax
from jax.experimental import pallas as pl
from jax.experimental.pallas import tpu as pltpu
from jax.sharding import PartitionSpec as P

ADAPTER_SCALE = 0.5
BLOCK = 4
MOST = 20
LANES = 128
F16_TOP = 14.0
PLANE = 4
HELD = 24


def in_hbm(value):
    return pltpu.with_memory_space_constraint(value, pltpu.HBM)


def xor_permute(value, group, offset):
    return lax.ppermute(value, "tp", [(i, i ^ offset) for i in range(group)])


def column_blocks_kernel(groups, order_ref, hidden_ref, down_ref, *refs):
    out_refs, held_ref, sems = refs[:groups], refs[groups], refs[groups + 1]
    count, depth, width = held_ref.shape
    parts = width // LANES
    pieces = sems.shape[1]
    cut = depth // pieces

    def copy(block, piece):
        start = pl.multiple_of(order_ref[block] * width, LANES)
        lines = pl.ds(piece * cut, cut)
        return pltpu.make_async_copy(
            down_ref.at[lines, pl.ds(start, width)], held_ref.at[block, lines], sems.at[block, piece]
        )

    for block in range(count):
        for piece in range(pieces):
            copy(block, piece).start()
    share = count // groups
    for block in range(count):
        for piece in range(pieces):
            copy(block, piece).wait()
        product = jnp.dot(hidden_ref[...], held_ref[block], preferred_element_type=jnp.float32)
        for lane in range(parts):
            out_refs[block // share][block % share * parts + lane] = product[
                :, lane * LANES : (lane + 1) * LANES
            ]


def column_blocks(hidden, down_matrix, order, width, groups=1):
    rows, depth = hidden.shape
    count = order.shape[0]
    pieces = 2 if depth % 32 == 0 else 1
    vmem = pl.BlockSpec(memory_space=pltpu.VMEM)
    out = jax.ShapeDtypeStruct((count // groups * width // LANES, rows, LANES), jnp.float32)
    return pl.pallas_call(
        functools.partial(column_blocks_kernel, groups),
        out_shape=[out] * groups,
        in_specs=[
            pl.BlockSpec(memory_space=pltpu.SMEM),
            vmem,
            pl.BlockSpec(memory_space=pl.ANY),
        ],
        out_specs=[vmem] * groups,
        scratch_shapes=[
            pltpu.VMEM((count, depth, width), jnp.bfloat16),
            pltpu.SemaphoreType.DMA((count, pieces)),
        ],
        compiler_params=pltpu.CompilerParams(vmem_limit_bytes=(12 + 12 * groups) * 2**20),
        cost_estimate=pl.CostEstimate(flops=1000, bytes_accessed=1000, transcendentals=0),
    )(order, hidden, in_hbm(down_matrix))


def pack_scaled(value):
    peak = jnp.max(jnp.abs(value), axis=(0, 2), keepdims=True)
    exponent = jnp.ceil(jnp.log2(jnp.maximum(peak, 2.0**-100)))
    scaled = (value * jnp.exp2(F16_TOP - exponent)).astype(jnp.float16)
    marks = jnp.broadcast_to(exponent, (1,) + value.shape[1:]).astype(jnp.float16)
    return jnp.concatenate([scaled, marks], axis=0)


def unpack_scaled(packed):
    exponent = packed[-1:].astype(jnp.float32)
    return packed[:-1].astype(jnp.float32) * jnp.exp2(exponent - F16_TOP)


def pair_sums(hidden, down_matrix, group, order, width):
    half = group * width // LANES // PLANE
    rows = hidden.shape[0]
    share = group // PLANE

    def first():
        (far,) = column_blocks(hidden, down_matrix, order[:share], width)
        far_in = xor_permute(far, group, 1)
        (near,) = column_blocks(hidden, down_matrix, order[share : 2 * share], width)
        return pack_scaled(near + far_in)

    def first_idle():
        return jnp.zeros((half + 1, rows, LANES), jnp.float16)

    sent = lax.cond(order[0] >= 0, first, first_idle)
    pair_in = xor_permute(sent, group, 2)
    order, _ = lax.optimization_barrier((order, sent))

    def second():
        far, near = column_blocks(hidden, down_matrix, order[2 * share :], width, groups=2)
        return near + xor_permute(far, group, 1)

    def second_idle():
        return jnp.zeros((half, rows, LANES), jnp.float32)

    kept = lax.cond(order[1] >= 0, second, second_idle)
    return kept + unpack_scaled(pair_in)


def line_sums(pair, group, width):
    parts = width // LANES
    arrived = [
        xor_permute(pack_scaled(pair[i * parts : (i + 1) * parts]), group, PLANE * i)
        for i in range(1, group // PLANE)
    ]
    total = pair[:parts]
    for packed in arrived:
        total = total + unpack_scaled(packed)
    return total


def pack_kernel(
    blocks,
    orders,
    me_ref,
    slot_hbm,
    adapter_hbm,
    hidden_hbm,
    packed_ref,
    pick_ref,
    spread_ref,
    order_ref,
    kept_ref,
    slot_ref,
    adapter_ref,
    hidden_ref,
    sems,
):
    rows = hidden_ref.shape[0]
    group = slot_ref.shape[0]
    copies = [
        pltpu.make_async_copy(slot_hbm, slot_ref, sems.at[0]),
        pltpu.make_async_copy(adapter_hbm, adapter_ref, sems.at[1]),
        pltpu.make_async_copy(hidden_hbm, hidden_ref, sems.at[2]),
    ]
    for copy in copies:
        copy.start()
    me = me_ref[0]
    for i, (line, k) in enumerate(orders):
        order_ref[i] = me ^ (PLANE * line + k)
    ids = lax.broadcasted_iota(jnp.int32, (group, 1), 0)
    slots = jnp.zeros((group, 1), jnp.int32)
    copies[0].wait()
    for adapter in range(group):
        slots = jnp.where(ids == adapter, slot_ref[adapter], slots)
    copies[1].wait()
    adapter = adapter_ref[...]
    first = jnp.sum((adapter < ids).astype(jnp.int32), axis=1, keepdims=True)
    slot = jnp.sum(jnp.where(adapter == ids, slots, 0), axis=0, keepdims=True)
    first = jnp.sum(jnp.where(adapter == ids, first, 0), axis=0, keepdims=True)
    index = lax.broadcasted_iota(jnp.int32, (1, rows), 1) - first
    held = blocks * BLOCK
    spots = lax.broadcasted_iota(jnp.int32, (group * held, rows), 0)
    pick = jnp.where(spots == slot * held + index, 1.0, 0.0).astype(jnp.bfloat16)
    for k in range(PLANE):
        spots = lax.broadcasted_iota(jnp.int32, (HELD, rows), 0)
        mine = (slot == me ^ k) & (index == spots)
        pick_ref[k * HELD : (k + 1) * HELD] = jnp.where(mine, 1.0, 0.0).astype(jnp.bfloat16)
    lines = group // PLANE
    line = slot // PLANE
    member = (line == lax.broadcasted_iota(jnp.int32, (lines, rows), 0)).astype(jnp.float32)
    earlier = lax.broadcasted_iota(jnp.int32, (rows, rows), 0) < lax.broadcasted_iota(
        jnp.int32, (rows, rows), 1
    )
    ahead = jnp.dot(
        member.astype(jnp.bfloat16),
        jnp.where(earlier, 1.0, 0.0).astype(jnp.bfloat16),
        preferred_element_type=jnp.float32,
    )
    place = jnp.sum(member * ahead, axis=0, keepdims=True).astype(jnp.int32)
    most = spread_ref.shape[0] // lines
    spots = lax.broadcasted_iota(jnp.int32, (most, rows), 0)
    for i in range(lines):
        mine = (line == (me // PLANE) ^ i) & (place == spots)
        spread_ref[i * most : (i + 1) * most] = jnp.where(mine, 1.0, 0.0).astype(jnp.bfloat16)
    copies[2].wait()
    packed = jnp.dot(pick, hidden_ref[...], preferred_element_type=jnp.float32)
    packed_ref[...] = packed.astype(jnp.bfloat16).reshape(packed_ref.shape)
    kept_ref[...] = hidden_ref[...]


def plane_rows(rows, group):
    return min(PLANE * MOST, rows - (group - PLANE) * BLOCK)


def pack_rows(hidden, adapter_of_row, adapter_holder_slot, me, orders):
    rows, depth = hidden.shape
    group = adapter_holder_slot.shape[0]
    blocks = MOST // BLOCK
    vmem = pl.BlockSpec(memory_space=pltpu.VMEM)
    smem = pl.BlockSpec(memory_space=pltpu.SMEM)
    anywhere = pl.BlockSpec(memory_space=pltpu.HBM)
    return pl.pallas_call(
        functools.partial(pack_kernel, blocks, orders),
        out_shape=(
            jax.ShapeDtypeStruct((group * blocks, BLOCK, depth), jnp.bfloat16),
            jax.ShapeDtypeStruct((PLANE * HELD, rows), jnp.bfloat16),
            jax.ShapeDtypeStruct((group // PLANE * plane_rows(rows, group), rows), jnp.bfloat16),
            jax.ShapeDtypeStruct((len(orders),), jnp.int32),
            jax.ShapeDtypeStruct((rows, depth), jnp.bfloat16),
        ),
        in_specs=[smem, anywhere, anywhere, anywhere],
        out_specs=(vmem, vmem, vmem, smem, vmem),
        scratch_shapes=[
            pltpu.SMEM((group,), jnp.int32),
            pltpu.VMEM((1, rows), jnp.int32),
            pltpu.VMEM((rows, depth), jnp.bfloat16),
            pltpu.SemaphoreType.DMA((3,)),
        ],
        compiler_params=pltpu.CompilerParams(vmem_limit_bytes=24 * 2**20),
    )(me.reshape(1), in_hbm(adapter_holder_slot), in_hbm(adapter_of_row.reshape(1, rows)), in_hbm(hidden))


def adapter_kernel(parts, me_ref, rows_ref, expand_hbm, shrink_hbm, *refs):
    out_refs = refs[:PLANE]
    shrink_ref, expand_ref, total_ref, sems, expand_sem = refs[PLANE:]
    me = me_ref[0]
    group, _, depth = shrink_ref.shape
    blocks = MOST // BLOCK

    def copy(source):
        return pltpu.make_async_copy(
            shrink_hbm.at[:, pl.ds(source * depth, depth)], shrink_ref.at[source], sems.at[source]
        )

    for source in range(group):
        copy(source).start()
    expand_copy = pltpu.make_async_copy(expand_hbm, expand_ref, expand_sem)
    expand_copy.start()
    total = jnp.zeros((MOST, total_ref.shape[1]), jnp.float32)
    for source in range(group):
        copy(source).wait()
        own = rows_ref[source * blocks : (source + 1) * blocks].reshape(MOST, depth)
        total += lax.dot_general(
            own, shrink_ref[source], (((1,), (1,)), ((), ())), preferred_element_type=jnp.float32
        )
    total_ref[...] = jnp.zeros_like(total_ref)
    total_ref[:MOST] = total
    rank_rows = total_ref[...].astype(jnp.bfloat16)
    expand_copy.wait()
    width = parts * LANES
    for k in range(PLANE):
        for line in range(group // PLANE):
            target = me ^ (PLANE * line + k)
            columns = pl.ds(pl.multiple_of(target * width, LANES), width)
            piece = jnp.dot(rank_rows, expand_ref[:, columns], preferred_element_type=jnp.float32)
            piece = piece.astype(jnp.bfloat16)
            for part in range(parts):
                out_refs[k][line * parts + part] = piece[:, part * LANES : (part + 1) * LANES]


def adapter_output(gathered, shrink, expand, group, me):
    rank = shrink.shape[0]
    model_width = expand.shape[1]
    depth = gathered.shape[2]
    parts = model_width // group // LANES
    held = (model_width // PLANE // LANES, HELD, LANES)
    vmem = pl.BlockSpec(memory_space=pltpu.VMEM)
    return pl.pallas_call(
        functools.partial(adapter_kernel, parts),
        out_shape=[jax.ShapeDtypeStruct(held, jnp.bfloat16)] * PLANE,
        in_specs=[
            pl.BlockSpec(memory_space=pltpu.SMEM),
            vmem,
            pl.BlockSpec(memory_space=pl.ANY),
            pl.BlockSpec(memory_space=pl.ANY),
        ],
        out_specs=[vmem] * PLANE,
        scratch_shapes=[
            pltpu.VMEM((group, rank, depth), jnp.bfloat16),
            pltpu.VMEM((rank, model_width), jnp.bfloat16),
            pltpu.VMEM((HELD, rank), jnp.float32),
            pltpu.SemaphoreType.DMA((group,)),
            pltpu.SemaphoreType.DMA,
        ],
        compiler_params=pltpu.CompilerParams(vmem_limit_bytes=24 * 2**20),
    )(me.reshape(1), gathered, in_hbm(expand), in_hbm(shrink))


def line_kernel(pick_ref, spread_ref, *refs):
    in_refs, out_refs, held_ref = refs[:PLANE], refs[PLANE:-1], refs[-1]
    lines = len(out_refs)
    parts, most = out_refs[0].shape[:2]
    for k in range(PLANE):
        held_ref[:, k * HELD : (k + 1) * HELD] = in_refs[k][...]
    pick = lax.dot_general(
        spread_ref[:most], pick_ref[...], (((1,), (1,)), ((), ())), preferred_element_type=jnp.float32
    ).astype(jnp.bfloat16)
    for i in range(lines):
        for part in range(parts):
            piece = jnp.dot(pick, held_ref[i * parts + part], preferred_element_type=jnp.float32)
            out_refs[i][part] = piece.astype(jnp.bfloat16)


def line_rows(pick, spread, arrived, group):
    lines = group // PLANE
    blocks = arrived[0].shape[0]
    most = spread.shape[0] // lines
    vmem = pl.BlockSpec(memory_space=pltpu.VMEM)
    return pl.pallas_call(
        line_kernel,
        out_shape=[jax.ShapeDtypeStruct((blocks // lines, most, LANES), jnp.bfloat16)] * lines,
        in_specs=[vmem] * (2 + PLANE),
        out_specs=[vmem] * lines,
        scratch_shapes=[pltpu.VMEM((blocks, PLANE * HELD, LANES), jnp.bfloat16)],
        compiler_params=pltpu.CompilerParams(vmem_limit_bytes=24 * 2**20),
        cost_estimate=pl.CostEstimate(flops=1000, bytes_accessed=4_000_000, transcendentals=0),
    )(pick, spread, *arrived)


def final_kernel(base_ref, spread_ref, *refs):
    in_refs, out_ref = refs[:-1], refs[-1]
    parts, most = in_refs[0].shape[:2]
    for part in range(parts):
        total = base_ref[part]
        for i, in_ref in enumerate(in_refs):
            total += ADAPTER_SCALE * lax.dot_general(
                spread_ref[i * most : (i + 1) * most],
                in_ref[part],
                (((0,), (0,)), ((), ())),
                preferred_element_type=jnp.float32,
            )
        out_ref[:, part * LANES : (part + 1) * LANES] = total.astype(out_ref.dtype)


def add_adapters(base, spread, arrived):
    parts, rows, _ = base.shape
    vmem = pl.BlockSpec(memory_space=pltpu.VMEM)
    return pl.pallas_call(
        final_kernel,
        out_shape=jax.ShapeDtypeStruct((rows, parts * LANES), jnp.bfloat16),
        in_specs=[vmem] * (2 + len(arrived)),
        out_specs=vmem,
        compiler_params=pltpu.CompilerParams(vmem_limit_bytes=24 * 2**20),
    )(base, spread, *arrived)


def shards_by_blocks(
    hidden, down_matrix, shrink_matrices, expand_matrices, adapter_of_row, adapter_holder_slot
):
    group = lax.axis_size("tp")
    me = lax.axis_index("tp")
    rows, depth = hidden.shape
    width = down_matrix.shape[1] // group
    lines = group // PLANE
    orders = [(line, k) for k in (3, 2, 1, 0) for line in range(lines)]
    packed, pick, spread, order, kept_hidden = pack_rows(
        hidden, adapter_of_row, adapter_holder_slot, me, orders
    )
    gathered = lax.all_to_all(packed, "tp", split_axis=0, concat_axis=0, tiled=True)
    pair = pair_sums(kept_hidden, down_matrix, group, order, width)
    gathered, _ = lax.optimization_barrier((gathered, pair))
    shrink = jnp.swapaxes(shrink_matrices, 1, 2)[0]
    expand = jnp.swapaxes(expand_matrices, 1, 2)[0]
    outs = adapter_output(gathered, shrink, expand, group, me)
    pair, _ = lax.optimization_barrier((pair, outs[0]))
    base = line_sums(pair, group, width)
    arrived = [outs[0]] + [xor_permute(outs[k], group, k) for k in range(1, PLANE)]
    sent = line_rows(pick, spread, arrived, group)
    arrived = [sent[0]] + [xor_permute(sent[i], group, PLANE * i) for i in range(1, lines)]
    return add_adapters(base, spread, arrived)


def shards(
    hidden, down_matrix, shrink_matrices, expand_matrices, adapter_of_row, adapter_holder_slot
):
    group = lax.axis_size("tp")
    rows, depth = hidden.shape
    width = down_matrix.shape[1] // group
    if width % LANES == 0 and depth % LANES == 0 and group >= PLANE and group & (group - 1) == 0:
        return shards_by_blocks(
            hidden, down_matrix, shrink_matrices, expand_matrices, adapter_of_row, adapter_holder_slot
        )
    blocks = MOST // BLOCK
    adapter_ids = jnp.arange(group, dtype=jnp.int32)
    row_match = adapter_of_row[:, None] == adapter_ids[None, :]
    row_slot = jnp.sum(jnp.where(row_match, adapter_holder_slot[None, :], 0), axis=1)
    slot_mask = row_slot[None, :] == adapter_ids[:, None]
    before = jnp.cumsum(slot_mask.astype(jnp.int32), axis=1) - 1
    place = jnp.where(slot_mask, before, -1)
    pick = place[:, None, :] == jnp.arange(MOST, dtype=jnp.int32)[None, :, None]
    pick = pick.reshape(group * MOST, rows).astype(jnp.bfloat16)
    packed = jnp.dot(pick, hidden, preferred_element_type=jnp.float32).astype(jnp.bfloat16)
    packed = packed.reshape(group * blocks, BLOCK, depth)
    gathered = lax.all_to_all(packed, "tp", split_axis=0, concat_axis=0, tiled=True)
    partial_value = jnp.dot(hidden, down_matrix, preferred_element_type=jnp.float32)
    base = lax.psum_scatter(partial_value, "tp", scatter_dimension=1, tiled=True)
    own_rows = jnp.transpose(gathered.reshape(group, MOST, depth), (1, 0, 2))
    rank_rows = jnp.dot(
        own_rows.reshape(MOST, group * depth), shrink_matrices[0], preferred_element_type=jnp.float32
    ).astype(jnp.bfloat16)
    adapter_out = lax.dot_general(
        rank_rows, expand_matrices[0], (((1,), (1,)), ((), ())), preferred_element_type=jnp.float32
    ).astype(jnp.bfloat16)
    adapter_out = jnp.transpose(adapter_out.reshape(blocks, BLOCK, group, width), (2, 0, 1, 3))
    adapter_in = lax.all_to_all(
        adapter_out.reshape(group * blocks, BLOCK, width), "tp", split_axis=0, concat_axis=0, tiled=True
    )
    adapter_rows = lax.dot_general(
        pick,
        adapter_in.reshape(group * MOST, width),
        (((0,), (0,)), ((), ())),
        preferred_element_type=jnp.float32,
    )
    return (base + ADAPTER_SCALE * adapter_rows).astype(jnp.bfloat16)


def solution(mesh):
    in_specs = (
        P("rep", "tp"),
        P("tp", None),
        P(("rep", "tp"), None, None),
        P(("rep", "tp"), None, None),
        P("rep"),
        P("rep"),
    )
    out_specs = P("rep", "tp")
    return jax.shard_map(shards, mesh=mesh, in_specs=in_specs, out_specs=out_specs, check_vma=False)
```

```python
import functools

import jax
import jax.numpy as jnp
from jax import lax
from jax.experimental import pallas as pl
from jax.experimental.pallas import tpu as pltpu
from jax.sharding import PartitionSpec as P

ADAPTER_SCALE = 0.5
BLOCK = 4
MOST = 20
LANES = 128
F16_TOP = 14.0
PLANE = 4
HELD = 24


def in_hbm(value):
    return pltpu.with_memory_space_constraint(value, pltpu.HBM)


def xor_permute(value, group, offset):
    return lax.ppermute(value, "tp", [(i, i ^ offset) for i in range(group)])


def column_blocks_kernel(groups, order_ref, hidden_ref, down_ref, *refs):
    out_refs, held_ref, sems = refs[:groups], refs[groups], refs[groups + 1]
    count, depth, width = held_ref.shape
    parts = width // LANES
    pieces = sems.shape[1]
    cut = depth // pieces

    def copy(block, piece):
        start = pl.multiple_of(order_ref[block] * width, LANES)
        lines = pl.ds(piece * cut, cut)
        return pltpu.make_async_copy(
            down_ref.at[lines, pl.ds(start, width)], held_ref.at[block, lines], sems.at[block, piece]
        )

    for block in range(count):
        for piece in range(pieces):
            copy(block, piece).start()
    share = count // groups
    for block in range(count):
        for piece in range(pieces):
            copy(block, piece).wait()
        product = jnp.dot(hidden_ref[...], held_ref[block], preferred_element_type=jnp.float32)
        for lane in range(parts):
            out_refs[block // share][block % share * parts + lane] = product[
                :, lane * LANES : (lane + 1) * LANES
            ]


def column_blocks(hidden, down_matrix, order, width, groups=1):
    rows, depth = hidden.shape
    count = order.shape[0]
    pieces = 2 if depth % 32 == 0 else 1
    vmem = pl.BlockSpec(memory_space=pltpu.VMEM)
    out = jax.ShapeDtypeStruct((count // groups * width // LANES, rows, LANES), jnp.float32)
    return pl.pallas_call(
        functools.partial(column_blocks_kernel, groups),
        out_shape=[out] * groups,
        in_specs=[
            pl.BlockSpec(memory_space=pltpu.SMEM),
            vmem,
            pl.BlockSpec(memory_space=pl.ANY),
        ],
        out_specs=[vmem] * groups,
        scratch_shapes=[
            pltpu.VMEM((count, depth, width), jnp.bfloat16),
            pltpu.SemaphoreType.DMA((count, pieces)),
        ],
        compiler_params=pltpu.CompilerParams(vmem_limit_bytes=(12 + 12 * groups) * 2**20),
        cost_estimate=pl.CostEstimate(flops=1000, bytes_accessed=1000, transcendentals=0),
    )(order, hidden, in_hbm(down_matrix))


def pack_scaled(value):
    peak = jnp.max(jnp.abs(value), axis=(0, 2), keepdims=True)
    exponent = jnp.ceil(jnp.log2(jnp.maximum(peak, 2.0**-100)))
    scaled = (value * jnp.exp2(F16_TOP - exponent)).astype(jnp.float16)
    marks = jnp.broadcast_to(exponent, (1,) + value.shape[1:]).astype(jnp.float16)
    return jnp.concatenate([scaled, marks], axis=0)


def unpack_scaled(packed):
    exponent = packed[-1:].astype(jnp.float32)
    return packed[:-1].astype(jnp.float32) * jnp.exp2(exponent - F16_TOP)


def pair_sums(hidden, down_matrix, group, order, width):
    half = group * width // LANES // PLANE
    rows = hidden.shape[0]
    share = group // PLANE

    def first():
        (far,) = column_blocks(hidden, down_matrix, order[:share], width)
        far_in = xor_permute(far, group, 1)
        (near,) = column_blocks(hidden, down_matrix, order[share : 2 * share], width)
        return pack_scaled(near + far_in)

    def first_idle():
        return jnp.zeros((half + 1, rows, LANES), jnp.float16)

    sent = lax.cond(order[0] >= 0, first, first_idle)
    pair_in = xor_permute(sent, group, 2)
    order, _ = lax.optimization_barrier((order, sent))

    def second():
        far, near = column_blocks(hidden, down_matrix, order[2 * share :], width, groups=2)
        return near + xor_permute(far, group, 1)

    def second_idle():
        return jnp.zeros((half, rows, LANES), jnp.float32)

    kept = lax.cond(order[1] >= 0, second, second_idle)
    return kept + unpack_scaled(pair_in)


def line_sums(pair, group, width):
    parts = width // LANES
    arrived = [
        xor_permute(pack_scaled(pair[i * parts : (i + 1) * parts]), group, PLANE * i)
        for i in range(1, group // PLANE)
    ]
    total = pair[:parts]
    for packed in arrived:
        total = total + unpack_scaled(packed)
    return total


def pack_kernel(
    blocks,
    orders,
    me_ref,
    slot_hbm,
    adapter_hbm,
    hidden_hbm,
    packed_ref,
    pick_ref,
    spread_ref,
    order_ref,
    kept_ref,
    slot_ref,
    adapter_ref,
    hidden_ref,
    sems,
):
    rows = hidden_ref.shape[0]
    group = slot_ref.shape[0]
    copies = [
        pltpu.make_async_copy(slot_hbm, slot_ref, sems.at[0]),
        pltpu.make_async_copy(adapter_hbm, adapter_ref, sems.at[1]),
        pltpu.make_async_copy(hidden_hbm, hidden_ref, sems.at[2]),
    ]
    for copy in copies:
        copy.start()
    me = me_ref[0]
    for i, (line, k) in enumerate(orders):
        order_ref[i] = me ^ (PLANE * line + k)
    ids = lax.broadcasted_iota(jnp.int32, (group, 1), 0)
    slots = jnp.zeros((group, 1), jnp.int32)
    copies[0].wait()
    for adapter in range(group):
        slots = jnp.where(ids == adapter, slot_ref[adapter], slots)
    copies[1].wait()
    adapter = adapter_ref[...]
    first = jnp.sum((adapter < ids).astype(jnp.int32), axis=1, keepdims=True)
    slot = jnp.sum(jnp.where(adapter == ids, slots, 0), axis=0, keepdims=True)
    first = jnp.sum(jnp.where(adapter == ids, first, 0), axis=0, keepdims=True)
    index = lax.broadcasted_iota(jnp.int32, (1, rows), 1) - first
    held = blocks * BLOCK
    spots = lax.broadcasted_iota(jnp.int32, (group * held, rows), 0)
    pick = jnp.where(spots == slot * held + index, 1.0, 0.0).astype(jnp.bfloat16)
    for k in range(PLANE):
        spots = lax.broadcasted_iota(jnp.int32, (HELD, rows), 0)
        mine = (slot == me ^ k) & (index == spots)
        pick_ref[k * HELD : (k + 1) * HELD] = jnp.where(mine, 1.0, 0.0).astype(jnp.bfloat16)
    lines = group // PLANE
    line = slot // PLANE
    member = (line == lax.broadcasted_iota(jnp.int32, (lines, rows), 0)).astype(jnp.float32)
    earlier = lax.broadcasted_iota(jnp.int32, (rows, rows), 0) < lax.broadcasted_iota(
        jnp.int32, (rows, rows), 1
    )
    ahead = jnp.dot(
        member.astype(jnp.bfloat16),
        jnp.where(earlier, 1.0, 0.0).astype(jnp.bfloat16),
        preferred_element_type=jnp.float32,
    )
    place = jnp.sum(member * ahead, axis=0, keepdims=True).astype(jnp.int32)
    most = spread_ref.shape[0] // lines
    spots = lax.broadcasted_iota(jnp.int32, (most, rows), 0)
    for i in range(lines):
        mine = (line == (me // PLANE) ^ i) & (place == spots)
        spread_ref[i * most : (i + 1) * most] = jnp.where(mine, 1.0, 0.0).astype(jnp.bfloat16)
    copies[2].wait()
    packed = jnp.dot(pick, hidden_ref[...], preferred_element_type=jnp.float32)
    packed_ref[...] = packed.astype(jnp.bfloat16).reshape(packed_ref.shape)
    kept_ref[...] = hidden_ref[...]


def plane_rows(rows, group):
    return min(PLANE * MOST, rows - (group - PLANE) * BLOCK)


def pack_rows(hidden, adapter_of_row, adapter_holder_slot, me, orders):
    rows, depth = hidden.shape
    group = adapter_holder_slot.shape[0]
    blocks = MOST // BLOCK
    vmem = pl.BlockSpec(memory_space=pltpu.VMEM)
    smem = pl.BlockSpec(memory_space=pltpu.SMEM)
    anywhere = pl.BlockSpec(memory_space=pltpu.HBM)
    return pl.pallas_call(
        functools.partial(pack_kernel, blocks, orders),
        out_shape=(
            jax.ShapeDtypeStruct((group * blocks, BLOCK, depth), jnp.bfloat16),
            jax.ShapeDtypeStruct((PLANE * HELD, rows), jnp.bfloat16),
            jax.ShapeDtypeStruct((group // PLANE * plane_rows(rows, group), rows), jnp.bfloat16),
            jax.ShapeDtypeStruct((len(orders),), jnp.int32),
            jax.ShapeDtypeStruct((rows, depth), jnp.bfloat16),
        ),
        in_specs=[smem, anywhere, anywhere, anywhere],
        out_specs=(vmem, vmem, vmem, smem, vmem),
        scratch_shapes=[
            pltpu.SMEM((group,), jnp.int32),
            pltpu.VMEM((1, rows), jnp.int32),
            pltpu.VMEM((rows, depth), jnp.bfloat16),
            pltpu.SemaphoreType.DMA((3,)),
        ],
        compiler_params=pltpu.CompilerParams(vmem_limit_bytes=24 * 2**20),
    )(me.reshape(1), in_hbm(adapter_holder_slot), in_hbm(adapter_of_row.reshape(1, rows)), in_hbm(hidden))


def adapter_kernel(parts, me_ref, rows_ref, expand_hbm, shrink_hbm, *refs):
    out_refs = refs[:PLANE]
    shrink_ref, expand_ref, total_ref, sems, expand_sem = refs[PLANE:]
    me = me_ref[0]
    group, _, depth = shrink_ref.shape
    blocks = MOST // BLOCK

    def copy(source):
        return pltpu.make_async_copy(
            shrink_hbm.at[:, pl.ds(source * depth, depth)], shrink_ref.at[source], sems.at[source]
        )

    for source in range(group):
        copy(source).start()
    expand_copy = pltpu.make_async_copy(expand_hbm, expand_ref, expand_sem)
    expand_copy.start()
    total = jnp.zeros((MOST, total_ref.shape[1]), jnp.float32)
    for source in range(group):
        copy(source).wait()
        own = rows_ref[source * blocks : (source + 1) * blocks].reshape(MOST, depth)
        total += lax.dot_general(
            own, shrink_ref[source], (((1,), (1,)), ((), ())), preferred_element_type=jnp.float32
        )
    total_ref[...] = jnp.zeros_like(total_ref)
    total_ref[:MOST] = total
    rank_rows = total_ref[...].astype(jnp.bfloat16)
    expand_copy.wait()
    width = parts * LANES
    for k in range(PLANE):
        for line in range(group // PLANE):
            target = me ^ (PLANE * line + k)
            columns = pl.ds(pl.multiple_of(target * width, LANES), width)
            piece = jnp.dot(rank_rows, expand_ref[:, columns], preferred_element_type=jnp.float32)
            piece = piece.astype(jnp.bfloat16)
            for part in range(parts):
                out_refs[k][line * parts + part] = piece[:, part * LANES : (part + 1) * LANES]


def adapter_output(gathered, shrink, expand, group, me):
    rank = shrink.shape[0]
    model_width = expand.shape[1]
    depth = gathered.shape[2]
    parts = model_width // group // LANES
    held = (model_width // PLANE // LANES, HELD, LANES)
    vmem = pl.BlockSpec(memory_space=pltpu.VMEM)
    return pl.pallas_call(
        functools.partial(adapter_kernel, parts),
        out_shape=[jax.ShapeDtypeStruct(held, jnp.bfloat16)] * PLANE,
        in_specs=[
            pl.BlockSpec(memory_space=pltpu.SMEM),
            vmem,
            pl.BlockSpec(memory_space=pl.ANY),
            pl.BlockSpec(memory_space=pl.ANY),
        ],
        out_specs=[vmem] * PLANE,
        scratch_shapes=[
            pltpu.VMEM((group, rank, depth), jnp.bfloat16),
            pltpu.VMEM((rank, model_width), jnp.bfloat16),
            pltpu.VMEM((HELD, rank), jnp.float32),
            pltpu.SemaphoreType.DMA((group,)),
            pltpu.SemaphoreType.DMA,
        ],
        compiler_params=pltpu.CompilerParams(vmem_limit_bytes=24 * 2**20),
    )(me.reshape(1), gathered, in_hbm(expand), in_hbm(shrink))


def line_kernel(pick_ref, spread_ref, *refs):
    in_refs, out_refs, held_ref = refs[:PLANE], refs[PLANE:-1], refs[-1]
    lines = len(out_refs)
    parts, most = out_refs[0].shape[:2]
    for k in range(PLANE):
        held_ref[:, k * HELD : (k + 1) * HELD] = in_refs[k][...]
    pick = lax.dot_general(
        spread_ref[:most], pick_ref[...], (((1,), (1,)), ((), ())), preferred_element_type=jnp.float32
    ).astype(jnp.bfloat16)
    for i in range(lines):
        for part in range(parts):
            piece = jnp.dot(pick, held_ref[i * parts + part], preferred_element_type=jnp.float32)
            out_refs[i][part] = piece.astype(jnp.bfloat16)


def line_rows(pick, spread, arrived, group):
    lines = group // PLANE
    blocks = arrived[0].shape[0]
    most = spread.shape[0] // lines
    vmem = pl.BlockSpec(memory_space=pltpu.VMEM)
    return pl.pallas_call(
        line_kernel,
        out_shape=[jax.ShapeDtypeStruct((blocks // lines, most, LANES), jnp.bfloat16)] * lines,
        in_specs=[vmem] * (2 + PLANE),
        out_specs=[vmem] * lines,
        scratch_shapes=[pltpu.VMEM((blocks, PLANE * HELD, LANES), jnp.bfloat16)],
        compiler_params=pltpu.CompilerParams(vmem_limit_bytes=24 * 2**20),
        cost_estimate=pl.CostEstimate(flops=1000, bytes_accessed=40_000_000, transcendentals=0),
    )(pick, spread, *arrived)


def final_kernel(base_ref, spread_ref, *refs):
    in_refs, out_ref = refs[:-1], refs[-1]
    parts, most = in_refs[0].shape[:2]
    for part in range(parts):
        total = base_ref[part]
        for i, in_ref in enumerate(in_refs):
            total += ADAPTER_SCALE * lax.dot_general(
                spread_ref[i * most : (i + 1) * most],
                in_ref[part],
                (((0,), (0,)), ((), ())),
                preferred_element_type=jnp.float32,
            )
        out_ref[:, part * LANES : (part + 1) * LANES] = total.astype(out_ref.dtype)


def add_adapters(base, spread, arrived):
    parts, rows, _ = base.shape
    vmem = pl.BlockSpec(memory_space=pltpu.VMEM)
    return pl.pallas_call(
        final_kernel,
        out_shape=jax.ShapeDtypeStruct((rows, parts * LANES), jnp.bfloat16),
        in_specs=[vmem] * (2 + len(arrived)),
        out_specs=vmem,
        compiler_params=pltpu.CompilerParams(vmem_limit_bytes=24 * 2**20),
    )(base, spread, *arrived)


def shards_by_blocks(
    hidden, down_matrix, shrink_matrices, expand_matrices, adapter_of_row, adapter_holder_slot
):
    group = lax.axis_size("tp")
    me = lax.axis_index("tp")
    rows, depth = hidden.shape
    width = down_matrix.shape[1] // group
    lines = group // PLANE
    orders = [(line, k) for k in (3, 2, 1, 0) for line in range(lines)]
    packed, pick, spread, order, kept_hidden = pack_rows(
        hidden, adapter_of_row, adapter_holder_slot, me, orders
    )
    gathered = lax.all_to_all(packed, "tp", split_axis=0, concat_axis=0, tiled=True)
    pair = pair_sums(kept_hidden, down_matrix, group, order, width)
    gathered, _ = lax.optimization_barrier((gathered, pair))
    shrink = jnp.swapaxes(shrink_matrices, 1, 2)[0]
    expand = jnp.swapaxes(expand_matrices, 1, 2)[0]
    outs = adapter_output(gathered, shrink, expand, group, me)
    pair, _ = lax.optimization_barrier((pair, outs[0]))
    base = line_sums(pair, group, width)
    arrived = [outs[0]] + [xor_permute(outs[k], group, k) for k in range(1, PLANE)]
    sent = line_rows(pick, spread, arrived, group)
    arrived = [sent[0]] + [xor_permute(sent[i], group, PLANE * i) for i in range(1, lines)]
    return add_adapters(base, spread, arrived)


def shards(
    hidden, down_matrix, shrink_matrices, expand_matrices, adapter_of_row, adapter_holder_slot
):
    group = lax.axis_size("tp")
    rows, depth = hidden.shape
    width = down_matrix.shape[1] // group
    if width % LANES == 0 and depth % LANES == 0 and group >= PLANE and group & (group - 1) == 0:
        return shards_by_blocks(
            hidden, down_matrix, shrink_matrices, expand_matrices, adapter_of_row, adapter_holder_slot
        )
    blocks = MOST // BLOCK
    adapter_ids = jnp.arange(group, dtype=jnp.int32)
    row_match = adapter_of_row[:, None] == adapter_ids[None, :]
    row_slot = jnp.sum(jnp.where(row_match, adapter_holder_slot[None, :], 0), axis=1)
    slot_mask = row_slot[None, :] == adapter_ids[:, None]
    before = jnp.cumsum(slot_mask.astype(jnp.int32), axis=1) - 1
    place = jnp.where(slot_mask, before, -1)
    pick = place[:, None, :] == jnp.arange(MOST, dtype=jnp.int32)[None, :, None]
    pick = pick.reshape(group * MOST, rows).astype(jnp.bfloat16)
    packed = jnp.dot(pick, hidden, preferred_element_type=jnp.float32).astype(jnp.bfloat16)
    packed = packed.reshape(group * blocks, BLOCK, depth)
    gathered = lax.all_to_all(packed, "tp", split_axis=0, concat_axis=0, tiled=True)
    partial_value = jnp.dot(hidden, down_matrix, preferred_element_type=jnp.float32)
    base = lax.psum_scatter(partial_value, "tp", scatter_dimension=1, tiled=True)
    own_rows = jnp.transpose(gathered.reshape(group, MOST, depth), (1, 0, 2))
    rank_rows = jnp.dot(
        own_rows.reshape(MOST, group * depth), shrink_matrices[0], preferred_element_type=jnp.float32
    ).astype(jnp.bfloat16)
    adapter_out = lax.dot_general(
        rank_rows, expand_matrices[0], (((1,), (1,)), ((), ())), preferred_element_type=jnp.float32
    ).astype(jnp.bfloat16)
    adapter_out = jnp.transpose(adapter_out.reshape(blocks, BLOCK, group, width), (2, 0, 1, 3))
    adapter_in = lax.all_to_all(
        adapter_out.reshape(group * blocks, BLOCK, width), "tp", split_axis=0, concat_axis=0, tiled=True
    )
    adapter_rows = lax.dot_general(
        pick,
        adapter_in.reshape(group * MOST, width),
        (((0,), (0,)), ((), ())),
        preferred_element_type=jnp.float32,
    )
    return (base + ADAPTER_SCALE * adapter_rows).astype(jnp.bfloat16)


def solution(mesh):
    in_specs = (
        P("rep", "tp"),
        P("tp", None),
        P(("rep", "tp"), None, None),
        P(("rep", "tp"), None, None),
        P("rep"),
        P("rep"),
    )
    out_specs = P("rep", "tp")
    return jax.shard_map(shards, mesh=mesh, in_specs=in_specs, out_specs=out_specs, check_vma=False)
```

```python
import functools

import jax
import jax.numpy as jnp
from jax import lax
from jax.experimental import pallas as pl
from jax.experimental.pallas import tpu as pltpu
from jax.sharding import PartitionSpec as P

ADAPTER_SCALE = 0.5
BLOCK = 4
MOST = 20
LANES = 128
F16_TOP = 14.0
PLANE = 4
HELD = 24
MARK_ROWS = 16


def in_hbm(value):
    return pltpu.with_memory_space_constraint(value, pltpu.HBM)


def xor_permute(value, group, offset):
    return lax.ppermute(value, "tp", [(i, i ^ offset) for i in range(group)])


def column_blocks_kernel(groups, order_ref, hidden_ref, down_ref, *refs):
    out_refs, held_ref, sems = refs[:groups], refs[groups], refs[groups + 1]
    count, depth, width = held_ref.shape
    parts = width // LANES
    pieces = sems.shape[1]
    cut = depth // pieces

    def copy(block, piece):
        start = pl.multiple_of(order_ref[block] * width, LANES)
        lines = pl.ds(piece * cut, cut)
        return pltpu.make_async_copy(
            down_ref.at[lines, pl.ds(start, width)], held_ref.at[block, lines], sems.at[block, piece]
        )

    for block in range(count):
        for piece in range(pieces):
            copy(block, piece).start()
    share = count // groups
    for block in range(count):
        for piece in range(pieces):
            copy(block, piece).wait()
        product = jnp.dot(hidden_ref[...], held_ref[block], preferred_element_type=jnp.float32)
        for lane in range(parts):
            out_refs[block // share][block % share * parts + lane] = product[
                :, lane * LANES : (lane + 1) * LANES
            ]


def column_blocks(hidden, down_matrix, order, width, groups=1):
    rows, depth = hidden.shape
    count = order.shape[0]
    pieces = 2 if depth % 32 == 0 else 1
    vmem = pl.BlockSpec(memory_space=pltpu.VMEM)
    out = jax.ShapeDtypeStruct((count // groups * width // LANES, rows, LANES), jnp.float32)
    return pl.pallas_call(
        functools.partial(column_blocks_kernel, groups),
        out_shape=[out] * groups,
        in_specs=[
            pl.BlockSpec(memory_space=pltpu.SMEM),
            vmem,
            pl.BlockSpec(memory_space=pl.ANY),
        ],
        out_specs=[vmem] * groups,
        scratch_shapes=[
            pltpu.VMEM((count, depth, width), jnp.bfloat16),
            pltpu.SemaphoreType.DMA((count, pieces)),
        ],
        compiler_params=pltpu.CompilerParams(vmem_limit_bytes=(12 + 12 * groups) * 2**20),
        cost_estimate=pl.CostEstimate(flops=1000, bytes_accessed=1000, transcendentals=0),
    )(order, hidden, in_hbm(down_matrix))


def pack_scaled(value):
    blocks, rows, lanes = value.shape
    peak = jnp.max(jnp.abs(value), axis=(0, 2))
    exponent = jnp.ceil(jnp.log2(jnp.maximum(peak, 2.0**-100)))
    scaled = (value * jnp.exp2(F16_TOP - exponent)[None, :, None]).astype(jnp.float16)
    marks = jnp.pad(exponent.astype(jnp.float16)[None], ((0, MARK_ROWS - 1), (0, lanes - rows)))
    return jnp.concatenate([scaled.reshape(blocks * rows, lanes), marks], axis=0)


def unpack_scaled(packed, rows):
    values, exponent = packed[:-MARK_ROWS], packed[-MARK_ROWS, :rows].astype(jnp.float32)
    values = values.reshape(-1, rows, packed.shape[1]).astype(jnp.float32)
    return values * jnp.exp2(exponent - F16_TOP)[None, :, None]


def pair_sums(hidden, down_matrix, group, order, width):
    half = group * width // LANES // PLANE
    rows = hidden.shape[0]
    share = group // PLANE

    def first():
        (far,) = column_blocks(hidden, down_matrix, order[:share], width)
        far_in = xor_permute(far, group, 1)
        (near,) = column_blocks(hidden, down_matrix, order[share : 2 * share], width)
        return pack_scaled(near + far_in)

    def first_idle():
        return jnp.zeros((half * rows + MARK_ROWS, LANES), jnp.float16)

    sent = lax.cond(order[0] >= 0, first, first_idle)
    pair_in = xor_permute(sent, group, 2)
    order, _ = lax.optimization_barrier((order, sent))

    def second():
        far, near = column_blocks(hidden, down_matrix, order[2 * share :], width, groups=2)
        return near + xor_permute(far, group, 1)

    def second_idle():
        return jnp.zeros((half, rows, LANES), jnp.float32)

    kept = lax.cond(order[1] >= 0, second, second_idle)
    return kept + unpack_scaled(pair_in, rows)


def line_sums(pair, group, width):
    rows = pair.shape[1]
    parts = width // LANES
    arrived = [
        xor_permute(pack_scaled(pair[i * parts : (i + 1) * parts]), group, 4 * i)
        for i in range(1, group // 4)
    ]
    total = pair[:parts]
    for packed in arrived:
        total = total + unpack_scaled(packed, rows)
    return jnp.transpose(total, (1, 0, 2)).reshape(rows, width)


def pack_kernel(
    blocks,
    orders,
    me_ref,
    slot_hbm,
    adapter_hbm,
    hidden_hbm,
    packed_ref,
    pick_ref,
    order_ref,
    kept_ref,
    slot_ref,
    adapter_ref,
    hidden_ref,
    sems,
):
    rows = hidden_ref.shape[0]
    group = slot_ref.shape[0]
    copies = [
        pltpu.make_async_copy(slot_hbm, slot_ref, sems.at[0]),
        pltpu.make_async_copy(adapter_hbm, adapter_ref, sems.at[1]),
        pltpu.make_async_copy(hidden_hbm, hidden_ref, sems.at[2]),
    ]
    for copy in copies:
        copy.start()
    for i, offset in enumerate(orders):
        order_ref[i] = me_ref[0] ^ offset
    ids = lax.broadcasted_iota(jnp.int32, (group, 1), 0)
    slots = jnp.zeros((group, 1), jnp.int32)
    copies[0].wait()
    for adapter in range(group):
        slots = jnp.where(ids == adapter, slot_ref[adapter], slots)
    copies[1].wait()
    adapter = adapter_ref[...]
    first = jnp.sum((adapter < ids).astype(jnp.int32), axis=1, keepdims=True)
    shift = jnp.where(adapter == ids, slots * (blocks * BLOCK) - first, 0)
    place = jnp.sum(shift, axis=0, keepdims=True) + lax.broadcasted_iota(jnp.int32, (1, rows), 1)
    spots = lax.broadcasted_iota(jnp.int32, (group * blocks * BLOCK, rows), 0)
    pick = jnp.where(spots == place, 1.0, 0.0).astype(jnp.bfloat16)
    for k in range(PLANE):
        line = lax.broadcasted_iota(jnp.int32, (HELD, rows), 0)
        mine = (line + (me_ref[0] ^ k) * (blocks * BLOCK) == place) & (line < blocks * BLOCK)
        pick_ref[k * HELD : (k + 1) * HELD] = jnp.where(mine, 1.0, 0.0).astype(jnp.bfloat16)
    copies[2].wait()
    packed = jnp.dot(pick, hidden_ref[...], preferred_element_type=jnp.float32)
    packed_ref[...] = packed.astype(jnp.bfloat16).reshape(packed_ref.shape)
    kept_ref[...] = hidden_ref[...]


def pack_rows(hidden, adapter_of_row, adapter_holder_slot, me, orders):
    rows, depth = hidden.shape
    group = adapter_holder_slot.shape[0]
    blocks = MOST // BLOCK
    vmem = pl.BlockSpec(memory_space=pltpu.VMEM)
    smem = pl.BlockSpec(memory_space=pltpu.SMEM)
    anywhere = pl.BlockSpec(memory_space=pltpu.HBM)
    return pl.pallas_call(
        functools.partial(pack_kernel, blocks, orders),
        out_shape=(
            jax.ShapeDtypeStruct((group * blocks, BLOCK, depth), jnp.bfloat16),
            jax.ShapeDtypeStruct((PLANE * HELD, rows), jnp.bfloat16),
            jax.ShapeDtypeStruct((len(orders),), jnp.int32),
            jax.ShapeDtypeStruct((rows, depth), jnp.bfloat16),
        ),
        in_specs=[smem, anywhere, anywhere, anywhere],
        out_specs=(vmem, vmem, smem, vmem),
        scratch_shapes=[
            pltpu.SMEM((group,), jnp.int32),
            pltpu.VMEM((1, rows), jnp.int32),
            pltpu.VMEM((rows, depth), jnp.bfloat16),
            pltpu.SemaphoreType.DMA((3,)),
        ],
        compiler_params=pltpu.CompilerParams(vmem_limit_bytes=24 * 2**20),
    )(me.reshape(1), in_hbm(adapter_holder_slot), in_hbm(adapter_of_row.reshape(1, rows)), in_hbm(hidden))


def adapter_kernel(parts, me_ref, rows_ref, expand_hbm, shrink_hbm, *refs):
    out_refs = refs[:PLANE]
    shrink_ref, expand_ref, total_ref, sems, expand_sem = refs[PLANE:]
    me = me_ref[0]
    group, _, depth = shrink_ref.shape
    blocks = MOST // BLOCK

    def copy(source):
        return pltpu.make_async_copy(
            shrink_hbm.at[:, pl.ds(source * depth, depth)], shrink_ref.at[source], sems.at[source]
        )

    for source in range(group):
        copy(source).start()
    expand_copy = pltpu.make_async_copy(expand_hbm, expand_ref, expand_sem)
    expand_copy.start()
    total = jnp.zeros((MOST, total_ref.shape[1]), jnp.float32)
    for source in range(group):
        copy(source).wait()
        own = rows_ref[source * blocks : (source + 1) * blocks].reshape(MOST, depth)
        total += lax.dot_general(
            own, shrink_ref[source], (((1,), (1,)), ((), ())), preferred_element_type=jnp.float32
        )
    total_ref[...] = jnp.zeros_like(total_ref)
    total_ref[:MOST] = total
    rank_rows = total_ref[...].astype(jnp.bfloat16)
    expand_copy.wait()
    width = parts * LANES
    for k in range(PLANE):
        for line in range(group // PLANE):
            target = me ^ (PLANE * line + k)
            columns = pl.ds(pl.multiple_of(target * width, LANES), width)
            piece = jnp.dot(rank_rows, expand_ref[:, columns], preferred_element_type=jnp.float32)
            piece = piece.astype(jnp.bfloat16)
            for part in range(parts):
                out_refs[k][line * parts + part] = piece[:, part * LANES : (part + 1) * LANES]


def adapter_output(gathered, shrink, expand, group, me):
    rank = shrink.shape[0]
    model_width = expand.shape[1]
    depth = gathered.shape[2]
    parts = model_width // group // LANES
    held = (model_width // PLANE // LANES, HELD, LANES)
    vmem = pl.BlockSpec(memory_space=pltpu.VMEM)
    return pl.pallas_call(
        functools.partial(adapter_kernel, parts),
        out_shape=[jax.ShapeDtypeStruct(held, jnp.bfloat16)] * PLANE,
        in_specs=[
            pl.BlockSpec(memory_space=pltpu.SMEM),
            vmem,
            pl.BlockSpec(memory_space=pl.ANY),
            pl.BlockSpec(memory_space=pl.ANY),
        ],
        out_specs=[vmem] * PLANE,
        scratch_shapes=[
            pltpu.VMEM((group, rank, depth), jnp.bfloat16),
            pltpu.VMEM((rank, model_width), jnp.bfloat16),
            pltpu.VMEM((HELD, rank), jnp.float32),
            pltpu.SemaphoreType.DMA((group,)),
            pltpu.SemaphoreType.DMA,
        ],
        compiler_params=pltpu.CompilerParams(vmem_limit_bytes=24 * 2**20),
    )(me.reshape(1), gathered, in_hbm(expand), in_hbm(shrink))


def merge_kernel(pair_ref, pick_ref, *refs):
    in_refs, out_ref, held_ref = refs[:PLANE], refs[PLANE], refs[PLANE + 1]
    for k in range(PLANE):
        held_ref[:, k * HELD : (k + 1) * HELD] = in_refs[k][...]
    pick = pick_ref[...]
    for part in range(pair_ref.shape[0]):
        adapter_rows = lax.dot_general(
            pick, held_ref[part], (((0,), (0,)), ((), ())), preferred_element_type=jnp.float32
        )
        out_ref[part] = pair_ref[part] + ADAPTER_SCALE * adapter_rows


def merge_adapters(pair, pick, arrived):
    vmem = pl.BlockSpec(memory_space=pltpu.VMEM)
    return pl.pallas_call(
        merge_kernel,
        out_shape=jax.ShapeDtypeStruct(pair.shape, jnp.float32),
        in_specs=[vmem] * (2 + PLANE),
        out_specs=vmem,
        scratch_shapes=[pltpu.VMEM((pair.shape[0], PLANE * HELD, LANES), jnp.bfloat16)],
        compiler_params=pltpu.CompilerParams(vmem_limit_bytes=24 * 2**20),
    )(pair, pick, *arrived)


def shards_by_blocks(
    hidden, down_matrix, shrink_matrices, expand_matrices, adapter_of_row, adapter_holder_slot
):
    group = lax.axis_size("tp")
    me = lax.axis_index("tp")
    rows, depth = hidden.shape
    width = down_matrix.shape[1] // group
    quads = list(range(0, group, 4))
    orders = [q + k for k in (3, 2, 1, 0) for q in quads]
    packed, pick, order, kept_hidden = pack_rows(
        hidden, adapter_of_row, adapter_holder_slot, me, orders
    )
    gathered = lax.all_to_all(packed, "tp", split_axis=0, concat_axis=0, tiled=True)
    shrink = jnp.swapaxes(shrink_matrices, 1, 2)[0]
    pair = pair_sums(kept_hidden, down_matrix, group, order, width)
    gathered, _ = lax.optimization_barrier((gathered, pair))
    expand = jnp.swapaxes(expand_matrices, 1, 2)[0]
    outs = adapter_output(gathered, shrink, expand, group, me)
    arrived = [outs[0]] + [xor_permute(outs[k], group, k) for k in range(1, PLANE)]
    merged = merge_adapters(pair, pick, arrived)
    return line_sums(merged, group, width).astype(jnp.bfloat16)


def shards(
    hidden, down_matrix, shrink_matrices, expand_matrices, adapter_of_row, adapter_holder_slot
):
    group = lax.axis_size("tp")
    rows, depth = hidden.shape
    width = down_matrix.shape[1] // group
    if width % LANES == 0 and depth % LANES == 0 and rows <= LANES and group >= PLANE and group & (group - 1) == 0:
        return shards_by_blocks(
            hidden, down_matrix, shrink_matrices, expand_matrices, adapter_of_row, adapter_holder_slot
        )
    blocks = MOST // BLOCK
    adapter_ids = jnp.arange(group, dtype=jnp.int32)
    row_match = adapter_of_row[:, None] == adapter_ids[None, :]
    row_slot = jnp.sum(jnp.where(row_match, adapter_holder_slot[None, :], 0), axis=1)
    slot_mask = row_slot[None, :] == adapter_ids[:, None]
    before = jnp.cumsum(slot_mask.astype(jnp.int32), axis=1) - 1
    place = jnp.where(slot_mask, before, -1)
    pick = place[:, None, :] == jnp.arange(MOST, dtype=jnp.int32)[None, :, None]
    pick = pick.reshape(group * MOST, rows).astype(jnp.bfloat16)
    packed = jnp.dot(pick, hidden, preferred_element_type=jnp.float32).astype(jnp.bfloat16)
    packed = packed.reshape(group * blocks, BLOCK, depth)
    gathered = lax.all_to_all(packed, "tp", split_axis=0, concat_axis=0, tiled=True)
    partial_value = jnp.dot(hidden, down_matrix, preferred_element_type=jnp.float32)
    base = lax.psum_scatter(partial_value, "tp", scatter_dimension=1, tiled=True)
    own_rows = jnp.transpose(gathered.reshape(group, MOST, depth), (1, 0, 2))
    rank_rows = jnp.dot(
        own_rows.reshape(MOST, group * depth), shrink_matrices[0], preferred_element_type=jnp.float32
    ).astype(jnp.bfloat16)
    adapter_out = lax.dot_general(
        rank_rows, expand_matrices[0], (((1,), (1,)), ((), ())), preferred_element_type=jnp.float32
    ).astype(jnp.bfloat16)
    adapter_out = jnp.transpose(adapter_out.reshape(blocks, BLOCK, group, width), (2, 0, 1, 3))
    adapter_in = lax.all_to_all(
        adapter_out.reshape(group * blocks, BLOCK, width), "tp", split_axis=0, concat_axis=0, tiled=True
    )
    adapter_rows = lax.dot_general(
        pick,
        adapter_in.reshape(group * MOST, width),
        (((0,), (0,)), ((), ())),
        preferred_element_type=jnp.float32,
    )
    return (base + ADAPTER_SCALE * adapter_rows).astype(jnp.bfloat16)


def solution(mesh):
    in_specs = (
        P("rep", "tp"),
        P("tp", None),
        P(("rep", "tp"), None, None),
        P(("rep", "tp"), None, None),
        P("rep"),
        P("rep"),
    )
    out_specs = P("rep", "tp")
    return jax.shard_map(shards, mesh=mesh, in_specs=in_specs, out_specs=out_specs, check_vma=False)
```

```python
import functools

import jax
import jax.numpy as jnp
from jax import lax
from jax.experimental import pallas as pl
from jax.experimental.pallas import tpu as pltpu
from jax.sharding import PartitionSpec as P

ADAPTER_SCALE = 0.5
BLOCK = 4
MOST = 20
LANES = 128
F16_TOP = 14.0
PLANE = 4
HELD = 24
MARK_ROWS = 16


def in_hbm(value):
    return pltpu.with_memory_space_constraint(value, pltpu.HBM)


def xor_permute(value, group, offset):
    return lax.ppermute(value, "tp", [(i, i ^ offset) for i in range(group)])


def column_blocks_kernel(groups, order_ref, hidden_ref, down_ref, *refs):
    out_refs, held_ref, sems = refs[:groups], refs[groups], refs[groups + 1]
    count, depth, width = held_ref.shape
    parts = width // LANES
    pieces = sems.shape[1]
    cut = depth // pieces

    def copy(block, piece):
        start = pl.multiple_of(order_ref[block] * width, LANES)
        lines = pl.ds(piece * cut, cut)
        return pltpu.make_async_copy(
            down_ref.at[lines, pl.ds(start, width)], held_ref.at[block, lines], sems.at[block, piece]
        )

    for block in range(count):
        for piece in range(pieces):
            copy(block, piece).start()
    share = count // groups
    for block in range(count):
        for piece in range(pieces):
            copy(block, piece).wait()
        product = jnp.dot(hidden_ref[...], held_ref[block], preferred_element_type=jnp.float32)
        for lane in range(parts):
            out_refs[block // share][block % share * parts + lane] = product[
                :, lane * LANES : (lane + 1) * LANES
            ]


def column_blocks(hidden, down_matrix, order, width, groups=1):
    rows, depth = hidden.shape
    count = order.shape[0]
    pieces = 2 if depth % 32 == 0 else 1
    vmem = pl.BlockSpec(memory_space=pltpu.VMEM)
    out = jax.ShapeDtypeStruct((count // groups * width // LANES, rows, LANES), jnp.float32)
    return pl.pallas_call(
        functools.partial(column_blocks_kernel, groups),
        out_shape=[out] * groups,
        in_specs=[
            pl.BlockSpec(memory_space=pltpu.SMEM),
            vmem,
            pl.BlockSpec(memory_space=pl.ANY),
        ],
        out_specs=[vmem] * groups,
        scratch_shapes=[
            pltpu.VMEM((count, depth, width), jnp.bfloat16),
            pltpu.SemaphoreType.DMA((count, pieces)),
        ],
        compiler_params=pltpu.CompilerParams(vmem_limit_bytes=(12 + 12 * groups) * 2**20),
        cost_estimate=pl.CostEstimate(flops=1000, bytes_accessed=1000, transcendentals=0),
    )(order, hidden, in_hbm(down_matrix))


def pack_scaled(value):
    blocks, rows, lanes = value.shape
    peak = jnp.max(jnp.abs(value), axis=(0, 2))
    exponent = jnp.ceil(jnp.log2(jnp.maximum(peak, 2.0**-100)))
    scaled = (value * jnp.exp2(F16_TOP - exponent)[None, :, None]).astype(jnp.float16)
    marks = jnp.pad(exponent.astype(jnp.float16)[None], ((0, MARK_ROWS - 1), (0, lanes - rows)))
    return jnp.concatenate([scaled.reshape(blocks * rows, lanes), marks], axis=0)


def unpack_scaled(packed, rows):
    values, exponent = packed[:-MARK_ROWS], packed[-MARK_ROWS, :rows].astype(jnp.float32)
    values = values.reshape(-1, rows, packed.shape[1]).astype(jnp.float32)
    return values * jnp.exp2(exponent - F16_TOP)[None, :, None]


def pair_sums(hidden, down_matrix, group, order, width):
    half = group * width // LANES // PLANE
    rows = hidden.shape[0]
    share = group // PLANE

    def first():
        (far,) = column_blocks(hidden, down_matrix, order[:share], width)
        far_in = xor_permute(far, group, 1)
        (near,) = column_blocks(hidden, down_matrix, order[share : 2 * share], width)
        return pack_scaled(near + far_in)

    def first_idle():
        return jnp.zeros((half * rows + MARK_ROWS, LANES), jnp.float16)

    sent = lax.cond(order[0] >= 0, first, first_idle)
    pair_in = xor_permute(sent, group, 2)
    order, _ = lax.optimization_barrier((order, sent))

    def second():
        far, near = column_blocks(hidden, down_matrix, order[2 * share :], width, groups=2)
        return near + xor_permute(far, group, 1)

    def second_idle():
        return jnp.zeros((half, rows, LANES), jnp.float32)

    kept = lax.cond(order[1] >= 0, second, second_idle)
    return kept, pair_in


def line_sums(pair, group, width):
    rows = pair.shape[1]
    parts = width // LANES
    arrived = [
        xor_permute(pack_scaled(pair[i * parts : (i + 1) * parts]), group, 4 * i)
        for i in range(1, group // 4)
    ]
    total = pair[:parts]
    for packed in arrived:
        total = total + unpack_scaled(packed, rows)
    return jnp.transpose(total, (1, 0, 2)).reshape(rows, width)


def pack_kernel(
    blocks,
    orders,
    me_ref,
    slot_hbm,
    adapter_hbm,
    hidden_hbm,
    packed_ref,
    pick_ref,
    order_ref,
    kept_ref,
    slot_ref,
    adapter_ref,
    hidden_ref,
    sems,
):
    rows = hidden_ref.shape[0]
    group = slot_ref.shape[0]
    copies = [
        pltpu.make_async_copy(slot_hbm, slot_ref, sems.at[0]),
        pltpu.make_async_copy(adapter_hbm, adapter_ref, sems.at[1]),
        pltpu.make_async_copy(hidden_hbm, hidden_ref, sems.at[2]),
    ]
    for copy in copies:
        copy.start()
    for i, offset in enumerate(orders):
        order_ref[i] = me_ref[0] ^ offset
    ids = lax.broadcasted_iota(jnp.int32, (group, 1), 0)
    slots = jnp.zeros((group, 1), jnp.int32)
    copies[0].wait()
    for adapter in range(group):
        slots = jnp.where(ids == adapter, slot_ref[adapter], slots)
    copies[1].wait()
    adapter = adapter_ref[...]
    first = jnp.sum((adapter < ids).astype(jnp.int32), axis=1, keepdims=True)
    shift = jnp.where(adapter == ids, slots * (blocks * BLOCK) - first, 0)
    place = jnp.sum(shift, axis=0, keepdims=True) + lax.broadcasted_iota(jnp.int32, (1, rows), 1)
    spots = lax.broadcasted_iota(jnp.int32, (group * blocks * BLOCK, rows), 0)
    pick = jnp.where(spots == place, 1.0, 0.0).astype(jnp.bfloat16)
    for k in range(PLANE):
        line = lax.broadcasted_iota(jnp.int32, (HELD, rows), 0)
        mine = (line + (me_ref[0] ^ k) * (blocks * BLOCK) == place) & (line < blocks * BLOCK)
        pick_ref[k * HELD : (k + 1) * HELD] = jnp.where(mine, 1.0, 0.0).astype(jnp.bfloat16)
    copies[2].wait()
    packed = jnp.dot(pick, hidden_ref[...], preferred_element_type=jnp.float32)
    packed_ref[...] = packed.astype(jnp.bfloat16).reshape(packed_ref.shape)
    kept_ref[...] = hidden_ref[...]


def pack_rows(hidden, adapter_of_row, adapter_holder_slot, me, orders):
    rows, depth = hidden.shape
    group = adapter_holder_slot.shape[0]
    blocks = MOST // BLOCK
    vmem = pl.BlockSpec(memory_space=pltpu.VMEM)
    smem = pl.BlockSpec(memory_space=pltpu.SMEM)
    anywhere = pl.BlockSpec(memory_space=pltpu.HBM)
    return pl.pallas_call(
        functools.partial(pack_kernel, blocks, orders),
        out_shape=(
            jax.ShapeDtypeStruct((group * blocks, BLOCK, depth), jnp.bfloat16),
            jax.ShapeDtypeStruct((PLANE * HELD, rows), jnp.bfloat16),
            jax.ShapeDtypeStruct((len(orders),), jnp.int32),
            jax.ShapeDtypeStruct((rows, depth), jnp.bfloat16),
        ),
        in_specs=[smem, anywhere, anywhere, anywhere],
        out_specs=(vmem, vmem, smem, vmem),
        scratch_shapes=[
            pltpu.SMEM((group,), jnp.int32),
            pltpu.VMEM((1, rows), jnp.int32),
            pltpu.VMEM((rows, depth), jnp.bfloat16),
            pltpu.SemaphoreType.DMA((3,)),
        ],
        compiler_params=pltpu.CompilerParams(vmem_limit_bytes=24 * 2**20),
    )(me.reshape(1), in_hbm(adapter_holder_slot), in_hbm(adapter_of_row.reshape(1, rows)), in_hbm(hidden))


def adapter_kernel(parts, me_ref, rows_ref, expand_hbm, shrink_hbm, *refs):
    out_refs = refs[:PLANE]
    shrink_ref, expand_ref, total_ref, sems, expand_sem = refs[PLANE:]
    me = me_ref[0]
    group, _, depth = shrink_ref.shape
    blocks = MOST // BLOCK

    def copy(source):
        return pltpu.make_async_copy(
            shrink_hbm.at[:, pl.ds(source * depth, depth)], shrink_ref.at[source], sems.at[source]
        )

    for source in range(group):
        copy(source).start()
    expand_copy = pltpu.make_async_copy(expand_hbm, expand_ref, expand_sem)
    expand_copy.start()
    total = jnp.zeros((MOST, total_ref.shape[1]), jnp.float32)
    for source in range(group):
        copy(source).wait()
        own = rows_ref[source * blocks : (source + 1) * blocks].reshape(MOST, depth)
        total += lax.dot_general(
            own, shrink_ref[source], (((1,), (1,)), ((), ())), preferred_element_type=jnp.float32
        )
    total_ref[...] = jnp.zeros_like(total_ref)
    total_ref[:MOST] = total
    rank_rows = total_ref[...].astype(jnp.bfloat16)
    expand_copy.wait()
    width = parts * LANES
    for k in range(PLANE):
        for line in range(group // PLANE):
            target = me ^ (PLANE * line + k)
            columns = pl.ds(pl.multiple_of(target * width, LANES), width)
            piece = jnp.dot(rank_rows, expand_ref[:, columns], preferred_element_type=jnp.float32)
            piece = piece.astype(jnp.bfloat16)
            for part in range(parts):
                out_refs[k][line * parts + part] = piece[:, part * LANES : (part + 1) * LANES]


def adapter_output(gathered, shrink, expand, group, me):
    rank = shrink.shape[0]
    model_width = expand.shape[1]
    depth = gathered.shape[2]
    parts = model_width // group // LANES
    held = (model_width // PLANE // LANES, HELD, LANES)
    vmem = pl.BlockSpec(memory_space=pltpu.VMEM)
    return pl.pallas_call(
        functools.partial(adapter_kernel, parts),
        out_shape=[jax.ShapeDtypeStruct(held, jnp.bfloat16)] * PLANE,
        in_specs=[
            pl.BlockSpec(memory_space=pltpu.SMEM),
            vmem,
            pl.BlockSpec(memory_space=pl.ANY),
            pl.BlockSpec(memory_space=pl.ANY),
        ],
        out_specs=[vmem] * PLANE,
        scratch_shapes=[
            pltpu.VMEM((group, rank, depth), jnp.bfloat16),
            pltpu.VMEM((rank, model_width), jnp.bfloat16),
            pltpu.VMEM((HELD, rank), jnp.float32),
            pltpu.SemaphoreType.DMA((group,)),
            pltpu.SemaphoreType.DMA,
        ],
        compiler_params=pltpu.CompilerParams(vmem_limit_bytes=24 * 2**20),
    )(me.reshape(1), gathered, in_hbm(expand), in_hbm(shrink))


def merge_kernel(pair_ref, pick_ref, *refs):
    in_refs, out_ref, held_ref = refs[:PLANE], refs[PLANE], refs[PLANE + 1]
    for k in range(PLANE):
        held_ref[:, k * HELD : (k + 1) * HELD] = in_refs[k][...]
    pick = pick_ref[...]
    for part in range(pair_ref.shape[0]):
        adapter_rows = lax.dot_general(
            pick, held_ref[part], (((0,), (0,)), ((), ())), preferred_element_type=jnp.float32
        )
        out_ref[part] = pair_ref[part] + ADAPTER_SCALE * adapter_rows


def merge_adapters(pair, pick, arrived):
    vmem = pl.BlockSpec(memory_space=pltpu.VMEM)
    return pl.pallas_call(
        merge_kernel,
        out_shape=jax.ShapeDtypeStruct(pair.shape, jnp.float32),
        in_specs=[vmem] * (2 + PLANE),
        out_specs=vmem,
        scratch_shapes=[pltpu.VMEM((pair.shape[0], PLANE * HELD, LANES), jnp.bfloat16)],
        compiler_params=pltpu.CompilerParams(vmem_limit_bytes=24 * 2**20),
    )(pair, pick, *arrived)


def shards_by_blocks(
    hidden, down_matrix, shrink_matrices, expand_matrices, adapter_of_row, adapter_holder_slot
):
    group = lax.axis_size("tp")
    me = lax.axis_index("tp")
    rows, depth = hidden.shape
    width = down_matrix.shape[1] // group
    quads = list(range(0, group, 4))
    orders = [q + k for k in (3, 2, 1, 0) for q in quads]
    packed, pick, order, kept_hidden = pack_rows(
        hidden, adapter_of_row, adapter_holder_slot, me, orders
    )
    gathered = lax.all_to_all(packed, "tp", split_axis=0, concat_axis=0, tiled=True)
    shrink = jnp.swapaxes(shrink_matrices, 1, 2)[0]
    kept, pair_in = pair_sums(kept_hidden, down_matrix, group, order, width)
    gathered, _ = lax.optimization_barrier((gathered, kept))
    expand = jnp.swapaxes(expand_matrices, 1, 2)[0]
    outs = adapter_output(gathered, shrink, expand, group, me)
    arrived = [outs[0]] + [xor_permute(outs[k], group, k) for k in range(1, PLANE)]
    pair = kept + unpack_scaled(pair_in, rows)
    merged = merge_adapters(pair, pick, arrived)
    return line_sums(merged, group, width).astype(jnp.bfloat16)


def shards(
    hidden, down_matrix, shrink_matrices, expand_matrices, adapter_of_row, adapter_holder_slot
):
    group = lax.axis_size("tp")
    rows, depth = hidden.shape
    width = down_matrix.shape[1] // group
    if width % LANES == 0 and depth % LANES == 0 and rows <= LANES and group >= PLANE and group & (group - 1) == 0:
        return shards_by_blocks(
            hidden, down_matrix, shrink_matrices, expand_matrices, adapter_of_row, adapter_holder_slot
        )
    blocks = MOST // BLOCK
    adapter_ids = jnp.arange(group, dtype=jnp.int32)
    row_match = adapter_of_row[:, None] == adapter_ids[None, :]
    row_slot = jnp.sum(jnp.where(row_match, adapter_holder_slot[None, :], 0), axis=1)
    slot_mask = row_slot[None, :] == adapter_ids[:, None]
    before = jnp.cumsum(slot_mask.astype(jnp.int32), axis=1) - 1
    place = jnp.where(slot_mask, before, -1)
    pick = place[:, None, :] == jnp.arange(MOST, dtype=jnp.int32)[None, :, None]
    pick = pick.reshape(group * MOST, rows).astype(jnp.bfloat16)
    packed = jnp.dot(pick, hidden, preferred_element_type=jnp.float32).astype(jnp.bfloat16)
    packed = packed.reshape(group * blocks, BLOCK, depth)
    gathered = lax.all_to_all(packed, "tp", split_axis=0, concat_axis=0, tiled=True)
    partial_value = jnp.dot(hidden, down_matrix, preferred_element_type=jnp.float32)
    base = lax.psum_scatter(partial_value, "tp", scatter_dimension=1, tiled=True)
    own_rows = jnp.transpose(gathered.reshape(group, MOST, depth), (1, 0, 2))
    rank_rows = jnp.dot(
        own_rows.reshape(MOST, group * depth), shrink_matrices[0], preferred_element_type=jnp.float32
    ).astype(jnp.bfloat16)
    adapter_out = lax.dot_general(
        rank_rows, expand_matrices[0], (((1,), (1,)), ((), ())), preferred_element_type=jnp.float32
    ).astype(jnp.bfloat16)
    adapter_out = jnp.transpose(adapter_out.reshape(blocks, BLOCK, group, width), (2, 0, 1, 3))
    adapter_in = lax.all_to_all(
        adapter_out.reshape(group * blocks, BLOCK, width), "tp", split_axis=0, concat_axis=0, tiled=True
    )
    adapter_rows = lax.dot_general(
        pick,
        adapter_in.reshape(group * MOST, width),
        (((0,), (0,)), ((), ())),
        preferred_element_type=jnp.float32,
    )
    return (base + ADAPTER_SCALE * adapter_rows).astype(jnp.bfloat16)


def solution(mesh):
    in_specs = (
        P("rep", "tp"),
        P("tp", None),
        P(("rep", "tp"), None, None),
        P(("rep", "tp"), None, None),
        P("rep"),
        P("rep"),
    )
    out_specs = P("rep", "tp")
    return jax.shard_map(shards, mesh=mesh, in_specs=in_specs, out_specs=out_specs, check_vma=False)
```

```python
import functools

import jax
import jax.numpy as jnp
from jax import lax
from jax.experimental import pallas as pl
from jax.experimental.pallas import tpu as pltpu
from jax.sharding import PartitionSpec as P

ADAPTER_SCALE = 0.5
BLOCK = 4
MOST = 20
LANES = 128
F16_TOP = 14.0
PLANE = 4
MARK_ROWS = 16


def in_hbm(value):
    return pltpu.with_memory_space_constraint(value, pltpu.HBM)


def xor_permute(value, group, offset):
    return lax.ppermute(value, "tp", [(i, i ^ offset) for i in range(group)])


def column_blocks_kernel(groups, order_ref, hidden_ref, down_ref, *refs):
    out_refs, held_ref, sems = refs[:groups], refs[groups], refs[groups + 1]
    count, depth, width = held_ref.shape
    parts = width // LANES
    pieces = sems.shape[1]
    cut = depth // pieces

    def copy(block, piece):
        start = pl.multiple_of(order_ref[block] * width, LANES)
        lines = pl.ds(piece * cut, cut)
        return pltpu.make_async_copy(
            down_ref.at[lines, pl.ds(start, width)], held_ref.at[block, lines], sems.at[block, piece]
        )

    for block in range(count):
        for piece in range(pieces):
            copy(block, piece).start()
    share = count // groups
    for block in range(count):
        for piece in range(pieces):
            copy(block, piece).wait()
        product = jnp.dot(hidden_ref[...], held_ref[block], preferred_element_type=jnp.float32)
        for lane in range(parts):
            out_refs[block // share][block % share * parts + lane] = product[
                :, lane * LANES : (lane + 1) * LANES
            ]


def column_blocks(hidden, down_matrix, order, width, groups=1):
    rows, depth = hidden.shape
    count = order.shape[0]
    pieces = 2 if depth % 32 == 0 else 1
    vmem = pl.BlockSpec(memory_space=pltpu.VMEM)
    out = jax.ShapeDtypeStruct((count // groups * width // LANES, rows, LANES), jnp.float32)
    return pl.pallas_call(
        functools.partial(column_blocks_kernel, groups),
        out_shape=[out] * groups,
        in_specs=[
            pl.BlockSpec(memory_space=pltpu.SMEM),
            vmem,
            pl.BlockSpec(memory_space=pl.ANY),
        ],
        out_specs=[vmem] * groups,
        scratch_shapes=[
            pltpu.VMEM((count, depth, width), jnp.bfloat16),
            pltpu.SemaphoreType.DMA((count, pieces)),
        ],
        compiler_params=pltpu.CompilerParams(vmem_limit_bytes=(12 + 12 * groups) * 2**20),
        cost_estimate=pl.CostEstimate(flops=1000, bytes_accessed=1000, transcendentals=0),
    )(order, hidden, in_hbm(down_matrix))


def pack_scaled(value):
    blocks, rows, lanes = value.shape
    peak = jnp.max(jnp.abs(value), axis=(0, 2))
    exponent = jnp.ceil(jnp.log2(jnp.maximum(peak, 2.0**-100)))
    scaled = (value * jnp.exp2(F16_TOP - exponent)[None, :, None]).astype(jnp.float16)
    marks = jnp.pad(exponent.astype(jnp.float16)[None], ((0, MARK_ROWS - 1), (0, lanes - rows)))
    return jnp.concatenate([scaled.reshape(blocks * rows, lanes), marks], axis=0)


def unpack_scaled(packed, rows):
    values, exponent = packed[:-MARK_ROWS], packed[-MARK_ROWS, :rows].astype(jnp.float32)
    values = values.reshape(-1, rows, packed.shape[1]).astype(jnp.float32)
    return values * jnp.exp2(exponent - F16_TOP)[None, :, None]


def pair_sums(hidden, down_matrix, group, order, width):
    half = group * width // LANES // PLANE
    rows = hidden.shape[0]
    share = group // PLANE

    def first():
        (far,) = column_blocks(hidden, down_matrix, order[:share], width)
        far_in = xor_permute(far, group, 1)
        (near,) = column_blocks(hidden, down_matrix, order[share : 2 * share], width)
        return pack_scaled(near + far_in)

    def first_idle():
        return jnp.zeros((half * rows + MARK_ROWS, LANES), jnp.float16)

    sent = lax.cond(order[0] >= 0, first, first_idle)
    pair_in = xor_permute(sent, group, 2)
    order, _ = lax.optimization_barrier((order, sent))

    def second():
        far, near = column_blocks(hidden, down_matrix, order[2 * share :], width, groups=2)
        return near + xor_permute(far, group, 1)

    def second_idle():
        return jnp.zeros((half, rows, LANES), jnp.float32)

    kept = lax.cond(order[1] >= 0, second, second_idle)
    return kept, pair_in


def line_sums(kept, pair_in, flag, group, width):
    rows = kept.shape[1]
    parts = width // LANES

    def work():
        pair = kept + unpack_scaled(pair_in, rows)
        arrived = [
            xor_permute(pack_scaled(pair[i * parts : (i + 1) * parts]), group, PLANE * i)
            for i in range(1, group // PLANE)
        ]
        total = pair[:parts]
        for packed in arrived:
            total = total + unpack_scaled(packed, rows)
        return total

    def idle():
        return jnp.zeros((parts, rows, LANES), jnp.float32)

    return lax.cond(flag >= 0, work, idle)


def pack_kernel(
    blocks,
    orders,
    me_ref,
    slot_hbm,
    adapter_hbm,
    hidden_hbm,
    packed_ref,
    pick_ref,
    order_ref,
    kept_ref,
    slot_ref,
    adapter_ref,
    hidden_ref,
    sems,
):
    rows = hidden_ref.shape[0]
    group = slot_ref.shape[0]
    copies = [
        pltpu.make_async_copy(slot_hbm, slot_ref, sems.at[0]),
        pltpu.make_async_copy(adapter_hbm, adapter_ref, sems.at[1]),
        pltpu.make_async_copy(hidden_hbm, hidden_ref, sems.at[2]),
    ]
    for copy in copies:
        copy.start()
    for i, offset in enumerate(orders):
        order_ref[i] = me_ref[0] ^ offset
    ids = lax.broadcasted_iota(jnp.int32, (group, 1), 0)
    slots = jnp.zeros((group, 1), jnp.int32)
    copies[0].wait()
    for adapter in range(group):
        slots = jnp.where(ids == adapter, slot_ref[adapter], slots)
    copies[1].wait()
    adapter = adapter_ref[...]
    first = jnp.sum((adapter < ids).astype(jnp.int32), axis=1, keepdims=True)
    shift = jnp.where(adapter == ids, slots * (blocks * BLOCK) - first, 0)
    place = jnp.sum(shift, axis=0, keepdims=True) + lax.broadcasted_iota(jnp.int32, (1, rows), 1)
    spots = lax.broadcasted_iota(jnp.int32, (group * blocks * BLOCK, rows), 0)
    pick = jnp.where(spots == place, 1.0, 0.0).astype(jnp.bfloat16)
    pick_ref[...] = pick
    copies[2].wait()
    packed = jnp.dot(pick, hidden_ref[...], preferred_element_type=jnp.float32)
    packed_ref[...] = packed.astype(jnp.bfloat16).reshape(packed_ref.shape)
    kept_ref[...] = hidden_ref[...]


def pack_rows(hidden, adapter_of_row, adapter_holder_slot, me, orders):
    rows, depth = hidden.shape
    group = adapter_holder_slot.shape[0]
    blocks = MOST // BLOCK
    vmem = pl.BlockSpec(memory_space=pltpu.VMEM)
    smem = pl.BlockSpec(memory_space=pltpu.SMEM)
    anywhere = pl.BlockSpec(memory_space=pltpu.HBM)
    return pl.pallas_call(
        functools.partial(pack_kernel, blocks, orders),
        out_shape=(
            jax.ShapeDtypeStruct((group * blocks, BLOCK, depth), jnp.bfloat16),
            jax.ShapeDtypeStruct((group * MOST, rows), jnp.bfloat16),
            jax.ShapeDtypeStruct((len(orders),), jnp.int32),
            jax.ShapeDtypeStruct((rows, depth), jnp.bfloat16),
        ),
        in_specs=[smem, anywhere, anywhere, anywhere],
        out_specs=(vmem, vmem, smem, vmem),
        scratch_shapes=[
            pltpu.SMEM((group,), jnp.int32),
            pltpu.VMEM((1, rows), jnp.int32),
            pltpu.VMEM((rows, depth), jnp.bfloat16),
            pltpu.SemaphoreType.DMA((3,)),
        ],
        compiler_params=pltpu.CompilerParams(vmem_limit_bytes=24 * 2**20),
    )(me.reshape(1), in_hbm(adapter_holder_slot), in_hbm(adapter_of_row.reshape(1, rows)), in_hbm(hidden))


def adapter_kernel(rows_ref, expand_hbm, shrink_hbm, out_ref, flag_ref, *refs):
    shrink_ref, expand_ref, sems, expand_sem = refs
    group, _, depth = shrink_ref.shape
    blocks = MOST // BLOCK
    width = out_ref.shape[2]
    flag_ref[0] = group

    def copy(source):
        return pltpu.make_async_copy(
            shrink_hbm.at[:, pl.ds(source * depth, depth)], shrink_ref.at[source], sems.at[source]
        )

    for source in range(group):
        copy(source).start()
    expand_copy = pltpu.make_async_copy(expand_hbm, expand_ref, expand_sem)
    expand_copy.start()
    total = jnp.zeros((MOST, shrink_ref.shape[1]), jnp.float32)
    for source in range(group):
        copy(source).wait()
        own = rows_ref[source * blocks : (source + 1) * blocks].reshape(MOST, depth)
        total += lax.dot_general(
            own, shrink_ref[source], (((1,), (1,)), ((), ())), preferred_element_type=jnp.float32
        )
    rank_rows = total.astype(jnp.bfloat16)
    expand_copy.wait()
    for target in range(group):
        piece = jnp.dot(
            rank_rows,
            expand_ref[:, target * width : (target + 1) * width],
            preferred_element_type=jnp.float32,
        )
        out_ref[target * blocks : (target + 1) * blocks] = piece.astype(jnp.bfloat16).reshape(
            blocks, BLOCK, width
        )


def adapter_output(gathered, shrink, expand, group):
    rank = shrink.shape[0]
    model_width = expand.shape[1]
    depth = gathered.shape[2]
    vmem = pl.BlockSpec(memory_space=pltpu.VMEM)
    return pl.pallas_call(
        adapter_kernel,
        out_shape=[
            jax.ShapeDtypeStruct((gathered.shape[0], BLOCK, model_width // group), jnp.bfloat16),
            jax.ShapeDtypeStruct((1,), jnp.int32),
        ],
        in_specs=[vmem, pl.BlockSpec(memory_space=pl.ANY), pl.BlockSpec(memory_space=pl.ANY)],
        out_specs=[vmem, pl.BlockSpec(memory_space=pltpu.SMEM)],
        scratch_shapes=[
            pltpu.VMEM((group, rank, depth), jnp.bfloat16),
            pltpu.VMEM((rank, model_width), jnp.bfloat16),
            pltpu.SemaphoreType.DMA((group,)),
            pltpu.SemaphoreType.DMA,
        ],
        compiler_params=pltpu.CompilerParams(vmem_limit_bytes=24 * 2**20),
    )(gathered, in_hbm(expand), in_hbm(shrink))


def final_kernel(base_ref, pick_ref, rows_ref, out_ref):
    adapter_rows = lax.dot_general(
        pick_ref[...],
        rows_ref[...].reshape(pick_ref.shape[0], out_ref.shape[1]),
        (((0,), (0,)), ((), ())),
        preferred_element_type=jnp.float32,
    )
    for part in range(base_ref.shape[0]):
        lanes = slice(part * LANES, (part + 1) * LANES)
        total = base_ref[part] + ADAPTER_SCALE * adapter_rows[:, lanes]
        out_ref[:, lanes] = total.astype(out_ref.dtype)


def add_adapters(base, pick, arrived):
    parts, rows, _ = base.shape
    vmem = pl.BlockSpec(memory_space=pltpu.VMEM)
    return pl.pallas_call(
        final_kernel,
        out_shape=jax.ShapeDtypeStruct((rows, parts * LANES), jnp.bfloat16),
        in_specs=[vmem] * 3,
        out_specs=vmem,
        compiler_params=pltpu.CompilerParams(vmem_limit_bytes=24 * 2**20),
    )(base, pick, arrived)


def shards_by_blocks(
    hidden, down_matrix, shrink_matrices, expand_matrices, adapter_of_row, adapter_holder_slot
):
    group = lax.axis_size("tp")
    me = lax.axis_index("tp")
    rows, depth = hidden.shape
    width = down_matrix.shape[1] // group
    quads = list(range(0, group, 4))
    orders = [q + k for k in (3, 2, 1, 0) for q in quads]
    packed, pick, order, kept_hidden = pack_rows(
        hidden, adapter_of_row, adapter_holder_slot, me, orders
    )
    gathered = lax.all_to_all(packed, "tp", split_axis=0, concat_axis=0, tiled=True)
    shrink = jnp.swapaxes(shrink_matrices, 1, 2)[0]
    kept, pair_in = pair_sums(kept_hidden, down_matrix, group, order, width)
    gathered, _ = lax.optimization_barrier((gathered, kept))
    expand = jnp.swapaxes(expand_matrices, 1, 2)[0]
    adapter_out, flag = adapter_output(gathered, shrink, expand, group)
    arrived = lax.all_to_all(adapter_out, "tp", split_axis=0, concat_axis=0, tiled=True)
    base = line_sums(kept, pair_in, flag[0], group, width)
    return add_adapters(base, pick, arrived)


def shards(
    hidden, down_matrix, shrink_matrices, expand_matrices, adapter_of_row, adapter_holder_slot
):
    group = lax.axis_size("tp")
    rows, depth = hidden.shape
    width = down_matrix.shape[1] // group
    if width % LANES == 0 and depth % LANES == 0 and rows <= LANES and group >= PLANE and group & (group - 1) == 0:
        return shards_by_blocks(
            hidden, down_matrix, shrink_matrices, expand_matrices, adapter_of_row, adapter_holder_slot
        )
    blocks = MOST // BLOCK
    adapter_ids = jnp.arange(group, dtype=jnp.int32)
    row_match = adapter_of_row[:, None] == adapter_ids[None, :]
    row_slot = jnp.sum(jnp.where(row_match, adapter_holder_slot[None, :], 0), axis=1)
    slot_mask = row_slot[None, :] == adapter_ids[:, None]
    before = jnp.cumsum(slot_mask.astype(jnp.int32), axis=1) - 1
    place = jnp.where(slot_mask, before, -1)
    pick = place[:, None, :] == jnp.arange(MOST, dtype=jnp.int32)[None, :, None]
    pick = pick.reshape(group * MOST, rows).astype(jnp.bfloat16)
    packed = jnp.dot(pick, hidden, preferred_element_type=jnp.float32).astype(jnp.bfloat16)
    packed = packed.reshape(group * blocks, BLOCK, depth)
    gathered = lax.all_to_all(packed, "tp", split_axis=0, concat_axis=0, tiled=True)
    partial_value = jnp.dot(hidden, down_matrix, preferred_element_type=jnp.float32)
    base = lax.psum_scatter(partial_value, "tp", scatter_dimension=1, tiled=True)
    own_rows = jnp.transpose(gathered.reshape(group, MOST, depth), (1, 0, 2))
    rank_rows = jnp.dot(
        own_rows.reshape(MOST, group * depth), shrink_matrices[0], preferred_element_type=jnp.float32
    ).astype(jnp.bfloat16)
    adapter_out = lax.dot_general(
        rank_rows, expand_matrices[0], (((1,), (1,)), ((), ())), preferred_element_type=jnp.float32
    ).astype(jnp.bfloat16)
    adapter_out = jnp.transpose(adapter_out.reshape(blocks, BLOCK, group, width), (2, 0, 1, 3))
    adapter_in = lax.all_to_all(
        adapter_out.reshape(group * blocks, BLOCK, width), "tp", split_axis=0, concat_axis=0, tiled=True
    )
    adapter_rows = lax.dot_general(
        pick,
        adapter_in.reshape(group * MOST, width),
        (((0,), (0,)), ((), ())),
        preferred_element_type=jnp.float32,
    )
    return (base + ADAPTER_SCALE * adapter_rows).astype(jnp.bfloat16)


def solution(mesh):
    in_specs = (
        P("rep", "tp"),
        P("tp", None),
        P(("rep", "tp"), None, None),
        P(("rep", "tp"), None, None),
        P("rep"),
        P("rep"),
    )
    out_specs = P("rep", "tp")
    return jax.shard_map(shards, mesh=mesh, in_specs=in_specs, out_specs=out_specs, check_vma=False)
```

```python
import functools

import jax
import jax.numpy as jnp
from jax import lax
from jax.experimental import pallas as pl
from jax.experimental.pallas import tpu as pltpu
from jax.sharding import PartitionSpec as P

ADAPTER_SCALE = 0.5
BLOCK = 4
MOST = 20
LANES = 128
F16_TOP = 14.0
PLANE = 4
MARK_ROWS = 16


def in_hbm(value):
    return pltpu.with_memory_space_constraint(value, pltpu.HBM)


def xor_permute(value, group, offset):
    return lax.ppermute(value, "tp", [(i, i ^ offset) for i in range(group)])


def column_blocks_kernel(groups, order_ref, hidden_ref, down_ref, *refs):
    out_refs, held_ref, sems = refs[:groups], refs[groups], refs[groups + 1]
    count, depth, width = held_ref.shape
    parts = width // LANES
    pieces = sems.shape[1]
    cut = depth // pieces

    def copy(block, piece):
        start = pl.multiple_of(order_ref[block] * width, LANES)
        lines = pl.ds(piece * cut, cut)
        return pltpu.make_async_copy(
            down_ref.at[lines, pl.ds(start, width)], held_ref.at[block, lines], sems.at[block, piece]
        )

    for block in range(count):
        for piece in range(pieces):
            copy(block, piece).start()
    share = count // groups
    for block in range(count):
        for piece in range(pieces):
            copy(block, piece).wait()
        product = jnp.dot(hidden_ref[...], held_ref[block], preferred_element_type=jnp.float32)
        for lane in range(parts):
            out_refs[block // share][block % share * parts + lane] = product[
                :, lane * LANES : (lane + 1) * LANES
            ]


def column_blocks(hidden, down_matrix, order, width, groups=1):
    rows, depth = hidden.shape
    count = order.shape[0]
    pieces = 2 if depth % 32 == 0 else 1
    vmem = pl.BlockSpec(memory_space=pltpu.VMEM)
    out = jax.ShapeDtypeStruct((count // groups * width // LANES, rows, LANES), jnp.float32)
    return pl.pallas_call(
        functools.partial(column_blocks_kernel, groups),
        out_shape=[out] * groups,
        in_specs=[
            pl.BlockSpec(memory_space=pltpu.SMEM),
            vmem,
            pl.BlockSpec(memory_space=pl.ANY),
        ],
        out_specs=[vmem] * groups,
        scratch_shapes=[
            pltpu.VMEM((count, depth, width), jnp.bfloat16),
            pltpu.SemaphoreType.DMA((count, pieces)),
        ],
        compiler_params=pltpu.CompilerParams(vmem_limit_bytes=(12 + 12 * groups) * 2**20),
        cost_estimate=pl.CostEstimate(flops=1000, bytes_accessed=1000, transcendentals=0),
    )(order, hidden, in_hbm(down_matrix))


def pack_scaled(value):
    blocks, rows, lanes = value.shape
    peak = jnp.max(jnp.abs(value), axis=(0, 2))
    exponent = jnp.ceil(jnp.log2(jnp.maximum(peak, 2.0**-100)))
    scaled = (value * jnp.exp2(F16_TOP - exponent)[None, :, None]).astype(jnp.float16)
    marks = jnp.pad(exponent.astype(jnp.float16)[None], ((0, MARK_ROWS - 1), (0, lanes - rows)))
    return jnp.concatenate([scaled.reshape(blocks * rows, lanes), marks], axis=0)


def unpack_scaled(packed, rows):
    values, exponent = packed[:-MARK_ROWS], packed[-MARK_ROWS, :rows].astype(jnp.float32)
    values = values.reshape(-1, rows, packed.shape[1]).astype(jnp.float32)
    return values * jnp.exp2(exponent - F16_TOP)[None, :, None]


def pair_sums(hidden, down_matrix, group, order, width):
    half = group * width // LANES // PLANE
    rows = hidden.shape[0]
    share = group // PLANE

    def first():
        (far,) = column_blocks(hidden, down_matrix, order[:share], width)
        far_in = xor_permute(far, group, 1)
        (near,) = column_blocks(hidden, down_matrix, order[share : 2 * share], width)
        return pack_scaled(near + far_in)

    def first_idle():
        return jnp.zeros((half * rows + MARK_ROWS, LANES), jnp.float16)

    sent = lax.cond(order[0] >= 0, first, first_idle)
    pair_in = xor_permute(sent, group, 2)
    order, _ = lax.optimization_barrier((order, sent))

    def second():
        far, near = column_blocks(hidden, down_matrix, order[2 * share :], width, groups=2)
        return near + xor_permute(far, group, 1)

    def second_idle():
        return jnp.zeros((half, rows, LANES), jnp.float32)

    kept = lax.cond(order[1] >= 0, second, second_idle)
    return kept, pair_in


def line_sums(kept, pair_in, flag, group, width):
    rows = kept.shape[1]
    parts = width // LANES

    def work():
        pair = kept + unpack_scaled(pair_in, rows)
        arrived = [
            xor_permute(pack_scaled(pair[i * parts : (i + 1) * parts]), group, PLANE * i)
            for i in range(1, group // PLANE)
        ]
        total = pair[:parts]
        for packed in arrived:
            total = total + unpack_scaled(packed, rows)
        return total

    def idle():
        return jnp.zeros((parts, rows, LANES), jnp.float32)

    return lax.cond(flag >= 0, work, idle)


def pack_kernel(
    blocks,
    orders,
    me_ref,
    slot_hbm,
    adapter_hbm,
    hidden_hbm,
    packed_ref,
    pick_ref,
    order_ref,
    kept_ref,
    slot_ref,
    adapter_ref,
    hidden_ref,
    sems,
):
    rows = hidden_ref.shape[0]
    group = slot_ref.shape[0]
    copies = [
        pltpu.make_async_copy(slot_hbm, slot_ref, sems.at[0]),
        pltpu.make_async_copy(adapter_hbm, adapter_ref, sems.at[1]),
        pltpu.make_async_copy(hidden_hbm, hidden_ref, sems.at[2]),
    ]
    for copy in copies:
        copy.start()
    for i, offset in enumerate(orders):
        order_ref[i] = me_ref[0] ^ offset
    ids = lax.broadcasted_iota(jnp.int32, (group, 1), 0)
    slots = jnp.zeros((group, 1), jnp.int32)
    copies[0].wait()
    for adapter in range(group):
        slots = jnp.where(ids == adapter, slot_ref[adapter], slots)
    copies[1].wait()
    adapter = adapter_ref[...]
    first = jnp.sum((adapter < ids).astype(jnp.int32), axis=1, keepdims=True)
    shift = jnp.where(adapter == ids, slots * (blocks * BLOCK) - first, 0)
    place = jnp.sum(shift, axis=0, keepdims=True) + lax.broadcasted_iota(jnp.int32, (1, rows), 1)
    spots = lax.broadcasted_iota(jnp.int32, (group * blocks * BLOCK, rows), 0)
    pick = jnp.where(spots == place, 1.0, 0.0).astype(jnp.bfloat16)
    pick_ref[...] = pick
    copies[2].wait()
    packed = jnp.dot(pick, hidden_ref[...], preferred_element_type=jnp.float32)
    packed_ref[...] = packed.astype(jnp.bfloat16).reshape(packed_ref.shape)
    kept_ref[...] = hidden_ref[...]


def pack_rows(hidden, adapter_of_row, adapter_holder_slot, me, orders):
    rows, depth = hidden.shape
    group = adapter_holder_slot.shape[0]
    blocks = MOST // BLOCK
    vmem = pl.BlockSpec(memory_space=pltpu.VMEM)
    smem = pl.BlockSpec(memory_space=pltpu.SMEM)
    anywhere = pl.BlockSpec(memory_space=pltpu.HBM)
    return pl.pallas_call(
        functools.partial(pack_kernel, blocks, orders),
        out_shape=(
            jax.ShapeDtypeStruct((group * blocks, BLOCK, depth), jnp.bfloat16),
            jax.ShapeDtypeStruct((group * MOST, rows), jnp.bfloat16),
            jax.ShapeDtypeStruct((len(orders),), jnp.int32),
            jax.ShapeDtypeStruct((rows, depth), jnp.bfloat16),
        ),
        in_specs=[smem, anywhere, anywhere, anywhere],
        out_specs=(vmem, vmem, smem, vmem),
        scratch_shapes=[
            pltpu.SMEM((group,), jnp.int32),
            pltpu.VMEM((1, rows), jnp.int32),
            pltpu.VMEM((rows, depth), jnp.bfloat16),
            pltpu.SemaphoreType.DMA((3,)),
        ],
        compiler_params=pltpu.CompilerParams(vmem_limit_bytes=24 * 2**20),
    )(me.reshape(1), in_hbm(adapter_holder_slot), in_hbm(adapter_of_row.reshape(1, rows)), in_hbm(hidden))


def adapter_kernel(rows_ref, expand_hbm, shrink_hbm, out_ref, flag_ref, *refs):
    shrink_ref, expand_ref, sems, expand_sem = refs
    group, _, depth = shrink_ref.shape
    blocks = MOST // BLOCK
    width = out_ref.shape[2]
    flag_ref[0] = group

    def copy(source):
        return pltpu.make_async_copy(
            shrink_hbm.at[:, pl.ds(source * depth, depth)], shrink_ref.at[source], sems.at[source]
        )

    for source in range(group):
        copy(source).start()
    expand_copy = pltpu.make_async_copy(expand_hbm, expand_ref, expand_sem)
    expand_copy.start()
    total = jnp.zeros((MOST, shrink_ref.shape[1]), jnp.float32)
    for source in range(group):
        copy(source).wait()
        own = rows_ref[source * blocks : (source + 1) * blocks].reshape(MOST, depth)
        total += lax.dot_general(
            own, shrink_ref[source], (((1,), (1,)), ((), ())), preferred_element_type=jnp.float32
        )
    rank_rows = total.astype(jnp.bfloat16)
    expand_copy.wait()
    for target in range(group):
        piece = jnp.dot(
            rank_rows,
            expand_ref[:, target * width : (target + 1) * width],
            preferred_element_type=jnp.float32,
        )
        out_ref[target * blocks : (target + 1) * blocks] = piece.astype(jnp.bfloat16).reshape(
            blocks, BLOCK, width
        )


def adapter_output(gathered, shrink, expand, group):
    rank = shrink.shape[0]
    model_width = expand.shape[1]
    depth = gathered.shape[2]
    vmem = pl.BlockSpec(memory_space=pltpu.VMEM)
    return pl.pallas_call(
        adapter_kernel,
        out_shape=[
            jax.ShapeDtypeStruct((gathered.shape[0], BLOCK, model_width // group), jnp.bfloat16),
            jax.ShapeDtypeStruct((1,), jnp.int32),
        ],
        in_specs=[vmem, pl.BlockSpec(memory_space=pl.ANY), pl.BlockSpec(memory_space=pl.ANY)],
        out_specs=[vmem, pl.BlockSpec(memory_space=pltpu.SMEM)],
        scratch_shapes=[
            pltpu.VMEM((group, rank, depth), jnp.bfloat16),
            pltpu.VMEM((rank, model_width), jnp.bfloat16),
            pltpu.SemaphoreType.DMA((group,)),
            pltpu.SemaphoreType.DMA,
        ],
        compiler_params=pltpu.CompilerParams(vmem_limit_bytes=24 * 2**20),
    )(gathered, in_hbm(expand), in_hbm(shrink))


def final_kernel(base_ref, pick_ref, rows_ref, out_ref):
    adapter_rows = lax.dot_general(
        pick_ref[...],
        rows_ref[...].reshape(pick_ref.shape[0], out_ref.shape[1]),
        (((0,), (0,)), ((), ())),
        preferred_element_type=jnp.float32,
    )
    for part in range(base_ref.shape[0]):
        lanes = slice(part * LANES, (part + 1) * LANES)
        total = base_ref[part] + ADAPTER_SCALE * adapter_rows[:, lanes]
        out_ref[:, lanes] = total.astype(out_ref.dtype)


def add_adapters(base, pick, arrived):
    parts, rows, _ = base.shape
    vmem = pl.BlockSpec(memory_space=pltpu.VMEM)
    return pl.pallas_call(
        final_kernel,
        out_shape=jax.ShapeDtypeStruct((rows, parts * LANES), jnp.bfloat16),
        in_specs=[vmem] * 3,
        out_specs=vmem,
        compiler_params=pltpu.CompilerParams(vmem_limit_bytes=24 * 2**20),
    )(base, pick, arrived)


def shards_by_blocks(
    hidden, down_matrix, shrink_matrices, expand_matrices, adapter_of_row, adapter_holder_slot
):
    group = lax.axis_size("tp")
    me = lax.axis_index("tp")
    rows, depth = hidden.shape
    width = down_matrix.shape[1] // group
    quads = list(range(0, group, 4))
    orders = [q + k for k in (3, 2, 1, 0) for q in quads]
    packed, pick, order, kept_hidden = pack_rows(
        hidden, adapter_of_row, adapter_holder_slot, me, orders
    )
    gathered = lax.all_to_all(packed, "tp", split_axis=0, concat_axis=0, tiled=True)
    shrink = jnp.swapaxes(shrink_matrices, 1, 2)[0]
    kept, pair_in = pair_sums(kept_hidden, down_matrix, group, order, width)
    gathered, _, pair_in = lax.optimization_barrier((gathered, kept, pair_in))
    expand = jnp.swapaxes(expand_matrices, 1, 2)[0]
    adapter_out, flag = adapter_output(gathered, shrink, expand, group)
    arrived = lax.all_to_all(adapter_out, "tp", split_axis=0, concat_axis=0, tiled=True)
    base = line_sums(kept, pair_in, flag[0], group, width)
    return add_adapters(base, pick, arrived)


def shards(
    hidden, down_matrix, shrink_matrices, expand_matrices, adapter_of_row, adapter_holder_slot
):
    group = lax.axis_size("tp")
    rows, depth = hidden.shape
    width = down_matrix.shape[1] // group
    if width % LANES == 0 and depth % LANES == 0 and rows <= LANES and group >= PLANE and group & (group - 1) == 0:
        return shards_by_blocks(
            hidden, down_matrix, shrink_matrices, expand_matrices, adapter_of_row, adapter_holder_slot
        )
    blocks = MOST // BLOCK
    adapter_ids = jnp.arange(group, dtype=jnp.int32)
    row_match = adapter_of_row[:, None] == adapter_ids[None, :]
    row_slot = jnp.sum(jnp.where(row_match, adapter_holder_slot[None, :], 0), axis=1)
    slot_mask = row_slot[None, :] == adapter_ids[:, None]
    before = jnp.cumsum(slot_mask.astype(jnp.int32), axis=1) - 1
    place = jnp.where(slot_mask, before, -1)
    pick = place[:, None, :] == jnp.arange(MOST, dtype=jnp.int32)[None, :, None]
    pick = pick.reshape(group * MOST, rows).astype(jnp.bfloat16)
    packed = jnp.dot(pick, hidden, preferred_element_type=jnp.float32).astype(jnp.bfloat16)
    packed = packed.reshape(group * blocks, BLOCK, depth)
    gathered = lax.all_to_all(packed, "tp", split_axis=0, concat_axis=0, tiled=True)
    partial_value = jnp.dot(hidden, down_matrix, preferred_element_type=jnp.float32)
    base = lax.psum_scatter(partial_value, "tp", scatter_dimension=1, tiled=True)
    own_rows = jnp.transpose(gathered.reshape(group, MOST, depth), (1, 0, 2))
    rank_rows = jnp.dot(
        own_rows.reshape(MOST, group * depth), shrink_matrices[0], preferred_element_type=jnp.float32
    ).astype(jnp.bfloat16)
    adapter_out = lax.dot_general(
        rank_rows, expand_matrices[0], (((1,), (1,)), ((), ())), preferred_element_type=jnp.float32
    ).astype(jnp.bfloat16)
    adapter_out = jnp.transpose(adapter_out.reshape(blocks, BLOCK, group, width), (2, 0, 1, 3))
    adapter_in = lax.all_to_all(
        adapter_out.reshape(group * blocks, BLOCK, width), "tp", split_axis=0, concat_axis=0, tiled=True
    )
    adapter_rows = lax.dot_general(
        pick,
        adapter_in.reshape(group * MOST, width),
        (((0,), (0,)), ((), ())),
        preferred_element_type=jnp.float32,
    )
    return (base + ADAPTER_SCALE * adapter_rows).astype(jnp.bfloat16)


def solution(mesh):
    in_specs = (
        P("rep", "tp"),
        P("tp", None),
        P(("rep", "tp"), None, None),
        P(("rep", "tp"), None, None),
        P("rep"),
        P("rep"),
    )
    out_specs = P("rep", "tp")
    return jax.shard_map(shards, mesh=mesh, in_specs=in_specs, out_specs=out_specs, check_vma=False)
```

```python
import functools

import jax
import jax.numpy as jnp
from jax import lax
from jax.experimental import pallas as pl
from jax.experimental.pallas import tpu as pltpu
from jax.sharding import PartitionSpec as P

ADAPTER_SCALE = 0.5
BLOCK = 4
MOST = 20
LANES = 128
F16_TOP = 14.0
PLANE = 4
HELD = 24
MARK_ROWS = 16


def in_hbm(value):
    return pltpu.with_memory_space_constraint(value, pltpu.HBM)


def xor_permute(value, group, offset):
    return lax.ppermute(value, "tp", [(i, i ^ offset) for i in range(group)])


def column_blocks_kernel(groups, order_ref, hidden_ref, down_ref, *refs):
    out_refs, held_ref, sems = refs[:groups], refs[groups], refs[groups + 1]
    count, depth, width = held_ref.shape
    parts = width // LANES
    pieces = sems.shape[1]
    cut = depth // pieces

    def copy(block, piece):
        start = pl.multiple_of(order_ref[block] * width, LANES)
        lines = pl.ds(piece * cut, cut)
        return pltpu.make_async_copy(
            down_ref.at[lines, pl.ds(start, width)], held_ref.at[block, lines], sems.at[block, piece]
        )

    for block in range(count):
        for piece in range(pieces):
            copy(block, piece).start()
    share = count // groups
    for block in range(count):
        for piece in range(pieces):
            copy(block, piece).wait()
        product = jnp.dot(hidden_ref[...], held_ref[block], preferred_element_type=jnp.float32)
        for lane in range(parts):
            out_refs[block // share][block % share * parts + lane] = product[
                :, lane * LANES : (lane + 1) * LANES
            ]


def column_blocks(hidden, down_matrix, order, width, groups=1):
    rows, depth = hidden.shape
    count = order.shape[0]
    pieces = 2 if depth % 32 == 0 else 1
    vmem = pl.BlockSpec(memory_space=pltpu.VMEM)
    out = jax.ShapeDtypeStruct((count // groups * width // LANES, rows, LANES), jnp.float32)
    return pl.pallas_call(
        functools.partial(column_blocks_kernel, groups),
        out_shape=[out] * groups,
        in_specs=[
            pl.BlockSpec(memory_space=pltpu.SMEM),
            vmem,
            pl.BlockSpec(memory_space=pl.ANY),
        ],
        out_specs=[vmem] * groups,
        scratch_shapes=[
            pltpu.VMEM((count, depth, width), jnp.bfloat16),
            pltpu.SemaphoreType.DMA((count, pieces)),
        ],
        compiler_params=pltpu.CompilerParams(vmem_limit_bytes=(12 + 12 * groups) * 2**20),
        cost_estimate=pl.CostEstimate(flops=1000, bytes_accessed=1000, transcendentals=0),
    )(order, hidden, in_hbm(down_matrix))


def pack_scaled(value):
    blocks, rows, lanes = value.shape
    peak = jnp.max(jnp.abs(value), axis=(0, 2))
    exponent = jnp.ceil(jnp.log2(jnp.maximum(peak, 2.0**-100)))
    scaled = (value * jnp.exp2(F16_TOP - exponent)[None, :, None]).astype(jnp.float16)
    marks = jnp.pad(exponent.astype(jnp.float16)[None], ((0, MARK_ROWS - 1), (0, lanes - rows)))
    return jnp.concatenate([scaled.reshape(blocks * rows, lanes), marks], axis=0)


def unpack_scaled(packed, rows):
    values, exponent = packed[:-MARK_ROWS], packed[-MARK_ROWS, :rows].astype(jnp.float32)
    values = values.reshape(-1, rows, packed.shape[1]).astype(jnp.float32)
    return values * jnp.exp2(exponent - F16_TOP)[None, :, None]


def pair_sums(hidden, down_matrix, group, order, width):
    half = group * width // LANES // PLANE
    rows = hidden.shape[0]
    share = group // PLANE

    def first():
        (far,) = column_blocks(hidden, down_matrix, order[:share], width)
        far_in = xor_permute(far, group, 1)
        (near,) = column_blocks(hidden, down_matrix, order[share : 2 * share], width)
        return pack_scaled(near + far_in)

    def first_idle():
        return jnp.zeros((half * rows + MARK_ROWS, LANES), jnp.float16)

    sent = lax.cond(order[0] >= 0, first, first_idle)
    pair_in = xor_permute(sent, group, 2)
    order, _ = lax.optimization_barrier((order, sent))

    def second():
        far, near = column_blocks(hidden, down_matrix, order[2 * share :], width, groups=2)
        return near + xor_permute(far, group, 1)

    def second_idle():
        return jnp.zeros((half, rows, LANES), jnp.float32)

    kept = lax.cond(order[1] >= 0, second, second_idle)
    return kept, pair_in


def line_sums(pair, group, width):
    rows = pair.shape[1]
    parts = width // LANES
    arrived = [
        xor_permute(pack_scaled(pair[i * parts : (i + 1) * parts]), group, 4 * i)
        for i in range(1, group // 4)
    ]
    total = pair[:parts]
    for packed in arrived:
        total = total + unpack_scaled(packed, rows)
    return jnp.transpose(total, (1, 0, 2)).reshape(rows, width)


def pack_kernel(
    blocks,
    orders,
    me_ref,
    slot_hbm,
    adapter_hbm,
    hidden_hbm,
    packed_ref,
    pick_ref,
    order_ref,
    kept_ref,
    slot_ref,
    adapter_ref,
    hidden_ref,
    sems,
):
    rows = hidden_ref.shape[0]
    group = slot_ref.shape[0]
    copies = [
        pltpu.make_async_copy(slot_hbm, slot_ref, sems.at[0]),
        pltpu.make_async_copy(adapter_hbm, adapter_ref, sems.at[1]),
        pltpu.make_async_copy(hidden_hbm, hidden_ref, sems.at[2]),
    ]
    for copy in copies:
        copy.start()
    for i, offset in enumerate(orders):
        order_ref[i] = me_ref[0] ^ offset
    ids = lax.broadcasted_iota(jnp.int32, (group, 1), 0)
    slots = jnp.zeros((group, 1), jnp.int32)
    copies[0].wait()
    for adapter in range(group):
        slots = jnp.where(ids == adapter, slot_ref[adapter], slots)
    copies[1].wait()
    adapter = adapter_ref[...]
    first = jnp.sum((adapter < ids).astype(jnp.int32), axis=1, keepdims=True)
    slot = jnp.sum(jnp.where(adapter == ids, slots, 0), axis=0, keepdims=True)
    first = jnp.sum(jnp.where(adapter == ids, first, 0), axis=0, keepdims=True)
    index = lax.broadcasted_iota(jnp.int32, (1, rows), 1) - first
    held = blocks * BLOCK
    rank = lax.rem(slot, PLANE) * (group // PLANE) + lax.div(slot, PLANE)
    spots = lax.broadcasted_iota(jnp.int32, (group * held, rows), 0)
    pick = jnp.where(spots == rank * held + index, 1.0, 0.0).astype(jnp.bfloat16)
    for k in range(PLANE):
        line = lax.broadcasted_iota(jnp.int32, (HELD, rows), 0)
        mine = (slot == me_ref[0] ^ k) & (index == line)
        pick_ref[k * HELD : (k + 1) * HELD] = jnp.where(mine, 1.0, 0.0).astype(jnp.bfloat16)
    copies[2].wait()
    packed = jnp.dot(pick, hidden_ref[...], preferred_element_type=jnp.float32)
    packed_ref[...] = packed.astype(jnp.bfloat16).reshape(packed_ref.shape)
    kept_ref[...] = hidden_ref[...]


def pack_rows(hidden, adapter_of_row, adapter_holder_slot, me, orders):
    rows, depth = hidden.shape
    group = adapter_holder_slot.shape[0]
    blocks = MOST // BLOCK
    vmem = pl.BlockSpec(memory_space=pltpu.VMEM)
    smem = pl.BlockSpec(memory_space=pltpu.SMEM)
    anywhere = pl.BlockSpec(memory_space=pltpu.HBM)
    return pl.pallas_call(
        functools.partial(pack_kernel, blocks, orders),
        out_shape=(
            jax.ShapeDtypeStruct((group * blocks, BLOCK, depth), jnp.bfloat16),
            jax.ShapeDtypeStruct((PLANE * HELD, rows), jnp.bfloat16),
            jax.ShapeDtypeStruct((len(orders),), jnp.int32),
            jax.ShapeDtypeStruct((rows, depth), jnp.bfloat16),
        ),
        in_specs=[smem, anywhere, anywhere, anywhere],
        out_specs=(vmem, vmem, smem, vmem),
        scratch_shapes=[
            pltpu.SMEM((group,), jnp.int32),
            pltpu.VMEM((1, rows), jnp.int32),
            pltpu.VMEM((rows, depth), jnp.bfloat16),
            pltpu.SemaphoreType.DMA((3,)),
        ],
        compiler_params=pltpu.CompilerParams(vmem_limit_bytes=24 * 2**20),
    )(me.reshape(1), in_hbm(adapter_holder_slot), in_hbm(adapter_of_row.reshape(1, rows)), in_hbm(hidden))


def adapter_kernel(parts, ranks, me_ref, rows_ref, expand_hbm, shrink_hbm, *refs):
    out_refs = refs[:PLANE]
    shrink_ref, expand_ref, total_ref, sems, expand_sem = refs[PLANE:]
    me = me_ref[0]
    group, _, depth = shrink_ref.shape
    blocks = MOST // BLOCK

    def copy(source):
        return pltpu.make_async_copy(
            shrink_hbm.at[:, pl.ds(ranks[source] * depth, depth)],
            shrink_ref.at[source],
            sems.at[source],
        )

    for source in range(group):
        copy(source).start()
    expand_copy = pltpu.make_async_copy(expand_hbm, expand_ref, expand_sem)
    expand_copy.start()
    total = jnp.zeros((MOST, total_ref.shape[1]), jnp.float32)
    for source in range(group):
        copy(source).wait()
        own = rows_ref[source * blocks : (source + 1) * blocks].reshape(MOST, depth)
        total += lax.dot_general(
            own, shrink_ref[source], (((1,), (1,)), ((), ())), preferred_element_type=jnp.float32
        )
    total_ref[...] = jnp.zeros_like(total_ref)
    total_ref[:MOST] = total
    rank_rows = total_ref[...].astype(jnp.bfloat16)
    expand_copy.wait()
    width = parts * LANES
    for k in range(PLANE):
        for line in range(group // PLANE):
            target = me ^ (PLANE * line + k)
            columns = pl.ds(pl.multiple_of(target * width, LANES), width)
            piece = jnp.dot(rank_rows, expand_ref[:, columns], preferred_element_type=jnp.float32)
            piece = piece.astype(jnp.bfloat16)
            for part in range(parts):
                out_refs[k][line * parts + part] = piece[:, part * LANES : (part + 1) * LANES]


def adapter_output(gathered, shrink, expand, group, me, ranks):
    rank = shrink.shape[0]
    model_width = expand.shape[1]
    depth = gathered.shape[2]
    parts = model_width // group // LANES
    held = (model_width // PLANE // LANES, HELD, LANES)
    vmem = pl.BlockSpec(memory_space=pltpu.VMEM)
    return pl.pallas_call(
        functools.partial(adapter_kernel, parts, ranks),
        out_shape=[jax.ShapeDtypeStruct(held, jnp.bfloat16)] * PLANE,
        in_specs=[
            pl.BlockSpec(memory_space=pltpu.SMEM),
            vmem,
            pl.BlockSpec(memory_space=pl.ANY),
            pl.BlockSpec(memory_space=pl.ANY),
        ],
        out_specs=[vmem] * PLANE,
        scratch_shapes=[
            pltpu.VMEM((group, rank, depth), jnp.bfloat16),
            pltpu.VMEM((rank, model_width), jnp.bfloat16),
            pltpu.VMEM((HELD, rank), jnp.float32),
            pltpu.SemaphoreType.DMA((group,)),
            pltpu.SemaphoreType.DMA,
        ],
        compiler_params=pltpu.CompilerParams(vmem_limit_bytes=24 * 2**20),
    )(me.reshape(1), gathered, in_hbm(expand), in_hbm(shrink))


def merge_kernel(pair_ref, pick_ref, *refs):
    in_refs, out_ref, held_ref = refs[:PLANE], refs[PLANE], refs[PLANE + 1]
    for k in range(PLANE):
        held_ref[:, k * HELD : (k + 1) * HELD] = in_refs[k][...]
    pick = pick_ref[...]
    for part in range(pair_ref.shape[0]):
        adapter_rows = lax.dot_general(
            pick, held_ref[part], (((0,), (0,)), ((), ())), preferred_element_type=jnp.float32
        )
        out_ref[part] = pair_ref[part] + ADAPTER_SCALE * adapter_rows


def merge_adapters(pair, pick, arrived):
    vmem = pl.BlockSpec(memory_space=pltpu.VMEM)
    return pl.pallas_call(
        merge_kernel,
        out_shape=jax.ShapeDtypeStruct(pair.shape, jnp.float32),
        in_specs=[vmem] * (2 + PLANE),
        out_specs=vmem,
        scratch_shapes=[pltpu.VMEM((pair.shape[0], PLANE * HELD, LANES), jnp.bfloat16)],
        compiler_params=pltpu.CompilerParams(vmem_limit_bytes=24 * 2**20),
    )(pair, pick, *arrived)


def shards_by_blocks(
    hidden, down_matrix, shrink_matrices, expand_matrices, adapter_of_row, adapter_holder_slot
):
    group = lax.axis_size("tp")
    me = lax.axis_index("tp")
    rows, depth = hidden.shape
    width = down_matrix.shape[1] // group
    quads = list(range(0, group, 4))
    orders = [q + k for k in (3, 2, 1, 0) for q in quads]
    lines = group // PLANE
    ranks = [PLANE * (i % lines) + i // lines for i in range(group)]
    packed, pick, order, kept_hidden = pack_rows(
        hidden, adapter_of_row, adapter_holder_slot, me, orders
    )
    gathered = lax.all_to_all(
        packed, "tp", split_axis=0, concat_axis=0, axis_index_groups=[ranks], tiled=True
    )
    shrink = jnp.swapaxes(shrink_matrices, 1, 2)[0]
    kept, pair_in = pair_sums(kept_hidden, down_matrix, group, order, width)
    gathered, _ = lax.optimization_barrier((gathered, kept))
    expand = jnp.swapaxes(expand_matrices, 1, 2)[0]
    outs = adapter_output(gathered, shrink, expand, group, me, ranks)
    arrived = [outs[0]] + [xor_permute(outs[k], group, k) for k in range(1, PLANE)]
    pair = kept + unpack_scaled(pair_in, rows)
    merged = merge_adapters(pair, pick, arrived)
    return line_sums(merged, group, width).astype(jnp.bfloat16)


def shards(
    hidden, down_matrix, shrink_matrices, expand_matrices, adapter_of_row, adapter_holder_slot
):
    group = lax.axis_size("tp")
    rows, depth = hidden.shape
    width = down_matrix.shape[1] // group
    if width % LANES == 0 and depth % LANES == 0 and rows <= LANES and group >= PLANE and group & (group - 1) == 0:
        return shards_by_blocks(
            hidden, down_matrix, shrink_matrices, expand_matrices, adapter_of_row, adapter_holder_slot
        )
    blocks = MOST // BLOCK
    adapter_ids = jnp.arange(group, dtype=jnp.int32)
    row_match = adapter_of_row[:, None] == adapter_ids[None, :]
    row_slot = jnp.sum(jnp.where(row_match, adapter_holder_slot[None, :], 0), axis=1)
    slot_mask = row_slot[None, :] == adapter_ids[:, None]
    before = jnp.cumsum(slot_mask.astype(jnp.int32), axis=1) - 1
    place = jnp.where(slot_mask, before, -1)
    pick = place[:, None, :] == jnp.arange(MOST, dtype=jnp.int32)[None, :, None]
    pick = pick.reshape(group * MOST, rows).astype(jnp.bfloat16)
    packed = jnp.dot(pick, hidden, preferred_element_type=jnp.float32).astype(jnp.bfloat16)
    packed = packed.reshape(group * blocks, BLOCK, depth)
    gathered = lax.all_to_all(packed, "tp", split_axis=0, concat_axis=0, tiled=True)
    partial_value = jnp.dot(hidden, down_matrix, preferred_element_type=jnp.float32)
    base = lax.psum_scatter(partial_value, "tp", scatter_dimension=1, tiled=True)
    own_rows = jnp.transpose(gathered.reshape(group, MOST, depth), (1, 0, 2))
    rank_rows = jnp.dot(
        own_rows.reshape(MOST, group * depth), shrink_matrices[0], preferred_element_type=jnp.float32
    ).astype(jnp.bfloat16)
    adapter_out = lax.dot_general(
        rank_rows, expand_matrices[0], (((1,), (1,)), ((), ())), preferred_element_type=jnp.float32
    ).astype(jnp.bfloat16)
    adapter_out = jnp.transpose(adapter_out.reshape(blocks, BLOCK, group, width), (2, 0, 1, 3))
    adapter_in = lax.all_to_all(
        adapter_out.reshape(group * blocks, BLOCK, width), "tp", split_axis=0, concat_axis=0, tiled=True
    )
    adapter_rows = lax.dot_general(
        pick,
        adapter_in.reshape(group * MOST, width),
        (((0,), (0,)), ((), ())),
        preferred_element_type=jnp.float32,
    )
    return (base + ADAPTER_SCALE * adapter_rows).astype(jnp.bfloat16)


def solution(mesh):
    in_specs = (
        P("rep", "tp"),
        P("tp", None),
        P(("rep", "tp"), None, None),
        P(("rep", "tp"), None, None),
        P("rep"),
        P("rep"),
    )
    out_specs = P("rep", "tp")
    return jax.shard_map(shards, mesh=mesh, in_specs=in_specs, out_specs=out_specs, check_vma=False)
```

```python
import functools
import math

import jax
import jax.numpy as jnp
from jax import lax
from jax.experimental import pallas as pl
from jax.experimental.pallas import tpu as pltpu
from jax.sharding import PartitionSpec as P

ADAPTER_SCALE = 0.5
BLOCK = 4
MOST = 20
LANES = 128
F16_TOP = 14.0
PLANE = 4
HELD = 24
MARK_ROWS = 16


def in_hbm(value):
    return pltpu.with_memory_space_constraint(value, pltpu.HBM)


def xor_permute(value, group, offset):
    return lax.ppermute(value, "tp", [(i, i ^ offset) for i in range(group)])


def column_blocks_kernel(groups, order_ref, hidden_ref, down_ref, *refs):
    out_refs, held_ref, sems = refs[:groups], refs[groups], refs[groups + 1]
    count, depth, width = held_ref.shape
    parts = width // LANES
    pieces = sems.shape[1]
    cut = depth // pieces

    def copy(block, piece):
        start = pl.multiple_of(order_ref[block] * width, LANES)
        lines = pl.ds(piece * cut, cut)
        return pltpu.make_async_copy(
            down_ref.at[lines, pl.ds(start, width)], held_ref.at[block, lines], sems.at[block, piece]
        )

    for block in range(count):
        for piece in range(pieces):
            copy(block, piece).start()
    share = count // groups
    for block in range(count):
        for piece in range(pieces):
            copy(block, piece).wait()
        product = jnp.dot(hidden_ref[...], held_ref[block], preferred_element_type=jnp.float32)
        for lane in range(parts):
            out_refs[block // share][block % share * parts + lane] = product[
                :, lane * LANES : (lane + 1) * LANES
            ]


def column_blocks(hidden, down_matrix, order, width, groups=1):
    rows, depth = hidden.shape
    count = order.shape[0]
    pieces = 2 if depth % 32 == 0 else 1
    vmem = pl.BlockSpec(memory_space=pltpu.VMEM)
    out = jax.ShapeDtypeStruct((count // groups * width // LANES, rows, LANES), jnp.float32)
    return pl.pallas_call(
        functools.partial(column_blocks_kernel, groups),
        out_shape=[out] * groups,
        in_specs=[
            pl.BlockSpec(memory_space=pltpu.SMEM),
            vmem,
            pl.BlockSpec(memory_space=pl.ANY),
        ],
        out_specs=[vmem] * groups,
        scratch_shapes=[
            pltpu.VMEM((count, depth, width), jnp.bfloat16),
            pltpu.SemaphoreType.DMA((count, pieces)),
        ],
        compiler_params=pltpu.CompilerParams(vmem_limit_bytes=(12 + 12 * groups) * 2**20),
        cost_estimate=pl.CostEstimate(flops=1000, bytes_accessed=1000, transcendentals=0),
    )(order, hidden, in_hbm(down_matrix))


def pack_scaled(value):
    blocks, rows, lanes = value.shape
    peak = jnp.max(jnp.abs(value), axis=(0, 2))
    exponent = jnp.ceil(jnp.log2(jnp.maximum(peak, 2.0**-100)))
    scaled = (value * jnp.exp2(F16_TOP - exponent)[None, :, None]).astype(jnp.float16)
    marks = jnp.pad(exponent.astype(jnp.float16)[None], ((0, MARK_ROWS - 1), (0, lanes - rows)))
    return jnp.concatenate([scaled.reshape(blocks * rows, lanes), marks], axis=0)


def unpack_scaled(packed, rows):
    values, exponent = packed[:-MARK_ROWS], packed[-MARK_ROWS, :rows].astype(jnp.float32)
    values = values.reshape(-1, rows, packed.shape[1]).astype(jnp.float32)
    return values * jnp.exp2(exponent - F16_TOP)[None, :, None]


def pair_sums(hidden, down_matrix, group, order, width):
    half = group * width // LANES // PLANE
    rows = hidden.shape[0]
    share = group // PLANE

    def first():
        (far,) = column_blocks(hidden, down_matrix, order[:share], width)
        far_in = xor_permute(far, group, 1)
        (near,) = column_blocks(hidden, down_matrix, order[share : 2 * share], width)
        return pack_scaled(near + far_in)

    def first_idle():
        return jnp.zeros((half * rows + MARK_ROWS, LANES), jnp.float16)

    sent = lax.cond(order[0] >= 0, first, first_idle)
    pair_in = xor_permute(sent, group, 2)
    order, _ = lax.optimization_barrier((order, sent))

    def second():
        far, near = column_blocks(hidden, down_matrix, order[2 * share :], width, groups=2)
        return near + xor_permute(far, group, 1)

    def second_idle():
        return jnp.zeros((half, rows, LANES), jnp.float32)

    kept = lax.cond(order[1] >= 0, second, second_idle)
    return kept, pair_in


def line_sums(pair, group, width):
    rows = pair.shape[1]
    parts = width // LANES
    arrived = [
        xor_permute(pack_scaled(pair[i * parts : (i + 1) * parts]), group, 4 * i)
        for i in range(1, group // 4)
    ]
    total = pair[:parts]
    for packed in arrived:
        total = total + unpack_scaled(packed, rows)
    return jnp.transpose(total, (1, 0, 2)).reshape(rows, width)


def pack_kernel(
    blocks,
    orders,
    me_ref,
    slot_hbm,
    adapter_hbm,
    hidden_hbm,
    packed_ref,
    pick_ref,
    order_ref,
    kept_ref,
    slot_ref,
    adapter_ref,
    hidden_ref,
    sems,
):
    rows = hidden_ref.shape[0]
    group = slot_ref.shape[0]
    copies = [
        pltpu.make_async_copy(slot_hbm, slot_ref, sems.at[0]),
        pltpu.make_async_copy(adapter_hbm, adapter_ref, sems.at[1]),
        pltpu.make_async_copy(hidden_hbm, hidden_ref, sems.at[2]),
    ]
    for copy in copies:
        copy.start()
    for i, offset in enumerate(orders):
        order_ref[i] = me_ref[0] ^ offset
    ids = lax.broadcasted_iota(jnp.int32, (group, 1), 0)
    slots = jnp.zeros((group, 1), jnp.int32)
    copies[0].wait()
    for adapter in range(group):
        slots = jnp.where(ids == adapter, slot_ref[adapter], slots)
    copies[1].wait()
    adapter = adapter_ref[...]
    first = jnp.sum((adapter < ids).astype(jnp.int32), axis=1, keepdims=True)
    shift = jnp.where(adapter == ids, slots * (blocks * BLOCK) - first, 0)
    place = jnp.sum(shift, axis=0, keepdims=True) + lax.broadcasted_iota(jnp.int32, (1, rows), 1)
    spots = lax.broadcasted_iota(jnp.int32, (group * blocks * BLOCK, rows), 0)
    pick = jnp.where(spots == place, 1.0, 0.0).astype(jnp.bfloat16)
    for k in range(PLANE):
        line = lax.broadcasted_iota(jnp.int32, (HELD, rows), 0)
        mine = (line + (me_ref[0] ^ k) * (blocks * BLOCK) == place) & (line < blocks * BLOCK)
        pick_ref[k * HELD : (k + 1) * HELD] = jnp.where(mine, 1.0, 0.0).astype(jnp.bfloat16)
    copies[2].wait()
    packed = jnp.dot(pick, hidden_ref[...], preferred_element_type=jnp.float32)
    packed_ref[...] = packed.astype(jnp.bfloat16).reshape(packed_ref.shape)
    kept_ref[...] = hidden_ref[...]


def pack_rows(hidden, adapter_of_row, adapter_holder_slot, me, orders):
    rows, depth = hidden.shape
    group = adapter_holder_slot.shape[0]
    blocks = MOST // BLOCK
    vmem = pl.BlockSpec(memory_space=pltpu.VMEM)
    smem = pl.BlockSpec(memory_space=pltpu.SMEM)
    anywhere = pl.BlockSpec(memory_space=pltpu.HBM)
    return pl.pallas_call(
        functools.partial(pack_kernel, blocks, orders),
        out_shape=(
            jax.ShapeDtypeStruct((group * blocks, BLOCK, depth), jnp.bfloat16),
            jax.ShapeDtypeStruct((PLANE * HELD, rows), jnp.bfloat16),
            jax.ShapeDtypeStruct((len(orders),), jnp.int32),
            jax.ShapeDtypeStruct((rows, depth), jnp.bfloat16),
        ),
        in_specs=[smem, anywhere, anywhere, anywhere],
        out_specs=(vmem, vmem, smem, vmem),
        scratch_shapes=[
            pltpu.SMEM((group,), jnp.int32),
            pltpu.VMEM((1, rows), jnp.int32),
            pltpu.VMEM((rows, depth), jnp.bfloat16),
            pltpu.SemaphoreType.DMA((3,)),
        ],
        compiler_params=pltpu.CompilerParams(vmem_limit_bytes=24 * 2**20),
    )(me.reshape(1), in_hbm(adapter_holder_slot), in_hbm(adapter_of_row.reshape(1, rows)), in_hbm(hidden))


def rank_kernel(rows_ref, shrink_hbm, out_ref, shrink_ref, total_ref, sems):
    group, _, depth = shrink_ref.shape
    blocks = MOST // BLOCK

    def copy(source):
        return pltpu.make_async_copy(
            shrink_hbm.at[:, pl.ds(source * depth, depth)], shrink_ref.at[source], sems.at[source]
        )

    for source in range(group):
        copy(source).start()
    total = jnp.zeros((MOST, shrink_ref.shape[1]), jnp.float32)
    for source in range(group):
        copy(source).wait()
        own = rows_ref[source * blocks : (source + 1) * blocks].reshape(MOST, depth)
        total += lax.dot_general(
            own, shrink_ref[source], (((1,), (1,)), ((), ())), preferred_element_type=jnp.float32
        )
    total_ref[...] = jnp.zeros_like(total_ref)
    total_ref[:MOST] = total
    out_ref[...] = total_ref[...].astype(out_ref.dtype)


def rank_rows_of(gathered, shrink, group):
    rank = shrink.shape[0]
    depth = gathered.shape[2]
    vmem = pl.BlockSpec(memory_space=pltpu.VMEM)
    return pl.pallas_call(
        rank_kernel,
        out_shape=jax.ShapeDtypeStruct((HELD, rank), jnp.bfloat16),
        in_specs=[vmem, pl.BlockSpec(memory_space=pl.ANY)],
        out_specs=vmem,
        scratch_shapes=[
            pltpu.VMEM((group, rank, depth), jnp.bfloat16),
            pltpu.VMEM((HELD, rank), jnp.float32),
            pltpu.SemaphoreType.DMA((group,)),
        ],
        compiler_params=pltpu.CompilerParams(vmem_limit_bytes=24 * 2**20),
    )(gathered, in_hbm(shrink))


def columns_kernel(width, me_ref, expand_hbm, *refs):
    out_refs, sems = refs[:PLANE], refs[PLANE]
    lines = out_refs[0].shape[1] // width
    copies = []
    for k in range(PLANE):
        for line in range(lines):
            target = me_ref[0] ^ (PLANE * line + k)
            columns = pl.ds(pl.multiple_of(target * width, LANES), width)
            copies.append(
                pltpu.make_async_copy(
                    expand_hbm.at[:, columns],
                    out_refs[k].at[:, pl.ds(line * width, width)],
                    sems.at[k, line],
                )
            )
    for copy in copies:
        copy.start()
    for copy in copies:
        copy.wait()


def plane_columns(expand, group, me):
    rank, model_width = expand.shape
    vmem = pl.BlockSpec(memory_space=pltpu.VMEM)
    return pl.pallas_call(
        functools.partial(columns_kernel, model_width // group),
        out_shape=[jax.ShapeDtypeStruct((rank, model_width // PLANE), jnp.bfloat16)] * PLANE,
        in_specs=[pl.BlockSpec(memory_space=pltpu.SMEM), pl.BlockSpec(memory_space=pl.ANY)],
        out_specs=[vmem] * PLANE,
        scratch_shapes=[pltpu.SemaphoreType.DMA((PLANE, group // PLANE))],
        compiler_params=pltpu.CompilerParams(vmem_limit_bytes=24 * 2**20),
    )(me.reshape(1), in_hbm(expand))


def merge_kernel(pair_ref, pick_ref, *refs):
    rank_refs, column_refs, out_ref = refs[:PLANE], refs[PLANE : 2 * PLANE], refs[2 * PLANE]
    spread = [
        lax.dot_general(
            pick_ref[k * HELD : (k + 1) * HELD],
            rank_refs[k][...],
            (((0,), (0,)), ((), ())),
            preferred_element_type=jnp.float32,
        ).astype(jnp.bfloat16)
        for k in range(PLANE)
    ]
    blocks = out_ref.shape[0]
    step = math.gcd(blocks, 4)
    for first in range(0, blocks, step):
        columns = slice(first * LANES, (first + step) * LANES)
        adapter_rows = jnp.dot(
            spread[0], column_refs[0][:, columns], preferred_element_type=jnp.float32
        )
        for k in range(1, PLANE):
            adapter_rows += jnp.dot(
                spread[k], column_refs[k][:, columns], preferred_element_type=jnp.float32
            )
        for part in range(step):
            lanes = slice(part * LANES, (part + 1) * LANES)
            out_ref[first + part] = pair_ref[first + part] + ADAPTER_SCALE * adapter_rows[:, lanes]


def merge_adapters(pair, pick, ranks, columns):
    vmem = pl.BlockSpec(memory_space=pltpu.VMEM)
    return pl.pallas_call(
        merge_kernel,
        out_shape=jax.ShapeDtypeStruct(pair.shape, jnp.float32),
        in_specs=[vmem] * (2 + 2 * PLANE),
        out_specs=vmem,
        compiler_params=pltpu.CompilerParams(vmem_limit_bytes=24 * 2**20),
    )(pair, pick, *ranks, *columns)


def shards_by_blocks(
    hidden, down_matrix, shrink_matrices, expand_matrices, adapter_of_row, adapter_holder_slot
):
    group = lax.axis_size("tp")
    me = lax.axis_index("tp")
    rows, depth = hidden.shape
    width = down_matrix.shape[1] // group
    quads = list(range(0, group, 4))
    orders = [q + k for k in (3, 2, 1, 0) for q in quads]
    packed, pick, order, kept_hidden = pack_rows(
        hidden, adapter_of_row, adapter_holder_slot, me, orders
    )
    gathered = lax.all_to_all(packed, "tp", split_axis=0, concat_axis=0, tiled=True)
    shrink = jnp.swapaxes(shrink_matrices, 1, 2)[0]
    kept, pair_in = pair_sums(kept_hidden, down_matrix, group, order, width)
    gathered, _ = lax.optimization_barrier((gathered, kept))
    expand = jnp.swapaxes(expand_matrices, 1, 2)[0]
    expand, _ = lax.optimization_barrier((expand, kept))
    columns = plane_columns(expand, group, me)
    columns = [columns[0]] + [xor_permute(columns[k], group, k) for k in range(1, PLANE)]
    rank_rows = rank_rows_of(gathered, shrink, group)
    ranks = [rank_rows] + [xor_permute(rank_rows, group, k) for k in range(1, PLANE)]
    pair = kept + unpack_scaled(pair_in, rows)
    merged = merge_adapters(pair, pick, ranks, columns)
    return line_sums(merged, group, width).astype(jnp.bfloat16)


def shards(
    hidden, down_matrix, shrink_matrices, expand_matrices, adapter_of_row, adapter_holder_slot
):
    group = lax.axis_size("tp")
    rows, depth = hidden.shape
    width = down_matrix.shape[1] // group
    if width % LANES == 0 and depth % LANES == 0 and rows <= LANES and group >= PLANE and group & (group - 1) == 0:
        return shards_by_blocks(
            hidden, down_matrix, shrink_matrices, expand_matrices, adapter_of_row, adapter_holder_slot
        )
    blocks = MOST // BLOCK
    adapter_ids = jnp.arange(group, dtype=jnp.int32)
    row_match = adapter_of_row[:, None] == adapter_ids[None, :]
    row_slot = jnp.sum(jnp.where(row_match, adapter_holder_slot[None, :], 0), axis=1)
    slot_mask = row_slot[None, :] == adapter_ids[:, None]
    before = jnp.cumsum(slot_mask.astype(jnp.int32), axis=1) - 1
    place = jnp.where(slot_mask, before, -1)
    pick = place[:, None, :] == jnp.arange(MOST, dtype=jnp.int32)[None, :, None]
    pick = pick.reshape(group * MOST, rows).astype(jnp.bfloat16)
    packed = jnp.dot(pick, hidden, preferred_element_type=jnp.float32).astype(jnp.bfloat16)
    packed = packed.reshape(group * blocks, BLOCK, depth)
    gathered = lax.all_to_all(packed, "tp", split_axis=0, concat_axis=0, tiled=True)
    partial_value = jnp.dot(hidden, down_matrix, preferred_element_type=jnp.float32)
    base = lax.psum_scatter(partial_value, "tp", scatter_dimension=1, tiled=True)
    own_rows = jnp.transpose(gathered.reshape(group, MOST, depth), (1, 0, 2))
    rank_rows = jnp.dot(
        own_rows.reshape(MOST, group * depth), shrink_matrices[0], preferred_element_type=jnp.float32
    ).astype(jnp.bfloat16)
    adapter_out = lax.dot_general(
        rank_rows, expand_matrices[0], (((1,), (1,)), ((), ())), preferred_element_type=jnp.float32
    ).astype(jnp.bfloat16)
    adapter_out = jnp.transpose(adapter_out.reshape(blocks, BLOCK, group, width), (2, 0, 1, 3))
    adapter_in = lax.all_to_all(
        adapter_out.reshape(group * blocks, BLOCK, width), "tp", split_axis=0, concat_axis=0, tiled=True
    )
    adapter_rows = lax.dot_general(
        pick,
        adapter_in.reshape(group * MOST, width),
        (((0,), (0,)), ((), ())),
        preferred_element_type=jnp.float32,
    )
    return (base + ADAPTER_SCALE * adapter_rows).astype(jnp.bfloat16)


def solution(mesh):
    in_specs = (
        P("rep", "tp"),
        P("tp", None),
        P(("rep", "tp"), None, None),
        P(("rep", "tp"), None, None),
        P("rep"),
        P("rep"),
    )
    out_specs = P("rep", "tp")
    return jax.shard_map(shards, mesh=mesh, in_specs=in_specs, out_specs=out_specs, check_vma=False)
```

```python
import functools

import jax
import jax.numpy as jnp
from jax import lax
from jax.experimental import pallas as pl
from jax.experimental.pallas import tpu as pltpu
from jax.sharding import PartitionSpec as P

ADAPTER_SCALE = 0.5
BLOCK = 4
MOST = 20
LANES = 128
F16_TOP = 14.0
PLANE = 4
HELD = 24
MARK_ROWS = 16


def in_hbm(value):
    return pltpu.with_memory_space_constraint(value, pltpu.HBM)


def xor_permute(value, group, offset):
    return lax.ppermute(value, "tp", [(i, i ^ offset) for i in range(group)])


def column_blocks_kernel(groups, order_ref, hidden_ref, down_ref, *refs):
    out_refs, held_ref, sems = refs[:groups], refs[groups], refs[groups + 1]
    count, depth, width = held_ref.shape
    parts = width // LANES
    pieces = sems.shape[1]
    cut = depth // pieces

    def copy(block, piece):
        start = pl.multiple_of(order_ref[block] * width, LANES)
        lines = pl.ds(piece * cut, cut)
        return pltpu.make_async_copy(
            down_ref.at[lines, pl.ds(start, width)], held_ref.at[block, lines], sems.at[block, piece]
        )

    for block in range(count):
        for piece in range(pieces):
            copy(block, piece).start()
    share = count // groups
    for block in range(count):
        for piece in range(pieces):
            copy(block, piece).wait()
        product = jnp.dot(hidden_ref[...], held_ref[block], preferred_element_type=jnp.float32)
        for lane in range(parts):
            out_refs[block // share][block % share * parts + lane] = product[
                :, lane * LANES : (lane + 1) * LANES
            ]


def column_blocks(hidden, down_matrix, order, width, groups=1):
    rows, depth = hidden.shape
    count = order.shape[0]
    pieces = 2 if depth % 32 == 0 else 1
    vmem = pl.BlockSpec(memory_space=pltpu.VMEM)
    out = jax.ShapeDtypeStruct((count // groups * width // LANES, rows, LANES), jnp.float32)
    return pl.pallas_call(
        functools.partial(column_blocks_kernel, groups),
        out_shape=[out] * groups,
        in_specs=[
            pl.BlockSpec(memory_space=pltpu.SMEM),
            vmem,
            pl.BlockSpec(memory_space=pl.ANY),
        ],
        out_specs=[vmem] * groups,
        scratch_shapes=[
            pltpu.VMEM((count, depth, width), jnp.bfloat16),
            pltpu.SemaphoreType.DMA((count, pieces)),
        ],
        compiler_params=pltpu.CompilerParams(vmem_limit_bytes=(12 + 12 * groups) * 2**20),
        cost_estimate=pl.CostEstimate(flops=1000, bytes_accessed=1000, transcendentals=0),
    )(order, hidden, in_hbm(down_matrix))


def pack_scaled(value):
    blocks, rows, lanes = value.shape
    peak = jnp.max(jnp.abs(value), axis=(0, 2))
    exponent = jnp.ceil(jnp.log2(jnp.maximum(peak, 2.0**-100)))
    scaled = (value * jnp.exp2(F16_TOP - exponent)[None, :, None]).astype(jnp.float16)
    marks = jnp.pad(exponent.astype(jnp.float16)[None], ((0, MARK_ROWS - 1), (0, lanes - rows)))
    return jnp.concatenate([scaled.reshape(blocks * rows, lanes), marks], axis=0)


def unpack_scaled(packed, rows):
    values, exponent = packed[:-MARK_ROWS], packed[-MARK_ROWS, :rows].astype(jnp.float32)
    values = values.reshape(-1, rows, packed.shape[1]).astype(jnp.float32)
    return values * jnp.exp2(exponent - F16_TOP)[None, :, None]


def pair_sums(hidden, down_matrix, group, order, width):
    half = group * width // LANES // PLANE
    rows = hidden.shape[0]
    share = group // PLANE

    def first():
        (far,) = column_blocks(hidden, down_matrix, order[:share], width)
        far_in = xor_permute(far, group, 1)
        (near,) = column_blocks(hidden, down_matrix, order[share : 2 * share], width)
        return pack_scaled(near + far_in)

    def first_idle():
        return jnp.zeros((half * rows + MARK_ROWS, LANES), jnp.float16)

    sent = lax.cond(order[0] >= 0, first, first_idle)
    pair_in = xor_permute(sent, group, 2)
    order, _ = lax.optimization_barrier((order, sent))

    def second():
        far, near = column_blocks(hidden, down_matrix, order[2 * share :], width, groups=2)
        return near + xor_permute(far, group, 1)

    def second_idle():
        return jnp.zeros((half, rows, LANES), jnp.float32)

    kept = lax.cond(order[1] >= 0, second, second_idle)
    return kept, pair_in


def exchange_sum(kept, sent, group, offset):
    return kept + unpack_scaled(xor_permute(pack_scaled(sent), group, offset), kept.shape[1])


def line_sums(merged, group):
    if group != 4 * PLANE:
        (whole,) = merged
        return sum_direct(whole, group)
    near_kept, near_sent, far_kept, far_sent = merged
    half = near_kept.shape[0] // 2
    far = exchange_sum(far_kept, far_sent, group, 2 * PLANE)
    near = exchange_sum(near_kept, near_sent, group, PLANE)
    near = exchange_sum(near[:half], near[half:], group, 2 * PLANE)
    far = exchange_sum(far[:half], far[half:], group, PLANE)
    return jnp.concatenate([near, far], axis=0)


def sum_direct(whole, group):
    lines = group // PLANE
    parts = whole.shape[0] // lines
    total = whole[:parts]
    for i in range(1, lines):
        total = exchange_sum(total, whole[i * parts : (i + 1) * parts], group, PLANE * i)
    return total


def pack_kernel(
    blocks,
    orders,
    me_ref,
    slot_hbm,
    adapter_hbm,
    hidden_hbm,
    packed_ref,
    pick_ref,
    order_ref,
    kept_ref,
    slot_ref,
    adapter_ref,
    hidden_ref,
    sems,
):
    rows = hidden_ref.shape[0]
    group = slot_ref.shape[0]
    copies = [
        pltpu.make_async_copy(slot_hbm, slot_ref, sems.at[0]),
        pltpu.make_async_copy(adapter_hbm, adapter_ref, sems.at[1]),
        pltpu.make_async_copy(hidden_hbm, hidden_ref, sems.at[2]),
    ]
    for copy in copies:
        copy.start()
    for i, offset in enumerate(orders):
        order_ref[i] = me_ref[0] ^ offset
    ids = lax.broadcasted_iota(jnp.int32, (group, 1), 0)
    slots = jnp.zeros((group, 1), jnp.int32)
    copies[0].wait()
    for adapter in range(group):
        slots = jnp.where(ids == adapter, slot_ref[adapter], slots)
    copies[1].wait()
    adapter = adapter_ref[...]
    first = jnp.sum((adapter < ids).astype(jnp.int32), axis=1, keepdims=True)
    shift = jnp.where(adapter == ids, slots * (blocks * BLOCK) - first, 0)
    place = jnp.sum(shift, axis=0, keepdims=True) + lax.broadcasted_iota(jnp.int32, (1, rows), 1)
    spots = lax.broadcasted_iota(jnp.int32, (group * blocks * BLOCK, rows), 0)
    pick = jnp.where(spots == place, 1.0, 0.0).astype(jnp.bfloat16)
    for k in range(PLANE):
        line = lax.broadcasted_iota(jnp.int32, (HELD, rows), 0)
        mine = (line + (me_ref[0] ^ k) * (blocks * BLOCK) == place) & (line < blocks * BLOCK)
        pick_ref[k * HELD : (k + 1) * HELD] = jnp.where(mine, 1.0, 0.0).astype(jnp.bfloat16)
    copies[2].wait()
    packed = jnp.dot(pick, hidden_ref[...], preferred_element_type=jnp.float32)
    packed_ref[...] = packed.astype(jnp.bfloat16).reshape(packed_ref.shape)
    kept_ref[...] = hidden_ref[...]


def pack_rows(hidden, adapter_of_row, adapter_holder_slot, me, orders):
    rows, depth = hidden.shape
    group = adapter_holder_slot.shape[0]
    blocks = MOST // BLOCK
    vmem = pl.BlockSpec(memory_space=pltpu.VMEM)
    smem = pl.BlockSpec(memory_space=pltpu.SMEM)
    anywhere = pl.BlockSpec(memory_space=pltpu.HBM)
    return pl.pallas_call(
        functools.partial(pack_kernel, blocks, orders),
        out_shape=(
            jax.ShapeDtypeStruct((group * blocks, BLOCK, depth), jnp.bfloat16),
            jax.ShapeDtypeStruct((PLANE * HELD, rows), jnp.bfloat16),
            jax.ShapeDtypeStruct((len(orders),), jnp.int32),
            jax.ShapeDtypeStruct((rows, depth), jnp.bfloat16),
        ),
        in_specs=[smem, anywhere, anywhere, anywhere],
        out_specs=(vmem, vmem, smem, vmem),
        scratch_shapes=[
            pltpu.SMEM((group,), jnp.int32),
            pltpu.VMEM((1, rows), jnp.int32),
            pltpu.VMEM((rows, depth), jnp.bfloat16),
            pltpu.SemaphoreType.DMA((3,)),
        ],
        compiler_params=pltpu.CompilerParams(vmem_limit_bytes=24 * 2**20),
    )(me.reshape(1), in_hbm(adapter_holder_slot), in_hbm(adapter_of_row.reshape(1, rows)), in_hbm(hidden))


def adapter_kernel(parts, me_ref, rows_ref, expand_hbm, shrink_hbm, *refs):
    out_refs = refs[:PLANE]
    shrink_ref, expand_ref, total_ref, sems, expand_sem = refs[PLANE:]
    me = me_ref[0]
    group, _, depth = shrink_ref.shape
    blocks = MOST // BLOCK

    def copy(source):
        return pltpu.make_async_copy(
            shrink_hbm.at[:, pl.ds(source * depth, depth)], shrink_ref.at[source], sems.at[source]
        )

    for source in range(group):
        copy(source).start()
    expand_copy = pltpu.make_async_copy(expand_hbm, expand_ref, expand_sem)
    expand_copy.start()
    total = jnp.zeros((MOST, total_ref.shape[1]), jnp.float32)
    for source in range(group):
        copy(source).wait()
        own = rows_ref[source * blocks : (source + 1) * blocks].reshape(MOST, depth)
        total += lax.dot_general(
            own, shrink_ref[source], (((1,), (1,)), ((), ())), preferred_element_type=jnp.float32
        )
    total_ref[...] = jnp.zeros_like(total_ref)
    total_ref[:MOST] = total
    rank_rows = total_ref[...].astype(jnp.bfloat16)
    expand_copy.wait()
    width = parts * LANES
    for k in range(PLANE):
        for line in range(group // PLANE):
            target = me ^ (PLANE * line + k)
            columns = pl.ds(pl.multiple_of(target * width, LANES), width)
            piece = jnp.dot(rank_rows, expand_ref[:, columns], preferred_element_type=jnp.float32)
            piece = piece.astype(jnp.bfloat16)
            for part in range(parts):
                out_refs[k][line * parts + part] = piece[:, part * LANES : (part + 1) * LANES]


def adapter_output(gathered, shrink, expand, group, me):
    rank = shrink.shape[0]
    model_width = expand.shape[1]
    depth = gathered.shape[2]
    parts = model_width // group // LANES
    held = (model_width // PLANE // LANES, HELD, LANES)
    vmem = pl.BlockSpec(memory_space=pltpu.VMEM)
    return pl.pallas_call(
        functools.partial(adapter_kernel, parts),
        out_shape=[jax.ShapeDtypeStruct(held, jnp.bfloat16)] * PLANE,
        in_specs=[
            pl.BlockSpec(memory_space=pltpu.SMEM),
            vmem,
            pl.BlockSpec(memory_space=pl.ANY),
            pl.BlockSpec(memory_space=pl.ANY),
        ],
        out_specs=[vmem] * PLANE,
        scratch_shapes=[
            pltpu.VMEM((group, rank, depth), jnp.bfloat16),
            pltpu.VMEM((rank, model_width), jnp.bfloat16),
            pltpu.VMEM((HELD, rank), jnp.float32),
            pltpu.SemaphoreType.DMA((group,)),
            pltpu.SemaphoreType.DMA,
        ],
        compiler_params=pltpu.CompilerParams(vmem_limit_bytes=24 * 2**20),
    )(me.reshape(1), gathered, in_hbm(expand), in_hbm(shrink))


def merge_kernel(places, pair_ref, pick_ref, *refs):
    in_refs, out_refs, held_ref = refs[:PLANE], refs[PLANE:-1], refs[-1]
    for k in range(PLANE):
        held_ref[:, k * HELD : (k + 1) * HELD] = in_refs[k][...]
    pick = pick_ref[...]
    for out_ref, blocks in zip(out_refs, places):
        for i, block in enumerate(blocks):
            adapter_rows = lax.dot_general(
                pick, held_ref[block], (((0,), (0,)), ((), ())), preferred_element_type=jnp.float32
            )
            out_ref[i] = pair_ref[block] + ADAPTER_SCALE * adapter_rows


def merge_adapters(pair, pick, arrived, group):
    blocks, rows, _ = pair.shape
    if group == 4 * PLANE:
        parts = blocks // 4
        half = parts // 2

        def pieces(first, *lines):
            return [line * parts + first + i for line in lines for i in range(half)]

        places = [pieces(0, 0, 2), pieces(0, 1, 3), pieces(half, 0, 1), pieces(half, 2, 3)]
    else:
        places = [list(range(blocks))]
    vmem = pl.BlockSpec(memory_space=pltpu.VMEM)
    return pl.pallas_call(
        functools.partial(merge_kernel, places),
        out_shape=[jax.ShapeDtypeStruct((len(p), rows, LANES), jnp.float32) for p in places],
        in_specs=[vmem] * (2 + PLANE),
        out_specs=[vmem] * len(places),
        scratch_shapes=[pltpu.VMEM((blocks, PLANE * HELD, LANES), jnp.bfloat16)],
        compiler_params=pltpu.CompilerParams(vmem_limit_bytes=24 * 2**20),
    )(pair, pick, *arrived)


def shards_by_blocks(
    hidden, down_matrix, shrink_matrices, expand_matrices, adapter_of_row, adapter_holder_slot
):
    group = lax.axis_size("tp")
    me = lax.axis_index("tp")
    rows, depth = hidden.shape
    width = down_matrix.shape[1] // group
    quads = list(range(0, group, 4))
    orders = [q + k for k in (3, 2, 1, 0) for q in quads]
    packed, pick, order, kept_hidden = pack_rows(
        hidden, adapter_of_row, adapter_holder_slot, me, orders
    )
    gathered = lax.all_to_all(packed, "tp", split_axis=0, concat_axis=0, tiled=True)
    shrink = jnp.swapaxes(shrink_matrices, 1, 2)[0]
    kept, pair_in = pair_sums(kept_hidden, down_matrix, group, order, width)
    gathered, _ = lax.optimization_barrier((gathered, kept))
    expand = jnp.swapaxes(expand_matrices, 1, 2)[0]
    outs = adapter_output(gathered, shrink, expand, group, me)
    arrived = [outs[0]] + [xor_permute(outs[k], group, k) for k in range(1, PLANE)]
    pair = kept + unpack_scaled(pair_in, rows)
    total = line_sums(merge_adapters(pair, pick, arrived, group), group)
    return jnp.transpose(total, (1, 0, 2)).reshape(rows, width).astype(jnp.bfloat16)


def shards(
    hidden, down_matrix, shrink_matrices, expand_matrices, adapter_of_row, adapter_holder_slot
):
    group = lax.axis_size("tp")
    rows, depth = hidden.shape
    width = down_matrix.shape[1] // group
    if width % (2 * LANES) == 0 and depth % LANES == 0 and rows <= LANES and group >= PLANE and group & (group - 1) == 0:
        return shards_by_blocks(
            hidden, down_matrix, shrink_matrices, expand_matrices, adapter_of_row, adapter_holder_slot
        )
    blocks = MOST // BLOCK
    adapter_ids = jnp.arange(group, dtype=jnp.int32)
    row_match = adapter_of_row[:, None] == adapter_ids[None, :]
    row_slot = jnp.sum(jnp.where(row_match, adapter_holder_slot[None, :], 0), axis=1)
    slot_mask = row_slot[None, :] == adapter_ids[:, None]
    before = jnp.cumsum(slot_mask.astype(jnp.int32), axis=1) - 1
    place = jnp.where(slot_mask, before, -1)
    pick = place[:, None, :] == jnp.arange(MOST, dtype=jnp.int32)[None, :, None]
    pick = pick.reshape(group * MOST, rows).astype(jnp.bfloat16)
    packed = jnp.dot(pick, hidden, preferred_element_type=jnp.float32).astype(jnp.bfloat16)
    packed = packed.reshape(group * blocks, BLOCK, depth)
    gathered = lax.all_to_all(packed, "tp", split_axis=0, concat_axis=0, tiled=True)
    partial_value = jnp.dot(hidden, down_matrix, preferred_element_type=jnp.float32)
    base = lax.psum_scatter(partial_value, "tp", scatter_dimension=1, tiled=True)
    own_rows = jnp.transpose(gathered.reshape(group, MOST, depth), (1, 0, 2))
    rank_rows = jnp.dot(
        own_rows.reshape(MOST, group * depth), shrink_matrices[0], preferred_element_type=jnp.float32
    ).astype(jnp.bfloat16)
    adapter_out = lax.dot_general(
        rank_rows, expand_matrices[0], (((1,), (1,)), ((), ())), preferred_element_type=jnp.float32
    ).astype(jnp.bfloat16)
    adapter_out = jnp.transpose(adapter_out.reshape(blocks, BLOCK, group, width), (2, 0, 1, 3))
    adapter_in = lax.all_to_all(
        adapter_out.reshape(group * blocks, BLOCK, width), "tp", split_axis=0, concat_axis=0, tiled=True
    )
    adapter_rows = lax.dot_general(
        pick,
        adapter_in.reshape(group * MOST, width),
        (((0,), (0,)), ((), ())),
        preferred_element_type=jnp.float32,
    )
    return (base + ADAPTER_SCALE * adapter_rows).astype(jnp.bfloat16)


def solution(mesh):
    in_specs = (
        P("rep", "tp"),
        P("tp", None),
        P(("rep", "tp"), None, None),
        P(("rep", "tp"), None, None),
        P("rep"),
        P("rep"),
    )
    out_specs = P("rep", "tp")
    return jax.shard_map(shards, mesh=mesh, in_specs=in_specs, out_specs=out_specs, check_vma=False)
```

```python
import functools

import jax
import jax.numpy as jnp
from jax import lax
from jax.experimental import pallas as pl
from jax.experimental.pallas import tpu as pltpu
from jax.sharding import PartitionSpec as P

ADAPTER_SCALE = 0.5
BLOCK = 4
MOST = 20
LANES = 128
F16_TOP = 14.0
PLANE = 4
HELD = 24
MARK_ROWS = 16


def in_hbm(value):
    return pltpu.with_memory_space_constraint(value, pltpu.HBM)


def xor_permute(value, group, offset):
    return lax.ppermute(value, "tp", [(i, i ^ offset) for i in range(group)])


def column_blocks_kernel(groups, order_ref, hidden_ref, down_ref, *refs):
    out_refs, held_ref, sems = refs[:groups], refs[groups], refs[groups + 1]
    count, depth, width = held_ref.shape
    parts = width // LANES
    pieces = sems.shape[1]
    cut = depth // pieces

    def copy(block, piece):
        start = pl.multiple_of(order_ref[block] * width, LANES)
        lines = pl.ds(piece * cut, cut)
        return pltpu.make_async_copy(
            down_ref.at[lines, pl.ds(start, width)], held_ref.at[block, lines], sems.at[block, piece]
        )

    for block in range(count):
        for piece in range(pieces):
            copy(block, piece).start()
    share = count // groups
    for block in range(count):
        for piece in range(pieces):
            copy(block, piece).wait()
        product = jnp.dot(hidden_ref[...], held_ref[block], preferred_element_type=jnp.float32)
        for lane in range(parts):
            out_refs[block // share][block % share * parts + lane] = product[
                :, lane * LANES : (lane + 1) * LANES
            ]


def column_blocks(hidden, down_matrix, order, width, groups=1):
    rows, depth = hidden.shape
    count = order.shape[0]
    pieces = 2 if depth % 32 == 0 else 1
    vmem = pl.BlockSpec(memory_space=pltpu.VMEM)
    out = jax.ShapeDtypeStruct((count // groups * width // LANES, rows, LANES), jnp.float32)
    return pl.pallas_call(
        functools.partial(column_blocks_kernel, groups),
        out_shape=[out] * groups,
        in_specs=[
            pl.BlockSpec(memory_space=pltpu.SMEM),
            vmem,
            pl.BlockSpec(memory_space=pl.ANY),
        ],
        out_specs=[vmem] * groups,
        scratch_shapes=[
            pltpu.VMEM((count, depth, width), jnp.bfloat16),
            pltpu.SemaphoreType.DMA((count, pieces)),
        ],
        compiler_params=pltpu.CompilerParams(vmem_limit_bytes=(12 + 12 * groups) * 2**20),
        cost_estimate=pl.CostEstimate(flops=1000, bytes_accessed=1000, transcendentals=0),
    )(order, hidden, in_hbm(down_matrix))


def pack_scaled(value):
    blocks, rows, lanes = value.shape
    peak = jnp.max(jnp.abs(value), axis=(0, 2))
    exponent = jnp.ceil(jnp.log2(jnp.maximum(peak, 2.0**-100)))
    scaled = (value * jnp.exp2(F16_TOP - exponent)[None, :, None]).astype(jnp.float16)
    marks = jnp.pad(exponent.astype(jnp.float16)[None], ((0, MARK_ROWS - 1), (0, lanes - rows)))
    return jnp.concatenate([scaled.reshape(blocks * rows, lanes), marks], axis=0)


def unpack_scaled(packed, rows):
    values, exponent = packed[:-MARK_ROWS], packed[-MARK_ROWS, :rows].astype(jnp.float32)
    values = values.reshape(-1, rows, packed.shape[1]).astype(jnp.float32)
    return values * jnp.exp2(exponent - F16_TOP)[None, :, None]


def pair_sums(hidden, down_matrix, group, order, width):
    half = group * width // LANES // PLANE
    rows = hidden.shape[0]
    share = group // PLANE

    def first():
        (far,) = column_blocks(hidden, down_matrix, order[:share], width)
        far_in = xor_permute(far, group, 1)
        (near,) = column_blocks(hidden, down_matrix, order[share : 2 * share], width)
        return pack_scaled(near + far_in)

    def first_idle():
        return jnp.zeros((half * rows + MARK_ROWS, LANES), jnp.float16)

    sent = lax.cond(order[0] >= 0, first, first_idle)
    pair_in = xor_permute(sent, group, 2)
    order, _ = lax.optimization_barrier((order, sent))

    def second():
        far, near = column_blocks(hidden, down_matrix, order[2 * share :], width, groups=2)
        return near + xor_permute(far, group, 1)

    def second_idle():
        return jnp.zeros((half, rows, LANES), jnp.float32)

    kept = lax.cond(order[1] >= 0, second, second_idle)
    return kept, pair_in


def line_sums(pair, group, width):
    rows = pair.shape[1]
    parts = width // LANES
    arrived = [
        xor_permute(pack_scaled(pair[i * parts : (i + 1) * parts]), group, 4 * i)
        for i in range(1, group // 4)
    ]
    total = pair[:parts]
    for packed in arrived:
        total = total + unpack_scaled(packed, rows)
    return jnp.transpose(total, (1, 0, 2)).reshape(rows, width)


def pack_kernel(
    blocks,
    orders,
    me_ref,
    slot_hbm,
    adapter_hbm,
    hidden_hbm,
    packed_hbm,
    pick_ref,
    order_ref,
    kept_ref,
    slot_ref,
    adapter_ref,
    hidden_ref,
    packed_ref,
    sems,
    out_sems,
):
    rows = hidden_ref.shape[0]
    group = slot_ref.shape[0]
    copies = [
        pltpu.make_async_copy(slot_hbm, slot_ref, sems.at[0]),
        pltpu.make_async_copy(adapter_hbm, adapter_ref, sems.at[1]),
        pltpu.make_async_copy(hidden_hbm, hidden_ref, sems.at[2]),
    ]
    for copy in copies:
        copy.start()
    for i, offset in enumerate(orders):
        order_ref[i] = me_ref[0] ^ offset
    ids = lax.broadcasted_iota(jnp.int32, (group, 1), 0)
    slots = jnp.zeros((group, 1), jnp.int32)
    copies[0].wait()
    for adapter in range(group):
        slots = jnp.where(ids == adapter, slot_ref[adapter], slots)
    copies[1].wait()
    adapter = adapter_ref[...]
    first = jnp.sum((adapter < ids).astype(jnp.int32), axis=1, keepdims=True)
    shift = jnp.where(adapter == ids, slots * (blocks * BLOCK) - first, 0)
    place = jnp.sum(shift, axis=0, keepdims=True) + lax.broadcasted_iota(jnp.int32, (1, rows), 1)
    copies[2].wait()
    pieces = out_sems.shape[0]
    size = packed_ref.shape[0] // pieces
    outs = []
    for piece in range(pieces):
        spots = lax.broadcasted_iota(jnp.int32, (size * BLOCK, rows), 0) + piece * size * BLOCK
        pick = jnp.where(spots == place, 1.0, 0.0).astype(jnp.bfloat16)
        packed = jnp.dot(pick, hidden_ref[...], preferred_element_type=jnp.float32)
        part = pl.ds(piece * size, size)
        packed_ref[part] = packed.astype(jnp.bfloat16).reshape(size, BLOCK, packed.shape[1])
        out = pltpu.make_async_copy(packed_ref.at[part], packed_hbm.at[part], out_sems.at[piece])
        out.start()
        outs.append(out)
    kept_ref[...] = hidden_ref[...]
    for k in range(PLANE):
        line = lax.broadcasted_iota(jnp.int32, (HELD, rows), 0)
        mine = (line + (me_ref[0] ^ k) * (blocks * BLOCK) == place) & (line < blocks * BLOCK)
        pick_ref[k * HELD : (k + 1) * HELD] = jnp.where(mine, 1.0, 0.0).astype(jnp.bfloat16)
    for out in outs:
        out.wait()


def pack_rows(hidden, adapter_of_row, adapter_holder_slot, me, orders):
    rows, depth = hidden.shape
    group = adapter_holder_slot.shape[0]
    blocks = MOST // BLOCK
    vmem = pl.BlockSpec(memory_space=pltpu.VMEM)
    smem = pl.BlockSpec(memory_space=pltpu.SMEM)
    anywhere = pl.BlockSpec(memory_space=pltpu.HBM)
    return pl.pallas_call(
        functools.partial(pack_kernel, blocks, orders),
        out_shape=(
            jax.ShapeDtypeStruct((group * blocks, BLOCK, depth), jnp.bfloat16),
            jax.ShapeDtypeStruct((PLANE * HELD, rows), jnp.bfloat16),
            jax.ShapeDtypeStruct((len(orders),), jnp.int32),
            jax.ShapeDtypeStruct((rows, depth), jnp.bfloat16),
        ),
        in_specs=[smem, anywhere, anywhere, anywhere],
        out_specs=(anywhere, vmem, smem, vmem),
        scratch_shapes=[
            pltpu.SMEM((group,), jnp.int32),
            pltpu.VMEM((1, rows), jnp.int32),
            pltpu.VMEM((rows, depth), jnp.bfloat16),
            pltpu.VMEM((group * blocks, BLOCK, depth), jnp.bfloat16),
            pltpu.SemaphoreType.DMA((3,)),
            pltpu.SemaphoreType.DMA((4,)),
        ],
        compiler_params=pltpu.CompilerParams(vmem_limit_bytes=24 * 2**20),
    )(me.reshape(1), in_hbm(adapter_holder_slot), in_hbm(adapter_of_row.reshape(1, rows)), in_hbm(hidden))


def adapter_kernel(parts, me_ref, rows_ref, expand_hbm, shrink_hbm, *refs):
    out_refs = refs[:PLANE]
    shrink_ref, expand_ref, total_ref, own_ref, sems, expand_sem = refs[PLANE:]
    me = me_ref[0]
    group, _, depth = shrink_ref.shape
    blocks = MOST // BLOCK

    def copy(source):
        return pltpu.make_async_copy(
            shrink_hbm.at[:, pl.ds(source * depth, depth)], shrink_ref.at[source], sems.at[source]
        )

    for source in range(group):
        copy(source).start()
    expand_copy = pltpu.make_async_copy(expand_hbm, expand_ref, expand_sem)
    expand_copy.start()
    for source in range(group):
        own = rows_ref[source * blocks : (source + 1) * blocks]
        own_ref[source, :MOST] = own.reshape(MOST, depth)
    total = jnp.zeros((MOST, total_ref.shape[1]), jnp.float32)
    for source in range(group):
        copy(source).wait()
        total += lax.dot_general(
            own_ref[source, :MOST], shrink_ref[source], (((1,), (1,)), ((), ())), preferred_element_type=jnp.float32
        )
    total_ref[...] = jnp.zeros_like(total_ref)
    total_ref[:MOST] = total
    rank_rows = total_ref[...].astype(jnp.bfloat16)
    expand_copy.wait()
    width = parts * LANES
    for k in range(PLANE):
        for line in range(group // PLANE):
            target = me ^ (PLANE * line + k)
            columns = pl.ds(pl.multiple_of(target * width, LANES), width)
            piece = jnp.dot(rank_rows, expand_ref[:, columns], preferred_element_type=jnp.float32)
            piece = piece.astype(jnp.bfloat16)
            for part in range(parts):
                out_refs[k][line * parts + part] = piece[:, part * LANES : (part + 1) * LANES]


def adapter_output(gathered, shrink, expand, group, me):
    rank = shrink.shape[0]
    model_width = expand.shape[1]
    depth = gathered.shape[2]
    parts = model_width // group // LANES
    held = (model_width // PLANE // LANES, HELD, LANES)
    vmem = pl.BlockSpec(memory_space=pltpu.VMEM)
    return pl.pallas_call(
        functools.partial(adapter_kernel, parts),
        out_shape=[jax.ShapeDtypeStruct(held, jnp.bfloat16)] * PLANE,
        in_specs=[
            pl.BlockSpec(memory_space=pltpu.SMEM),
            vmem,
            pl.BlockSpec(memory_space=pl.ANY),
            pl.BlockSpec(memory_space=pl.ANY),
        ],
        out_specs=[vmem] * PLANE,
        scratch_shapes=[
            pltpu.VMEM((group, rank, depth), jnp.bfloat16),
            pltpu.VMEM((rank, model_width), jnp.bfloat16),
            pltpu.VMEM((HELD, rank), jnp.float32),
            pltpu.VMEM((group, 2 * 16, depth), jnp.bfloat16),
            pltpu.SemaphoreType.DMA((group,)),
            pltpu.SemaphoreType.DMA,
        ],
        compiler_params=pltpu.CompilerParams(vmem_limit_bytes=24 * 2**20),
    )(me.reshape(1), gathered, in_hbm(expand), in_hbm(shrink))


def merge_kernel(pair_ref, pick_ref, *refs):
    in_refs, out_ref, held_ref = refs[:PLANE], refs[PLANE], refs[PLANE + 1]
    for k in range(PLANE):
        held_ref[:, k * HELD : (k + 1) * HELD] = in_refs[k][...]
    pick = pick_ref[...]
    for part in range(pair_ref.shape[0]):
        adapter_rows = lax.dot_general(
            pick, held_ref[part], (((0,), (0,)), ((), ())), preferred_element_type=jnp.float32
        )
        out_ref[part] = pair_ref[part] + ADAPTER_SCALE * adapter_rows


def merge_adapters(pair, pick, arrived):
    vmem = pl.BlockSpec(memory_space=pltpu.VMEM)
    return pl.pallas_call(
        merge_kernel,
        out_shape=jax.ShapeDtypeStruct(pair.shape, jnp.float32),
        in_specs=[vmem] * (2 + PLANE),
        out_specs=vmem,
        scratch_shapes=[pltpu.VMEM((pair.shape[0], PLANE * HELD, LANES), jnp.bfloat16)],
        compiler_params=pltpu.CompilerParams(vmem_limit_bytes=24 * 2**20),
    )(pair, pick, *arrived)


def shards_by_blocks(
    hidden, down_matrix, shrink_matrices, expand_matrices, adapter_of_row, adapter_holder_slot
):
    group = lax.axis_size("tp")
    me = lax.axis_index("tp")
    rows, depth = hidden.shape
    width = down_matrix.shape[1] // group
    quads = list(range(0, group, 4))
    orders = [q + k for k in (3, 2, 1, 0) for q in quads]
    packed, pick, order, kept_hidden = pack_rows(
        hidden, adapter_of_row, adapter_holder_slot, me, orders
    )
    gathered = lax.all_to_all(packed, "tp", split_axis=0, concat_axis=0, tiled=True)
    shrink = jnp.swapaxes(shrink_matrices, 1, 2)[0]
    kept, pair_in = pair_sums(kept_hidden, down_matrix, group, order, width)
    gathered, _ = lax.optimization_barrier((gathered, kept))
    expand = jnp.swapaxes(expand_matrices, 1, 2)[0]
    outs = adapter_output(gathered, shrink, expand, group, me)
    arrived = [outs[0]] + [xor_permute(outs[k], group, k) for k in range(1, PLANE)]
    pair = kept + unpack_scaled(pair_in, rows)
    merged = merge_adapters(pair, pick, arrived)
    return line_sums(merged, group, width).astype(jnp.bfloat16)


def shards(
    hidden, down_matrix, shrink_matrices, expand_matrices, adapter_of_row, adapter_holder_slot
):
    group = lax.axis_size("tp")
    rows, depth = hidden.shape
    width = down_matrix.shape[1] // group
    if width % LANES == 0 and depth % LANES == 0 and rows <= LANES and group >= PLANE and group & (group - 1) == 0:
        return shards_by_blocks(
            hidden, down_matrix, shrink_matrices, expand_matrices, adapter_of_row, adapter_holder_slot
        )
    blocks = MOST // BLOCK
    adapter_ids = jnp.arange(group, dtype=jnp.int32)
    row_match = adapter_of_row[:, None] == adapter_ids[None, :]
    row_slot = jnp.sum(jnp.where(row_match, adapter_holder_slot[None, :], 0), axis=1)
    slot_mask = row_slot[None, :] == adapter_ids[:, None]
    before = jnp.cumsum(slot_mask.astype(jnp.int32), axis=1) - 1
    place = jnp.where(slot_mask, before, -1)
    pick = place[:, None, :] == jnp.arange(MOST, dtype=jnp.int32)[None, :, None]
    pick = pick.reshape(group * MOST, rows).astype(jnp.bfloat16)
    packed = jnp.dot(pick, hidden, preferred_element_type=jnp.float32).astype(jnp.bfloat16)
    packed = packed.reshape(group * blocks, BLOCK, depth)
    gathered = lax.all_to_all(packed, "tp", split_axis=0, concat_axis=0, tiled=True)
    partial_value = jnp.dot(hidden, down_matrix, preferred_element_type=jnp.float32)
    base = lax.psum_scatter(partial_value, "tp", scatter_dimension=1, tiled=True)
    own_rows = jnp.transpose(gathered.reshape(group, MOST, depth), (1, 0, 2))
    rank_rows = jnp.dot(
        own_rows.reshape(MOST, group * depth), shrink_matrices[0], preferred_element_type=jnp.float32
    ).astype(jnp.bfloat16)
    adapter_out = lax.dot_general(
        rank_rows, expand_matrices[0], (((1,), (1,)), ((), ())), preferred_element_type=jnp.float32
    ).astype(jnp.bfloat16)
    adapter_out = jnp.transpose(adapter_out.reshape(blocks, BLOCK, group, width), (2, 0, 1, 3))
    adapter_in = lax.all_to_all(
        adapter_out.reshape(group * blocks, BLOCK, width), "tp", split_axis=0, concat_axis=0, tiled=True
    )
    adapter_rows = lax.dot_general(
        pick,
        adapter_in.reshape(group * MOST, width),
        (((0,), (0,)), ((), ())),
        preferred_element_type=jnp.float32,
    )
    return (base + ADAPTER_SCALE * adapter_rows).astype(jnp.bfloat16)


def solution(mesh):
    in_specs = (
        P("rep", "tp"),
        P("tp", None),
        P(("rep", "tp"), None, None),
        P(("rep", "tp"), None, None),
        P("rep"),
        P("rep"),
    )
    out_specs = P("rep", "tp")
    return jax.shard_map(shards, mesh=mesh, in_specs=in_specs, out_specs=out_specs, check_vma=False)
```

```python
import functools

import jax
import jax.numpy as jnp
from jax import lax
from jax.experimental import pallas as pl
from jax.experimental.pallas import tpu as pltpu
from jax.sharding import PartitionSpec as P

ADAPTER_SCALE = 0.5
BLOCK = 4
MOST = 20
LANES = 128
F16_TOP = 14.0
PLANE = 4
HELD = 24
MARK_ROWS = 16


def in_hbm(value):
    return pltpu.with_memory_space_constraint(value, pltpu.HBM)


def xor_permute(value, group, offset):
    return lax.ppermute(value, "tp", [(i, i ^ offset) for i in range(group)])


def column_blocks_kernel(groups, order_ref, hidden_ref, down_ref, *refs):
    out_refs, held_ref, sems = refs[:groups], refs[groups], refs[groups + 1]
    count, depth, width = held_ref.shape
    parts = width // LANES
    pieces = sems.shape[1]
    cut = depth // pieces

    def copy(block, piece):
        start = pl.multiple_of(order_ref[block] * width, LANES)
        lines = pl.ds(piece * cut, cut)
        return pltpu.make_async_copy(
            down_ref.at[lines, pl.ds(start, width)], held_ref.at[block, lines], sems.at[block, piece]
        )

    for block in range(count):
        for piece in range(pieces):
            copy(block, piece).start()
    share = count // groups
    for block in range(count):
        for piece in range(pieces):
            copy(block, piece).wait()
        product = jnp.dot(hidden_ref[...], held_ref[block], preferred_element_type=jnp.float32)
        for lane in range(parts):
            out_refs[block // share][block % share * parts + lane] = product[
                :, lane * LANES : (lane + 1) * LANES
            ]


def column_blocks(hidden, down_matrix, order, width, groups=1):
    rows, depth = hidden.shape
    count = order.shape[0]
    pieces = 2 if depth % 32 == 0 else 1
    vmem = pl.BlockSpec(memory_space=pltpu.VMEM)
    out = jax.ShapeDtypeStruct((count // groups * width // LANES, rows, LANES), jnp.float32)
    return pl.pallas_call(
        functools.partial(column_blocks_kernel, groups),
        out_shape=[out] * groups,
        in_specs=[
            pl.BlockSpec(memory_space=pltpu.SMEM),
            vmem,
            pl.BlockSpec(memory_space=pl.ANY),
        ],
        out_specs=[vmem] * groups,
        scratch_shapes=[
            pltpu.VMEM((count, depth, width), jnp.bfloat16),
            pltpu.SemaphoreType.DMA((count, pieces)),
        ],
        compiler_params=pltpu.CompilerParams(vmem_limit_bytes=(12 + 12 * groups) * 2**20),
        cost_estimate=pl.CostEstimate(flops=1000, bytes_accessed=1000, transcendentals=0),
    )(order, hidden, in_hbm(down_matrix))


def pack_scaled(value):
    blocks, rows, lanes = value.shape
    peak = jnp.max(jnp.abs(value), axis=(0, 2))
    exponent = jnp.ceil(jnp.log2(jnp.maximum(peak, 2.0**-100)))
    scaled = (value * jnp.exp2(F16_TOP - exponent)[None, :, None]).astype(jnp.float16)
    marks = jnp.pad(exponent.astype(jnp.float16)[None], ((0, MARK_ROWS - 1), (0, lanes - rows)))
    return jnp.concatenate([scaled.reshape(blocks * rows, lanes), marks], axis=0)


def unpack_scaled(packed, rows):
    values, exponent = packed[:-MARK_ROWS], packed[-MARK_ROWS, :rows].astype(jnp.float32)
    values = values.reshape(-1, rows, packed.shape[1]).astype(jnp.float32)
    return values * jnp.exp2(exponent - F16_TOP)[None, :, None]


def pair_sums(hidden, down_matrix, group, order, width):
    half = group * width // LANES // PLANE
    rows = hidden.shape[0]
    share = group // PLANE

    def first():
        (far,) = column_blocks(hidden, down_matrix, order[:share], width)
        far_in = xor_permute(far, group, 1)
        (near,) = column_blocks(hidden, down_matrix, order[share : 2 * share], width)
        return pack_scaled(near + far_in)

    def first_idle():
        return jnp.zeros((half * rows + MARK_ROWS, LANES), jnp.float16)

    sent = lax.cond(order[0] >= 0, first, first_idle)
    pair_in = xor_permute(sent, group, 2)
    order, _ = lax.optimization_barrier((order, sent))

    def second():
        far, near = column_blocks(hidden, down_matrix, order[2 * share :], width, groups=2)
        return near + xor_permute(far, group, 1)

    def second_idle():
        return jnp.zeros((half, rows, LANES), jnp.float32)

    kept = lax.cond(order[1] >= 0, second, second_idle)
    return kept, pair_in


def line_sums(pair, group, width):
    rows = pair.shape[1]
    parts = width // LANES
    arrived = [
        xor_permute(pack_scaled(pair[i * parts : (i + 1) * parts]), group, 4 * i)
        for i in range(1, group // 4)
    ]
    total = pair[:parts]
    for packed in arrived:
        total = total + unpack_scaled(packed, rows)
    return jnp.transpose(total, (1, 0, 2)).reshape(rows, width)


def pack_kernel(
    blocks,
    orders,
    me_ref,
    slot_hbm,
    adapter_hbm,
    hidden_hbm,
    packed_ref,
    pick_ref,
    order_ref,
    kept_ref,
    slot_ref,
    adapter_ref,
    hidden_ref,
    sems,
):
    rows = hidden_ref.shape[0]
    group = slot_ref.shape[0]
    copies = [
        pltpu.make_async_copy(slot_hbm, slot_ref, sems.at[0]),
        pltpu.make_async_copy(adapter_hbm, adapter_ref, sems.at[1]),
        pltpu.make_async_copy(hidden_hbm, hidden_ref, sems.at[2]),
    ]
    for copy in copies:
        copy.start()
    for i, offset in enumerate(orders):
        order_ref[i] = me_ref[0] ^ offset
    ids = lax.broadcasted_iota(jnp.int32, (group, 1), 0)
    slots = jnp.zeros((group, 1), jnp.int32)
    copies[0].wait()
    for adapter in range(group):
        slots = jnp.where(ids == adapter, slot_ref[adapter], slots)
    copies[1].wait()
    adapter = adapter_ref[...]
    first = jnp.sum((adapter < ids).astype(jnp.int32), axis=1, keepdims=True)
    shift = jnp.where(adapter == ids, slots * (blocks * BLOCK) - first, 0)
    place = jnp.sum(shift, axis=0, keepdims=True) + lax.broadcasted_iota(jnp.int32, (1, rows), 1)
    spots = lax.broadcasted_iota(jnp.int32, (group * blocks * BLOCK, rows), 0)
    pick = jnp.where(spots == place, 1.0, 0.0).astype(jnp.bfloat16)
    for k in range(PLANE):
        line = lax.broadcasted_iota(jnp.int32, (HELD, rows), 0)
        mine = (line + (me_ref[0] ^ k) * (blocks * BLOCK) == place) & (line < blocks * BLOCK)
        pick_ref[k * HELD : (k + 1) * HELD] = jnp.where(mine, 1.0, 0.0).astype(jnp.bfloat16)
    copies[2].wait()
    packed = jnp.dot(pick, hidden_ref[...], preferred_element_type=jnp.float32)
    packed_ref[...] = packed.astype(jnp.bfloat16).reshape(packed_ref.shape)
    kept_ref[...] = hidden_ref[...]


def pack_rows(hidden, adapter_of_row, adapter_holder_slot, me, orders):
    rows, depth = hidden.shape
    group = adapter_holder_slot.shape[0]
    blocks = MOST // BLOCK
    vmem = pl.BlockSpec(memory_space=pltpu.VMEM)
    smem = pl.BlockSpec(memory_space=pltpu.SMEM)
    anywhere = pl.BlockSpec(memory_space=pltpu.HBM)
    return pl.pallas_call(
        functools.partial(pack_kernel, blocks, orders),
        out_shape=(
            jax.ShapeDtypeStruct((group * blocks, BLOCK, depth), jnp.bfloat16),
            jax.ShapeDtypeStruct((PLANE * HELD, rows), jnp.bfloat16),
            jax.ShapeDtypeStruct((len(orders),), jnp.int32),
            jax.ShapeDtypeStruct((rows, depth), jnp.bfloat16),
        ),
        in_specs=[smem, anywhere, anywhere, anywhere],
        out_specs=(vmem, vmem, smem, vmem),
        scratch_shapes=[
            pltpu.SMEM((group,), jnp.int32),
            pltpu.VMEM((1, rows), jnp.int32),
            pltpu.VMEM((rows, depth), jnp.bfloat16),
            pltpu.SemaphoreType.DMA((3,)),
        ],
        compiler_params=pltpu.CompilerParams(vmem_limit_bytes=24 * 2**20),
    )(me.reshape(1), in_hbm(adapter_holder_slot), in_hbm(adapter_of_row.reshape(1, rows)), in_hbm(hidden))


def adapter_kernel(parts, me_ref, rows_ref, expand_hbm, shrink_hbm, *refs):
    out_refs = refs[:PLANE]
    shrink_ref, expand_ref, total_ref, own_ref, sems, expand_sem = refs[PLANE:]
    me = me_ref[0]
    group, _, depth = shrink_ref.shape
    blocks = MOST // BLOCK

    def copy(source):
        return pltpu.make_async_copy(
            shrink_hbm.at[:, pl.ds(source * depth, depth)], shrink_ref.at[source], sems.at[source]
        )

    for source in range(group):
        copy(source).start()
    expand_copy = pltpu.make_async_copy(expand_hbm, expand_ref, expand_sem)
    expand_copy.start()
    for source in range(group):
        own = rows_ref[source * blocks : (source + 1) * blocks]
        own_ref[source, :MOST] = own.reshape(MOST, depth)
    total = jnp.zeros((MOST, total_ref.shape[1]), jnp.float32)
    for source in range(group):
        copy(source).wait()
        total += lax.dot_general(
            own_ref[source, :MOST], shrink_ref[source], (((1,), (1,)), ((), ())), preferred_element_type=jnp.float32
        )
    total_ref[...] = jnp.zeros_like(total_ref)
    total_ref[:MOST] = total
    rank_rows = total_ref[...].astype(jnp.bfloat16)
    expand_copy.wait()
    width = parts * LANES
    for k in range(PLANE):
        for line in range(group // PLANE):
            target = me ^ (PLANE * line + k)
            columns = pl.ds(pl.multiple_of(target * width, LANES), width)
            piece = jnp.dot(rank_rows, expand_ref[:, columns], preferred_element_type=jnp.float32)
            piece = piece.astype(jnp.bfloat16)
            for part in range(parts):
                out_refs[k][line * parts + part] = piece[:, part * LANES : (part + 1) * LANES]


def adapter_output(gathered, shrink, expand, group, me):
    rank = shrink.shape[0]
    model_width = expand.shape[1]
    depth = gathered.shape[2]
    parts = model_width // group // LANES
    held = (model_width // PLANE // LANES, HELD, LANES)
    vmem = pl.BlockSpec(memory_space=pltpu.VMEM)
    return pl.pallas_call(
        functools.partial(adapter_kernel, parts),
        out_shape=[jax.ShapeDtypeStruct(held, jnp.bfloat16)] * PLANE,
        in_specs=[
            pl.BlockSpec(memory_space=pltpu.SMEM),
            vmem,
            pl.BlockSpec(memory_space=pl.ANY),
            pl.BlockSpec(memory_space=pl.ANY),
        ],
        out_specs=[vmem] * PLANE,
        scratch_shapes=[
            pltpu.VMEM((group, rank, depth), jnp.bfloat16),
            pltpu.VMEM((rank, model_width), jnp.bfloat16),
            pltpu.VMEM((HELD, rank), jnp.float32),
            pltpu.VMEM((group, 2 * 16, depth), jnp.bfloat16),
            pltpu.SemaphoreType.DMA((group,)),
            pltpu.SemaphoreType.DMA,
        ],
        compiler_params=pltpu.CompilerParams(vmem_limit_bytes=24 * 2**20),
    )(me.reshape(1), gathered, in_hbm(expand), in_hbm(shrink))


def merge_kernel(pair_ref, pick_ref, *refs):
    in_refs, out_ref, held_ref = refs[:PLANE], refs[PLANE], refs[PLANE + 1]
    for k in range(PLANE):
        held_ref[:, k * HELD : (k + 1) * HELD] = in_refs[k][...]
    pick = pick_ref[...]
    for part in range(pair_ref.shape[0]):
        adapter_rows = lax.dot_general(
            pick, held_ref[part], (((0,), (0,)), ((), ())), preferred_element_type=jnp.float32
        )
        out_ref[part] = pair_ref[part] + ADAPTER_SCALE * adapter_rows


def merge_adapters(pair, pick, arrived):
    vmem = pl.BlockSpec(memory_space=pltpu.VMEM)
    return pl.pallas_call(
        merge_kernel,
        out_shape=jax.ShapeDtypeStruct(pair.shape, jnp.float32),
        in_specs=[vmem] * (2 + PLANE),
        out_specs=vmem,
        scratch_shapes=[pltpu.VMEM((pair.shape[0], PLANE * HELD, LANES), jnp.bfloat16)],
        compiler_params=pltpu.CompilerParams(vmem_limit_bytes=24 * 2**20),
    )(pair, pick, *arrived)


def shards_by_blocks(
    hidden, down_matrix, shrink_matrices, expand_matrices, adapter_of_row, adapter_holder_slot
):
    group = lax.axis_size("tp")
    me = lax.axis_index("tp")
    rows, depth = hidden.shape
    width = down_matrix.shape[1] // group
    quads = list(range(0, group, 4))
    orders = [q + k for k in (3, 2, 1, 0) for q in quads]
    packed, pick, order, kept_hidden = pack_rows(
        hidden, adapter_of_row, adapter_holder_slot, me, orders
    )
    packed = pltpu.with_memory_space_constraint(packed, pltpu.VMEM)
    gathered = lax.all_to_all(packed, "tp", split_axis=0, concat_axis=0, tiled=True)
    shrink = jnp.swapaxes(shrink_matrices, 1, 2)[0]
    kept, pair_in = pair_sums(kept_hidden, down_matrix, group, order, width)
    gathered, _ = lax.optimization_barrier((gathered, kept))
    expand = jnp.swapaxes(expand_matrices, 1, 2)[0]
    outs = adapter_output(gathered, shrink, expand, group, me)
    arrived = [outs[0]] + [xor_permute(outs[k], group, k) for k in range(1, PLANE)]
    pair = kept + unpack_scaled(pair_in, rows)
    merged = merge_adapters(pair, pick, arrived)
    return line_sums(merged, group, width).astype(jnp.bfloat16)


def shards(
    hidden, down_matrix, shrink_matrices, expand_matrices, adapter_of_row, adapter_holder_slot
):
    group = lax.axis_size("tp")
    rows, depth = hidden.shape
    width = down_matrix.shape[1] // group
    if width % LANES == 0 and depth % LANES == 0 and rows <= LANES and group >= PLANE and group & (group - 1) == 0:
        return shards_by_blocks(
            hidden, down_matrix, shrink_matrices, expand_matrices, adapter_of_row, adapter_holder_slot
        )
    blocks = MOST // BLOCK
    adapter_ids = jnp.arange(group, dtype=jnp.int32)
    row_match = adapter_of_row[:, None] == adapter_ids[None, :]
    row_slot = jnp.sum(jnp.where(row_match, adapter_holder_slot[None, :], 0), axis=1)
    slot_mask = row_slot[None, :] == adapter_ids[:, None]
    before = jnp.cumsum(slot_mask.astype(jnp.int32), axis=1) - 1
    place = jnp.where(slot_mask, before, -1)
    pick = place[:, None, :] == jnp.arange(MOST, dtype=jnp.int32)[None, :, None]
    pick = pick.reshape(group * MOST, rows).astype(jnp.bfloat16)
    packed = jnp.dot(pick, hidden, preferred_element_type=jnp.float32).astype(jnp.bfloat16)
    packed = packed.reshape(group * blocks, BLOCK, depth)
    gathered = lax.all_to_all(packed, "tp", split_axis=0, concat_axis=0, tiled=True)
    partial_value = jnp.dot(hidden, down_matrix, preferred_element_type=jnp.float32)
    base = lax.psum_scatter(partial_value, "tp", scatter_dimension=1, tiled=True)
    own_rows = jnp.transpose(gathered.reshape(group, MOST, depth), (1, 0, 2))
    rank_rows = jnp.dot(
        own_rows.reshape(MOST, group * depth), shrink_matrices[0], preferred_element_type=jnp.float32
    ).astype(jnp.bfloat16)
    adapter_out = lax.dot_general(
        rank_rows, expand_matrices[0], (((1,), (1,)), ((), ())), preferred_element_type=jnp.float32
    ).astype(jnp.bfloat16)
    adapter_out = jnp.transpose(adapter_out.reshape(blocks, BLOCK, group, width), (2, 0, 1, 3))
    adapter_in = lax.all_to_all(
        adapter_out.reshape(group * blocks, BLOCK, width), "tp", split_axis=0, concat_axis=0, tiled=True
    )
    adapter_rows = lax.dot_general(
        pick,
        adapter_in.reshape(group * MOST, width),
        (((0,), (0,)), ((), ())),
        preferred_element_type=jnp.float32,
    )
    return (base + ADAPTER_SCALE * adapter_rows).astype(jnp.bfloat16)


def solution(mesh):
    in_specs = (
        P("rep", "tp"),
        P("tp", None),
        P(("rep", "tp"), None, None),
        P(("rep", "tp"), None, None),
        P("rep"),
        P("rep"),
    )
    out_specs = P("rep", "tp")
    return jax.shard_map(shards, mesh=mesh, in_specs=in_specs, out_specs=out_specs, check_vma=False)
```

```python
import functools

import jax
import jax.numpy as jnp
from jax import lax
from jax.experimental import pallas as pl
from jax.experimental.pallas import tpu as pltpu
from jax.sharding import PartitionSpec as P

ADAPTER_SCALE = 0.5
BLOCK = 4
MOST = 20
LANES = 128
F16_TOP = 14.0
PLANE = 4
HELD = 24
MARK_ROWS = 16


def in_hbm(value):
    return pltpu.with_memory_space_constraint(value, pltpu.HBM)


def xor_permute(value, group, offset):
    return lax.ppermute(value, "tp", [(i, i ^ offset) for i in range(group)])


def column_blocks_kernel(groups, order_ref, hidden_ref, down_ref, *refs):
    out_refs, held_ref, sems = refs[:groups], refs[groups], refs[groups + 1]
    count, depth, width = held_ref.shape
    parts = width // LANES
    pieces = sems.shape[1]
    cut = depth // pieces

    def copy(block, piece):
        start = pl.multiple_of(order_ref[block] * width, LANES)
        lines = pl.ds(piece * cut, cut)
        return pltpu.make_async_copy(
            down_ref.at[lines, pl.ds(start, width)], held_ref.at[block, lines], sems.at[block, piece]
        )

    for block in range(count):
        for piece in range(pieces):
            copy(block, piece).start()
    share = count // groups
    for block in range(count):
        for piece in range(pieces):
            copy(block, piece).wait()
        product = jnp.dot(hidden_ref[...], held_ref[block], preferred_element_type=jnp.float32)
        for lane in range(parts):
            out_refs[block // share][block % share * parts + lane] = product[
                :, lane * LANES : (lane + 1) * LANES
            ]


def column_blocks(hidden, down_matrix, order, width, groups=1):
    rows, depth = hidden.shape
    count = order.shape[0]
    pieces = 2 if depth % 32 == 0 else 1
    vmem = pl.BlockSpec(memory_space=pltpu.VMEM)
    out = jax.ShapeDtypeStruct((count // groups * width // LANES, rows, LANES), jnp.float32)
    return pl.pallas_call(
        functools.partial(column_blocks_kernel, groups),
        out_shape=[out] * groups,
        in_specs=[
            pl.BlockSpec(memory_space=pltpu.SMEM),
            vmem,
            pl.BlockSpec(memory_space=pl.ANY),
        ],
        out_specs=[vmem] * groups,
        scratch_shapes=[
            pltpu.VMEM((count, depth, width), jnp.bfloat16),
            pltpu.SemaphoreType.DMA((count, pieces)),
        ],
        compiler_params=pltpu.CompilerParams(vmem_limit_bytes=(12 + 12 * groups) * 2**20),
        cost_estimate=pl.CostEstimate(flops=1000, bytes_accessed=1000, transcendentals=0),
    )(order, hidden, in_hbm(down_matrix))


def pack_scaled(value):
    blocks, rows, lanes = value.shape
    peak = jnp.max(jnp.abs(value), axis=(0, 2))
    exponent = jnp.ceil(jnp.log2(jnp.maximum(peak, 2.0**-100)))
    scaled = (value * jnp.exp2(F16_TOP - exponent)[None, :, None]).astype(jnp.float16)
    marks = jnp.pad(exponent.astype(jnp.float16)[None], ((0, MARK_ROWS - 1), (0, lanes - rows)))
    return jnp.concatenate([scaled.reshape(blocks * rows, lanes), marks], axis=0)


def unpack_scaled(packed, rows):
    values, exponent = packed[:-MARK_ROWS], packed[-MARK_ROWS, :rows].astype(jnp.float32)
    values = values.reshape(-1, rows, packed.shape[1]).astype(jnp.float32)
    return values * jnp.exp2(exponent - F16_TOP)[None, :, None]


def pair_sums(hidden, down_matrix, group, order, width):
    half = group * width // LANES // PLANE
    rows = hidden.shape[0]
    share = group // PLANE

    def first():
        (far,) = column_blocks(hidden, down_matrix, order[:share], width)
        far_in = xor_permute(far, group, 1)
        (near,) = column_blocks(hidden, down_matrix, order[share : 2 * share], width)
        return pack_scaled(near + far_in)

    def first_idle():
        return jnp.zeros((half * rows + MARK_ROWS, LANES), jnp.float16)

    sent = lax.cond(order[0] >= 0, first, first_idle)
    pair_in = xor_permute(sent, group, 2)
    order, _ = lax.optimization_barrier((order, sent))

    def second():
        far, near = column_blocks(hidden, down_matrix, order[2 * share :], width, groups=2)
        return near + xor_permute(far, group, 1)

    def second_idle():
        return jnp.zeros((half, rows, LANES), jnp.float32)

    kept = lax.cond(order[1] >= 0, second, second_idle)
    return kept, pair_in


def line_sums(pair, group, width):
    rows = pair.shape[1]
    parts = width // LANES
    arrived = [
        xor_permute(pack_scaled(pair[i * parts : (i + 1) * parts]), group, 4 * i)
        for i in range(1, group // 4)
    ]
    total = pair[:parts]
    for packed in arrived:
        total = total + unpack_scaled(packed, rows)
    return jnp.transpose(total, (1, 0, 2)).reshape(rows, width)


def pack_kernel(
    blocks,
    orders,
    me_ref,
    slot_hbm,
    adapter_hbm,
    hidden_hbm,
    packed_ref,
    pick_ref,
    order_ref,
    kept_ref,
    slot_ref,
    adapter_ref,
    hidden_ref,
    sems,
):
    rows = hidden_ref.shape[0]
    group = slot_ref.shape[0]
    copies = [
        pltpu.make_async_copy(slot_hbm, slot_ref, sems.at[0]),
        pltpu.make_async_copy(adapter_hbm, adapter_ref, sems.at[1]),
        pltpu.make_async_copy(hidden_hbm, hidden_ref, sems.at[2]),
    ]
    for copy in copies:
        copy.start()
    for i, offset in enumerate(orders):
        order_ref[i] = me_ref[0] ^ offset
    ids = lax.broadcasted_iota(jnp.int32, (group, 1), 0)
    slots = jnp.zeros((group, 1), jnp.int32)
    copies[0].wait()
    for adapter in range(group):
        slots = jnp.where(ids == adapter, slot_ref[adapter], slots)
    copies[1].wait()
    adapter = adapter_ref[...]
    first = jnp.sum((adapter < ids).astype(jnp.int32), axis=1, keepdims=True)
    slot = jnp.sum(jnp.where(adapter == ids, slots, 0), axis=0, keepdims=True)
    first = jnp.sum(jnp.where(adapter == ids, first, 0), axis=0, keepdims=True)
    index = lax.broadcasted_iota(jnp.int32, (1, rows), 1) - first
    held = blocks * BLOCK
    far = lax.rem(lax.div(slot, 2), 2)
    rank = far * (group // 2) + lax.div(slot, PLANE) * 2 + lax.rem(slot, 2)
    spots = lax.broadcasted_iota(jnp.int32, (group * held, rows), 0)
    pick = jnp.where(spots == rank * held + index, 1.0, 0.0).astype(jnp.bfloat16)
    for k in range(PLANE):
        line = lax.broadcasted_iota(jnp.int32, (HELD, rows), 0)
        mine = (slot == me_ref[0] ^ k) & (index == line)
        pick_ref[k * HELD : (k + 1) * HELD] = jnp.where(mine, 1.0, 0.0).astype(jnp.bfloat16)
    copies[2].wait()
    packed = jnp.dot(pick, hidden_ref[...], preferred_element_type=jnp.float32)
    packed_ref[...] = packed.astype(jnp.bfloat16).reshape(packed_ref.shape)
    kept_ref[...] = hidden_ref[...]


def pack_rows(hidden, adapter_of_row, adapter_holder_slot, me, orders):
    rows, depth = hidden.shape
    group = adapter_holder_slot.shape[0]
    blocks = MOST // BLOCK
    vmem = pl.BlockSpec(memory_space=pltpu.VMEM)
    smem = pl.BlockSpec(memory_space=pltpu.SMEM)
    anywhere = pl.BlockSpec(memory_space=pltpu.HBM)
    return pl.pallas_call(
        functools.partial(pack_kernel, blocks, orders),
        out_shape=(
            jax.ShapeDtypeStruct((group * blocks, BLOCK, depth), jnp.bfloat16),
            jax.ShapeDtypeStruct((PLANE * HELD, rows), jnp.bfloat16),
            jax.ShapeDtypeStruct((len(orders),), jnp.int32),
            jax.ShapeDtypeStruct((rows, depth), jnp.bfloat16),
        ),
        in_specs=[smem, anywhere, anywhere, anywhere],
        out_specs=(vmem, vmem, smem, vmem),
        scratch_shapes=[
            pltpu.SMEM((group,), jnp.int32),
            pltpu.VMEM((1, rows), jnp.int32),
            pltpu.VMEM((rows, depth), jnp.bfloat16),
            pltpu.SemaphoreType.DMA((3,)),
        ],
        compiler_params=pltpu.CompilerParams(vmem_limit_bytes=24 * 2**20),
    )(me.reshape(1), in_hbm(adapter_holder_slot), in_hbm(adapter_of_row.reshape(1, rows)), in_hbm(hidden))


def adapter_kernel(parts, ranks, me_ref, rows_ref, expand_hbm, shrink_hbm, *refs):
    out_refs = refs[:PLANE]
    shrink_ref, expand_ref, total_ref, own_ref, sems, expand_sem = refs[PLANE:]
    me = me_ref[0]
    group, _, depth = shrink_ref.shape
    blocks = MOST // BLOCK

    def copy(source):
        return pltpu.make_async_copy(
            shrink_hbm.at[:, pl.ds(ranks[source] * depth, depth)],
            shrink_ref.at[source],
            sems.at[source],
        )

    for source in range(group):
        copy(source).start()
    expand_copy = pltpu.make_async_copy(expand_hbm, expand_ref, expand_sem)
    expand_copy.start()
    for source in range(group):
        own = rows_ref[source * blocks : (source + 1) * blocks]
        own_ref[source, :MOST] = own.reshape(MOST, depth)
    total = jnp.zeros((MOST, total_ref.shape[1]), jnp.float32)
    for source in range(group):
        copy(source).wait()
        total += lax.dot_general(
            own_ref[source, :MOST], shrink_ref[source], (((1,), (1,)), ((), ())), preferred_element_type=jnp.float32
        )
    total_ref[...] = jnp.zeros_like(total_ref)
    total_ref[:MOST] = total
    rank_rows = total_ref[...].astype(jnp.bfloat16)
    expand_copy.wait()
    width = parts * LANES
    for k in range(PLANE):
        for line in range(group // PLANE):
            target = me ^ (PLANE * line + k)
            columns = pl.ds(pl.multiple_of(target * width, LANES), width)
            piece = jnp.dot(rank_rows, expand_ref[:, columns], preferred_element_type=jnp.float32)
            piece = piece.astype(jnp.bfloat16)
            for part in range(parts):
                out_refs[k][line * parts + part] = piece[:, part * LANES : (part + 1) * LANES]


def adapter_output(gathered, shrink, expand, group, me, ranks):
    rank = shrink.shape[0]
    model_width = expand.shape[1]
    depth = gathered.shape[2]
    parts = model_width // group // LANES
    held = (model_width // PLANE // LANES, HELD, LANES)
    vmem = pl.BlockSpec(memory_space=pltpu.VMEM)
    return pl.pallas_call(
        functools.partial(adapter_kernel, parts, ranks),
        out_shape=[jax.ShapeDtypeStruct(held, jnp.bfloat16)] * PLANE,
        in_specs=[
            pl.BlockSpec(memory_space=pltpu.SMEM),
            vmem,
            pl.BlockSpec(memory_space=pl.ANY),
            pl.BlockSpec(memory_space=pl.ANY),
        ],
        out_specs=[vmem] * PLANE,
        scratch_shapes=[
            pltpu.VMEM((group, rank, depth), jnp.bfloat16),
            pltpu.VMEM((rank, model_width), jnp.bfloat16),
            pltpu.VMEM((HELD, rank), jnp.float32),
            pltpu.VMEM((group, 2 * 16, depth), jnp.bfloat16),
            pltpu.SemaphoreType.DMA((group,)),
            pltpu.SemaphoreType.DMA,
        ],
        compiler_params=pltpu.CompilerParams(vmem_limit_bytes=24 * 2**20),
    )(me.reshape(1), gathered, in_hbm(expand), in_hbm(shrink))


def merge_kernel(pair_ref, pick_ref, *refs):
    in_refs, out_ref, held_ref = refs[:PLANE], refs[PLANE], refs[PLANE + 1]
    for k in range(PLANE):
        held_ref[:, k * HELD : (k + 1) * HELD] = in_refs[k][...]
    pick = pick_ref[...]
    for part in range(pair_ref.shape[0]):
        adapter_rows = lax.dot_general(
            pick, held_ref[part], (((0,), (0,)), ((), ())), preferred_element_type=jnp.float32
        )
        out_ref[part] = pair_ref[part] + ADAPTER_SCALE * adapter_rows


def merge_adapters(pair, pick, arrived):
    vmem = pl.BlockSpec(memory_space=pltpu.VMEM)
    return pl.pallas_call(
        merge_kernel,
        out_shape=jax.ShapeDtypeStruct(pair.shape, jnp.float32),
        in_specs=[vmem] * (2 + PLANE),
        out_specs=vmem,
        scratch_shapes=[pltpu.VMEM((pair.shape[0], PLANE * HELD, LANES), jnp.bfloat16)],
        compiler_params=pltpu.CompilerParams(vmem_limit_bytes=24 * 2**20),
    )(pair, pick, *arrived)


def shards_by_blocks(
    hidden, down_matrix, shrink_matrices, expand_matrices, adapter_of_row, adapter_holder_slot
):
    group = lax.axis_size("tp")
    me = lax.axis_index("tp")
    rows, depth = hidden.shape
    width = down_matrix.shape[1] // group
    quads = list(range(0, group, 4))
    orders = [q + k for k in (3, 2, 1, 0) for q in quads]
    half = group // 2
    ranks = [i % half // 2 * PLANE + i // half * 2 + i % 2 for i in range(group)]
    packed, pick, order, kept_hidden = pack_rows(
        hidden, adapter_of_row, adapter_holder_slot, me, orders
    )
    gathered = lax.all_to_all(
        packed, "tp", split_axis=0, concat_axis=0, axis_index_groups=[ranks], tiled=True
    )
    shrink = jnp.swapaxes(shrink_matrices, 1, 2)[0]
    kept, pair_in = pair_sums(kept_hidden, down_matrix, group, order, width)
    gathered, _ = lax.optimization_barrier((gathered, kept))
    expand = jnp.swapaxes(expand_matrices, 1, 2)[0]
    outs = adapter_output(gathered, shrink, expand, group, me, ranks)
    arrived = [outs[0]] + [xor_permute(outs[k], group, k) for k in range(1, PLANE)]
    pair = kept + unpack_scaled(pair_in, rows)
    merged = merge_adapters(pair, pick, arrived)
    return line_sums(merged, group, width).astype(jnp.bfloat16)


def shards(
    hidden, down_matrix, shrink_matrices, expand_matrices, adapter_of_row, adapter_holder_slot
):
    group = lax.axis_size("tp")
    rows, depth = hidden.shape
    width = down_matrix.shape[1] // group
    if width % LANES == 0 and depth % LANES == 0 and rows <= LANES and group >= PLANE and group & (group - 1) == 0:
        return shards_by_blocks(
            hidden, down_matrix, shrink_matrices, expand_matrices, adapter_of_row, adapter_holder_slot
        )
    blocks = MOST // BLOCK
    adapter_ids = jnp.arange(group, dtype=jnp.int32)
    row_match = adapter_of_row[:, None] == adapter_ids[None, :]
    row_slot = jnp.sum(jnp.where(row_match, adapter_holder_slot[None, :], 0), axis=1)
    slot_mask = row_slot[None, :] == adapter_ids[:, None]
    before = jnp.cumsum(slot_mask.astype(jnp.int32), axis=1) - 1
    place = jnp.where(slot_mask, before, -1)
    pick = place[:, None, :] == jnp.arange(MOST, dtype=jnp.int32)[None, :, None]
    pick = pick.reshape(group * MOST, rows).astype(jnp.bfloat16)
    packed = jnp.dot(pick, hidden, preferred_element_type=jnp.float32).astype(jnp.bfloat16)
    packed = packed.reshape(group * blocks, BLOCK, depth)
    gathered = lax.all_to_all(packed, "tp", split_axis=0, concat_axis=0, tiled=True)
    partial_value = jnp.dot(hidden, down_matrix, preferred_element_type=jnp.float32)
    base = lax.psum_scatter(partial_value, "tp", scatter_dimension=1, tiled=True)
    own_rows = jnp.transpose(gathered.reshape(group, MOST, depth), (1, 0, 2))
    rank_rows = jnp.dot(
        own_rows.reshape(MOST, group * depth), shrink_matrices[0], preferred_element_type=jnp.float32
    ).astype(jnp.bfloat16)
    adapter_out = lax.dot_general(
        rank_rows, expand_matrices[0], (((1,), (1,)), ((), ())), preferred_element_type=jnp.float32
    ).astype(jnp.bfloat16)
    adapter_out = jnp.transpose(adapter_out.reshape(blocks, BLOCK, group, width), (2, 0, 1, 3))
    adapter_in = lax.all_to_all(
        adapter_out.reshape(group * blocks, BLOCK, width), "tp", split_axis=0, concat_axis=0, tiled=True
    )
    adapter_rows = lax.dot_general(
        pick,
        adapter_in.reshape(group * MOST, width),
        (((0,), (0,)), ((), ())),
        preferred_element_type=jnp.float32,
    )
    return (base + ADAPTER_SCALE * adapter_rows).astype(jnp.bfloat16)


def solution(mesh):
    in_specs = (
        P("rep", "tp"),
        P("tp", None),
        P(("rep", "tp"), None, None),
        P(("rep", "tp"), None, None),
        P("rep"),
        P("rep"),
    )
    out_specs = P("rep", "tp")
    return jax.shard_map(shards, mesh=mesh, in_specs=in_specs, out_specs=out_specs, check_vma=False)
```

```python
import functools

import jax
import jax.numpy as jnp
from jax import lax
from jax.experimental import pallas as pl
from jax.experimental.pallas import tpu as pltpu
from jax.sharding import PartitionSpec as P

ADAPTER_SCALE = 0.5
BLOCK = 4
MOST = 20
LANES = 128
F16_TOP = 14.0
PLANE = 4
HELD = 32
MARK_ROWS = 16


def in_hbm(value):
    return pltpu.with_memory_space_constraint(value, pltpu.HBM)


def xor_permute(value, group, offset):
    return lax.ppermute(value, "tp", [(i, i ^ offset) for i in range(group)])


def column_blocks_kernel(groups, order_ref, hidden_ref, down_ref, *refs):
    out_refs, held_ref, sems = refs[:groups], refs[groups], refs[groups + 1]
    count, depth, width = held_ref.shape
    parts = width // LANES
    pieces = sems.shape[1]
    cut = depth // pieces

    def copy(block, piece):
        start = pl.multiple_of(order_ref[block] * width, LANES)
        lines = pl.ds(piece * cut, cut)
        return pltpu.make_async_copy(
            down_ref.at[lines, pl.ds(start, width)], held_ref.at[block, lines], sems.at[block, piece]
        )

    for block in range(count):
        for piece in range(pieces):
            copy(block, piece).start()
    share = count // groups
    for block in range(count):
        for piece in range(pieces):
            copy(block, piece).wait()
        product = jnp.dot(hidden_ref[...], held_ref[block], preferred_element_type=jnp.float32)
        for lane in range(parts):
            out_refs[block // share][block % share * parts + lane] = product[
                :, lane * LANES : (lane + 1) * LANES
            ]


def column_blocks(hidden, down_matrix, order, width, groups=1):
    rows, depth = hidden.shape
    count = order.shape[0]
    pieces = 2 if depth % 32 == 0 else 1
    vmem = pl.BlockSpec(memory_space=pltpu.VMEM)
    out = jax.ShapeDtypeStruct((count // groups * width // LANES, rows, LANES), jnp.float32)
    return pl.pallas_call(
        functools.partial(column_blocks_kernel, groups),
        out_shape=[out] * groups,
        in_specs=[
            pl.BlockSpec(memory_space=pltpu.SMEM),
            vmem,
            pl.BlockSpec(memory_space=pl.ANY),
        ],
        out_specs=[vmem] * groups,
        scratch_shapes=[
            pltpu.VMEM((count, depth, width), jnp.bfloat16),
            pltpu.SemaphoreType.DMA((count, pieces)),
        ],
        compiler_params=pltpu.CompilerParams(vmem_limit_bytes=(12 + 12 * groups) * 2**20),
        cost_estimate=pl.CostEstimate(flops=1000, bytes_accessed=1000, transcendentals=0),
    )(order, hidden, in_hbm(down_matrix))


def pack_scaled(value):
    blocks, rows, lanes = value.shape
    peak = jnp.max(jnp.abs(value), axis=(0, 2))
    exponent = jnp.ceil(jnp.log2(jnp.maximum(peak, 2.0**-100)))
    scaled = (value * jnp.exp2(F16_TOP - exponent)[None, :, None]).astype(jnp.float16)
    marks = jnp.pad(exponent.astype(jnp.float16)[None], ((0, MARK_ROWS - 1), (0, lanes - rows)))
    return jnp.concatenate([scaled.reshape(blocks * rows, lanes), marks], axis=0)


def unpack_scaled(packed, rows):
    values, exponent = packed[:-MARK_ROWS], packed[-MARK_ROWS, :rows].astype(jnp.float32)
    values = values.reshape(-1, rows, packed.shape[1]).astype(jnp.float32)
    return values * jnp.exp2(exponent - F16_TOP)[None, :, None]


def pair_sums(hidden, down_matrix, group, order, width):
    half = group * width // LANES // PLANE
    rows = hidden.shape[0]
    share = group // PLANE

    def first():
        (far,) = column_blocks(hidden, down_matrix, order[:share], width)
        far_in = xor_permute(far, group, 1)
        (near,) = column_blocks(hidden, down_matrix, order[share : 2 * share], width)
        return pack_scaled(near + far_in)

    def first_idle():
        return jnp.zeros((half * rows + MARK_ROWS, LANES), jnp.float16)

    sent = lax.cond(order[0] >= 0, first, first_idle)
    pair_in = xor_permute(sent, group, 2)
    order, _ = lax.optimization_barrier((order, sent))

    def second():
        far, near = column_blocks(hidden, down_matrix, order[2 * share :], width, groups=2)
        return near + xor_permute(far, group, 1)

    def second_idle():
        return jnp.zeros((half, rows, LANES), jnp.float32)

    kept = lax.cond(order[1] >= 0, second, second_idle)
    return kept, pair_in


def line_sums(pair, group, width):
    rows = pair.shape[1]
    parts = width // LANES
    arrived = [
        xor_permute(pack_scaled(pair[i * parts : (i + 1) * parts]), group, 4 * i)
        for i in range(1, group // 4)
    ]
    total = pair[:parts]
    for packed in arrived:
        total = total + unpack_scaled(packed, rows)
    return jnp.transpose(total, (1, 0, 2)).reshape(rows, width)


def pack_kernel(
    blocks,
    orders,
    me_ref,
    slot_hbm,
    adapter_hbm,
    hidden_hbm,
    packed_ref,
    pick_ref,
    order_ref,
    kept_ref,
    slot_ref,
    adapter_ref,
    hidden_ref,
    sems,
):
    rows = hidden_ref.shape[0]
    group = slot_ref.shape[0]
    copies = [
        pltpu.make_async_copy(slot_hbm, slot_ref, sems.at[0]),
        pltpu.make_async_copy(adapter_hbm, adapter_ref, sems.at[1]),
        pltpu.make_async_copy(hidden_hbm, hidden_ref, sems.at[2]),
    ]
    for copy in copies:
        copy.start()
    for i, offset in enumerate(orders):
        order_ref[i] = me_ref[0] ^ offset
    ids = lax.broadcasted_iota(jnp.int32, (group, 1), 0)
    slots = jnp.zeros((group, 1), jnp.int32)
    copies[0].wait()
    for adapter in range(group):
        slots = jnp.where(ids == adapter, slot_ref[adapter], slots)
    copies[1].wait()
    adapter = adapter_ref[...]
    first = jnp.sum((adapter < ids).astype(jnp.int32), axis=1, keepdims=True)
    slot = jnp.sum(jnp.where(adapter == ids, slots, 0), axis=0, keepdims=True)
    first = jnp.sum(jnp.where(adapter == ids, first, 0), axis=0, keepdims=True)
    index = lax.broadcasted_iota(jnp.int32, (1, rows), 1) - first
    held = blocks * BLOCK
    far = lax.rem(lax.div(slot, 2), 2)
    rank = far * (group // 2) + lax.div(slot, PLANE) * 2 + lax.rem(slot, 2)
    spots = lax.broadcasted_iota(jnp.int32, (group * held, rows), 0)
    pick = jnp.where(spots == rank * held + index, 1.0, 0.0).astype(jnp.bfloat16)
    for k in range(PLANE):
        line = lax.broadcasted_iota(jnp.int32, (HELD, rows), 0)
        mine = (slot == me_ref[0] ^ k) & (index == line)
        pick_ref[k * HELD : (k + 1) * HELD] = jnp.where(mine, 1.0, 0.0).astype(jnp.bfloat16)
    copies[2].wait()
    packed = jnp.dot(pick, hidden_ref[...], preferred_element_type=jnp.float32)
    packed_ref[...] = packed.astype(jnp.bfloat16).reshape(packed_ref.shape)
    kept_ref[...] = hidden_ref[...]


def pack_rows(hidden, adapter_of_row, adapter_holder_slot, me, orders):
    rows, depth = hidden.shape
    group = adapter_holder_slot.shape[0]
    blocks = MOST // BLOCK
    vmem = pl.BlockSpec(memory_space=pltpu.VMEM)
    smem = pl.BlockSpec(memory_space=pltpu.SMEM)
    anywhere = pl.BlockSpec(memory_space=pltpu.HBM)
    return pl.pallas_call(
        functools.partial(pack_kernel, blocks, orders),
        out_shape=(
            jax.ShapeDtypeStruct((group * blocks, BLOCK, depth), jnp.bfloat16),
            jax.ShapeDtypeStruct((PLANE * HELD, rows), jnp.bfloat16),
            jax.ShapeDtypeStruct((len(orders),), jnp.int32),
            jax.ShapeDtypeStruct((rows, depth), jnp.bfloat16),
        ),
        in_specs=[smem, anywhere, anywhere, anywhere],
        out_specs=(vmem, vmem, smem, vmem),
        scratch_shapes=[
            pltpu.SMEM((group,), jnp.int32),
            pltpu.VMEM((1, rows), jnp.int32),
            pltpu.VMEM((rows, depth), jnp.bfloat16),
            pltpu.SemaphoreType.DMA((3,)),
        ],
        compiler_params=pltpu.CompilerParams(vmem_limit_bytes=24 * 2**20),
    )(me.reshape(1), in_hbm(adapter_holder_slot), in_hbm(adapter_of_row.reshape(1, rows)), in_hbm(hidden))


def adapter_kernel(parts, ranks, me_ref, rows_ref, expand_hbm, shrink_hbm, *refs):
    out_refs = refs[:PLANE]
    shrink_ref, expand_ref, own_ref, sems, expand_sem = refs[PLANE:]
    me = me_ref[0]
    group, _, depth = shrink_ref.shape
    blocks = MOST // BLOCK

    def copy(source):
        return pltpu.make_async_copy(
            shrink_hbm.at[:, pl.ds(ranks[source] * depth, depth)],
            shrink_ref.at[source],
            sems.at[source],
        )

    for source in range(group // 2):
        copy(source).start()
    for source in range(group):
        own = rows_ref[source * blocks : (source + 1) * blocks]
        own_ref[source, :MOST] = own.reshape(MOST, depth)
        if source == group // 2 - 1:
            for later in range(group // 2, group):
                copy(later).start()
            expand_copy = pltpu.make_async_copy(expand_hbm, expand_ref, expand_sem)
            expand_copy.start()
    total = jnp.zeros((MOST, shrink_ref.shape[1]), jnp.float32)
    for source in range(group):
        copy(source).wait()
        total += lax.dot_general(
            own_ref[source, :MOST],
            shrink_ref[source],
            (((1,), (1,)), ((), ())),
            preferred_element_type=jnp.float32,
        )
    rank_rows = total.astype(jnp.bfloat16)
    expand_copy.wait()
    width = parts * LANES
    for k in range(PLANE):
        for line in range(group // PLANE):
            target = me ^ (PLANE * line + k)
            columns = pl.ds(pl.multiple_of(target * width, LANES), width)
            piece = jnp.dot(rank_rows, expand_ref[:, columns], preferred_element_type=jnp.float32)
            piece = piece.astype(jnp.bfloat16)
            for part in range(parts):
                first = (line * parts + part) * blocks
                lanes = piece[:, part * LANES : (part + 1) * LANES]
                out_refs[k][first : first + blocks] = lanes.reshape(blocks, BLOCK, LANES)


def adapter_output(gathered, shrink, expand, group, me, ranks):
    rank = shrink.shape[0]
    model_width = expand.shape[1]
    depth = gathered.shape[2]
    parts = model_width // group // LANES
    held = (model_width // PLANE // LANES * (MOST // BLOCK), BLOCK, LANES)
    vmem = pl.BlockSpec(memory_space=pltpu.VMEM)
    return pl.pallas_call(
        functools.partial(adapter_kernel, parts, ranks),
        out_shape=[jax.ShapeDtypeStruct(held, jnp.bfloat16)] * PLANE,
        in_specs=[
            pl.BlockSpec(memory_space=pltpu.SMEM),
            vmem,
            pl.BlockSpec(memory_space=pl.ANY),
            pl.BlockSpec(memory_space=pl.ANY),
        ],
        out_specs=[vmem] * PLANE,
        scratch_shapes=[
            pltpu.VMEM((group, rank, depth), jnp.bfloat16),
            pltpu.VMEM((rank, model_width), jnp.bfloat16),
            pltpu.VMEM((group, HELD, depth), jnp.bfloat16),
            pltpu.SemaphoreType.DMA((group,)),
            pltpu.SemaphoreType.DMA,
        ],
        compiler_params=pltpu.CompilerParams(vmem_limit_bytes=24 * 2**20),
    )(me.reshape(1), gathered, in_hbm(expand), in_hbm(shrink))


def merge_kernel(pair_ref, pick_ref, *refs):
    in_refs, out_ref, held_ref = refs[:PLANE], refs[PLANE], refs[PLANE + 1]
    blocks = MOST // BLOCK
    held_ref[...] = jnp.zeros_like(held_ref)
    pick = pick_ref[...]
    for part in range(pair_ref.shape[0]):
        for k in range(PLANE):
            rows = in_refs[k][part * blocks : (part + 1) * blocks].reshape(MOST, LANES)
            held_ref[part, k * HELD : k * HELD + MOST] = rows
        adapter_rows = lax.dot_general(
            pick, held_ref[part], (((0,), (0,)), ((), ())), preferred_element_type=jnp.float32
        )
        out_ref[part] = pair_ref[part] + ADAPTER_SCALE * adapter_rows


def merge_adapters(pair, pick, arrived):
    vmem = pl.BlockSpec(memory_space=pltpu.VMEM)
    return pl.pallas_call(
        merge_kernel,
        out_shape=jax.ShapeDtypeStruct(pair.shape, jnp.float32),
        in_specs=[vmem] * (2 + PLANE),
        out_specs=vmem,
        scratch_shapes=[pltpu.VMEM((pair.shape[0], PLANE * HELD, LANES), jnp.bfloat16)],
        compiler_params=pltpu.CompilerParams(vmem_limit_bytes=24 * 2**20),
    )(pair, pick, *arrived)


def shards_by_blocks(
    hidden, down_matrix, shrink_matrices, expand_matrices, adapter_of_row, adapter_holder_slot
):
    group = lax.axis_size("tp")
    me = lax.axis_index("tp")
    rows, depth = hidden.shape
    width = down_matrix.shape[1] // group
    quads = list(range(0, group, 4))
    orders = [q + k for k in (3, 2, 1, 0) for q in quads]
    half = group // 2
    ranks = [i % half // 2 * PLANE + i // half * 2 + i % 2 for i in range(group)]
    packed, pick, order, kept_hidden = pack_rows(
        hidden, adapter_of_row, adapter_holder_slot, me, orders
    )
    gathered = lax.all_to_all(
        packed, "tp", split_axis=0, concat_axis=0, axis_index_groups=[ranks], tiled=True
    )
    shrink = jnp.swapaxes(shrink_matrices, 1, 2)[0]
    kept, pair_in = pair_sums(kept_hidden, down_matrix, group, order, width)
    gathered, _ = lax.optimization_barrier((gathered, kept))
    expand = jnp.swapaxes(expand_matrices, 1, 2)[0]
    outs = adapter_output(gathered, shrink, expand, group, me, ranks)
    arrived = [outs[0]] + [xor_permute(outs[k], group, k) for k in range(1, PLANE)]
    pair = kept + unpack_scaled(pair_in, rows)
    merged = merge_adapters(pair, pick, arrived)
    return line_sums(merged, group, width).astype(jnp.bfloat16)


def shards(
    hidden, down_matrix, shrink_matrices, expand_matrices, adapter_of_row, adapter_holder_slot
):
    group = lax.axis_size("tp")
    rows, depth = hidden.shape
    width = down_matrix.shape[1] // group
    if width % LANES == 0 and depth % LANES == 0 and rows <= LANES and group >= PLANE and group & (group - 1) == 0:
        return shards_by_blocks(
            hidden, down_matrix, shrink_matrices, expand_matrices, adapter_of_row, adapter_holder_slot
        )
    blocks = MOST // BLOCK
    adapter_ids = jnp.arange(group, dtype=jnp.int32)
    row_match = adapter_of_row[:, None] == adapter_ids[None, :]
    row_slot = jnp.sum(jnp.where(row_match, adapter_holder_slot[None, :], 0), axis=1)
    slot_mask = row_slot[None, :] == adapter_ids[:, None]
    before = jnp.cumsum(slot_mask.astype(jnp.int32), axis=1) - 1
    place = jnp.where(slot_mask, before, -1)
    pick = place[:, None, :] == jnp.arange(MOST, dtype=jnp.int32)[None, :, None]
    pick = pick.reshape(group * MOST, rows).astype(jnp.bfloat16)
    packed = jnp.dot(pick, hidden, preferred_element_type=jnp.float32).astype(jnp.bfloat16)
    packed = packed.reshape(group * blocks, BLOCK, depth)
    gathered = lax.all_to_all(packed, "tp", split_axis=0, concat_axis=0, tiled=True)
    partial_value = jnp.dot(hidden, down_matrix, preferred_element_type=jnp.float32)
    base = lax.psum_scatter(partial_value, "tp", scatter_dimension=1, tiled=True)
    own_rows = jnp.transpose(gathered.reshape(group, MOST, depth), (1, 0, 2))
    rank_rows = jnp.dot(
        own_rows.reshape(MOST, group * depth), shrink_matrices[0], preferred_element_type=jnp.float32
    ).astype(jnp.bfloat16)
    adapter_out = lax.dot_general(
        rank_rows, expand_matrices[0], (((1,), (1,)), ((), ())), preferred_element_type=jnp.float32
    ).astype(jnp.bfloat16)
    adapter_out = jnp.transpose(adapter_out.reshape(blocks, BLOCK, group, width), (2, 0, 1, 3))
    adapter_in = lax.all_to_all(
        adapter_out.reshape(group * blocks, BLOCK, width), "tp", split_axis=0, concat_axis=0, tiled=True
    )
    adapter_rows = lax.dot_general(
        pick,
        adapter_in.reshape(group * MOST, width),
        (((0,), (0,)), ((), ())),
        preferred_element_type=jnp.float32,
    )
    return (base + ADAPTER_SCALE * adapter_rows).astype(jnp.bfloat16)


def solution(mesh):
    in_specs = (
        P("rep", "tp"),
        P("tp", None),
        P(("rep", "tp"), None, None),
        P(("rep", "tp"), None, None),
        P("rep"),
        P("rep"),
    )
    out_specs = P("rep", "tp")
    return jax.shard_map(shards, mesh=mesh, in_specs=in_specs, out_specs=out_specs, check_vma=False)
```

```python
import functools

import jax
import jax.numpy as jnp
from jax import lax
from jax.experimental import pallas as pl
from jax.experimental.pallas import tpu as pltpu
from jax.sharding import PartitionSpec as P

ADAPTER_SCALE = 0.5
BLOCK = 4
MOST = 20
LANES = 128
F16_TOP = 14.0
PLANE = 4
HELD = 32
MARK_ROWS = 8


def in_hbm(value):
    return pltpu.with_memory_space_constraint(value, pltpu.HBM)


def xor_permute(value, group, offset):
    return lax.ppermute(value, "tp", [(i, i ^ offset) for i in range(group)])


def column_blocks_kernel(groups, order_ref, hidden_ref, down_ref, *refs):
    out_refs, held_ref, sems = refs[:groups], refs[groups], refs[groups + 1]
    count, depth, width = held_ref.shape
    parts = width // LANES
    pieces = sems.shape[1]
    cut = depth // pieces

    def copy(block, piece):
        start = pl.multiple_of(order_ref[block] * width, LANES)
        lines = pl.ds(piece * cut, cut)
        return pltpu.make_async_copy(
            down_ref.at[lines, pl.ds(start, width)], held_ref.at[block, lines], sems.at[block, piece]
        )

    for block in range(count):
        for piece in range(pieces):
            copy(block, piece).start()
    share = count // groups
    for block in range(count):
        for piece in range(pieces):
            copy(block, piece).wait()
        product = jnp.dot(hidden_ref[...], held_ref[block], preferred_element_type=jnp.float32)
        for lane in range(parts):
            out_refs[block // share][block % share * parts + lane] = product[
                :, lane * LANES : (lane + 1) * LANES
            ]


def column_blocks(hidden, down_matrix, order, width, groups=1):
    rows, depth = hidden.shape
    count = order.shape[0]
    pieces = 2 if depth % 32 == 0 else 1
    vmem = pl.BlockSpec(memory_space=pltpu.VMEM)
    out = jax.ShapeDtypeStruct((count // groups * width // LANES, rows, LANES), jnp.float32)
    return pl.pallas_call(
        functools.partial(column_blocks_kernel, groups),
        out_shape=[out] * groups,
        in_specs=[
            pl.BlockSpec(memory_space=pltpu.SMEM),
            vmem,
            pl.BlockSpec(memory_space=pl.ANY),
        ],
        out_specs=[vmem] * groups,
        scratch_shapes=[
            pltpu.VMEM((count, depth, width), jnp.bfloat16),
            pltpu.SemaphoreType.DMA((count, pieces)),
        ],
        compiler_params=pltpu.CompilerParams(vmem_limit_bytes=(12 + 12 * groups) * 2**20),
        cost_estimate=pl.CostEstimate(flops=1000, bytes_accessed=1000, transcendentals=0),
    )(order, hidden, in_hbm(down_matrix))


def pack_scaled(value):
    blocks, rows, lanes = value.shape
    peak = jnp.max(jnp.abs(value), axis=(0, 2))
    exponent = jnp.ceil(jnp.log2(jnp.maximum(peak, 2.0**-100)))
    scaled = (value * jnp.exp2(F16_TOP - exponent)[None, :, None]).astype(jnp.float16)
    marks = jnp.pad(exponent.astype(jnp.float16)[None], ((0, MARK_ROWS - 1), (0, lanes - rows)))
    return jnp.concatenate([scaled.reshape(blocks * rows, lanes), marks], axis=0)


def unpack_scaled(packed, rows):
    values, exponent = packed[:-MARK_ROWS], packed[-MARK_ROWS, :rows].astype(jnp.float32)
    values = values.reshape(-1, rows, packed.shape[1]).astype(jnp.float32)
    return values * jnp.exp2(exponent - F16_TOP)[None, :, None]


def pair_sums(hidden, down_matrix, group, order, width):
    half = group * width // LANES // PLANE
    rows = hidden.shape[0]
    share = group // PLANE

    def first():
        (far,) = column_blocks(hidden, down_matrix, order[:share], width)
        far_in = xor_permute(far, group, 1)
        (near,) = column_blocks(hidden, down_matrix, order[share : 2 * share], width)
        return pack_scaled(near + far_in)

    def first_idle():
        return jnp.zeros((half * rows + MARK_ROWS, LANES), jnp.float16)

    sent = lax.cond(order[0] >= 0, first, first_idle)
    pair_in = xor_permute(sent, group, 2)
    order, _ = lax.optimization_barrier((order, sent))

    def second():
        far, near = column_blocks(hidden, down_matrix, order[2 * share :], width, groups=2)
        return near + xor_permute(far, group, 1)

    def second_idle():
        return jnp.zeros((half, rows, LANES), jnp.float32)

    kept = lax.cond(order[1] >= 0, second, second_idle)
    return kept, pair_in


def line_sums(pair, group, width):
    rows = pair.shape[1]
    parts = width // LANES

    def flat(value):
        return jnp.transpose(value, (1, 0, 2)).reshape(rows, width)

    arrived = [
        xor_permute(pack_scaled(pair[i * parts : (i + 1) * parts]), group, PLANE * i)
        for i in range(1, group // PLANE)
    ]
    total = pair[:parts]
    for packed in arrived[:-1]:
        total = total + unpack_scaled(packed, rows)
    total = lax.optimization_barrier(flat(total))
    return total + flat(unpack_scaled(arrived[-1], rows))


def pack_kernel(
    blocks,
    orders,
    me_ref,
    slot_hbm,
    adapter_hbm,
    hidden_hbm,
    packed_ref,
    pick_ref,
    order_ref,
    kept_ref,
    slot_ref,
    adapter_ref,
    hidden_ref,
    sems,
):
    rows = hidden_ref.shape[0]
    group = slot_ref.shape[0]
    copies = [
        pltpu.make_async_copy(slot_hbm, slot_ref, sems.at[0]),
        pltpu.make_async_copy(adapter_hbm, adapter_ref, sems.at[1]),
        pltpu.make_async_copy(hidden_hbm, hidden_ref, sems.at[2]),
    ]
    for copy in copies[::-1]:
        copy.start()
    for i, offset in enumerate(orders):
        order_ref[i] = me_ref[0] ^ offset
    ids = lax.broadcasted_iota(jnp.int32, (group, 1), 0)
    slots = jnp.zeros((group, 1), jnp.int32)
    copies[0].wait()
    for adapter in range(group):
        slots = jnp.where(ids == adapter, slot_ref[adapter], slots)
    copies[1].wait()
    adapter = adapter_ref[...]
    first = jnp.sum((adapter < ids).astype(jnp.int32), axis=1, keepdims=True)
    slot = jnp.sum(jnp.where(adapter == ids, slots, 0), axis=0, keepdims=True)
    first = jnp.sum(jnp.where(adapter == ids, first, 0), axis=0, keepdims=True)
    index = lax.broadcasted_iota(jnp.int32, (1, rows), 1) - first
    held = blocks * BLOCK
    far = lax.rem(lax.div(slot, 2), 2)
    rank = far * (group // 2) + lax.div(slot, PLANE) * 2 + lax.rem(slot, 2)
    spots = lax.broadcasted_iota(jnp.int32, (group * held, rows), 0)
    pick = jnp.where(spots == rank * held + index, 1.0, 0.0).astype(jnp.bfloat16)
    for k in range(PLANE):
        line = lax.broadcasted_iota(jnp.int32, (HELD, rows), 0)
        mine = (slot == me_ref[0] ^ k) & (index == line)
        pick_ref[k * HELD : (k + 1) * HELD] = jnp.where(mine, 1.0, 0.0).astype(jnp.bfloat16)
    copies[2].wait()
    packed = jnp.dot(pick, hidden_ref[...], preferred_element_type=jnp.float32)
    packed_ref[...] = packed.astype(jnp.bfloat16).reshape(packed_ref.shape)
    kept_ref[...] = hidden_ref[...]


def pack_rows(hidden, adapter_of_row, adapter_holder_slot, me, orders):
    rows, depth = hidden.shape
    group = adapter_holder_slot.shape[0]
    blocks = MOST // BLOCK
    vmem = pl.BlockSpec(memory_space=pltpu.VMEM)
    smem = pl.BlockSpec(memory_space=pltpu.SMEM)
    anywhere = pl.BlockSpec(memory_space=pltpu.HBM)
    return pl.pallas_call(
        functools.partial(pack_kernel, blocks, orders),
        out_shape=(
            jax.ShapeDtypeStruct((group * blocks, BLOCK, depth), jnp.bfloat16),
            jax.ShapeDtypeStruct((PLANE * HELD, rows), jnp.bfloat16),
            jax.ShapeDtypeStruct((len(orders),), jnp.int32),
            jax.ShapeDtypeStruct((rows, depth), jnp.bfloat16),
        ),
        in_specs=[smem, anywhere, anywhere, anywhere],
        out_specs=(vmem, vmem, smem, vmem),
        scratch_shapes=[
            pltpu.SMEM((group,), jnp.int32),
            pltpu.VMEM((1, rows), jnp.int32),
            pltpu.VMEM((rows, depth), jnp.bfloat16),
            pltpu.SemaphoreType.DMA((3,)),
        ],
        compiler_params=pltpu.CompilerParams(vmem_limit_bytes=24 * 2**20),
    )(me.reshape(1), in_hbm(adapter_holder_slot), in_hbm(adapter_of_row.reshape(1, rows)), in_hbm(hidden))


def adapter_kernel(parts, ranks, me_ref, rows_ref, expand_hbm, shrink_hbm, *refs):
    out_refs = refs[:PLANE]
    shrink_ref, expand_ref, own_ref, sems, expand_sem = refs[PLANE:]
    me = me_ref[0]
    group, _, depth = shrink_ref.shape
    blocks = MOST // BLOCK

    def copy(source):
        return pltpu.make_async_copy(
            shrink_hbm.at[:, pl.ds(ranks[source] * depth, depth)],
            shrink_ref.at[source],
            sems.at[source],
        )

    for source in range(group // 2):
        copy(source).start()
    for source in range(group):
        own = rows_ref[source * blocks : (source + 1) * blocks]
        own_ref[source, :MOST] = own.reshape(MOST, depth)
        if source == group // 2 - 1:
            for later in range(group // 2, group):
                copy(later).start()
            expand_copy = pltpu.make_async_copy(expand_hbm, expand_ref, expand_sem)
            expand_copy.start()
    total = jnp.zeros((MOST, shrink_ref.shape[1]), jnp.float32)
    for source in range(group):
        copy(source).wait()
        total += lax.dot_general(
            own_ref[source, :MOST],
            shrink_ref[source],
            (((1,), (1,)), ((), ())),
            preferred_element_type=jnp.float32,
        )
    rank_rows = total.astype(jnp.bfloat16)
    expand_copy.wait()
    width = parts * LANES
    for k in range(PLANE):
        for line in range(group // PLANE):
            target = me ^ (PLANE * line + k)
            columns = pl.ds(pl.multiple_of(target * width, LANES), width)
            piece = jnp.dot(rank_rows, expand_ref[:, columns], preferred_element_type=jnp.float32)
            piece = piece.astype(jnp.bfloat16)
            for part in range(parts):
                first = (line * parts + part) * blocks
                lanes = piece[:, part * LANES : (part + 1) * LANES]
                out_refs[k][first : first + blocks] = lanes.reshape(blocks, BLOCK, LANES)


def adapter_output(gathered, shrink, expand, group, me, ranks):
    rank = shrink.shape[0]
    model_width = expand.shape[1]
    depth = gathered.shape[2]
    parts = model_width // group // LANES
    held = (model_width // PLANE // LANES * (MOST // BLOCK), BLOCK, LANES)
    vmem = pl.BlockSpec(memory_space=pltpu.VMEM)
    return pl.pallas_call(
        functools.partial(adapter_kernel, parts, ranks),
        out_shape=[jax.ShapeDtypeStruct(held, jnp.bfloat16)] * PLANE,
        in_specs=[
            pl.BlockSpec(memory_space=pltpu.SMEM),
            vmem,
            pl.BlockSpec(memory_space=pl.ANY),
            pl.BlockSpec(memory_space=pl.ANY),
        ],
        out_specs=[vmem] * PLANE,
        scratch_shapes=[
            pltpu.VMEM((group, rank, depth), jnp.bfloat16),
            pltpu.VMEM((rank, model_width), jnp.bfloat16),
            pltpu.VMEM((group, HELD, depth), jnp.bfloat16),
            pltpu.SemaphoreType.DMA((group,)),
            pltpu.SemaphoreType.DMA,
        ],
        compiler_params=pltpu.CompilerParams(vmem_limit_bytes=24 * 2**20),
    )(me.reshape(1), gathered, in_hbm(expand), in_hbm(shrink))


def merge_kernel(pair_ref, pick_ref, *refs):
    in_refs, out_ref, held_ref = refs[:PLANE], refs[PLANE], refs[PLANE + 1]
    blocks = MOST // BLOCK
    held_ref[...] = jnp.zeros_like(held_ref)
    pick = pick_ref[...]
    for part in range(pair_ref.shape[0]):
        for k in range(PLANE):
            rows = in_refs[k][part * blocks : (part + 1) * blocks].reshape(MOST, LANES)
            held_ref[part, k * HELD : k * HELD + MOST] = rows
        adapter_rows = lax.dot_general(
            pick, held_ref[part], (((0,), (0,)), ((), ())), preferred_element_type=jnp.float32
        )
        out_ref[part] = pair_ref[part] + ADAPTER_SCALE * adapter_rows


def merge_adapters(pair, pick, arrived):
    vmem = pl.BlockSpec(memory_space=pltpu.VMEM)
    return pl.pallas_call(
        merge_kernel,
        out_shape=jax.ShapeDtypeStruct(pair.shape, jnp.float32),
        in_specs=[vmem] * (2 + PLANE),
        out_specs=vmem,
        scratch_shapes=[pltpu.VMEM((pair.shape[0], PLANE * HELD, LANES), jnp.bfloat16)],
        compiler_params=pltpu.CompilerParams(vmem_limit_bytes=24 * 2**20),
    )(pair, pick, *arrived)


def shards_by_blocks(
    hidden, down_matrix, shrink_matrices, expand_matrices, adapter_of_row, adapter_holder_slot
):
    group = lax.axis_size("tp")
    me = lax.axis_index("tp")
    rows, depth = hidden.shape
    width = down_matrix.shape[1] // group
    quads = list(range(0, group, 4))
    orders = [q + k for k in (3, 2, 1, 0) for q in quads]
    half = group // 2
    ranks = [i % half // 2 * PLANE + i // half * 2 + i % 2 for i in range(group)]
    packed, pick, order, kept_hidden = pack_rows(
        hidden, adapter_of_row, adapter_holder_slot, me, orders
    )
    gathered = lax.all_to_all(
        packed, "tp", split_axis=0, concat_axis=0, axis_index_groups=[ranks], tiled=True
    )
    shrink = jnp.swapaxes(shrink_matrices, 1, 2)[0]
    kept, pair_in = pair_sums(kept_hidden, down_matrix, group, order, width)
    gathered, _ = lax.optimization_barrier((gathered, kept))
    expand = jnp.swapaxes(expand_matrices, 1, 2)[0]
    outs = adapter_output(gathered, shrink, expand, group, me, ranks)
    arrived = [outs[0]] + [xor_permute(outs[k], group, k) for k in range(1, PLANE)]
    pair = kept + unpack_scaled(pair_in, rows)
    merged = merge_adapters(pair, pick, arrived)
    return line_sums(merged, group, width).astype(jnp.bfloat16)


def shards(
    hidden, down_matrix, shrink_matrices, expand_matrices, adapter_of_row, adapter_holder_slot
):
    group = lax.axis_size("tp")
    rows, depth = hidden.shape
    width = down_matrix.shape[1] // group
    if width % LANES == 0 and depth % LANES == 0 and rows <= LANES and group > PLANE and group & (group - 1) == 0:
        return shards_by_blocks(
            hidden, down_matrix, shrink_matrices, expand_matrices, adapter_of_row, adapter_holder_slot
        )
    blocks = MOST // BLOCK
    adapter_ids = jnp.arange(group, dtype=jnp.int32)
    row_match = adapter_of_row[:, None] == adapter_ids[None, :]
    row_slot = jnp.sum(jnp.where(row_match, adapter_holder_slot[None, :], 0), axis=1)
    slot_mask = row_slot[None, :] == adapter_ids[:, None]
    before = jnp.cumsum(slot_mask.astype(jnp.int32), axis=1) - 1
    place = jnp.where(slot_mask, before, -1)
    pick = place[:, None, :] == jnp.arange(MOST, dtype=jnp.int32)[None, :, None]
    pick = pick.reshape(group * MOST, rows).astype(jnp.bfloat16)
    packed = jnp.dot(pick, hidden, preferred_element_type=jnp.float32).astype(jnp.bfloat16)
    packed = packed.reshape(group * blocks, BLOCK, depth)
    gathered = lax.all_to_all(packed, "tp", split_axis=0, concat_axis=0, tiled=True)
    partial_value = jnp.dot(hidden, down_matrix, preferred_element_type=jnp.float32)
    base = lax.psum_scatter(partial_value, "tp", scatter_dimension=1, tiled=True)
    own_rows = jnp.transpose(gathered.reshape(group, MOST, depth), (1, 0, 2))
    rank_rows = jnp.dot(
        own_rows.reshape(MOST, group * depth), shrink_matrices[0], preferred_element_type=jnp.float32
    ).astype(jnp.bfloat16)
    adapter_out = lax.dot_general(
        rank_rows, expand_matrices[0], (((1,), (1,)), ((), ())), preferred_element_type=jnp.float32
    ).astype(jnp.bfloat16)
    adapter_out = jnp.transpose(adapter_out.reshape(blocks, BLOCK, group, width), (2, 0, 1, 3))
    adapter_in = lax.all_to_all(
        adapter_out.reshape(group * blocks, BLOCK, width), "tp", split_axis=0, concat_axis=0, tiled=True
    )
    adapter_rows = lax.dot_general(
        pick,
        adapter_in.reshape(group * MOST, width),
        (((0,), (0,)), ((), ())),
        preferred_element_type=jnp.float32,
    )
    return (base + ADAPTER_SCALE * adapter_rows).astype(jnp.bfloat16)


def solution(mesh):
    in_specs = (
        P("rep", "tp"),
        P("tp", None),
        P(("rep", "tp"), None, None),
        P(("rep", "tp"), None, None),
        P("rep"),
        P("rep"),
    )
    out_specs = P("rep", "tp")
    return jax.shard_map(shards, mesh=mesh, in_specs=in_specs, out_specs=out_specs, check_vma=False)
```

```python
import functools

import jax
import jax.numpy as jnp
from jax import lax
from jax.experimental import pallas as pl
from jax.experimental.pallas import tpu as pltpu
from jax.sharding import PartitionSpec as P

ADAPTER_SCALE = 0.5
BLOCK = 4
MOST = 20
LANES = 128
F16_TOP = 14.0
PLANE = 4
HELD = 32
MARK_ROWS = 16


def in_hbm(value):
    return pltpu.with_memory_space_constraint(value, pltpu.HBM)


def xor_permute(value, group, offset):
    return lax.ppermute(value, "tp", [(i, i ^ offset) for i in range(group)])


def column_blocks_kernel(groups, order_ref, hidden_ref, down_ref, *refs):
    out_refs, held_ref, sems = refs[:groups], refs[groups], refs[groups + 1]
    count, depth, width = held_ref.shape
    parts = width // LANES
    pieces = sems.shape[1]
    cut = depth // pieces

    def copy(block, piece):
        start = pl.multiple_of(order_ref[block] * width, LANES)
        lines = pl.ds(piece * cut, cut)
        return pltpu.make_async_copy(
            down_ref.at[lines, pl.ds(start, width)], held_ref.at[block, lines], sems.at[block, piece]
        )

    for block in range(count):
        for piece in range(pieces):
            copy(block, piece).start()
    share = count // groups
    for block in range(count):
        for piece in range(pieces):
            copy(block, piece).wait()
        product = jnp.dot(hidden_ref[...], held_ref[block], preferred_element_type=jnp.float32)
        for lane in range(parts):
            out_refs[block // share][block % share * parts + lane] = product[
                :, lane * LANES : (lane + 1) * LANES
            ]


def column_blocks(hidden, down_matrix, order, width, groups=1):
    rows, depth = hidden.shape
    count = order.shape[0]
    pieces = 2 if depth % 32 == 0 else 1
    vmem = pl.BlockSpec(memory_space=pltpu.VMEM)
    out = jax.ShapeDtypeStruct((count // groups * width // LANES, rows, LANES), jnp.float32)
    return pl.pallas_call(
        functools.partial(column_blocks_kernel, groups),
        out_shape=[out] * groups,
        in_specs=[
            pl.BlockSpec(memory_space=pltpu.SMEM),
            vmem,
            pl.BlockSpec(memory_space=pl.ANY),
        ],
        out_specs=[vmem] * groups,
        scratch_shapes=[
            pltpu.VMEM((count, depth, width), jnp.bfloat16),
            pltpu.SemaphoreType.DMA((count, pieces)),
        ],
        compiler_params=pltpu.CompilerParams(vmem_limit_bytes=(12 + 12 * groups) * 2**20),
        cost_estimate=pl.CostEstimate(flops=1000, bytes_accessed=1000, transcendentals=0),
    )(order, hidden, in_hbm(down_matrix))


def pack_scaled(value):
    blocks, rows, lanes = value.shape
    peak = jnp.max(jnp.abs(value), axis=(0, 2))
    exponent = jnp.ceil(jnp.log2(jnp.maximum(peak, 2.0**-100)))
    scaled = (value * jnp.exp2(F16_TOP - exponent)[None, :, None]).astype(jnp.float16)
    marks = jnp.pad(exponent.astype(jnp.float16)[None], ((0, MARK_ROWS - 1), (0, lanes - rows)))
    return jnp.concatenate([scaled.reshape(blocks * rows, lanes), marks], axis=0)


def unpack_scaled(packed, rows):
    values, exponent = packed[:-MARK_ROWS], packed[-MARK_ROWS, :rows].astype(jnp.float32)
    values = values.reshape(-1, rows, packed.shape[1]).astype(jnp.float32)
    return values * jnp.exp2(exponent - F16_TOP)[None, :, None]


def pair_sums(hidden, down_matrix, group, order, width):
    half = group * width // LANES // PLANE
    rows = hidden.shape[0]
    share = group // PLANE

    def first():
        (far,) = column_blocks(hidden, down_matrix, order[:share], width)
        far_in = xor_permute(far, group, 1)
        (near,) = column_blocks(hidden, down_matrix, order[share : 2 * share], width)
        return pack_scaled(near + far_in)

    def first_idle():
        return jnp.zeros((half * rows + MARK_ROWS, LANES), jnp.float16)

    sent = lax.cond(order[0] >= 0, first, first_idle)
    order, _ = lax.optimization_barrier((order, sent))

    def second():
        far, near = column_blocks(hidden, down_matrix, order[2 * share :], width, groups=2)
        return near + xor_permute(far, group, 1)

    def second_idle():
        return jnp.zeros((half, rows, LANES), jnp.float32)

    kept = lax.cond(order[1] >= 0, second, second_idle)
    sent, _ = lax.optimization_barrier((sent, kept))
    pair_in = xor_permute(sent, group, 2)
    return kept, pair_in


def line_sums(pair, group, width):
    rows = pair.shape[1]
    parts = width // LANES
    arrived = [
        xor_permute(pack_scaled(pair[i * parts : (i + 1) * parts]), group, 4 * i)
        for i in range(1, group // 4)
    ]
    total = pair[:parts]
    for packed in arrived:
        total = total + unpack_scaled(packed, rows)
    return jnp.transpose(total, (1, 0, 2)).reshape(rows, width)


def pack_kernel(
    blocks,
    orders,
    me_ref,
    slot_hbm,
    adapter_hbm,
    hidden_hbm,
    packed_ref,
    pick_ref,
    order_ref,
    kept_ref,
    slot_ref,
    adapter_ref,
    hidden_ref,
    sems,
):
    rows = hidden_ref.shape[0]
    group = slot_ref.shape[0]
    copies = [
        pltpu.make_async_copy(slot_hbm, slot_ref, sems.at[0]),
        pltpu.make_async_copy(adapter_hbm, adapter_ref, sems.at[1]),
        pltpu.make_async_copy(hidden_hbm, hidden_ref, sems.at[2]),
    ]
    for copy in copies:
        copy.start()
    for i, offset in enumerate(orders):
        order_ref[i] = me_ref[0] ^ offset
    ids = lax.broadcasted_iota(jnp.int32, (group, 1), 0)
    slots = jnp.zeros((group, 1), jnp.int32)
    copies[0].wait()
    for adapter in range(group):
        slots = jnp.where(ids == adapter, slot_ref[adapter], slots)
    copies[1].wait()
    adapter = adapter_ref[...]
    first = jnp.sum((adapter < ids).astype(jnp.int32), axis=1, keepdims=True)
    slot = jnp.sum(jnp.where(adapter == ids, slots, 0), axis=0, keepdims=True)
    first = jnp.sum(jnp.where(adapter == ids, first, 0), axis=0, keepdims=True)
    index = lax.broadcasted_iota(jnp.int32, (1, rows), 1) - first
    held = blocks * BLOCK
    far = lax.rem(lax.div(slot, 2), 2)
    rank = far * (group // 2) + lax.div(slot, PLANE) * 2 + lax.rem(slot, 2)
    spots = lax.broadcasted_iota(jnp.int32, (group * held, rows), 0)
    pick = jnp.where(spots == rank * held + index, 1.0, 0.0).astype(jnp.bfloat16)
    for k in range(PLANE):
        line = lax.broadcasted_iota(jnp.int32, (HELD, rows), 0)
        mine = (slot == me_ref[0] ^ k) & (index == line)
        pick_ref[k * HELD : (k + 1) * HELD] = jnp.where(mine, 1.0, 0.0).astype(jnp.bfloat16)
    copies[2].wait()
    packed = jnp.dot(pick, hidden_ref[...], preferred_element_type=jnp.float32)
    packed_ref[...] = packed.astype(jnp.bfloat16).reshape(packed_ref.shape)
    kept_ref[...] = hidden_ref[...]


def pack_rows(hidden, adapter_of_row, adapter_holder_slot, me, orders):
    rows, depth = hidden.shape
    group = adapter_holder_slot.shape[0]
    blocks = MOST // BLOCK
    vmem = pl.BlockSpec(memory_space=pltpu.VMEM)
    smem = pl.BlockSpec(memory_space=pltpu.SMEM)
    anywhere = pl.BlockSpec(memory_space=pltpu.HBM)
    return pl.pallas_call(
        functools.partial(pack_kernel, blocks, orders),
        out_shape=(
            jax.ShapeDtypeStruct((group * blocks, BLOCK, depth), jnp.bfloat16),
            jax.ShapeDtypeStruct((PLANE * HELD, rows), jnp.bfloat16),
            jax.ShapeDtypeStruct((len(orders),), jnp.int32),
            jax.ShapeDtypeStruct((rows, depth), jnp.bfloat16),
        ),
        in_specs=[smem, anywhere, anywhere, anywhere],
        out_specs=(vmem, vmem, smem, vmem),
        scratch_shapes=[
            pltpu.SMEM((group,), jnp.int32),
            pltpu.VMEM((1, rows), jnp.int32),
            pltpu.VMEM((rows, depth), jnp.bfloat16),
            pltpu.SemaphoreType.DMA((3,)),
        ],
        compiler_params=pltpu.CompilerParams(vmem_limit_bytes=24 * 2**20),
    )(me.reshape(1), in_hbm(adapter_holder_slot), in_hbm(adapter_of_row.reshape(1, rows)), in_hbm(hidden))


def adapter_kernel(parts, ranks, me_ref, rows_ref, expand_hbm, shrink_hbm, *refs):
    out_refs = refs[:PLANE]
    shrink_ref, expand_ref, own_ref, sems, expand_sem = refs[PLANE:]
    me = me_ref[0]
    group, _, depth = shrink_ref.shape
    blocks = MOST // BLOCK

    def copy(source):
        return pltpu.make_async_copy(
            shrink_hbm.at[:, pl.ds(ranks[source] * depth, depth)],
            shrink_ref.at[source],
            sems.at[source],
        )

    for source in range(group // 2):
        copy(source).start()
    for source in range(group):
        own = rows_ref[source * blocks : (source + 1) * blocks]
        own_ref[source, :MOST] = own.reshape(MOST, depth)
        if source == group // 2 - 1:
            for later in range(group // 2, group):
                copy(later).start()
            expand_copy = pltpu.make_async_copy(expand_hbm, expand_ref, expand_sem)
            expand_copy.start()
    total = jnp.zeros((MOST, shrink_ref.shape[1]), jnp.float32)
    for source in range(group):
        copy(source).wait()
        total += lax.dot_general(
            own_ref[source, :MOST],
            shrink_ref[source],
            (((1,), (1,)), ((), ())),
            preferred_element_type=jnp.float32,
        )
    rank_rows = total.astype(jnp.bfloat16)
    expand_copy.wait()
    width = parts * LANES
    for k in range(PLANE):
        for line in range(group // PLANE):
            target = me ^ (PLANE * line + k)
            columns = pl.ds(pl.multiple_of(target * width, LANES), width)
            piece = jnp.dot(rank_rows, expand_ref[:, columns], preferred_element_type=jnp.float32)
            piece = piece.astype(jnp.bfloat16)
            for part in range(parts):
                first = (line * parts + part) * blocks
                lanes = piece[:, part * LANES : (part + 1) * LANES]
                out_refs[k][first : first + blocks] = lanes.reshape(blocks, BLOCK, LANES)


def adapter_output(gathered, shrink, expand, group, me, ranks):
    rank = shrink.shape[0]
    model_width = expand.shape[1]
    depth = gathered.shape[2]
    parts = model_width // group // LANES
    held = (model_width // PLANE // LANES * (MOST // BLOCK), BLOCK, LANES)
    vmem = pl.BlockSpec(memory_space=pltpu.VMEM)
    return pl.pallas_call(
        functools.partial(adapter_kernel, parts, ranks),
        out_shape=[jax.ShapeDtypeStruct(held, jnp.bfloat16)] * PLANE,
        in_specs=[
            pl.BlockSpec(memory_space=pltpu.SMEM),
            vmem,
            pl.BlockSpec(memory_space=pl.ANY),
            pl.BlockSpec(memory_space=pl.ANY),
        ],
        out_specs=[vmem] * PLANE,
        scratch_shapes=[
            pltpu.VMEM((group, rank, depth), jnp.bfloat16),
            pltpu.VMEM((rank, model_width), jnp.bfloat16),
            pltpu.VMEM((group, HELD, depth), jnp.bfloat16),
            pltpu.SemaphoreType.DMA((group,)),
            pltpu.SemaphoreType.DMA,
        ],
        compiler_params=pltpu.CompilerParams(vmem_limit_bytes=24 * 2**20),
    )(me.reshape(1), gathered, in_hbm(expand), in_hbm(shrink))


def merge_kernel(pair_ref, pick_ref, *refs):
    in_refs, out_ref, held_ref = refs[:PLANE], refs[PLANE], refs[PLANE + 1]
    blocks = MOST // BLOCK
    held_ref[...] = jnp.zeros_like(held_ref)
    pick = pick_ref[...]
    for part in range(pair_ref.shape[0]):
        for k in range(PLANE):
            rows = in_refs[k][part * blocks : (part + 1) * blocks].reshape(MOST, LANES)
            held_ref[part, k * HELD : k * HELD + MOST] = rows
        adapter_rows = lax.dot_general(
            pick, held_ref[part], (((0,), (0,)), ((), ())), preferred_element_type=jnp.float32
        )
        out_ref[part] = pair_ref[part] + ADAPTER_SCALE * adapter_rows


def merge_adapters(pair, pick, arrived):
    vmem = pl.BlockSpec(memory_space=pltpu.VMEM)
    return pl.pallas_call(
        merge_kernel,
        out_shape=jax.ShapeDtypeStruct(pair.shape, jnp.float32),
        in_specs=[vmem] * (2 + PLANE),
        out_specs=vmem,
        scratch_shapes=[pltpu.VMEM((pair.shape[0], PLANE * HELD, LANES), jnp.bfloat16)],
        compiler_params=pltpu.CompilerParams(vmem_limit_bytes=24 * 2**20),
    )(pair, pick, *arrived)


def shards_by_blocks(
    hidden, down_matrix, shrink_matrices, expand_matrices, adapter_of_row, adapter_holder_slot
):
    group = lax.axis_size("tp")
    me = lax.axis_index("tp")
    rows, depth = hidden.shape
    width = down_matrix.shape[1] // group
    quads = list(range(0, group, 4))
    orders = [q + k for k in (3, 2, 1, 0) for q in quads]
    half = group // 2
    ranks = [i % half // 2 * PLANE + i // half * 2 + i % 2 for i in range(group)]
    packed, pick, order, kept_hidden = pack_rows(
        hidden, adapter_of_row, adapter_holder_slot, me, orders
    )
    gathered = lax.all_to_all(
        packed, "tp", split_axis=0, concat_axis=0, axis_index_groups=[ranks], tiled=True
    )
    shrink = jnp.swapaxes(shrink_matrices, 1, 2)[0]
    kept, pair_in = pair_sums(kept_hidden, down_matrix, group, order, width)
    gathered, _ = lax.optimization_barrier((gathered, kept))
    expand = jnp.swapaxes(expand_matrices, 1, 2)[0]
    outs = adapter_output(gathered, shrink, expand, group, me, ranks)
    arrived = [outs[0]] + [xor_permute(outs[k], group, k) for k in range(1, PLANE)]
    pair = kept + unpack_scaled(pair_in, rows)
    merged = merge_adapters(pair, pick, arrived)
    return line_sums(merged, group, width).astype(jnp.bfloat16)


def shards(
    hidden, down_matrix, shrink_matrices, expand_matrices, adapter_of_row, adapter_holder_slot
):
    group = lax.axis_size("tp")
    rows, depth = hidden.shape
    width = down_matrix.shape[1] // group
    if width % LANES == 0 and depth % LANES == 0 and rows <= LANES and group >= PLANE and group & (group - 1) == 0:
        return shards_by_blocks(
            hidden, down_matrix, shrink_matrices, expand_matrices, adapter_of_row, adapter_holder_slot
        )
    blocks = MOST // BLOCK
    adapter_ids = jnp.arange(group, dtype=jnp.int32)
    row_match = adapter_of_row[:, None] == adapter_ids[None, :]
    row_slot = jnp.sum(jnp.where(row_match, adapter_holder_slot[None, :], 0), axis=1)
    slot_mask = row_slot[None, :] == adapter_ids[:, None]
    before = jnp.cumsum(slot_mask.astype(jnp.int32), axis=1) - 1
    place = jnp.where(slot_mask, before, -1)
    pick = place[:, None, :] == jnp.arange(MOST, dtype=jnp.int32)[None, :, None]
    pick = pick.reshape(group * MOST, rows).astype(jnp.bfloat16)
    packed = jnp.dot(pick, hidden, preferred_element_type=jnp.float32).astype(jnp.bfloat16)
    packed = packed.reshape(group * blocks, BLOCK, depth)
    gathered = lax.all_to_all(packed, "tp", split_axis=0, concat_axis=0, tiled=True)
    partial_value = jnp.dot(hidden, down_matrix, preferred_element_type=jnp.float32)
    base = lax.psum_scatter(partial_value, "tp", scatter_dimension=1, tiled=True)
    own_rows = jnp.transpose(gathered.reshape(group, MOST, depth), (1, 0, 2))
    rank_rows = jnp.dot(
        own_rows.reshape(MOST, group * depth), shrink_matrices[0], preferred_element_type=jnp.float32
    ).astype(jnp.bfloat16)
    adapter_out = lax.dot_general(
        rank_rows, expand_matrices[0], (((1,), (1,)), ((), ())), preferred_element_type=jnp.float32
    ).astype(jnp.bfloat16)
    adapter_out = jnp.transpose(adapter_out.reshape(blocks, BLOCK, group, width), (2, 0, 1, 3))
    adapter_in = lax.all_to_all(
        adapter_out.reshape(group * blocks, BLOCK, width), "tp", split_axis=0, concat_axis=0, tiled=True
    )
    adapter_rows = lax.dot_general(
        pick,
        adapter_in.reshape(group * MOST, width),
        (((0,), (0,)), ((), ())),
        preferred_element_type=jnp.float32,
    )
    return (base + ADAPTER_SCALE * adapter_rows).astype(jnp.bfloat16)


def solution(mesh):
    in_specs = (
        P("rep", "tp"),
        P("tp", None),
        P(("rep", "tp"), None, None),
        P(("rep", "tp"), None, None),
        P("rep"),
        P("rep"),
    )
    out_specs = P("rep", "tp")
    return jax.shard_map(shards, mesh=mesh, in_specs=in_specs, out_specs=out_specs, check_vma=False)
```

```python
import functools

import jax
import jax.numpy as jnp
from jax import lax
from jax.experimental import pallas as pl
from jax.experimental.pallas import tpu as pltpu
from jax.sharding import PartitionSpec as P

ADAPTER_SCALE = 0.5
BLOCK = 4
MOST = 20
LANES = 128
F16_TOP = 14.0
PLANE = 4
HELD = 32
MARK_ROWS = 16


def in_hbm(value):
    return pltpu.with_memory_space_constraint(value, pltpu.HBM)


def xor_permute(value, group, offset):
    return lax.ppermute(value, "tp", [(i, i ^ offset) for i in range(group)])


def column_blocks_kernel(groups, order_ref, hidden_ref, down_ref, *refs):
    out_refs, held_ref, sems = refs[:groups], refs[groups], refs[groups + 1]
    count, depth, width = held_ref.shape
    parts = width // LANES
    pieces = sems.shape[1]
    cut = depth // pieces

    def copy(block, piece):
        start = pl.multiple_of(order_ref[block] * width, LANES)
        lines = pl.ds(piece * cut, cut)
        return pltpu.make_async_copy(
            down_ref.at[lines, pl.ds(start, width)], held_ref.at[block, lines], sems.at[block, piece]
        )

    for block in range(count):
        for piece in range(pieces):
            copy(block, piece).start()
    share = count // groups
    for block in range(count):
        for piece in range(pieces):
            copy(block, piece).wait()
        product = jnp.dot(hidden_ref[...], held_ref[block], preferred_element_type=jnp.float32)
        for lane in range(parts):
            out_refs[block // share][block % share * parts + lane] = product[
                :, lane * LANES : (lane + 1) * LANES
            ]


def column_blocks(hidden, down_matrix, order, width, groups=1):
    rows, depth = hidden.shape
    count = order.shape[0]
    pieces = 2 if depth % 32 == 0 else 1
    vmem = pl.BlockSpec(memory_space=pltpu.VMEM)
    out = jax.ShapeDtypeStruct((count // groups * width // LANES, rows, LANES), jnp.float32)
    return pl.pallas_call(
        functools.partial(column_blocks_kernel, groups),
        out_shape=[out] * groups,
        in_specs=[
            pl.BlockSpec(memory_space=pltpu.SMEM),
            vmem,
            pl.BlockSpec(memory_space=pl.ANY),
        ],
        out_specs=[vmem] * groups,
        scratch_shapes=[
            pltpu.VMEM((count, depth, width), jnp.bfloat16),
            pltpu.SemaphoreType.DMA((count, pieces)),
        ],
        compiler_params=pltpu.CompilerParams(vmem_limit_bytes=(12 + 12 * groups) * 2**20),
        cost_estimate=pl.CostEstimate(flops=1000, bytes_accessed=1000, transcendentals=0),
    )(order, hidden, in_hbm(down_matrix))


def pack_scaled(value):
    blocks, rows, lanes = value.shape
    peak = jnp.max(jnp.abs(value), axis=(0, 2))
    exponent = jnp.ceil(jnp.log2(jnp.maximum(peak, 2.0**-100)))
    scaled = (value * jnp.exp2(F16_TOP - exponent)[None, :, None]).astype(jnp.float16)
    marks = jnp.pad(exponent.astype(jnp.float16)[None], ((0, MARK_ROWS - 1), (0, lanes - rows)))
    return jnp.concatenate([scaled.reshape(blocks * rows, lanes), marks], axis=0)


def unpack_scaled(packed, rows):
    values, exponent = packed[:-MARK_ROWS], packed[-MARK_ROWS, :rows].astype(jnp.float32)
    values = values.reshape(-1, rows, packed.shape[1]).astype(jnp.float32)
    return values * jnp.exp2(exponent - F16_TOP)[None, :, None]


def pair_sums(hidden, down_matrix, group, order, width):
    half = group * width // LANES // PLANE
    rows = hidden.shape[0]
    share = group // PLANE

    def first():
        (far,) = column_blocks(hidden, down_matrix, order[:share], width)
        far_in = xor_permute(far, group, 1)
        (near,) = column_blocks(hidden, down_matrix, order[share : 2 * share], width)
        return pack_scaled(near + far_in)

    def first_idle():
        return jnp.zeros((half * rows + MARK_ROWS, LANES), jnp.float16)

    sent = lax.cond(order[0] >= 0, first, first_idle)
    pair_in = xor_permute(sent, group, 2)
    order, _ = lax.optimization_barrier((order, sent))

    def second():
        far, near = column_blocks(hidden, down_matrix, order[2 * share :], width, groups=2)
        return near + xor_permute(far, group, 1)

    def second_idle():
        return jnp.zeros((half, rows, LANES), jnp.float32)

    kept = lax.cond(order[1] >= 0, second, second_idle)
    return kept, pair_in


def line_sums(pair, group, width):
    rows = pair.shape[1]
    parts = width // LANES
    arrived = [
        xor_permute(pack_scaled(pair[i * parts : (i + 1) * parts]), group, 4 * i)
        for i in range(1, group // 4)
    ]
    total = pair[:parts]
    for packed in arrived:
        total = total + unpack_scaled(packed, rows)
    return jnp.transpose(total, (1, 0, 2)).reshape(rows, width)


def pack_kernel(
    blocks,
    orders,
    me_ref,
    slot_hbm,
    adapter_hbm,
    hidden_hbm,
    packed_ref,
    pick_ref,
    order_ref,
    kept_ref,
    slot_ref,
    adapter_ref,
    hidden_ref,
    sems,
):
    rows = hidden_ref.shape[0]
    group = slot_ref.shape[0]
    copies = [
        pltpu.make_async_copy(slot_hbm, slot_ref, sems.at[0]),
        pltpu.make_async_copy(adapter_hbm, adapter_ref, sems.at[1]),
        pltpu.make_async_copy(hidden_hbm, hidden_ref, sems.at[2]),
    ]
    for copy in copies:
        copy.start()
    for i, offset in enumerate(orders):
        order_ref[i] = me_ref[0] ^ offset
    ids = lax.broadcasted_iota(jnp.int32, (group, 1), 0)
    slots = jnp.zeros((group, 1), jnp.int32)
    copies[0].wait()
    for adapter in range(group):
        slots = jnp.where(ids == adapter, slot_ref[adapter], slots)
    copies[1].wait()
    adapter = adapter_ref[...]
    first = jnp.sum((adapter < ids).astype(jnp.int32), axis=1, keepdims=True)
    slot = jnp.sum(jnp.where(adapter == ids, slots, 0), axis=0, keepdims=True)
    first = jnp.sum(jnp.where(adapter == ids, first, 0), axis=0, keepdims=True)
    index = lax.broadcasted_iota(jnp.int32, (1, rows), 1) - first
    held = blocks * BLOCK
    far = lax.rem(lax.div(slot, 2), 2)
    rank = far * (group // 2) + lax.div(slot, PLANE) * 2 + lax.rem(slot, 2)
    spots = lax.broadcasted_iota(jnp.int32, (group * held, rows), 0)
    pick = jnp.where(spots == rank * held + index, 1.0, 0.0).astype(jnp.bfloat16)
    for k in range(PLANE):
        line = lax.broadcasted_iota(jnp.int32, (HELD, rows), 0)
        mine = (slot == me_ref[0] ^ k) & (index == line)
        pick_ref[k * HELD : (k + 1) * HELD] = jnp.where(mine, 1.0, 0.0).astype(jnp.bfloat16)
    copies[2].wait()
    packed = jnp.dot(pick, hidden_ref[...], preferred_element_type=jnp.float32)
    packed_ref[...] = packed.astype(jnp.bfloat16).reshape(packed_ref.shape)
    kept_ref[...] = hidden_ref[...]


def pack_rows(hidden, adapter_of_row, adapter_holder_slot, me, orders):
    rows, depth = hidden.shape
    group = adapter_holder_slot.shape[0]
    blocks = MOST // BLOCK
    vmem = pl.BlockSpec(memory_space=pltpu.VMEM)
    smem = pl.BlockSpec(memory_space=pltpu.SMEM)
    anywhere = pl.BlockSpec(memory_space=pltpu.HBM)
    return pl.pallas_call(
        functools.partial(pack_kernel, blocks, orders),
        out_shape=(
            jax.ShapeDtypeStruct((group * blocks, BLOCK, depth), jnp.bfloat16),
            jax.ShapeDtypeStruct((PLANE * HELD, rows), jnp.bfloat16),
            jax.ShapeDtypeStruct((len(orders),), jnp.int32),
            jax.ShapeDtypeStruct((rows, depth), jnp.bfloat16),
        ),
        in_specs=[smem, anywhere, anywhere, anywhere],
        out_specs=(vmem, vmem, smem, vmem),
        scratch_shapes=[
            pltpu.SMEM((group,), jnp.int32),
            pltpu.VMEM((1, rows), jnp.int32),
            pltpu.VMEM((rows, depth), jnp.bfloat16),
            pltpu.SemaphoreType.DMA((3,)),
        ],
        compiler_params=pltpu.CompilerParams(vmem_limit_bytes=24 * 2**20),
    )(me.reshape(1), in_hbm(adapter_holder_slot), in_hbm(adapter_of_row.reshape(1, rows)), in_hbm(hidden))


def adapter_kernel(parts, ranks, me_ref, rows_ref, expand_hbm, shrink_hbm, *refs):
    out_refs = refs[:PLANE]
    shrink_ref, expand_ref, own_ref, sems, expand_sem = refs[PLANE:]
    me = me_ref[0]
    chips = shrink_ref.shape[0]
    group, depth = 2 * chips, shrink_ref.shape[2] // 2
    blocks = MOST // BLOCK

    def copy(pair):
        return pltpu.make_async_copy(
            shrink_hbm.at[:, pl.ds(ranks[2 * pair] * depth, 2 * depth)],
            shrink_ref.at[pair],
            sems.at[pair],
        )

    for pair in range(chips // 2):
        copy(pair).start()
    for source in range(group):
        own = rows_ref[source * blocks : (source + 1) * blocks]
        first = source % 2 * depth
        own_ref[source // 2, :MOST, first : first + depth] = own.reshape(MOST, depth)
        if source == group // 2 - 1:
            for later in range(chips // 2, chips):
                copy(later).start()
            expand_copy = pltpu.make_async_copy(expand_hbm, expand_ref, expand_sem)
            expand_copy.start()
    total = jnp.zeros((MOST, shrink_ref.shape[1]), jnp.float32)
    for pair in range(chips):
        copy(pair).wait()
        total += lax.dot_general(
            own_ref[pair, :MOST],
            shrink_ref[pair],
            (((1,), (1,)), ((), ())),
            preferred_element_type=jnp.float32,
        )
    rank_rows = total.astype(jnp.bfloat16)
    expand_copy.wait()
    width = parts * LANES
    for k in range(PLANE):
        for line in range(group // PLANE):
            target = me ^ (PLANE * line + k)
            columns = pl.ds(pl.multiple_of(target * width, LANES), width)
            piece = jnp.dot(rank_rows, expand_ref[:, columns], preferred_element_type=jnp.float32)
            piece = piece.astype(jnp.bfloat16)
            for part in range(parts):
                first = (line * parts + part) * blocks
                lanes = piece[:, part * LANES : (part + 1) * LANES]
                out_refs[k][first : first + blocks] = lanes.reshape(blocks, BLOCK, LANES)


def adapter_output(gathered, shrink, expand, group, me, ranks):
    rank = shrink.shape[0]
    model_width = expand.shape[1]
    depth = gathered.shape[2]
    parts = model_width // group // LANES
    held = (model_width // PLANE // LANES * (MOST // BLOCK), BLOCK, LANES)
    vmem = pl.BlockSpec(memory_space=pltpu.VMEM)
    return pl.pallas_call(
        functools.partial(adapter_kernel, parts, ranks),
        out_shape=[jax.ShapeDtypeStruct(held, jnp.bfloat16)] * PLANE,
        in_specs=[
            pl.BlockSpec(memory_space=pltpu.SMEM),
            vmem,
            pl.BlockSpec(memory_space=pl.ANY),
            pl.BlockSpec(memory_space=pl.ANY),
        ],
        out_specs=[vmem] * PLANE,
        scratch_shapes=[
            pltpu.VMEM((group // 2, rank, 2 * depth), jnp.bfloat16),
            pltpu.VMEM((rank, model_width), jnp.bfloat16),
            pltpu.VMEM((group // 2, HELD, 2 * depth), jnp.bfloat16),
            pltpu.SemaphoreType.DMA((group // 2,)),
            pltpu.SemaphoreType.DMA,
        ],
        compiler_params=pltpu.CompilerParams(vmem_limit_bytes=24 * 2**20),
    )(me.reshape(1), gathered, in_hbm(expand), in_hbm(shrink))


def merge_kernel(pair_ref, pick_ref, *refs):
    in_refs, out_ref, held_ref = refs[:PLANE], refs[PLANE], refs[PLANE + 1]
    blocks = MOST // BLOCK
    held_ref[...] = jnp.zeros_like(held_ref)
    pick = pick_ref[...]
    for part in range(pair_ref.shape[0]):
        for k in range(PLANE):
            rows = in_refs[k][part * blocks : (part + 1) * blocks].reshape(MOST, LANES)
            held_ref[part, k * HELD : k * HELD + MOST] = rows
        adapter_rows = lax.dot_general(
            pick, held_ref[part], (((0,), (0,)), ((), ())), preferred_element_type=jnp.float32
        )
        out_ref[part] = pair_ref[part] + ADAPTER_SCALE * adapter_rows


def merge_adapters(pair, pick, arrived):
    vmem = pl.BlockSpec(memory_space=pltpu.VMEM)
    return pl.pallas_call(
        merge_kernel,
        out_shape=jax.ShapeDtypeStruct(pair.shape, jnp.float32),
        in_specs=[vmem] * (2 + PLANE),
        out_specs=vmem,
        scratch_shapes=[pltpu.VMEM((pair.shape[0], PLANE * HELD, LANES), jnp.bfloat16)],
        compiler_params=pltpu.CompilerParams(vmem_limit_bytes=24 * 2**20),
    )(pair, pick, *arrived)


def shards_by_blocks(
    hidden, down_matrix, shrink_matrices, expand_matrices, adapter_of_row, adapter_holder_slot
):
    group = lax.axis_size("tp")
    me = lax.axis_index("tp")
    rows, depth = hidden.shape
    width = down_matrix.shape[1] // group
    quads = list(range(0, group, 4))
    orders = [q + k for k in (3, 2, 1, 0) for q in quads]
    half = group // 2
    ranks = [i % half // 2 * PLANE + i // half * 2 + i % 2 for i in range(group)]
    packed, pick, order, kept_hidden = pack_rows(
        hidden, adapter_of_row, adapter_holder_slot, me, orders
    )
    gathered = lax.all_to_all(
        packed, "tp", split_axis=0, concat_axis=0, axis_index_groups=[ranks], tiled=True
    )
    shrink = jnp.swapaxes(shrink_matrices, 1, 2)[0]
    kept, pair_in = pair_sums(kept_hidden, down_matrix, group, order, width)
    gathered, _ = lax.optimization_barrier((gathered, kept))
    expand = jnp.swapaxes(expand_matrices, 1, 2)[0]
    outs = adapter_output(gathered, shrink, expand, group, me, ranks)
    arrived = [outs[0]] + [xor_permute(outs[k], group, k) for k in range(1, PLANE)]
    pair = kept + unpack_scaled(pair_in, rows)
    merged = merge_adapters(pair, pick, arrived)
    return line_sums(merged, group, width).astype(jnp.bfloat16)


def shards(
    hidden, down_matrix, shrink_matrices, expand_matrices, adapter_of_row, adapter_holder_slot
):
    group = lax.axis_size("tp")
    rows, depth = hidden.shape
    width = down_matrix.shape[1] // group
    if width % LANES == 0 and depth % LANES == 0 and rows <= LANES and group >= PLANE and group & (group - 1) == 0:
        return shards_by_blocks(
            hidden, down_matrix, shrink_matrices, expand_matrices, adapter_of_row, adapter_holder_slot
        )
    blocks = MOST // BLOCK
    adapter_ids = jnp.arange(group, dtype=jnp.int32)
    row_match = adapter_of_row[:, None] == adapter_ids[None, :]
    row_slot = jnp.sum(jnp.where(row_match, adapter_holder_slot[None, :], 0), axis=1)
    slot_mask = row_slot[None, :] == adapter_ids[:, None]
    before = jnp.cumsum(slot_mask.astype(jnp.int32), axis=1) - 1
    place = jnp.where(slot_mask, before, -1)
    pick = place[:, None, :] == jnp.arange(MOST, dtype=jnp.int32)[None, :, None]
    pick = pick.reshape(group * MOST, rows).astype(jnp.bfloat16)
    packed = jnp.dot(pick, hidden, preferred_element_type=jnp.float32).astype(jnp.bfloat16)
    packed = packed.reshape(group * blocks, BLOCK, depth)
    gathered = lax.all_to_all(packed, "tp", split_axis=0, concat_axis=0, tiled=True)
    partial_value = jnp.dot(hidden, down_matrix, preferred_element_type=jnp.float32)
    base = lax.psum_scatter(partial_value, "tp", scatter_dimension=1, tiled=True)
    own_rows = jnp.transpose(gathered.reshape(group, MOST, depth), (1, 0, 2))
    rank_rows = jnp.dot(
        own_rows.reshape(MOST, group * depth), shrink_matrices[0], preferred_element_type=jnp.float32
    ).astype(jnp.bfloat16)
    adapter_out = lax.dot_general(
        rank_rows, expand_matrices[0], (((1,), (1,)), ((), ())), preferred_element_type=jnp.float32
    ).astype(jnp.bfloat16)
    adapter_out = jnp.transpose(adapter_out.reshape(blocks, BLOCK, group, width), (2, 0, 1, 3))
    adapter_in = lax.all_to_all(
        adapter_out.reshape(group * blocks, BLOCK, width), "tp", split_axis=0, concat_axis=0, tiled=True
    )
    adapter_rows = lax.dot_general(
        pick,
        adapter_in.reshape(group * MOST, width),
        (((0,), (0,)), ((), ())),
        preferred_element_type=jnp.float32,
    )
    return (base + ADAPTER_SCALE * adapter_rows).astype(jnp.bfloat16)


def solution(mesh):
    in_specs = (
        P("rep", "tp"),
        P("tp", None),
        P(("rep", "tp"), None, None),
        P(("rep", "tp"), None, None),
        P("rep"),
        P("rep"),
    )
    out_specs = P("rep", "tp")
    return jax.shard_map(shards, mesh=mesh, in_specs=in_specs, out_specs=out_specs, check_vma=False)
```

```python
import functools

import jax
import jax.numpy as jnp
from jax import lax
from jax.experimental import pallas as pl
from jax.experimental.pallas import tpu as pltpu
from jax.sharding import PartitionSpec as P

ADAPTER_SCALE = 0.5
BLOCK = 4
MOST = 20
LANES = 128
F16_TOP = 14.0
PLANE = 4
HELD = 32
MARK_ROWS = 16


def in_hbm(value):
    return pltpu.with_memory_space_constraint(value, pltpu.HBM)


def xor_permute(value, group, offset):
    return lax.ppermute(value, "tp", [(i, i ^ offset) for i in range(group)])


def column_blocks_kernel(groups, order_ref, hidden_ref, down_ref, *refs):
    out_refs, held_ref, sems = refs[:groups], refs[groups], refs[groups + 1]
    count, depth, width = held_ref.shape
    parts = width // LANES
    pieces = sems.shape[1]
    cut = depth // pieces

    def copy(block, piece):
        start = pl.multiple_of(order_ref[block] * width, LANES)
        lines = pl.ds(piece * cut, cut)
        return pltpu.make_async_copy(
            down_ref.at[lines, pl.ds(start, width)], held_ref.at[block, lines], sems.at[block, piece]
        )

    for block in range(count):
        for piece in range(pieces):
            copy(block, piece).start()
    share = count // groups
    for block in range(count):
        for piece in range(pieces):
            copy(block, piece).wait()
        product = jnp.dot(hidden_ref[...], held_ref[block], preferred_element_type=jnp.float32)
        for lane in range(parts):
            out_refs[block // share][block % share * parts + lane] = product[
                :, lane * LANES : (lane + 1) * LANES
            ]


def column_blocks(hidden, down_matrix, order, width, groups=1):
    rows, depth = hidden.shape
    count = order.shape[0]
    pieces = 2 if depth % 32 == 0 else 1
    vmem = pl.BlockSpec(memory_space=pltpu.VMEM)
    out = jax.ShapeDtypeStruct((count // groups * width // LANES, rows, LANES), jnp.float32)
    return pl.pallas_call(
        functools.partial(column_blocks_kernel, groups),
        out_shape=[out] * groups,
        in_specs=[
            pl.BlockSpec(memory_space=pltpu.SMEM),
            vmem,
            pl.BlockSpec(memory_space=pl.ANY),
        ],
        out_specs=[vmem] * groups,
        scratch_shapes=[
            pltpu.VMEM((count, depth, width), jnp.bfloat16),
            pltpu.SemaphoreType.DMA((count, pieces)),
        ],
        compiler_params=pltpu.CompilerParams(vmem_limit_bytes=(12 + 12 * groups) * 2**20),
        cost_estimate=pl.CostEstimate(flops=1000, bytes_accessed=1000, transcendentals=0),
    )(order, hidden, in_hbm(down_matrix))


def pack_scaled(value):
    blocks, rows, lanes = value.shape
    peak = jnp.max(jnp.abs(value), axis=(0, 2))
    exponent = jnp.ceil(jnp.log2(jnp.maximum(peak, 2.0**-100)))
    scaled = (value * jnp.exp2(F16_TOP - exponent)[None, :, None]).astype(jnp.float16)
    marks = jnp.pad(exponent.astype(jnp.float16)[None], ((0, MARK_ROWS - 1), (0, lanes - rows)))
    return jnp.concatenate([scaled.reshape(blocks * rows, lanes), marks], axis=0)


def unpack_scaled(packed, rows):
    values, exponent = packed[:-MARK_ROWS], packed[-MARK_ROWS, :rows].astype(jnp.float32)
    values = values.reshape(-1, rows, packed.shape[1]).astype(jnp.float32)
    return values * jnp.exp2(exponent - F16_TOP)[None, :, None]


def pair_sums(hidden, down_matrix, group, order, width):
    half = group * width // LANES // PLANE
    rows = hidden.shape[0]
    share = group // PLANE

    def first():
        (far,) = column_blocks(hidden, down_matrix, order[:share], width)
        far_in = xor_permute(far, group, 1)
        (near,) = column_blocks(hidden, down_matrix, order[share : 2 * share], width)
        return pack_scaled(near + far_in)

    def first_idle():
        return jnp.zeros((half * rows + MARK_ROWS, LANES), jnp.float16)

    sent = lax.cond(order[0] >= 0, first, first_idle)
    pair_in = xor_permute(sent, group, 2)
    order, _ = lax.optimization_barrier((order, sent))

    def second():
        far, near = column_blocks(hidden, down_matrix, order[2 * share :], width, groups=2)
        return near + xor_permute(far, group, 1)

    def second_idle():
        return jnp.zeros((half, rows, LANES), jnp.float32)

    kept = lax.cond(order[1] >= 0, second, second_idle)
    return kept, pair_in


def line_sums(pair, group, width):
    rows = pair.shape[1]
    parts = width // LANES
    arrived = [
        xor_permute(pack_scaled(pair[i * parts : (i + 1) * parts]), group, 4 * i)
        for i in range(1, group // 4)
    ]
    total = pair[:parts]
    for packed in arrived:
        total = total + unpack_scaled(packed, rows)
    return jnp.transpose(total, (1, 0, 2)).reshape(rows, width)


def pack_kernel(
    blocks,
    orders,
    me_ref,
    slot_hbm,
    adapter_hbm,
    hidden_hbm,
    packed_ref,
    pick_ref,
    order_ref,
    kept_ref,
    slot_ref,
    adapter_ref,
    hidden_ref,
    sems,
):
    rows = hidden_ref.shape[0]
    group = slot_ref.shape[0]
    copies = [
        pltpu.make_async_copy(slot_hbm, slot_ref, sems.at[0]),
        pltpu.make_async_copy(adapter_hbm, adapter_ref, sems.at[1]),
        pltpu.make_async_copy(hidden_hbm, hidden_ref, sems.at[2]),
    ]
    for copy in copies:
        copy.start()
    for i, offset in enumerate(orders):
        order_ref[i] = me_ref[0] ^ offset
    ids = lax.broadcasted_iota(jnp.int32, (group, 1), 0)
    slots = jnp.zeros((group, 1), jnp.int32)
    copies[0].wait()
    for adapter in range(group):
        slots = jnp.where(ids == adapter, slot_ref[adapter], slots)
    copies[1].wait()
    adapter = adapter_ref[...]
    first = jnp.sum((adapter < ids).astype(jnp.int32), axis=1, keepdims=True)
    slot = jnp.sum(jnp.where(adapter == ids, slots, 0), axis=0, keepdims=True)
    first = jnp.sum(jnp.where(adapter == ids, first, 0), axis=0, keepdims=True)
    index = lax.broadcasted_iota(jnp.int32, (1, rows), 1) - first
    held = blocks * BLOCK
    far = lax.rem(lax.div(slot, 2), 2)
    rank = far * (group // 2) + lax.div(slot, PLANE) * 2 + lax.rem(slot, 2)
    spots = lax.broadcasted_iota(jnp.int32, (group * held, rows), 0)
    pick = jnp.where(spots == rank * held + index, 1.0, 0.0).astype(jnp.bfloat16)
    for k in range(PLANE):
        line = lax.broadcasted_iota(jnp.int32, (HELD, rows), 0)
        mine = (slot == me_ref[0] ^ k) & (index == line)
        pick_ref[k * HELD : (k + 1) * HELD] = jnp.where(mine, 1.0, 0.0).astype(jnp.bfloat16)
    copies[2].wait()
    packed = jnp.dot(pick, hidden_ref[...], preferred_element_type=jnp.float32)
    packed_ref[...] = packed.astype(jnp.bfloat16).reshape(packed_ref.shape)
    kept_ref[...] = hidden_ref[...]


def pack_rows(hidden, adapter_of_row, adapter_holder_slot, me, orders):
    rows, depth = hidden.shape
    group = adapter_holder_slot.shape[0]
    blocks = MOST // BLOCK
    vmem = pl.BlockSpec(memory_space=pltpu.VMEM)
    smem = pl.BlockSpec(memory_space=pltpu.SMEM)
    anywhere = pl.BlockSpec(memory_space=pltpu.HBM)
    return pl.pallas_call(
        functools.partial(pack_kernel, blocks, orders),
        out_shape=(
            jax.ShapeDtypeStruct((group * blocks, BLOCK, depth), jnp.bfloat16),
            jax.ShapeDtypeStruct((PLANE * HELD, rows), jnp.bfloat16),
            jax.ShapeDtypeStruct((len(orders),), jnp.int32),
            jax.ShapeDtypeStruct((rows, depth), jnp.bfloat16),
        ),
        in_specs=[smem, anywhere, anywhere, anywhere],
        out_specs=(vmem, vmem, smem, vmem),
        scratch_shapes=[
            pltpu.SMEM((group,), jnp.int32),
            pltpu.VMEM((1, rows), jnp.int32),
            pltpu.VMEM((rows, depth), jnp.bfloat16),
            pltpu.SemaphoreType.DMA((3,)),
        ],
        compiler_params=pltpu.CompilerParams(vmem_limit_bytes=24 * 2**20),
    )(me.reshape(1), in_hbm(adapter_holder_slot), in_hbm(adapter_of_row.reshape(1, rows)), in_hbm(hidden))


def adapter_kernel(parts, ranks, me_ref, rows_ref, expand_hbm, shrink_hbm, *refs):
    out_refs = refs[:PLANE]
    shrink_ref, expand_ref, own_ref, sems, expand_sem = refs[PLANE:]
    me = me_ref[0]
    chips = shrink_ref.shape[0]
    group, depth = 2 * chips, shrink_ref.shape[2] // 2
    blocks = MOST // BLOCK

    def copy(pair):
        return pltpu.make_async_copy(
            shrink_hbm.at[:, pl.ds(ranks[2 * pair] * depth, 2 * depth)],
            shrink_ref.at[pair],
            sems.at[pair],
        )

    for pair in range(chips // 2):
        copy(pair).start()
    for source in range(group):
        own = rows_ref[source * blocks : (source + 1) * blocks]
        first = source % 2 * depth
        own_ref[source // 2, :MOST, first : first + depth] = own.reshape(MOST, depth)
        if source == group // 2 - 1:
            for later in range(chips // 2, chips):
                copy(later).start()
            expand_copy = pltpu.make_async_copy(expand_hbm, expand_ref, expand_sem)
            expand_copy.start()
    total = jnp.zeros((MOST, shrink_ref.shape[1]), jnp.float32)
    for pair in range(chips):
        copy(pair).wait()
        total += lax.dot_general(
            own_ref[pair, :MOST],
            shrink_ref[pair],
            (((1,), (1,)), ((), ())),
            preferred_element_type=jnp.float32,
        )
    rank_rows = total.astype(jnp.bfloat16)
    expand_copy.wait()
    width = parts * LANES
    for k in range(PLANE):
        for line in range(group // PLANE):
            target = me ^ (PLANE * line + k)
            columns = pl.ds(pl.multiple_of(target * width, LANES), width)
            piece = jnp.dot(rank_rows, expand_ref[:, columns], preferred_element_type=jnp.float32)
            piece = piece.astype(jnp.bfloat16)
            for part in range(parts):
                first = (line * parts + part) * blocks
                lanes = piece[:, part * LANES : (part + 1) * LANES]
                out_refs[k][first : first + blocks] = lanes.reshape(blocks, BLOCK, LANES)


def adapter_output(gathered, shrink, expand, group, me, ranks):
    rank = shrink.shape[0]
    model_width = expand.shape[1]
    depth = gathered.shape[2]
    parts = model_width // group // LANES
    held = (model_width // PLANE // LANES * (MOST // BLOCK), BLOCK, LANES)
    vmem = pl.BlockSpec(memory_space=pltpu.VMEM)
    return pl.pallas_call(
        functools.partial(adapter_kernel, parts, ranks),
        out_shape=[jax.ShapeDtypeStruct(held, jnp.bfloat16)] * PLANE,
        in_specs=[
            pl.BlockSpec(memory_space=pltpu.SMEM),
            vmem,
            pl.BlockSpec(memory_space=pl.ANY),
            pl.BlockSpec(memory_space=pl.ANY),
        ],
        out_specs=[vmem] * PLANE,
        scratch_shapes=[
            pltpu.VMEM((group // 2, rank, 2 * depth), jnp.bfloat16),
            pltpu.VMEM((rank, model_width), jnp.bfloat16),
            pltpu.VMEM((group // 2, HELD, 2 * depth), jnp.bfloat16),
            pltpu.SemaphoreType.DMA((group // 2,)),
            pltpu.SemaphoreType.DMA,
        ],
        compiler_params=pltpu.CompilerParams(vmem_limit_bytes=24 * 2**20),
    )(me.reshape(1), gathered, in_hbm(expand), in_hbm(shrink))


def merge_kernel(pair_ref, pick_ref, *refs):
    in_refs, out_ref, held_ref = refs[:PLANE], refs[PLANE], refs[PLANE + 1]
    blocks = MOST // BLOCK
    held_ref[...] = jnp.zeros_like(held_ref)
    pick = pick_ref[...]
    for part in range(pair_ref.shape[0]):
        for k in range(PLANE):
            rows = in_refs[k][part * blocks : (part + 1) * blocks].reshape(MOST, LANES)
            held_ref[part, k * HELD : k * HELD + MOST] = rows
        adapter_rows = lax.dot_general(
            pick, held_ref[part], (((0,), (0,)), ((), ())), preferred_element_type=jnp.float32
        )
        out_ref[part] = pair_ref[part] + ADAPTER_SCALE * adapter_rows


def merge_adapters(pair, pick, arrived):
    vmem = pl.BlockSpec(memory_space=pltpu.VMEM)
    return pl.pallas_call(
        merge_kernel,
        out_shape=jax.ShapeDtypeStruct(pair.shape, jnp.float32),
        in_specs=[vmem] * (2 + PLANE),
        out_specs=vmem,
        scratch_shapes=[pltpu.VMEM((pair.shape[0], PLANE * HELD, LANES), jnp.bfloat16)],
        compiler_params=pltpu.CompilerParams(vmem_limit_bytes=24 * 2**20),
    )(pair, pick, *arrived)


def shards_by_blocks(
    hidden, down_matrix, shrink_matrices, expand_matrices, adapter_of_row, adapter_holder_slot
):
    group = lax.axis_size("tp")
    me = lax.axis_index("tp")
    rows, depth = hidden.shape
    width = down_matrix.shape[1] // group
    quads = list(range(0, group, 4))
    orders = [q + k for k in (3, 2, 1, 0) for q in quads]
    half = group // 2
    ranks = [i % half // 2 * PLANE + i // half * 2 + i % 2 for i in range(group)]
    packed, pick, order, kept_hidden = pack_rows(
        hidden, adapter_of_row, adapter_holder_slot, me, orders
    )
    gathered = lax.all_to_all(
        packed, "tp", split_axis=0, concat_axis=0, axis_index_groups=[ranks], tiled=True
    )
    shrink = jnp.swapaxes(shrink_matrices, 1, 2)[0]
    kept, pair_in = pair_sums(kept_hidden, down_matrix, group, order, width)
    gathered, _ = lax.optimization_barrier((gathered, kept))
    expand = jnp.swapaxes(expand_matrices, 1, 2)[0]
    outs = adapter_output(gathered, shrink, expand, group, me, ranks)
    across = [xor_permute(outs[k], group, k) for k in range(2, PLANE)]
    beside, _ = lax.optimization_barrier((outs[1], across[0]))
    arrived = [outs[0], xor_permute(beside, group, 1)] + across
    pair = kept + unpack_scaled(pair_in, rows)
    merged = merge_adapters(pair, pick, arrived)
    return line_sums(merged, group, width).astype(jnp.bfloat16)


def shards(
    hidden, down_matrix, shrink_matrices, expand_matrices, adapter_of_row, adapter_holder_slot
):
    group = lax.axis_size("tp")
    rows, depth = hidden.shape
    width = down_matrix.shape[1] // group
    if width % LANES == 0 and depth % LANES == 0 and rows <= LANES and group >= PLANE and group & (group - 1) == 0:
        return shards_by_blocks(
            hidden, down_matrix, shrink_matrices, expand_matrices, adapter_of_row, adapter_holder_slot
        )
    blocks = MOST // BLOCK
    adapter_ids = jnp.arange(group, dtype=jnp.int32)
    row_match = adapter_of_row[:, None] == adapter_ids[None, :]
    row_slot = jnp.sum(jnp.where(row_match, adapter_holder_slot[None, :], 0), axis=1)
    slot_mask = row_slot[None, :] == adapter_ids[:, None]
    before = jnp.cumsum(slot_mask.astype(jnp.int32), axis=1) - 1
    place = jnp.where(slot_mask, before, -1)
    pick = place[:, None, :] == jnp.arange(MOST, dtype=jnp.int32)[None, :, None]
    pick = pick.reshape(group * MOST, rows).astype(jnp.bfloat16)
    packed = jnp.dot(pick, hidden, preferred_element_type=jnp.float32).astype(jnp.bfloat16)
    packed = packed.reshape(group * blocks, BLOCK, depth)
    gathered = lax.all_to_all(packed, "tp", split_axis=0, concat_axis=0, tiled=True)
    partial_value = jnp.dot(hidden, down_matrix, preferred_element_type=jnp.float32)
    base = lax.psum_scatter(partial_value, "tp", scatter_dimension=1, tiled=True)
    own_rows = jnp.transpose(gathered.reshape(group, MOST, depth), (1, 0, 2))
    rank_rows = jnp.dot(
        own_rows.reshape(MOST, group * depth), shrink_matrices[0], preferred_element_type=jnp.float32
    ).astype(jnp.bfloat16)
    adapter_out = lax.dot_general(
        rank_rows, expand_matrices[0], (((1,), (1,)), ((), ())), preferred_element_type=jnp.float32
    ).astype(jnp.bfloat16)
    adapter_out = jnp.transpose(adapter_out.reshape(blocks, BLOCK, group, width), (2, 0, 1, 3))
    adapter_in = lax.all_to_all(
        adapter_out.reshape(group * blocks, BLOCK, width), "tp", split_axis=0, concat_axis=0, tiled=True
    )
    adapter_rows = lax.dot_general(
        pick,
        adapter_in.reshape(group * MOST, width),
        (((0,), (0,)), ((), ())),
        preferred_element_type=jnp.float32,
    )
    return (base + ADAPTER_SCALE * adapter_rows).astype(jnp.bfloat16)


def solution(mesh):
    in_specs = (
        P("rep", "tp"),
        P("tp", None),
        P(("rep", "tp"), None, None),
        P(("rep", "tp"), None, None),
        P("rep"),
        P("rep"),
    )
    out_specs = P("rep", "tp")
    return jax.shard_map(shards, mesh=mesh, in_specs=in_specs, out_specs=out_specs, check_vma=False)
```

```python
import functools

import jax
import jax.numpy as jnp
from jax import lax
from jax.experimental import pallas as pl
from jax.experimental.pallas import tpu as pltpu
from jax.sharding import PartitionSpec as P

ADAPTER_SCALE = 0.5
BLOCK = 4
MOST = 20
LANES = 128
F16_TOP = 14.0
PLANE = 4
HELD = 32
MARK_ROWS = 16


def in_hbm(value):
    return pltpu.with_memory_space_constraint(value, pltpu.HBM)


def xor_permute(value, group, offset):
    return lax.ppermute(value, "tp", [(i, i ^ offset) for i in range(group)])


def column_blocks_kernel(groups, order_ref, hidden_ref, down_ref, *refs):
    out_refs, held_ref, sems = refs[:groups], refs[groups], refs[groups + 1]
    count, depth, width = held_ref.shape
    parts = width // LANES
    pieces = sems.shape[1]
    cut = depth // pieces

    def copy(block, piece):
        start = pl.multiple_of(order_ref[block] * width, LANES)
        lines = pl.ds(piece * cut, cut)
        return pltpu.make_async_copy(
            down_ref.at[lines, pl.ds(start, width)], held_ref.at[block, lines], sems.at[block, piece]
        )

    for block in range(count):
        for piece in range(pieces):
            copy(block, piece).start()
    share = count // groups
    for block in range(count):
        for piece in range(pieces):
            copy(block, piece).wait()
        product = jnp.dot(hidden_ref[...], held_ref[block], preferred_element_type=jnp.float32)
        for lane in range(parts):
            out_refs[block // share][block % share * parts + lane] = product[
                :, lane * LANES : (lane + 1) * LANES
            ]


def column_blocks(hidden, down_matrix, order, width, groups=1):
    rows, depth = hidden.shape
    count = order.shape[0]
    pieces = 2 if depth % 32 == 0 else 1
    vmem = pl.BlockSpec(memory_space=pltpu.VMEM)
    out = jax.ShapeDtypeStruct((count // groups * width // LANES, rows, LANES), jnp.float32)
    return pl.pallas_call(
        functools.partial(column_blocks_kernel, groups),
        out_shape=[out] * groups,
        in_specs=[
            pl.BlockSpec(memory_space=pltpu.SMEM),
            vmem,
            pl.BlockSpec(memory_space=pl.ANY),
        ],
        out_specs=[vmem] * groups,
        scratch_shapes=[
            pltpu.VMEM((count, depth, width), jnp.bfloat16),
            pltpu.SemaphoreType.DMA((count, pieces)),
        ],
        compiler_params=pltpu.CompilerParams(vmem_limit_bytes=(12 + 12 * groups) * 2**20),
        cost_estimate=pl.CostEstimate(flops=1000, bytes_accessed=1000, transcendentals=0),
    )(order, hidden, in_hbm(down_matrix))


def pack_scaled(value):
    blocks, rows, lanes = value.shape
    peak = jnp.max(jnp.abs(value), axis=(0, 2))
    exponent = jnp.ceil(jnp.log2(jnp.maximum(peak, 2.0**-100)))
    scaled = (value * jnp.exp2(F16_TOP - exponent)[None, :, None]).astype(jnp.float16)
    marks = jnp.pad(exponent.astype(jnp.float16)[None], ((0, MARK_ROWS - 1), (0, lanes - rows)))
    return jnp.concatenate([scaled.reshape(blocks * rows, lanes), marks], axis=0)


def unpack_scaled(packed, rows):
    values, exponent = packed[:-MARK_ROWS], packed[-MARK_ROWS, :rows].astype(jnp.float32)
    values = values.reshape(-1, rows, packed.shape[1]).astype(jnp.float32)
    return values * jnp.exp2(exponent - F16_TOP)[None, :, None]


def pair_sums(hidden, down_matrix, group, order, width):
    half = group * width // LANES // PLANE
    rows = hidden.shape[0]
    share = group // PLANE

    def first():
        (far,) = column_blocks(hidden, down_matrix, order[:share], width)
        far_in = xor_permute(far, group, 1)
        (near,) = column_blocks(hidden, down_matrix, order[share : 2 * share], width)
        return pack_scaled(near + far_in)

    def first_idle():
        return jnp.zeros((half * rows + MARK_ROWS, LANES), jnp.float16)

    sent = lax.cond(order[0] >= 0, first, first_idle)
    pair_in = xor_permute(sent, group, 2)
    order, _ = lax.optimization_barrier((order, sent))

    def second():
        far, near = column_blocks(hidden, down_matrix, order[2 * share :], width, groups=2)
        return near + xor_permute(far, group, 1)

    def second_idle():
        return jnp.zeros((half, rows, LANES), jnp.float32)

    kept = lax.cond(order[1] >= 0, second, second_idle)
    return kept, pair_in


def line_sums(pair, group, width):
    rows = pair.shape[1]
    parts = width // LANES
    arrived = [
        xor_permute(pack_scaled(pair[i * parts : (i + 1) * parts]), group, 4 * i)
        for i in range(1, group // 4)
    ]
    total = pair[:parts]
    for packed in arrived:
        total = total + unpack_scaled(packed, rows)
    return jnp.transpose(total, (1, 0, 2)).reshape(rows, width)


def pack_kernel(
    blocks,
    orders,
    me_ref,
    slot_hbm,
    adapter_hbm,
    hidden_hbm,
    packed_ref,
    pick_ref,
    order_ref,
    slot_ref,
    adapter_ref,
    hidden_ref,
    sems,
):
    rows = hidden_ref.shape[0]
    group = slot_ref.shape[0]
    copies = [
        pltpu.make_async_copy(slot_hbm, slot_ref, sems.at[0]),
        pltpu.make_async_copy(adapter_hbm, adapter_ref, sems.at[1]),
        pltpu.make_async_copy(hidden_hbm, hidden_ref, sems.at[2]),
    ]
    for copy in copies:
        copy.start()
    for i, offset in enumerate(orders):
        order_ref[i] = me_ref[0] ^ offset
    ids = lax.broadcasted_iota(jnp.int32, (group, 1), 0)
    slots = jnp.zeros((group, 1), jnp.int32)
    copies[0].wait()
    for adapter in range(group):
        slots = jnp.where(ids == adapter, slot_ref[adapter], slots)
    copies[1].wait()
    adapter = adapter_ref[...]
    first = jnp.sum((adapter < ids).astype(jnp.int32), axis=1, keepdims=True)
    slot = jnp.sum(jnp.where(adapter == ids, slots, 0), axis=0, keepdims=True)
    first = jnp.sum(jnp.where(adapter == ids, first, 0), axis=0, keepdims=True)
    index = lax.broadcasted_iota(jnp.int32, (1, rows), 1) - first
    held = blocks * BLOCK
    far = lax.rem(lax.div(slot, 2), 2)
    rank = far * (group // 2) + lax.div(slot, PLANE) * 2 + lax.rem(slot, 2)
    spots = lax.broadcasted_iota(jnp.int32, (group * held, rows), 0)
    pick = jnp.where(spots == rank * held + index, 1.0, 0.0).astype(jnp.bfloat16)
    for k in range(PLANE):
        line = lax.broadcasted_iota(jnp.int32, (HELD, rows), 0)
        mine = (slot == me_ref[0] ^ k) & (index == line)
        pick_ref[k * HELD : (k + 1) * HELD] = jnp.where(mine, 1.0, 0.0).astype(jnp.bfloat16)
    copies[2].wait()
    packed = jnp.dot(pick, hidden_ref[...], preferred_element_type=jnp.float32)
    packed_ref[...] = packed.astype(jnp.bfloat16).reshape(packed_ref.shape)


def pack_rows(hidden, adapter_of_row, adapter_holder_slot, me, orders):
    rows, depth = hidden.shape
    group = adapter_holder_slot.shape[0]
    blocks = MOST // BLOCK
    vmem = pl.BlockSpec(memory_space=pltpu.VMEM)
    smem = pl.BlockSpec(memory_space=pltpu.SMEM)
    anywhere = pl.BlockSpec(memory_space=pltpu.HBM)
    return pl.pallas_call(
        functools.partial(pack_kernel, blocks, orders),
        out_shape=(
            jax.ShapeDtypeStruct((group * blocks, BLOCK, depth), jnp.bfloat16),
            jax.ShapeDtypeStruct((PLANE * HELD, rows), jnp.bfloat16),
            jax.ShapeDtypeStruct((len(orders),), jnp.int32),
        ),
        in_specs=[smem, anywhere, anywhere, anywhere],
        out_specs=(vmem, vmem, smem),
        scratch_shapes=[
            pltpu.SMEM((group,), jnp.int32),
            pltpu.VMEM((1, rows), jnp.int32),
            pltpu.VMEM((rows, depth), jnp.bfloat16),
            pltpu.SemaphoreType.DMA((3,)),
        ],
        compiler_params=pltpu.CompilerParams(vmem_limit_bytes=24 * 2**20),
    )(me.reshape(1), in_hbm(adapter_holder_slot), in_hbm(adapter_of_row.reshape(1, rows)), in_hbm(hidden))


def adapter_kernel(parts, ranks, me_ref, rows_ref, expand_hbm, shrink_hbm, *refs):
    out_refs = refs[:PLANE]
    shrink_ref, expand_ref, own_ref, sems, expand_sem = refs[PLANE:]
    me = me_ref[0]
    chips = shrink_ref.shape[0]
    group, depth = 2 * chips, shrink_ref.shape[2] // 2
    blocks = MOST // BLOCK

    def copy(pair):
        return pltpu.make_async_copy(
            shrink_hbm.at[:, pl.ds(ranks[2 * pair] * depth, 2 * depth)],
            shrink_ref.at[pair],
            sems.at[pair],
        )

    for pair in range(chips // 2):
        copy(pair).start()
    for source in range(group):
        own = rows_ref[source * blocks : (source + 1) * blocks]
        first = source % 2 * depth
        own_ref[source // 2, :MOST, first : first + depth] = own.reshape(MOST, depth)
        if source == group // 2 - 1:
            for later in range(chips // 2, chips):
                copy(later).start()
            expand_copy = pltpu.make_async_copy(expand_hbm, expand_ref, expand_sem)
            expand_copy.start()
    total = jnp.zeros((MOST, shrink_ref.shape[1]), jnp.float32)
    for pair in range(chips):
        copy(pair).wait()
        total += lax.dot_general(
            own_ref[pair, :MOST],
            shrink_ref[pair],
            (((1,), (1,)), ((), ())),
            preferred_element_type=jnp.float32,
        )
    rank_rows = total.astype(jnp.bfloat16)
    expand_copy.wait()
    width = parts * LANES
    for k in range(PLANE):
        for line in range(group // PLANE):
            target = me ^ (PLANE * line + k)
            columns = pl.ds(pl.multiple_of(target * width, LANES), width)
            piece = jnp.dot(rank_rows, expand_ref[:, columns], preferred_element_type=jnp.float32)
            piece = piece.astype(jnp.bfloat16)
            for part in range(parts):
                first = (line * parts + part) * blocks
                lanes = piece[:, part * LANES : (part + 1) * LANES]
                out_refs[k][first : first + blocks] = lanes.reshape(blocks, BLOCK, LANES)


def adapter_output(gathered, shrink, expand, group, me, ranks):
    rank = shrink.shape[0]
    model_width = expand.shape[1]
    depth = gathered.shape[2]
    parts = model_width // group // LANES
    held = (model_width // PLANE // LANES * (MOST // BLOCK), BLOCK, LANES)
    vmem = pl.BlockSpec(memory_space=pltpu.VMEM)
    return pl.pallas_call(
        functools.partial(adapter_kernel, parts, ranks),
        out_shape=[jax.ShapeDtypeStruct(held, jnp.bfloat16)] * PLANE,
        in_specs=[
            pl.BlockSpec(memory_space=pltpu.SMEM),
            vmem,
            pl.BlockSpec(memory_space=pl.ANY),
            pl.BlockSpec(memory_space=pl.ANY),
        ],
        out_specs=[vmem] * PLANE,
        scratch_shapes=[
            pltpu.VMEM((group // 2, rank, 2 * depth), jnp.bfloat16),
            pltpu.VMEM((rank, model_width), jnp.bfloat16),
            pltpu.VMEM((group // 2, HELD, 2 * depth), jnp.bfloat16),
            pltpu.SemaphoreType.DMA((group // 2,)),
            pltpu.SemaphoreType.DMA,
        ],
        compiler_params=pltpu.CompilerParams(vmem_limit_bytes=24 * 2**20),
    )(me.reshape(1), gathered, in_hbm(expand), in_hbm(shrink))


def merge_kernel(pair_ref, pick_ref, *refs):
    in_refs, out_ref, held_ref = refs[:PLANE], refs[PLANE], refs[PLANE + 1]
    blocks = MOST // BLOCK
    held_ref[...] = jnp.zeros_like(held_ref)
    pick = pick_ref[...]
    for part in range(pair_ref.shape[0]):
        for k in range(PLANE):
            rows = in_refs[k][part * blocks : (part + 1) * blocks].reshape(MOST, LANES)
            held_ref[part, k * HELD : k * HELD + MOST] = rows
        adapter_rows = lax.dot_general(
            pick, held_ref[part], (((0,), (0,)), ((), ())), preferred_element_type=jnp.float32
        )
        out_ref[part] = pair_ref[part] + ADAPTER_SCALE * adapter_rows


def merge_adapters(pair, pick, arrived):
    vmem = pl.BlockSpec(memory_space=pltpu.VMEM)
    return pl.pallas_call(
        merge_kernel,
        out_shape=jax.ShapeDtypeStruct(pair.shape, jnp.float32),
        in_specs=[vmem] * (2 + PLANE),
        out_specs=vmem,
        scratch_shapes=[pltpu.VMEM((pair.shape[0], PLANE * HELD, LANES), jnp.bfloat16)],
        compiler_params=pltpu.CompilerParams(vmem_limit_bytes=24 * 2**20),
    )(pair, pick, *arrived)


def shards_by_blocks(
    hidden, down_matrix, shrink_matrices, expand_matrices, adapter_of_row, adapter_holder_slot
):
    group = lax.axis_size("tp")
    me = lax.axis_index("tp")
    rows, depth = hidden.shape
    width = down_matrix.shape[1] // group
    quads = list(range(0, group, 4))
    orders = [q + k for k in (3, 2, 1, 0) for q in quads]
    half = group // 2
    ranks = [i % half // 2 * PLANE + i // half * 2 + i % 2 for i in range(group)]
    packed, pick, order = pack_rows(
        hidden, adapter_of_row, adapter_holder_slot, me, orders
    )
    gathered = lax.all_to_all(
        packed, "tp", split_axis=0, concat_axis=0, axis_index_groups=[ranks], tiled=True
    )
    shrink = jnp.swapaxes(shrink_matrices, 1, 2)[0]
    kept, pair_in = pair_sums(hidden, down_matrix, group, order, width)
    gathered, _ = lax.optimization_barrier((gathered, kept))
    expand = jnp.swapaxes(expand_matrices, 1, 2)[0]
    outs = adapter_output(gathered, shrink, expand, group, me, ranks)
    across = [xor_permute(outs[k], group, k) for k in range(2, PLANE)]
    beside, _ = lax.optimization_barrier((outs[1], across[0]))
    arrived = [outs[0], xor_permute(beside, group, 1)] + across
    pair = kept + unpack_scaled(pair_in, rows)
    merged = merge_adapters(pair, pick, arrived)
    return line_sums(merged, group, width).astype(jnp.bfloat16)


def shards(
    hidden, down_matrix, shrink_matrices, expand_matrices, adapter_of_row, adapter_holder_slot
):
    group = lax.axis_size("tp")
    rows, depth = hidden.shape
    width = down_matrix.shape[1] // group
    if width % LANES == 0 and depth % LANES == 0 and rows <= LANES and group >= PLANE and group & (group - 1) == 0:
        return shards_by_blocks(
            hidden, down_matrix, shrink_matrices, expand_matrices, adapter_of_row, adapter_holder_slot
        )
    blocks = MOST // BLOCK
    adapter_ids = jnp.arange(group, dtype=jnp.int32)
    row_match = adapter_of_row[:, None] == adapter_ids[None, :]
    row_slot = jnp.sum(jnp.where(row_match, adapter_holder_slot[None, :], 0), axis=1)
    slot_mask = row_slot[None, :] == adapter_ids[:, None]
    before = jnp.cumsum(slot_mask.astype(jnp.int32), axis=1) - 1
    place = jnp.where(slot_mask, before, -1)
    pick = place[:, None, :] == jnp.arange(MOST, dtype=jnp.int32)[None, :, None]
    pick = pick.reshape(group * MOST, rows).astype(jnp.bfloat16)
    packed = jnp.dot(pick, hidden, preferred_element_type=jnp.float32).astype(jnp.bfloat16)
    packed = packed.reshape(group * blocks, BLOCK, depth)
    gathered = lax.all_to_all(packed, "tp", split_axis=0, concat_axis=0, tiled=True)
    partial_value = jnp.dot(hidden, down_matrix, preferred_element_type=jnp.float32)
    base = lax.psum_scatter(partial_value, "tp", scatter_dimension=1, tiled=True)
    own_rows = jnp.transpose(gathered.reshape(group, MOST, depth), (1, 0, 2))
    rank_rows = jnp.dot(
        own_rows.reshape(MOST, group * depth), shrink_matrices[0], preferred_element_type=jnp.float32
    ).astype(jnp.bfloat16)
    adapter_out = lax.dot_general(
        rank_rows, expand_matrices[0], (((1,), (1,)), ((), ())), preferred_element_type=jnp.float32
    ).astype(jnp.bfloat16)
    adapter_out = jnp.transpose(adapter_out.reshape(blocks, BLOCK, group, width), (2, 0, 1, 3))
    adapter_in = lax.all_to_all(
        adapter_out.reshape(group * blocks, BLOCK, width), "tp", split_axis=0, concat_axis=0, tiled=True
    )
    adapter_rows = lax.dot_general(
        pick,
        adapter_in.reshape(group * MOST, width),
        (((0,), (0,)), ((), ())),
        preferred_element_type=jnp.float32,
    )
    return (base + ADAPTER_SCALE * adapter_rows).astype(jnp.bfloat16)


def solution(mesh):
    in_specs = (
        P("rep", "tp"),
        P("tp", None),
        P(("rep", "tp"), None, None),
        P(("rep", "tp"), None, None),
        P("rep"),
        P("rep"),
    )
    out_specs = P("rep", "tp")
    return jax.shard_map(shards, mesh=mesh, in_specs=in_specs, out_specs=out_specs, check_vma=False)
```
